32 devices in a mesh: dp: 16 (over z, y, core), blk: 2 (over x).
Axes of the slice: x: 2, y: 2, z: 4, core: 2. Of those that a mesh axis runs over, the one named last changes fastest.
Arguments:
- resid: bfloat16 [512, 2048], P('dp'), may hold values from -40 to 40
- queries: bfloat16 [512, 16, 128], P('dp', 'blk'), may hold values from -60 to 60
- new_kv: bfloat16 [512, 2, 8, 128], P('dp', None, 'blk'), may hold values from -6 to 6
- prefix_pool: bfloat16 [512, 128, 2, 8, 128], P('dp', None, None, 'blk'), may hold values from -6 to 6
- page_table: int32 [16, 32], P('dp'), may hold values from 0 to 31, each once within a row
- prompt_len: int32 [16], P('dp'), may hold values from 1 to 4096, 32768 in all
- tail_pool: bfloat16 [256, 128, 2, 8, 128], P('dp', None, None, 'blk'), may hold values from -6 to 6
- tail_len: int32 [16, 16], P('dp'), may hold values from 1 to 128, 1024 in all within a row
- migration: int32 [256], replicated, may hold values from 0 to 255, each once
- out_w: bfloat16 [2048, 2048], P('blk'), may hold values from -0.125 to 0.125
- mlp_gain: bfloat16 [2048], replicated, may hold values from 0.099609375 to 1.8984375
- gate_w: bfloat16 [2048, 6144], P('blk', 'dp'), may hold values from -0.125 to 0.125
- up_w: bfloat16 [2048, 6144], P('blk', 'dp'), may hold values from -0.125 to 0.125
- down_w: bfloat16 [6144, 2048], P('dp', 'blk'), may hold values from -0.078125 to 0.078125
- final_gain: bfloat16 [2048], P('blk'), may hold values from 0.099609375 to 1.8984375
- score_w: bfloat16 [2048], P('blk'), may hold values from -0.125 to 0.125
Outputs:
- hidden_out: bfloat16 [512, 2048], P('dp', 'blk')
- score: float32 [512], P('dp')
The draws below stay inside these ranges and needn't reach their ends.
Inputs may be any that keep to these rules, and one draw needn't show every extreme that they name: `page_table`: each row lists every page of the device's pool once. `migration`: names every continuation once.
All inputs are finite; a program needn't handle non-finite values. No bound on the sum of `prompt_len` on one device may be relied on, other than what follows from the above.
Results may differ from the reference program's by a relative error of at most 0.012.
Values may be sent and summed in bfloat16 or wider, within the bound.
No kernel may reach another device: no remote copies, remote signals or barrier semaphores. Data moves between devices by JAX's collectives and lax.ppermute only.
A program may use at most 64 MiB of HBM per device.

```python
import math
import jax
import jax.numpy as jnp
import numpy as np
from jax import lax

D = 2048
HQ = 16
KVH = 8
HD = 128
FF = 6144
CONT = 16
NEW = 2
PAGE = 128
PAGES = 32
TAIL = 128
CONTS = 256
TOKENS = 512
N_DP = 16


def fresh_pairs(key):
    raw = jax.random.normal(jax.random.fold_in(key, 11), (CONTS, NEW, 2, KVH, HD), jnp.float32)
    return jnp.clip(raw, -6.0, 6.0)


def draw_new_kv(key, part):
    return fresh_pairs(key).reshape(TOKENS, 2, KVH, HD).astype(jnp.bfloat16)


def draw_queries(key, part):
    base = 2.0 * jax.random.normal(jax.random.fold_in(key, 21), (CONTS, NEW, KVH, HQ // KVH, HD), jnp.float32)
    return jnp.clip(base, -60.0, 60.0).reshape(TOKENS, HQ, HD).astype(jnp.bfloat16)


def draw_resid(key, part):
    place = jnp.arange(D).astype(jnp.float32) / D
    columns = jnp.exp(jax.random.uniform(jax.random.fold_in(key, 31), (D,), jnp.float32, math.log(0.5), math.log(1.5))) * (1.0 + 2.0 * place)
    scales = jnp.exp(jax.random.uniform(jax.random.fold_in(key, 32), (TOKENS, 1), jnp.float32, math.log(0.5), math.log(2.0)))
    raw = jax.random.normal(jax.random.fold_in(key, 33), (TOKENS, D), jnp.float32)
    return jnp.clip(raw * columns * scales, -40.0, 40.0).astype(jnp.bfloat16)


def level_of(key, shape, cuts, least, top_value):
    def one(dim, parts):
        heights = jax.random.uniform(jax.random.fold_in(jax.random.fold_in(key, 6), dim), (parts,), jnp.float32, least / len(cuts), top_value / len(cuts))
        return jnp.repeat(jnp.exp(heights), shape[dim] // parts).reshape((-1,) + (1,) * (len(shape) - dim - 1))

    level = one(*cuts[0])
    for cut in cuts[1:]:
        level = level * one(*cut)
    return level


def length_profile(count, total, reach, slope):
    weights = [(1 << 20) // math.isqrt(standing ** slope) + 1 for standing in range(2, count + 1)]
    surplus, holding = total - reach - (count - 1), [1] * (count - 1)
    while surplus > 0:
        free = [i for i in range(count - 1) if holding[i] < reach]
        whole, budget = sum([weights[i] for i in free]), surplus
        for i in free:
            addition = min(reach - holding[i], max(1, budget * weights[i] // whole), surplus)
            holding[i] = holding[i] + addition
            surplus = surplus - addition
    return np.array([reach] + holding)


def uneven(key, count, total, most, lean):
    if count == 2:
        one = jax.random.randint(key, (), max(1, total - most), min(most, total - 1) + 1)
        return jnp.stack([one, total - one])
    sizes = jnp.asarray(length_profile(count, total, most, lean), jnp.int32)
    couples = (count - 1) // 2
    giver, sink = sizes[1:1 + 2 * couples:2], sizes[2:2 + 2 * couples:2]
    slack = jnp.minimum(giver - 1, most - sink)
    shifted = jax.random.randint(jax.random.fold_in(key, 1), (couples,), 0, 1 << 20) % (slack + 1)
    sizes = sizes.at[1:1 + 2 * couples:2].set(giver - shifted).at[2:2 + 2 * couples:2].set(sink + shifted)
    return sizes[jax.random.permutation(jax.random.fold_in(key, 2), count)]


def gaussian(key, shape, scale, bound, split=(), kind=jnp.bfloat16):
    factor_of = level_of(key, shape, split, -0.22, 0.18) if split else 1.0
    entries = jax.random.normal(key, shape, jnp.float32) * scale * factor_of
    return jnp.minimum(jnp.maximum(entries, -bound), bound).astype(kind)


def setup_inputs(seed: int = 0) -> dict:
    arg_keys = jax.random.split(jax.random.key(seed), 17)
    return {
        "resid": draw_resid(jax.random.fold_in(arg_keys[16], 71), 0),
        "queries": draw_queries(jax.random.fold_in(arg_keys[16], 71), 0),
        "new_kv": draw_new_kv(jax.random.fold_in(arg_keys[16], 71), 0),
        "prefix_pool": gaussian(arg_keys[3], (N_DP * PAGES, PAGE, 2, KVH, HD), 1.0, 6.0, ((0, 16), (3, 2))),
        "page_table": jax.vmap(lambda own: jax.random.permutation(own, PAGES))(jax.random.split(arg_keys[4], N_DP)).reshape((N_DP, PAGES)).astype(jnp.int32),
        "prompt_len": uneven(arg_keys[5], N_DP, N_DP * PAGES * PAGE // 2, PAGES * PAGE, 2).astype(jnp.int32),
        "tail_pool": gaussian(arg_keys[6], (CONTS, TAIL, 2, KVH, HD), 1.0, 6.0, ((0, 16), (3, 2))),
        "tail_len": jax.vmap(lambda own: uneven(own, CONT, CONT * TAIL // 2, TAIL, 2))(jax.random.split(arg_keys[7], N_DP)).reshape((N_DP, CONT)).astype(jnp.int32),
        "migration": jax.random.permutation(arg_keys[8], CONTS).astype(jnp.int32),
        "out_w": gaussian(arg_keys[9], (HQ * HD, D), (HQ * HD) ** -0.5, 0.125, ((0, 2),)),
        "mlp_gain": jnp.clip(1.0 + 0.18 * jax.random.normal(arg_keys[10], (D,), jnp.float32), 0.099609375, 1.8984375).astype(jnp.bfloat16),
        "gate_w": gaussian(arg_keys[11], (D, FF), D ** -0.5, 0.125, ((0, 2), (1, 16))),
        "up_w": gaussian(arg_keys[12], (D, FF), D ** -0.5, 0.125, ((0, 2), (1, 16))),
        "down_w": gaussian(arg_keys[13], (FF, D), FF ** -0.5, 0.078125, ((0, 16), (1, 2))),
        "final_gain": jnp.clip(1.0 + 0.18 * jax.random.normal(arg_keys[14], (D,), jnp.float32), 0.099609375, 1.8984375).astype(jnp.bfloat16),
        "score_w": gaussian(arg_keys[15], (D,), D ** -0.5, 0.125, ((0, 2),)),
    }


NEG = -1e+30
EPS = 1e-06

def attend_prompt(queries, pool, table, prompt_len, tails, tail_len, pairs):
    token_rows, heads, width = queries.shape
    groups = pairs.shape[2]
    repeat = heads // groups
    conts = tails.shape[0]
    fresh = token_rows // conts
    prefix = jnp.take(pool, table, axis=0).reshape(-1, 2, groups, width).astype(jnp.float32)
    span = prefix.shape[0]
    grouped = queries.reshape(conts, fresh, groups, repeat, width).astype(jnp.float32)
    recent = pairs.reshape(conts, fresh, 2, groups, width).astype(jnp.float32)
    tail_vals = tails.astype(jnp.float32)
    factor = 1.0 / math.sqrt(width)
    pre_scores = jnp.einsum('cngrd,pgd->gcnrp', grouped, prefix[:, 0]) * factor
    tail_scores = jnp.einsum('cngrd,ctgd->gcnrt', grouped, tail_vals[:, :, 0]) * factor
    new_scores = jnp.einsum('cngrd,cmgd->gcnrm', grouped, recent[:, :, 0]) * factor
    pre_mask = (jnp.arange(span) < prompt_len)[None, None, None, None, :]
    tail_mask = (jnp.arange(tails.shape[1])[None, :] < tail_len[:, None])[None, :, None, None, :]
    new_mask = (jnp.arange(fresh)[None, :] <= jnp.arange(fresh)[:, None])[None, None, :, None, :]
    pre_scores = jnp.where(pre_mask, pre_scores, NEG)
    tail_scores = jnp.where(tail_mask, tail_scores, NEG)
    new_scores = jnp.where(new_mask, new_scores, NEG)
    highest = jnp.maximum(jnp.maximum(lax.optimization_barrier(jnp.max(pre_scores, -1)), lax.optimization_barrier(jnp.max(tail_scores, -1))), lax.optimization_barrier(jnp.max(new_scores, -1)))[..., None]
    pre_weights = jnp.where(pre_mask, jnp.exp(pre_scores - highest), 0.0)
    tail_weights = jnp.where(tail_mask, jnp.exp(tail_scores - highest), 0.0)
    new_weights = jnp.where(new_mask, jnp.exp(new_scores - highest), 0.0)
    total = lax.optimization_barrier(jnp.sum(pre_weights, -1)) + lax.optimization_barrier(jnp.sum(tail_weights, -1)) + lax.optimization_barrier(jnp.sum(new_weights, -1))
    pre_round = lax.optimization_barrier(pre_weights.astype(jnp.bfloat16)).astype(jnp.float32)
    tail_round = lax.optimization_barrier(tail_weights.astype(jnp.bfloat16)).astype(jnp.float32)
    new_round = lax.optimization_barrier(new_weights.astype(jnp.bfloat16)).astype(jnp.float32)
    mixed = jnp.einsum('gcnrp,pgd->cngrd', pre_round, prefix[:, 1])
    mixed = mixed + jnp.einsum('gcnrt,ctgd->cngrd', tail_round, tail_vals[:, :, 1])
    mixed = mixed + jnp.einsum('gcnrm,cmgd->cngrd', new_round, recent[:, :, 1])
    mixed = mixed / jnp.transpose(total, (1, 2, 0, 3))[..., None]
    return mixed.reshape(token_rows, heads * width).astype(jnp.bfloat16)

def reference(resid, queries, new_kv, prefix_pool, page_table, prompt_len, tail_pool, tail_len, migration, out_w, mlp_gain, gate_w, up_w, down_w, final_gain, score_w):
    per_dev = CONT * NEW
    grouped = queries.reshape(N_DP, per_dev, HQ, HD)
    pools = prefix_pool.reshape(N_DP, PAGES, PAGE, 2, KVH, HD)
    tails = tail_pool.reshape(N_DP, CONT, TAIL, 2, KVH, HD)
    pairs = new_kv.reshape(N_DP, per_dev, 2, KVH, HD)

    def one_prompt(items):
        return attend_prompt(items[0], items[1], items[2], items[3], items[4], items[5], items[6])
    attn = lax.map(one_prompt, (grouped, pools, page_table, prompt_len, tails, tail_len, pairs))
    attn = attn.reshape(TOKENS, HQ * HD)
    mid = resid.astype(jnp.float32) + jnp.dot(attn, out_w, preferred_element_type=jnp.float32)
    normed = (mid * lax.rsqrt(lax.optimization_barrier(jnp.mean(mid * mid, -1, keepdims=True)) + EPS) * mlp_gain.astype(jnp.float32)).astype(jnp.bfloat16)
    gate = jnp.dot(normed, gate_w, preferred_element_type=jnp.float32)
    upper = jnp.dot(normed, up_w, preferred_element_type=jnp.float32)
    hidden = (jax.nn.silu(gate) * upper).astype(jnp.bfloat16)
    after = mid + jnp.dot(hidden, down_w, preferred_element_type=jnp.float32)
    moved = after.reshape(CONTS, NEW, D)[migration].reshape(TOKENS, D)
    weighted = final_gain.astype(jnp.float32) * score_w.astype(jnp.float32)
    score = lax.optimization_barrier(jnp.sum(moved * weighted, -1)) * lax.rsqrt(lax.optimization_barrier(jnp.mean(moved * moved, -1)) + EPS)
    return (moved.astype(jnp.bfloat16), score)
```

```python
import functools
import math

import jax
import jax.numpy as jnp
from jax import lax
from jax.experimental import pallas as pl
from jax.experimental.pallas import tpu as pltpu
from jax.sharding import PartitionSpec as P

D = 2048
NEW = 2
NEG = -1e30
EPS = 1e-06
MIB = 1 << 20

VMEM = pl.BlockSpec(memory_space=pltpu.VMEM)
SMEM = pl.BlockSpec(memory_space=pltpu.SMEM)
ANY = pl.BlockSpec(memory_space=pl.ANY)


def mm(a, b):
    return jnp.dot(a, b, preferred_element_type=jnp.float32)


def mm_t(a, b):
    return lax.dot_general(a, b, (((1,), (1,)), ((), ())), preferred_element_type=jnp.float32)


def attention_kernel(
    dims,
    table,
    prompt_len,
    tail_len,
    q_ref,
    new_ref,
    pool,
    tails,
    out_w,
    own_ref,
    send_ref,
    pages,
    tail_buf,
    w_buf,
    wide,
    q_wide,
    q_rows,
    new_wide,
    top,
    total,
    acc,
    attn,
    page_sems,
    tail_sems,
    w_sem,
):
    rows, heads, groups, width, n_pages, page, conts, tail = dims
    repeat = heads // groups
    step = 2 * groups
    page_rows = page * step
    chunk_pages = min(4, n_pages)
    chunk = chunk_pages * page
    chunk_rows = chunk * step
    quad = 8 // NEW
    quads = conts // quad
    quad_rows = quad * tail * step
    factor = math.log2(math.e) / math.sqrt(width)
    length = prompt_len[0]
    chunks = (length + chunk - 1) // chunk

    def page_copy(logical):
        physical = table[logical]
        return pltpu.make_async_copy(
            pool.at[pl.ds(pl.multiple_of(physical * page_rows, page_rows), page_rows), :],
            pages.at[pl.ds(pl.multiple_of(logical * page_rows, page_rows), page_rows), :],
            page_sems.at[logical],
        )

    def tail_copy(index):
        return pltpu.make_async_copy(
            tails.at[pl.ds(index * quad_rows, quad_rows), :],
            tail_buf.at[pl.ds(index * quad_rows, quad_rows), :],
            tail_sems.at[index],
        )

    w_copy = pltpu.make_async_copy(out_w, w_buf, w_sem)
    for index in range(quads):
        tail_copy(index).start()

    @pl.loop(0, chunks * chunk_pages)
    def _(logical):
        page_copy(logical).start()

    w_copy.start()

    q_wide[...] = q_ref[...].astype(jnp.float32)
    new_wide[...] = new_ref[...].astype(jnp.float32)
    row = lax.broadcasted_iota(jnp.int32, (rows, rows), 0)
    key = lax.broadcasted_iota(jnp.int32, (rows, rows), 1)
    fresh_ok = (row // NEW == key // NEW) & (key <= row)
    fresh_ok = jnp.concatenate([fresh_ok] * repeat, axis=0)
    for g in range(groups):
        for r in range(repeat):
            q_rows[g, r * rows : (r + 1) * rows, :] = q_wide[
                pl.ds(g * repeat + r, rows, stride=heads), :
            ]
        k = new_wide[pl.ds(g, rows, stride=step), :].astype(jnp.bfloat16)
        v = new_wide[pl.ds(groups + g, rows, stride=step), :].astype(jnp.bfloat16)
        s = mm_t(q_rows[g].astype(jnp.bfloat16), k) * factor
        s = jnp.where(fresh_ok, s, NEG)
        high = jnp.max(s, axis=1, keepdims=True)
        p = jnp.exp2(s - high)
        top[g] = jnp.broadcast_to(high, top.shape[1:])
        total[g] = jnp.broadcast_to(jnp.sum(p, axis=1, keepdims=True), total.shape[1:])
        acc[g] = mm(p.astype(jnp.bfloat16), v)

    quad_row = lax.broadcasted_iota(jnp.int32, (8, quad * tail), 0)
    quad_key = lax.broadcasted_iota(jnp.int32, (8, quad * tail), 1)
    for index in range(quads):
        tail_copy(index).wait()
        wide[0:quad_rows, :] = tail_buf[pl.ds(index * quad_rows, quad_rows), :].astype(jnp.float32)
        reach = jnp.zeros((8, quad * tail), jnp.int32)
        for c in range(quad):
            reach = jnp.where(quad_key // tail == c, tail_len[index * quad + c] + c * tail, reach)
        ok = (quad_row // NEW == quad_key // tail) & (quad_key < reach)
        ok = jnp.concatenate([ok] * repeat, axis=0)
        for g in range(groups):
            k = wide[pl.ds(g, quad * tail, stride=step), :].astype(jnp.bfloat16)
            v = wide[pl.ds(groups + g, quad * tail, stride=step), :].astype(jnp.bfloat16)
            at = [slice(r * rows + index * 8, r * rows + index * 8 + 8) for r in range(repeat)]
            q = jnp.concatenate([q_rows[g, a, :] for a in at], axis=0).astype(jnp.bfloat16)
            s = jnp.where(ok, mm_t(q, k) * factor, NEG)
            old = jnp.concatenate([top[g, a, 0:1] for a in at], axis=0)
            high = jnp.maximum(old, jnp.max(s, axis=1, keepdims=True))
            keep = jnp.exp2(old - high)
            p = jnp.exp2(s - high)
            added = jnp.sum(p, axis=1, keepdims=True)
            value = mm(p.astype(jnp.bfloat16), v)
            for r, a in enumerate(at):
                part = slice(r * 8, r * 8 + 8)
                top[g, a, :] = jnp.broadcast_to(high[part], (8, top.shape[2]))
                total[g, a, :] = total[g, a, :] * keep[part] + added[part]
                acc[g, a, :] = acc[g, a, :] * keep[part] + value[part]

    place = lax.broadcasted_iota(jnp.int32, (repeat * rows, chunk), 1)

    @pl.loop(0, chunks)
    def _(index):
        for i in range(chunk_pages):
            page_copy(index * chunk_pages + i).wait()
        start = pl.multiple_of(index * chunk_rows, chunk_rows)
        wide[0:chunk_rows, :] = pages[pl.ds(start, chunk_rows), :].astype(jnp.float32)
        ok = place < length - index * chunk
        for g in range(groups):
            k = wide[pl.ds(g, chunk, stride=step), :].astype(jnp.bfloat16)
            v = wide[pl.ds(groups + g, chunk, stride=step), :].astype(jnp.bfloat16)
            s = jnp.where(ok, mm_t(q_rows[g].astype(jnp.bfloat16), k) * factor, NEG)
            old = top[g, :, 0:1]
            high = jnp.maximum(old, jnp.max(s, axis=1, keepdims=True))
            keep = jnp.exp2(old - high)
            p = jnp.exp2(s - high)
            top[g] = jnp.broadcast_to(high, top.shape[1:])
            total[g] = total[g] * keep + jnp.sum(p, axis=1, keepdims=True)
            acc[g] = acc[g] * keep + mm(p.astype(jnp.bfloat16), v)

    for g in range(groups):
        out = (acc[g] / total[g]).astype(jnp.bfloat16)
        for r in range(repeat):
            head = g * repeat + r
            attn[:, head * width : (head + 1) * width] = out[r * rows : (r + 1) * rows]
    w_copy.wait()
    value = mm(attn[...], w_buf[...])
    own_ref[...] = value
    send_ref[...] = value.astype(jnp.bfloat16)


def attention(queries, new_kv, pool, table, prompt_len, tails, tail_len, out_w):
    rows, heads, width = queries.shape
    n_pages, page, _, groups, _ = pool.shape
    conts, tail = tails.shape[:2]
    step = 2 * groups
    features = out_w.shape[1]
    chunk_rows = max(min(4, n_pages) * page, (8 // NEW) * tail) * step
    stack = (heads // groups) * rows
    return pl.pallas_call(
        functools.partial(
            attention_kernel, (rows, heads, groups, width, n_pages, page, conts, tail)
        ),
        out_shape=(
            jax.ShapeDtypeStruct((rows, features), jnp.float32),
            jax.ShapeDtypeStruct((rows, features), jnp.bfloat16),
        ),
        in_specs=[SMEM, SMEM, SMEM, VMEM, VMEM, ANY, ANY, ANY],
        out_specs=(VMEM, VMEM),
        scratch_shapes=[
            pltpu.VMEM((n_pages * page * step, width), jnp.bfloat16),
            pltpu.VMEM((conts * tail * step, width), jnp.bfloat16),
            pltpu.VMEM(out_w.shape, jnp.bfloat16),
            pltpu.VMEM((chunk_rows, width), jnp.float32),
            pltpu.VMEM((rows * heads, width), jnp.float32),
            pltpu.VMEM((groups, stack, width), jnp.float32),
            pltpu.VMEM((rows * step, width), jnp.float32),
            pltpu.VMEM((groups, stack, 128), jnp.float32),
            pltpu.VMEM((groups, stack, 128), jnp.float32),
            pltpu.VMEM((groups, stack, width), jnp.float32),
            pltpu.VMEM((rows, heads * width), jnp.bfloat16),
            pltpu.SemaphoreType.DMA((n_pages,)),
            pltpu.SemaphoreType.DMA((conts * NEW // 8,)),
            pltpu.SemaphoreType.DMA,
        ],
        compiler_params=pltpu.CompilerParams(vmem_limit_bytes=40 * MIB),
        name="attention",
    )(
        table,
        prompt_len,
        tail_len,
        queries.reshape(rows * heads, width),
        new_kv.reshape(rows * step, width),
        pool.reshape(n_pages * page * step, width),
        tails.reshape(conts * tail * step, width),
        out_w,
    )


def norm_kernel(place, own, other, resid, gain, normed, middle, whole):
    features = normed.shape[1]
    mid = resid[...].astype(jnp.float32) + (own[...] + other[...].astype(jnp.float32))
    scale = lax.rsqrt(jnp.mean(mid * mid, axis=1, keepdims=True) + EPS)
    whole[...] = mid
    start = pl.multiple_of(place[0] * features, features)
    part = whole[:, pl.ds(start, features)]
    normed[...] = (part * scale * gain[:, pl.ds(start, features)]).astype(jnp.bfloat16)
    middle[...] = part


def normalize(block, own, other, resid, gain, features):
    rows = resid.shape[0]
    return pl.pallas_call(
        norm_kernel,
        out_shape=(
            jax.ShapeDtypeStruct((rows, features), jnp.bfloat16),
            jax.ShapeDtypeStruct((rows, features), jnp.float32),
        ),
        in_specs=[SMEM, VMEM, VMEM, VMEM, VMEM],
        out_specs=(VMEM, VMEM),
        scratch_shapes=[pltpu.VMEM(resid.shape, jnp.float32)],
        name="normalize",
    )(block, own, other, resid, gain.astype(jnp.float32).reshape(1, -1))


def units_kernel(n, *refs):
    pieces, gate_w, up_w, out, held = refs[:n], *refs[n:]
    at = 0
    for piece in pieces:
        held[at : at + piece.shape[0], :] = piece[...]
        at += piece.shape[0]
    units = gate_w.shape[1]
    out[:, :units] = mm(held[...], gate_w[...]).astype(jnp.bfloat16)
    out[:, units:] = mm(held[...], up_w[...]).astype(jnp.bfloat16)


def partial_units(pieces, gate_w, up_w):
    tokens = sum(piece.shape[0] for piece in pieces)
    features, units = gate_w.shape
    return pl.pallas_call(
        functools.partial(units_kernel, len(pieces)),
        out_shape=jax.ShapeDtypeStruct((tokens, 2 * units), jnp.bfloat16),
        in_specs=[VMEM] * (len(pieces) + 2),
        out_specs=VMEM,
        scratch_shapes=[pltpu.VMEM((tokens, features), jnp.bfloat16)],
        compiler_params=pltpu.CompilerParams(vmem_limit_bytes=32 * MIB),
        name="gate_up",
    )(*pieces, gate_w, up_w)


def down_kernel(split, place, own, other, source, middle, down_w, *refs):
    term = refs[-1]
    tokens, features = term.shape
    units = down_w.shape[0]
    rows = middle.shape[0]
    home = place[0]
    both = own[...].astype(jnp.float32) + other[...].astype(jnp.float32)
    gate, up = both[:, :units], both[:, units:]
    hidden = (gate / (1.0 + jnp.exp(-gate)) * up).astype(jnp.bfloat16)
    token = source[...]
    slot = token ^ place[1]
    pick = (lax.broadcasted_iota(jnp.int32, (tokens, tokens), 1) == slot).astype(jnp.bfloat16)
    moved = mm(pick, hidden).astype(jnp.bfloat16)
    mine = lax.broadcasted_iota(jnp.int32, (tokens, rows), 1) == token - home * rows
    mine = mine.astype(jnp.bfloat16)
    high = middle[...].astype(jnp.bfloat16)
    low = (middle[...] - high.astype(jnp.float32)).astype(jnp.bfloat16)
    term[...] = mm(moved, down_w[...]) + (mm(mine, high) + mm(mine, low))
    if not split:
        refs[0][...] = term[...]
        return
    keep, send = refs[0], refs[1]
    for index in range(tokens // rows // 2):
        for ref, offset in ((keep, 0), (send, 1)):
            dest = home ^ (2 * index + offset)
            block = term[pl.ds(pl.multiple_of(dest * rows, rows), rows), :]
            ref[index * rows : (index + 1) * rows, :] = block.astype(ref.dtype)


def down(split, place, own, other, source, middle, down_w):
    tokens = own.shape[0]
    features = down_w.shape[1]
    if split:
        out_shape = (
            jax.ShapeDtypeStruct((tokens // 2, features), jnp.float32),
            jax.ShapeDtypeStruct((tokens // 2, features), jnp.bfloat16),
        )
    else:
        out_shape = (jax.ShapeDtypeStruct((tokens, features), jnp.float32),)
    return pl.pallas_call(
        functools.partial(down_kernel, split),
        out_shape=out_shape,
        in_specs=[SMEM] + [VMEM] * 5,
        out_specs=(VMEM,) * len(out_shape),
        scratch_shapes=[pltpu.VMEM((tokens, features), jnp.float32)],
        compiler_params=pltpu.CompilerParams(vmem_limit_bytes=48 * MIB),
        name="down",
    )(place, own, other, source, middle, down_w)


def add_kernel(keep, other, *outs):
    rows = outs[0].shape[0]
    for index, out in enumerate(outs):
        at = slice(index * rows, (index + 1) * rows)
        out[...] = (keep[at, :] + other[at, :].astype(jnp.float32)).astype(out.dtype)


def add_parts(keep, other, rows):
    count = keep.shape[0] // rows
    features = keep.shape[1]
    return pl.pallas_call(
        add_kernel,
        out_shape=tuple(
            jax.ShapeDtypeStruct((rows, features), jnp.bfloat16 if i else jnp.float32)
            for i in range(count)
        ),
        in_specs=[VMEM, VMEM],
        out_specs=(VMEM,) * count,
        name="add_parts",
    )(keep, other)


def shards(
    n_dp,
    n_blk,
    resid,
    queries,
    new_kv,
    prefix_pool,
    page_table,
    prompt_len,
    tail_pool,
    tail_len,
    migration,
    out_w,
    mlp_gain,
    gate_w,
    up_w,
    down_w,
    final_gain,
    score_w,
):
    rows = resid.shape[0]
    features = gate_w.shape[0]
    home = lax.axis_index("dp").astype(jnp.int32)
    block = lax.axis_index("blk").astype(jnp.int32).reshape(1)
    paired = n_blk == 2
    near = n_dp <= 16 and n_dp & (n_dp - 1) == 0 and n_dp > 1 and rows & (rows - 1) == 0

    def swap_blk(value):
        return lax.ppermute(value, "blk", [(0, 1), (1, 0)])

    def swap_dp(value, index):
        return lax.ppermute(value, "dp", [(i, i ^ index) for i in range(n_dp)])

    own, send = attention(
        queries,
        new_kv,
        prefix_pool,
        page_table.reshape(-1),
        prompt_len,
        tail_pool,
        tail_len.reshape(-1),
        out_w,
    )
    if paired:
        other = swap_blk(send)
    else:
        own, other = jnp.zeros_like(own), lax.psum(send, "blk")
    normed, middle = normalize(block, own, other, resid, mlp_gain, features)

    if near:
        same = [normed] + [swap_dp(normed, index) for index in range(2, n_dp, 2)]
        cross = [swap_dp(piece, 1) for piece in same]
        pieces = [piece for pair in zip(same, cross) for piece in pair]
        flip = home * rows
    else:
        pieces = [lax.all_gather(normed, "dp", axis=0, tiled=True)]
        flip = jnp.zeros_like(home)
    units = partial_units(pieces, gate_w, up_w)
    if paired:
        other_units = swap_blk(units)
    else:
        units, other_units = jnp.zeros_like(units), lax.psum(units, "blk")

    source = migration[:, None] * NEW + jnp.arange(NEW, dtype=jnp.int32)[None, :]
    source = source.reshape(-1, 1)
    place = jnp.stack([home, flip])
    terms = down(near, place, units, other_units, source, middle, down_w)
    if near:
        keep, away = terms
        parts = add_parts(keep, swap_dp(away, 1), rows)
        moved = parts[0]
        for index in range(1, n_dp // 2):
            moved = moved + swap_dp(parts[index], 2 * index).astype(jnp.float32)
    else:
        moved = lax.psum_scatter(terms[0], "dp", scatter_dimension=0, tiled=True)
    weighted = final_gain.astype(jnp.float32) * score_w.astype(jnp.float32)
    stats = jnp.stack([jnp.sum(moved * moved, -1), jnp.sum(moved * weighted, -1)])
    stats = stats + swap_blk(stats) if paired else lax.psum(stats, "blk")
    score = stats[1] * lax.rsqrt(stats[0] / D + EPS)
    return (moved.astype(jnp.bfloat16), score)


def solution(mesh):
    return jax.shard_map(
        functools.partial(shards, mesh.shape["dp"], mesh.shape["blk"]),
        mesh=mesh,
        in_specs=(
            P("dp", None),
            P("dp", "blk", None),
            P("dp", None, "blk", None),
            P("dp", None, None, "blk", None),
            P("dp", None),
            P("dp"),
            P("dp", None, None, "blk", None),
            P("dp", None),
            P(),
            P("blk", None),
            P(),
            P("blk", "dp"),
            P("blk", "dp"),
            P("dp", "blk"),
            P("blk"),
            P("blk"),
        ),
        out_specs=(P("dp", "blk"), P("dp")),
        check_vma=False,
    )
```

```python
import functools
import math

import jax
import jax.numpy as jnp
from jax import lax
from jax.experimental import pallas as pl
from jax.experimental.pallas import tpu as pltpu
from jax.sharding import Mesh
from jax.sharding import PartitionSpec as P

D = 2048
NEW = 2
NEG = -1e30
EPS = 1e-06
MIB = 1 << 20
ATTENTION_VMEM = 60 * MIB

VMEM = pl.BlockSpec(memory_space=pltpu.VMEM)
SMEM = pl.BlockSpec(memory_space=pltpu.SMEM)
ANY = pl.BlockSpec(memory_space=pl.ANY)


def mm(a, b):
    return jnp.dot(a, b, preferred_element_type=jnp.float32)


def mm_t(a, b):
    return lax.dot_general(a, b, (((1,), (1,)), ((), ())), preferred_element_type=jnp.float32)


def attention_kernel(
    dims,
    table,
    prompt_len,
    tail_len,
    queries,
    new_kv,
    resid,
    pool,
    tails,
    out_w,
    own_ref,
    send_ref,
    pages,
    tail_buf,
    w_buf,
    q_buf,
    new_buf,
    resid_buf,
    apart,
    q_wide,
    q_rows,
    new_wide,
    top,
    total,
    acc,
    attn,
    page_sems,
    tail_sems,
    sems,
):
    rows, heads, groups, width, n_pages, page, conts, tail = dims
    repeat = heads // groups
    step = 2 * groups
    page_rows = page * step
    chunk_pages = min(4, n_pages)
    chunk = chunk_pages * page
    chunk_rows = chunk * step
    quad = 8 // NEW
    quads = conts // quad
    quad_keys = quad * tail
    quad_rows = quad_keys * step
    factor = math.log2(math.e) / math.sqrt(width)
    length = prompt_len[0]
    chunks = (length + chunk - 1) // chunk

    def page_copy(logical):
        physical = table[0, logical]
        return pltpu.make_async_copy(
            pool.at[pl.ds(pl.multiple_of(physical * page_rows, page_rows), page_rows), :],
            pages.at[pl.ds(pl.multiple_of(logical * page_rows, page_rows), page_rows), :],
            page_sems.at[logical],
        )

    def tail_copy(index):
        return pltpu.make_async_copy(
            tails.at[pl.ds(index * quad_rows, quad_rows), :],
            tail_buf.at[pl.ds(index * quad_rows, quad_rows), :],
            tail_sems.at[index],
        )

    q_copy = pltpu.make_async_copy(queries, q_buf, sems.at[0])
    new_copy = pltpu.make_async_copy(new_kv, new_buf, sems.at[1])
    w_copy = pltpu.make_async_copy(out_w, w_buf, sems.at[2])
    resid_copy = pltpu.make_async_copy(resid, resid_buf, sems.at[3])
    q_copy.start()
    new_copy.start()
    for index in range(quads):
        tail_copy(index).start()

    @pl.loop(0, chunks * chunk_pages)
    def _(logical):
        page_copy(logical).start()

    w_copy.start()
    resid_copy.start()

    block = 256
    tokens = block // step
    to = lax.broadcasted_iota(jnp.int32, (block, block), 0)
    came = lax.broadcasted_iota(jnp.int32, (block, block), 1)
    sort = (came == (to % tokens) * step + to // tokens).astype(jnp.bfloat16)

    def take_apart(buf, start, count):
        for pair in range(count // (2 * block)):
            at = start + pair * 2 * block
            x = jnp.concatenate([buf[pl.ds(at, block), :], buf[pl.ds(at + block, block), :]], 1)
            y = mm(sort, x).astype(jnp.bfloat16)
            for side in range(2):
                t = (2 * pair + side) * tokens
                for j in range(step):
                    apart[j, t : t + tokens, :] = y[
                        j * tokens : (j + 1) * tokens, side * width : (side + 1) * width
                    ]

    def lanes(p):
        out = p[:, :128]
        for i in range(1, p.shape[1] // 128):
            out = out + p[:, i * 128 : (i + 1) * 128]
        return out

    q_copy.wait()
    new_copy.wait()
    q_wide[...] = q_buf[...].astype(jnp.float32)
    new_wide[...] = new_buf[...].astype(jnp.float32)
    row = lax.broadcasted_iota(jnp.int32, (rows, rows), 0)
    key = lax.broadcasted_iota(jnp.int32, (rows, rows), 1)
    fresh_ok = (row // NEW == key // NEW) & (key <= row)
    fresh_ok = jnp.concatenate([fresh_ok] * repeat, axis=0)
    first = lax.broadcasted_iota(jnp.int32, total.shape[1:], 1) == 0
    for g in range(groups):
        for r in range(repeat):
            q_rows[g, r * rows : (r + 1) * rows, :] = q_wide[
                pl.ds(g * repeat + r, rows, stride=heads), :
            ]
        k = new_wide[pl.ds(g, rows, stride=step), :].astype(jnp.bfloat16)
        v = new_wide[pl.ds(groups + g, rows, stride=step), :].astype(jnp.bfloat16)
        s = mm_t(q_rows[g].astype(jnp.bfloat16), k) * factor
        s = jnp.where(fresh_ok, s, NEG)
        high = jnp.max(s, axis=1, keepdims=True)
        p = jnp.exp2(s - high)
        top[g] = jnp.broadcast_to(high, top.shape[1:])
        total[g] = jnp.where(first, jnp.sum(p, axis=1, keepdims=True), 0.0)
        acc[g] = mm(p.astype(jnp.bfloat16), v)

    quad_row = lax.broadcasted_iota(jnp.int32, (8, quad_keys), 0)
    quad_key = lax.broadcasted_iota(jnp.int32, (8, quad_keys), 1)
    for index in range(quads):
        tail_copy(index).wait()
        take_apart(tail_buf, index * quad_rows, quad_rows)
        reach = jnp.zeros((8, quad_keys), jnp.int32)
        for c in range(quad):
            reach = jnp.where(
                quad_key // tail == c, tail_len[0, index * quad + c] + c * tail, reach
            )
        ok = (quad_row // NEW == quad_key // tail) & (quad_key < reach)
        ok = jnp.concatenate([ok] * repeat, axis=0)
        for g in range(groups):
            k = apart[g, :quad_keys, :]
            v = apart[groups + g, :quad_keys, :]
            at = [slice(r * rows + index * 8, r * rows + index * 8 + 8) for r in range(repeat)]
            q = jnp.concatenate([q_rows[g, a, :] for a in at], axis=0).astype(jnp.bfloat16)
            s = jnp.where(ok, mm_t(q, k) * factor, NEG)
            old = jnp.concatenate([top[g, a, 0:1] for a in at], axis=0)
            high = jnp.maximum(old, jnp.max(s, axis=1, keepdims=True))
            keep = jnp.exp2(old - high)
            p = jnp.exp2(s - high)
            added = lanes(p)
            value = mm(p.astype(jnp.bfloat16), v)
            for r, a in enumerate(at):
                part = slice(r * 8, r * 8 + 8)
                top[g, a, :] = jnp.broadcast_to(high[part], (8, top.shape[2]))
                total[g, a, :] = total[g, a, :] * keep[part] + added[part]
                acc[g, a, :] = acc[g, a, :] * keep[part] + value[part]

    place = lax.broadcasted_iota(jnp.int32, (repeat * rows, chunk), 1)

    @pl.loop(0, chunks)
    def _(index):
        for i in range(chunk_pages):
            page_copy(index * chunk_pages + i).wait()
        take_apart(pages, pl.multiple_of(index * chunk_rows, chunk_rows), chunk_rows)
        ok = place < length - index * chunk
        for g in range(groups):
            k = apart[g, :chunk, :]
            v = apart[groups + g, :chunk, :]
            s = jnp.where(ok, mm_t(q_rows[g].astype(jnp.bfloat16), k) * factor, NEG)
            old = top[g, :, 0:1]
            high = jnp.maximum(old, jnp.max(s, axis=1, keepdims=True))
            keep = jnp.exp2(old - high)
            p = jnp.exp2(s - high)
            top[g] = jnp.broadcast_to(high, top.shape[1:])
            total[g] = total[g] * keep + lanes(p)
            acc[g] = acc[g] * keep + mm(p.astype(jnp.bfloat16), v)

    for g in range(groups):
        out = acc[g] / jnp.sum(total[g], axis=1, keepdims=True)
        out = out.astype(jnp.bfloat16)
        for r in range(repeat):
            head = g * repeat + r
            attn[:, head * width : (head + 1) * width] = out[r * rows : (r + 1) * rows]
    w_copy.wait()
    resid_copy.wait()
    value = mm(attn[...], w_buf[...])
    own_ref[...] = value + resid_buf[...].astype(jnp.float32)
    send_ref[...] = value.astype(jnp.bfloat16)


def attention(queries, new_kv, resid, pool, table, prompt_len, tails, tail_len, out_w):
    rows, heads, width = queries.shape
    n_pages, page, _, groups, _ = pool.shape
    conts, tail = tails.shape[:2]
    step = 2 * groups
    features = out_w.shape[1]
    most_keys = max(min(4, n_pages) * page, (8 // NEW) * tail)
    stack = (heads // groups) * rows
    return pl.pallas_call(
        functools.partial(
            attention_kernel, (rows, heads, groups, width, n_pages, page, conts, tail)
        ),
        out_shape=(
            jax.ShapeDtypeStruct((rows, features), jnp.float32),
            jax.ShapeDtypeStruct((rows, features), jnp.bfloat16),
        ),
        in_specs=[SMEM, SMEM, SMEM, ANY, ANY, ANY, ANY, ANY, ANY],
        out_specs=(VMEM, VMEM),
        scratch_shapes=[
            pltpu.VMEM((n_pages * page * step, width), jnp.bfloat16),
            pltpu.VMEM((conts * tail * step, width), jnp.bfloat16),
            pltpu.VMEM(out_w.shape, jnp.bfloat16),
            pltpu.VMEM((rows * heads, width), jnp.bfloat16),
            pltpu.VMEM((rows * step, width), jnp.bfloat16),
            pltpu.VMEM(resid.shape, jnp.bfloat16),
            pltpu.VMEM((step, most_keys, width), jnp.bfloat16),
            pltpu.VMEM((rows * heads, width), jnp.float32),
            pltpu.VMEM((groups, stack, width), jnp.float32),
            pltpu.VMEM((rows * step, width), jnp.float32),
            pltpu.VMEM((groups, stack, 128), jnp.float32),
            pltpu.VMEM((groups, stack, 128), jnp.float32),
            pltpu.VMEM((groups, stack, width), jnp.float32),
            pltpu.VMEM((rows, heads * width), jnp.bfloat16),
            pltpu.SemaphoreType.DMA((n_pages,)),
            pltpu.SemaphoreType.DMA((conts * NEW // 8,)),
            pltpu.SemaphoreType.DMA((4,)),
        ],
        compiler_params=pltpu.CompilerParams(vmem_limit_bytes=ATTENTION_VMEM),
        name="attention",
    )(
        table,
        prompt_len,
        tail_len,
        queries.reshape(rows * heads, width),
        new_kv.reshape(rows * step, width),
        resid,
        pool.reshape(n_pages * page * step, width),
        tails.reshape(conts * tail * step, width),
        out_w,
    )


def norm_kernel(place, own, other, gain, normed, middle, whole):
    copies, rows, features = normed.shape
    mid = own[...] + other[...].astype(jnp.float32)
    scale = lax.rsqrt(jnp.mean(mid * mid, axis=1, keepdims=True) + EPS)
    whole[...] = mid
    start = pl.multiple_of(place[0] * features, features)
    part = whole[:, pl.ds(start, features)]
    out = (part * scale * gain[:, pl.ds(start, features)]).astype(jnp.bfloat16)
    for index in range(copies):
        normed[index] = out
    middle[...] = part


def normalize(block, own, other, gain, features, copies):
    rows = own.shape[0]
    return pl.pallas_call(
        norm_kernel,
        out_shape=(
            jax.ShapeDtypeStruct((copies, rows, features), jnp.bfloat16),
            jax.ShapeDtypeStruct((rows, features), jnp.float32),
        ),
        in_specs=[SMEM, VMEM, VMEM, VMEM],
        out_specs=(VMEM, VMEM),
        scratch_shapes=[pltpu.VMEM(own.shape, jnp.float32)],
        name="normalize",
    )(block, own, other, gain.astype(jnp.float32).reshape(1, -1))


def units_kernel(near, far, gate_w, up_w, out, held):
    half = near.shape[0]
    held[:half, :] = near[...]
    held[half:, :] = far[...]
    units = gate_w.shape[1]
    out[:, :units] = mm(held[...], gate_w[...]).astype(jnp.bfloat16)
    out[:, units:] = mm(held[...], up_w[...]).astype(jnp.bfloat16)


def partial_units(near, far, gate_w, up_w):
    tokens = 2 * near.shape[0]
    features, units = gate_w.shape
    return pl.pallas_call(
        units_kernel,
        out_shape=jax.ShapeDtypeStruct((tokens, 2 * units), jnp.bfloat16),
        in_specs=[VMEM] * 4,
        out_specs=VMEM,
        scratch_shapes=[pltpu.VMEM((tokens, features), jnp.bfloat16)],
        compiler_params=pltpu.CompilerParams(vmem_limit_bytes=32 * MIB),
        name="gate_up",
    )(near, far, gate_w, up_w)


def down_kernel(place, own, other, source, middle, down_w, keep, send, term):
    tokens, features = term.shape
    units = down_w.shape[0]
    rows = middle.shape[0]
    chip, core = place[0], place[1]
    both = own[...].astype(jnp.float32) + other[...].astype(jnp.float32)
    gate, up = both[:, :units], both[:, units:]
    hidden = (gate / (1.0 + jnp.exp(-gate)) * up).astype(jnp.bfloat16)
    token = source[...]
    came = token // rows
    slot = ((came % 2) ^ core) * (tokens // 2) + (came // 2) * rows + token % rows
    pick = (lax.broadcasted_iota(jnp.int32, (tokens, tokens), 1) == slot).astype(jnp.bfloat16)
    moved = mm(pick, hidden).astype(jnp.bfloat16)
    local = token - (chip * 2 + core) * rows
    mine = lax.broadcasted_iota(jnp.int32, (tokens, rows), 1) == local
    mine = mine.astype(jnp.bfloat16)
    high = middle[...].astype(jnp.bfloat16)
    low = (middle[...] - high.astype(jnp.float32)).astype(jnp.bfloat16)
    term[...] = mm(moved, down_w[...]) + (mm(mine, high) + mm(mine, low))
    for index in range(tokens // rows // 2):
        at = slice(index * rows, (index + 1) * rows)
        start = pl.multiple_of((2 * index + core) * rows, rows)
        keep[at, :] = term[pl.ds(start, rows), :]
        start = pl.multiple_of((2 * index + (1 - core)) * rows, rows)
        send[at, :] = term[pl.ds(start, rows), :].astype(jnp.bfloat16)


def down(place, own, other, source, middle, down_w):
    tokens = own.shape[0]
    features = down_w.shape[1]
    return pl.pallas_call(
        down_kernel,
        out_shape=(
            jax.ShapeDtypeStruct((tokens // 2, features), jnp.float32),
            jax.ShapeDtypeStruct((tokens // 2, features), jnp.bfloat16),
        ),
        in_specs=[SMEM] + [VMEM] * 5,
        out_specs=(VMEM, VMEM),
        scratch_shapes=[pltpu.VMEM((tokens, features), jnp.float32)],
        compiler_params=pltpu.CompilerParams(vmem_limit_bytes=48 * MIB),
        name="down",
    )(place, own, other, source, middle, down_w)


def shards(
    n_chip,
    n_blk,
    resid,
    queries,
    new_kv,
    prefix_pool,
    page_table,
    prompt_len,
    tail_pool,
    tail_len,
    migration,
    out_w,
    mlp_gain,
    gate_w,
    up_w,
    down_w,
    final_gain,
    score_w,
):
    rows = resid.shape[0]
    features = gate_w.shape[0]
    chip = lax.axis_index("chip").astype(jnp.int32)
    core = lax.axis_index("core").astype(jnp.int32)
    block = lax.axis_index("blk").astype(jnp.int32).reshape(1)
    paired = n_blk == 2

    def swap(value, axis):
        return lax.ppermute(value, axis, [(0, 1), (1, 0)])

    own, send = attention(
        queries, new_kv, resid, prefix_pool, page_table, prompt_len, tail_pool, tail_len, out_w
    )
    if paired:
        other = swap(send, "blk")
    else:
        own, other = resid.astype(jnp.float32), lax.psum(send, "blk")
    normed, middle = normalize(block, own, other, mlp_gain, features, n_chip)

    near = lax.all_to_all(normed, "chip", 0, 0).reshape(n_chip * rows, features)
    units = partial_units(near, swap(near, "core"), gate_w, up_w)
    if paired:
        other_units = swap(units, "blk")
    else:
        units, other_units = jnp.zeros_like(units), lax.psum(units, "blk")

    source = migration[:, None] * NEW + jnp.arange(NEW, dtype=jnp.int32)[None, :]
    source = source.reshape(-1, 1)
    place = jnp.stack([chip, core])
    keep, away = down(place, units, other_units, source, middle, down_w)
    sums = (keep + swap(away, "core").astype(jnp.float32)).astype(jnp.bfloat16)
    parts = lax.all_to_all(sums.reshape(n_chip, rows, features), "chip", 0, 0)
    moved = jnp.sum(parts.astype(jnp.float32), axis=0)
    weighted = final_gain.astype(jnp.float32) * score_w.astype(jnp.float32)
    stats = jnp.stack([jnp.sum(moved * moved, -1), jnp.sum(moved * weighted, -1)])
    stats = stats + swap(stats, "blk") if paired else lax.psum(stats, "blk")
    score = stats[1] * lax.rsqrt(stats[0] / D + EPS)
    return (moved.astype(jnp.bfloat16), score)


def solution(mesh):
    n_chip, n_blk = mesh.shape["dp"] // 2, mesh.shape["blk"]
    split = Mesh(mesh.devices.reshape(n_chip, 2, n_blk), ("chip", "core", "blk"))
    dp = ("chip", "core")
    return jax.shard_map(
        functools.partial(shards, n_chip, n_blk),
        mesh=split,
        in_specs=(
            P(dp, None),
            P(dp, "blk", None),
            P(dp, None, "blk", None),
            P(dp, None, None, "blk", None),
            P(dp, None),
            P(dp),
            P(dp, None, None, "blk", None),
            P(dp, None),
            P(),
            P("blk", None),
            P(),
            P("blk", dp),
            P("blk", dp),
            P(dp, "blk"),
            P("blk"),
            P("blk"),
        ),
        out_specs=(P(dp, "blk"), P(dp)),
        check_vma=False,
    )
```

```python
import functools
import math

import jax
import jax.numpy as jnp
from jax import lax
from jax.experimental import pallas as pl
from jax.experimental.pallas import tpu as pltpu
from jax.sharding import Mesh
from jax.sharding import PartitionSpec as P

D = 2048
NEW = 2
NEG = -1e30
EPS = 1e-06
MIB = 1 << 20
ATTENTION_VMEM = 60 * MIB

VMEM = pl.BlockSpec(memory_space=pltpu.VMEM)
SMEM = pl.BlockSpec(memory_space=pltpu.SMEM)
ANY = pl.BlockSpec(memory_space=pl.ANY)


def mm(a, b):
    return jnp.dot(a, b, preferred_element_type=jnp.float32)


def mm_t(a, b):
    return lax.dot_general(a, b, (((1,), (1,)), ((), ())), preferred_element_type=jnp.float32)


def attention_kernel(
    dims,
    table,
    prompt_len,
    tail_len,
    queries,
    new_kv,
    resid,
    pool,
    tails,
    out_w,
    own_ref,
    send_ref,
    pages,
    tail_buf,
    w_buf,
    q_buf,
    new_buf,
    resid_buf,
    apart,
    tail_apart,
    q_wide,
    q_rows,
    new_wide,
    fresh_scores,
    tail_scores,
    scores,
    top,
    total,
    acc,
    attn,
    page_sems,
    tail_sems,
    sems,
):
    rows, heads, groups, width, n_pages, page, conts, tail, pair = dims
    repeat = heads // groups
    step = 2 * groups
    pairs = groups // pair
    stack = repeat * rows
    page_rows = page * step
    chunk_pages = math.gcd(8, n_pages)
    chunk = chunk_pages * page
    chunk_rows = chunk * step
    quad = 8 // NEW
    quads = conts // quad
    quad_keys = quad * tail
    quad_rows = quad_keys * step
    factor = math.log2(math.e) / math.sqrt(width)
    length = prompt_len[0]
    chunks = (length + chunk - 1) // chunk

    def page_copy(logical):
        physical = table[0, logical]
        return pltpu.make_async_copy(
            pool.at[pl.ds(pl.multiple_of(physical * page_rows, page_rows), page_rows), :],
            pages.at[pl.ds(pl.multiple_of(logical * page_rows, page_rows), page_rows), :],
            page_sems.at[logical],
        )

    def tail_copy(index):
        return pltpu.make_async_copy(
            tails.at[pl.ds(index * quad_rows, quad_rows), :],
            tail_buf.at[pl.ds(index * quad_rows, quad_rows), :],
            tail_sems.at[index],
        )

    q_copy = pltpu.make_async_copy(queries, q_buf, sems.at[0])
    new_copy = pltpu.make_async_copy(new_kv, new_buf, sems.at[1])
    w_copy = pltpu.make_async_copy(out_w, w_buf, sems.at[2])
    resid_copy = pltpu.make_async_copy(resid, resid_buf, sems.at[3])
    q_copy.start()
    new_copy.start()
    for index in range(quads):
        tail_copy(index).start()

    @pl.loop(0, chunks * chunk_pages)
    def _(logical):
        page_copy(logical).start()

    w_copy.start()
    resid_copy.start()

    block = 256
    tokens = block // step
    to = lax.broadcasted_iota(jnp.int32, (block, block), 0)
    came = lax.broadcasted_iota(jnp.int32, (block, block), 1)
    sort = (came == (to % tokens) * step + to // tokens).astype(jnp.bfloat16)

    def take_apart(buf, start, count, out, at):
        for two in range(count // (2 * block)):
            x0 = buf[pl.ds(start + two * 2 * block, block), :]
            x1 = buf[pl.ds(start + (two * 2 + 1) * block, block), :]
            y = mm(sort, jnp.concatenate([x0, x1], axis=1)).astype(jnp.bfloat16)
            for side in range(2):
                t = pl.ds(at + (2 * two + side) * tokens, tokens)
                for j in range(step):
                    kind, g = j // groups, j % groups
                    lane = (g % pair) * width
                    out[kind, g // pair, t, lane : lane + width] = y[
                        j * tokens : (j + 1) * tokens, side * width : (side + 1) * width
                    ]

    def blocks(x):
        return [x[:, i * 128 : (i + 1) * 128] for i in range(x.shape[1] // 128)]

    q_copy.wait()
    new_copy.wait()
    q_wide[...] = q_buf[...].astype(jnp.float32)
    new_wide[...] = new_buf[...].astype(jnp.float32)
    if pair > 1:
        q_rows[...] = jnp.zeros_like(q_rows)
    for g in range(groups):
        for r in range(repeat):
            at = (g % pair) * stack + r * rows
            lane = (g % pair) * width
            q_rows[g // pair, at : at + rows, lane : lane + width] = q_wide[
                pl.ds(g * repeat + r, rows, stride=heads), :
            ]

    def fresh(first, n):
        parts = [
            new_wide[pl.ds(first + n * pair + i, rows, stride=step), :] for i in range(pair)
        ]
        return jnp.concatenate(parts, axis=1).astype(jnp.bfloat16)

    row = lax.broadcasted_iota(jnp.int32, (rows, rows), 0)
    key = lax.broadcasted_iota(jnp.int32, (rows, rows), 1)
    fresh_ok = (row // NEW == key // NEW) & (key <= row)
    fresh_ok = jnp.concatenate([fresh_ok] * (pair * repeat), axis=0)
    for n in range(pairs):
        s = jnp.where(fresh_ok, mm_t(q_rows[n].astype(jnp.bfloat16), fresh(0, n)) * factor, NEG)
        fresh_scores[n] = s
        top[n] = jnp.broadcast_to(jnp.max(s, axis=1, keepdims=True), top.shape[1:])

    def quad_places(index):
        starts = [i * rows + index * 8 for i in range(pair * repeat)]
        return [slice(at, at + 8) for at in starts]

    quad_row = lax.broadcasted_iota(jnp.int32, (8, quad_keys), 0)
    quad_key = lax.broadcasted_iota(jnp.int32, (8, quad_keys), 1)
    for index in range(quads):
        tail_copy(index).wait()
        take_apart(tail_buf, index * quad_rows, quad_rows, tail_apart, index * quad_keys)
        reach = jnp.zeros((8, quad_keys), jnp.int32)
        for c in range(quad):
            reach = jnp.where(
                quad_key // tail == c, tail_len[0, index * quad + c] + c * tail, reach
            )
        ok = (quad_row // NEW == quad_key // tail) & (quad_key < reach)
        ok = jnp.concatenate([ok] * (pair * repeat), axis=0)
        keys = slice(index * quad_keys, (index + 1) * quad_keys)
        for n in range(pairs):
            q = jnp.concatenate([q_rows[n, a, :] for a in quad_places(index)], axis=0)
            s = mm_t(q.astype(jnp.bfloat16), tail_apart[0, n, keys, :]) * factor
            s = jnp.where(ok, s, NEG)
            tail_scores[n, index] = s
            high = functools.reduce(jnp.maximum, blocks(s))
            for i, a in enumerate(quad_places(index)):
                top[n, a, :] = jnp.maximum(top[n, a, :], high[i * 8 : (i + 1) * 8])

    place = lax.broadcasted_iota(jnp.int32, (8, chunk), 1)

    @pl.loop(0, chunks)
    def _(index):
        for i in range(chunk_pages):
            page_copy(index * chunk_pages + i).wait()
        first = pl.multiple_of(index * chunk, chunk)
        take_apart(pages, pl.multiple_of(index * chunk_rows, chunk_rows), chunk_rows, apart, first)
        ok = place[0:1] < length - index * chunk
        for n in range(pairs):
            s = mm_t(q_rows[n].astype(jnp.bfloat16), apart[0, n, pl.ds(first, chunk), :]) * factor
            s = jnp.where(ok, s, NEG)
            scores[n, :, pl.ds(first, chunk)] = s
            top[n] = functools.reduce(jnp.maximum, blocks(s), top[n])

    for n in range(pairs):
        high = jnp.broadcast_to(jnp.max(top[n], axis=1, keepdims=True), top.shape[1:])
        top[n] = high
        p = jnp.exp2(fresh_scores[n] - high[:, :rows])
        lane = lax.broadcasted_iota(jnp.int32, total.shape[1:], 1)
        total[n] = jnp.where(lane == 0, jnp.sum(p, axis=1, keepdims=True), 0.0)
        acc[n] = mm(p.astype(jnp.bfloat16), fresh(groups, n))

    def weigh(s, high):
        parts = [jnp.exp2(part - high) for part in blocks(s)]
        return jnp.concatenate(parts, axis=1).astype(jnp.bfloat16), functools.reduce(jnp.add, parts)

    for index in range(quads):
        keys = slice(index * quad_keys, (index + 1) * quad_keys)
        for n in range(pairs):
            high = jnp.concatenate([top[n, a, :] for a in quad_places(index)], axis=0)
            p, added = weigh(tail_scores[n, index], high)
            value = mm(p, tail_apart[1, n, keys, :])
            for i, a in enumerate(quad_places(index)):
                total[n, a, :] = total[n, a, :] + added[i * 8 : (i + 1) * 8]
                acc[n, a, :] = acc[n, a, :] + value[i * 8 : (i + 1) * 8]

    @pl.loop(0, chunks)
    def _(index):
        first = pl.multiple_of(index * chunk, chunk)
        for n in range(pairs):
            p, added = weigh(scores[n, :, pl.ds(first, chunk)], top[n])
            total[n] = total[n] + added
            acc[n] = acc[n] + mm(p, apart[1, n, pl.ds(first, chunk), :])

    for g in range(groups):
        at, lane = (g % pair) * stack, (g % pair) * width
        out = acc[g // pair, at : at + stack, lane : lane + width]
        out = out / jnp.sum(total[g // pair, at : at + stack, :], axis=1, keepdims=True)
        out = out.astype(jnp.bfloat16)
        for r in range(repeat):
            head = g * repeat + r
            attn[:, head * width : (head + 1) * width] = out[r * rows : (r + 1) * rows]
    w_copy.wait()
    resid_copy.wait()
    value = mm(attn[...], w_buf[...])
    own_ref[...] = value + resid_buf[...].astype(jnp.float32)
    send_ref[...] = value.astype(jnp.bfloat16)


def attention(queries, new_kv, resid, pool, table, prompt_len, tails, tail_len, out_w):
    rows, heads, width = queries.shape
    n_pages, page, _, groups, _ = pool.shape
    conts, tail = tails.shape[:2]
    step = 2 * groups
    features = out_w.shape[1]
    quads = conts * NEW // 8
    pair = 2 if groups % 2 == 0 else 1
    pairs = groups // pair
    repeat = heads // groups
    stack = pair * repeat * rows
    return pl.pallas_call(
        functools.partial(
            attention_kernel, (rows, heads, groups, width, n_pages, page, conts, tail, pair)
        ),
        out_shape=(
            jax.ShapeDtypeStruct((rows, features), jnp.float32),
            jax.ShapeDtypeStruct((rows, features), jnp.bfloat16),
        ),
        in_specs=[SMEM, SMEM, SMEM, ANY, ANY, ANY, ANY, ANY, ANY],
        out_specs=(VMEM, VMEM),
        scratch_shapes=[
            pltpu.VMEM((n_pages * page * step, width), jnp.bfloat16),
            pltpu.VMEM((conts * tail * step, width), jnp.bfloat16),
            pltpu.VMEM(out_w.shape, jnp.bfloat16),
            pltpu.VMEM((rows * heads, width), jnp.bfloat16),
            pltpu.VMEM((rows * step, width), jnp.bfloat16),
            pltpu.VMEM(resid.shape, jnp.bfloat16),
            pltpu.VMEM((2, pairs, n_pages * page, pair * width), jnp.bfloat16),
            pltpu.VMEM((2, pairs, conts * tail, pair * width), jnp.bfloat16),
            pltpu.VMEM((rows * heads, width), jnp.float32),
            pltpu.VMEM((pairs, stack, pair * width), jnp.float32),
            pltpu.VMEM((rows * step, width), jnp.float32),
            pltpu.VMEM((pairs, stack, rows), jnp.float32),
            pltpu.VMEM((pairs, quads, pair * repeat * 8, 8 // NEW * tail), jnp.float32),
            pltpu.VMEM((pairs, stack, n_pages * page), jnp.float32),
            pltpu.VMEM((pairs, stack, 128), jnp.float32),
            pltpu.VMEM((pairs, stack, 128), jnp.float32),
            pltpu.VMEM((pairs, stack, pair * width), jnp.float32),
            pltpu.VMEM((rows, heads * width), jnp.bfloat16),
            pltpu.SemaphoreType.DMA((n_pages,)),
            pltpu.SemaphoreType.DMA((quads,)),
            pltpu.SemaphoreType.DMA((4,)),
        ],
        compiler_params=pltpu.CompilerParams(vmem_limit_bytes=ATTENTION_VMEM),
        name="attention",
    )(
        table,
        prompt_len,
        tail_len,
        queries.reshape(rows * heads, width),
        new_kv.reshape(rows * step, width),
        resid,
        pool.reshape(n_pages * page * step, width),
        tails.reshape(conts * tail * step, width),
        out_w,
    )


def norm_kernel(place, own, other, gain, normed, middle, whole):
    copies, rows, features = normed.shape
    mid = own[...] + other[...].astype(jnp.float32)
    scale = lax.rsqrt(jnp.mean(mid * mid, axis=1, keepdims=True) + EPS)
    whole[...] = mid
    start = pl.multiple_of(place[0] * features, features)
    part = whole[:, pl.ds(start, features)]
    out = (part * scale * gain[:, pl.ds(start, features)]).astype(jnp.bfloat16)
    for index in range(copies):
        normed[index] = out
    middle[...] = part


def normalize(block, own, other, gain, features, copies):
    rows = own.shape[0]
    return pl.pallas_call(
        norm_kernel,
        out_shape=(
            jax.ShapeDtypeStruct((copies, rows, features), jnp.bfloat16),
            jax.ShapeDtypeStruct((rows, features), jnp.float32),
        ),
        in_specs=[SMEM, VMEM, VMEM, VMEM],
        out_specs=(VMEM, VMEM),
        scratch_shapes=[pltpu.VMEM(own.shape, jnp.float32)],
        compiler_params=pltpu.CompilerParams(vmem_limit_bytes=8 * MIB),
        name="normalize",
    )(block, own, other, gain.astype(jnp.float32).reshape(1, -1))


def units_kernel(near, far, gate_w, up_w, out, held):
    half = near.shape[0]
    held[:half, :] = near[...]
    held[half:, :] = far[...]
    units = gate_w.shape[1]
    out[:, :units] = mm(held[...], gate_w[...]).astype(jnp.bfloat16)
    out[:, units:] = mm(held[...], up_w[...]).astype(jnp.bfloat16)


def partial_units(near, far, gate_w, up_w):
    tokens = 2 * near.shape[0]
    features, units = gate_w.shape
    return pl.pallas_call(
        units_kernel,
        out_shape=jax.ShapeDtypeStruct((tokens, 2 * units), jnp.bfloat16),
        in_specs=[VMEM] * 4,
        out_specs=VMEM,
        scratch_shapes=[pltpu.VMEM((tokens, features), jnp.bfloat16)],
        compiler_params=pltpu.CompilerParams(vmem_limit_bytes=32 * MIB),
        name="gate_up",
    )(near, far, gate_w, up_w)


def down_kernel(direct, place, own, other, source, middle, down_w, keep, send, term):
    tokens, features = term.shape
    units = down_w.shape[0]
    rows = middle.shape[0]
    chip, core = place[0], place[1]
    both = own[...].astype(jnp.float32) + other[...].astype(jnp.float32)
    gate, up = both[:, :units], both[:, units:]
    hidden = (gate / (1.0 + jnp.exp(-gate)) * up).astype(jnp.bfloat16)
    token = source[...]
    came = token // rows
    slot = ((came % 2) ^ core) * (tokens // 2) + (came // 2) * rows + token % rows
    pick = (lax.broadcasted_iota(jnp.int32, (tokens, tokens), 1) == slot).astype(jnp.bfloat16)
    moved = mm(pick, hidden).astype(jnp.bfloat16)
    local = token - (chip * 2 + core) * rows
    mine = lax.broadcasted_iota(jnp.int32, (tokens, rows), 1) == local
    mine = mine.astype(jnp.bfloat16)
    high = middle[...].astype(jnp.bfloat16)
    low = (middle[...] - high.astype(jnp.float32)).astype(jnp.bfloat16)
    term[...] = mm(moved, down_w[...]) + (mm(mine, high) + mm(mine, low))
    for index in range(tokens // rows // 2):
        at = slice(index * rows, (index + 1) * rows)
        dest = index ^ chip if direct else index
        start = pl.multiple_of((2 * dest + core) * rows, rows)
        keep[at, :] = term[pl.ds(start, rows), :]
        start = pl.multiple_of((2 * dest + (1 - core)) * rows, rows)
        send[at, :] = term[pl.ds(start, rows), :].astype(jnp.bfloat16)


def down(direct, place, own, other, source, middle, down_w):
    tokens = own.shape[0]
    features = down_w.shape[1]
    return pl.pallas_call(
        functools.partial(down_kernel, direct),
        out_shape=(
            jax.ShapeDtypeStruct((tokens // 2, features), jnp.float32),
            jax.ShapeDtypeStruct((tokens // 2, features), jnp.bfloat16),
        ),
        in_specs=[SMEM] + [VMEM] * 5,
        out_specs=(VMEM, VMEM),
        scratch_shapes=[pltpu.VMEM((tokens, features), jnp.float32)],
        compiler_params=pltpu.CompilerParams(vmem_limit_bytes=48 * MIB),
        name="down",
    )(place, own, other, source, middle, down_w)


def add_kernel(keep, other, *outs):
    rows = outs[0].shape[0]
    for index, out in enumerate(outs):
        at = slice(index * rows, (index + 1) * rows)
        out[...] = (keep[at, :] + other[at, :].astype(jnp.float32)).astype(out.dtype)


def add_parts(keep, other, rows):
    count = keep.shape[0] // rows
    features = keep.shape[1]
    return pl.pallas_call(
        add_kernel,
        out_shape=tuple(
            jax.ShapeDtypeStruct((rows, features), jnp.bfloat16 if i else jnp.float32)
            for i in range(count)
        ),
        in_specs=[VMEM, VMEM],
        out_specs=(VMEM,) * count,
        compiler_params=pltpu.CompilerParams(vmem_limit_bytes=8 * MIB),
        name="add_parts",
    )(keep, other)


def shards(
    n_chip,
    n_blk,
    resid,
    queries,
    new_kv,
    prefix_pool,
    page_table,
    prompt_len,
    tail_pool,
    tail_len,
    migration,
    out_w,
    mlp_gain,
    gate_w,
    up_w,
    down_w,
    final_gain,
    score_w,
):
    rows = resid.shape[0]
    features = gate_w.shape[0]
    chip = lax.axis_index("chip").astype(jnp.int32)
    core = lax.axis_index("core").astype(jnp.int32)
    block = lax.axis_index("blk").astype(jnp.int32).reshape(1)
    paired = n_blk == 2
    direct = n_chip == 8

    def to_chip(value, index):
        return lax.ppermute(value, "chip", [(i, i ^ index) for i in range(n_chip)])

    def swap(value, axis):
        return lax.ppermute(value, axis, [(0, 1), (1, 0)])

    own, send = attention(
        queries, new_kv, resid, prefix_pool, page_table, prompt_len, tail_pool, tail_len, out_w
    )
    if paired:
        other = swap(send, "blk")
    else:
        own, other = resid.astype(jnp.float32), lax.psum(send, "blk")
    normed, middle = normalize(block, own, other, mlp_gain, features, n_chip)

    near = lax.all_to_all(normed, "chip", 0, 0).reshape(n_chip * rows, features)
    units = partial_units(near, swap(near, "core"), gate_w, up_w)
    if paired:
        other_units = swap(units, "blk")
    else:
        units, other_units = jnp.zeros_like(units), lax.psum(units, "blk")

    source = migration[:, None] * NEW + jnp.arange(NEW, dtype=jnp.int32)[None, :]
    source = source.reshape(-1, 1)
    place = jnp.stack([chip, core])
    keep, away = down(direct, place, units, other_units, source, middle, down_w)
    other_sums = swap(away, "core")
    if direct:
        parts = add_parts(keep, other_sums, rows)
        moved = parts[0]
        for index in (6, 4, 7, 5, 2, 3, 1):
            moved = moved + to_chip(parts[index], index).astype(jnp.float32)
    else:
        sums = (keep + other_sums.astype(jnp.float32)).astype(jnp.bfloat16)
        parts = lax.all_to_all(sums.reshape(n_chip, rows, features), "chip", 0, 0)
        moved = jnp.sum(parts.astype(jnp.float32), axis=0)
    weighted = final_gain.astype(jnp.float32) * score_w.astype(jnp.float32)
    stats = jnp.stack([jnp.sum(moved * moved, -1), jnp.sum(moved * weighted, -1)])
    stats = stats + swap(stats, "blk") if paired else lax.psum(stats, "blk")
    score = stats[1] * lax.rsqrt(stats[0] / D + EPS)
    return (moved.astype(jnp.bfloat16), score)


def solution(mesh):
    n_chip, n_blk = mesh.shape["dp"] // 2, mesh.shape["blk"]
    split = Mesh(mesh.devices.reshape(n_chip, 2, n_blk), ("chip", "core", "blk"))
    dp = ("chip", "core")
    return jax.shard_map(
        functools.partial(shards, n_chip, n_blk),
        mesh=split,
        in_specs=(
            P(dp, None),
            P(dp, "blk", None),
            P(dp, None, "blk", None),
            P(dp, None, None, "blk", None),
            P(dp, None),
            P(dp),
            P(dp, None, None, "blk", None),
            P(dp, None),
            P(),
            P("blk", None),
            P(),
            P("blk", dp),
            P("blk", dp),
            P(dp, "blk"),
            P("blk"),
            P("blk"),
        ),
        out_specs=(P(dp, "blk"), P(dp)),
        check_vma=False,
    )
```

```python
import functools
import math

import jax
import jax.numpy as jnp
from jax import lax
from jax.experimental import pallas as pl
from jax.experimental.pallas import tpu as pltpu
from jax.sharding import Mesh
from jax.sharding import PartitionSpec as P

D = 2048
NEW = 2
NEG = -1e30
EPS = 1e-06
MIB = 1 << 20
ATTENTION_VMEM = 60 * MIB

VMEM = pl.BlockSpec(memory_space=pltpu.VMEM)
SMEM = pl.BlockSpec(memory_space=pltpu.SMEM)
ANY = pl.BlockSpec(memory_space=pl.ANY)


def mm(a, b):
    return jnp.dot(a, b, preferred_element_type=jnp.float32)


def mm_t(a, b):
    return lax.dot_general(a, b, (((1,), (1,)), ((), ())), preferred_element_type=jnp.float32)


def attention_kernel(
    dims,
    table,
    prompt_len,
    tail_len,
    queries,
    new_kv,
    resid,
    pool,
    tails,
    out_w,
    own_ref,
    send_ref,
    pages,
    tail_buf,
    w_buf,
    q_buf,
    new_buf,
    resid_buf,
    apart,
    tail_apart,
    q_wide,
    q_rows,
    new_wide,
    fresh_scores,
    tail_scores,
    scores,
    top,
    total,
    acc,
    attn,
    page_sems,
    tail_sems,
    sems,
):
    rows, heads, groups, width, n_pages, page, conts, tail, pair = dims
    repeat = heads // groups
    step = 2 * groups
    pairs = groups // pair
    stack = repeat * rows
    page_rows = page * step
    chunk_pages = math.gcd(8, n_pages)
    chunk = chunk_pages * page
    chunk_rows = chunk * step
    quad = 8 // NEW
    quads = conts // quad
    quad_keys = quad * tail
    quad_rows = quad_keys * step
    factor = math.log2(math.e) / math.sqrt(width)
    length = prompt_len[0]
    chunks = (length + chunk - 1) // chunk

    def page_copy(logical):
        physical = table[0, logical]
        return pltpu.make_async_copy(
            pool.at[pl.ds(pl.multiple_of(physical * page_rows, page_rows), page_rows), :],
            pages.at[pl.ds(pl.multiple_of(logical * page_rows, page_rows), page_rows), :],
            page_sems.at[logical],
        )

    def tail_copy(index):
        return pltpu.make_async_copy(
            tails.at[pl.ds(index * quad_rows, quad_rows), :],
            tail_buf.at[pl.ds(index * quad_rows, quad_rows), :],
            tail_sems.at[index],
        )

    q_copy = pltpu.make_async_copy(queries, q_buf, sems.at[0])
    new_copy = pltpu.make_async_copy(new_kv, new_buf, sems.at[1])
    w_copy = pltpu.make_async_copy(out_w, w_buf, sems.at[2])
    resid_copy = pltpu.make_async_copy(resid, resid_buf, sems.at[3])
    q_copy.start()
    new_copy.start()
    for index in range(quads):
        tail_copy(index).start()

    @pl.loop(0, chunks * chunk_pages)
    def _(logical):
        page_copy(logical).start()

    w_copy.start()
    resid_copy.start()

    block = 256
    tokens = block // step
    to = lax.broadcasted_iota(jnp.int32, (block, block), 0)
    came = lax.broadcasted_iota(jnp.int32, (block, block), 1)
    sort = (came == (to % tokens) * step + to // tokens).astype(jnp.bfloat16)

    def take_apart(buf, start, count, out, at):
        for two in range(count // (2 * block)):
            x0 = buf[pl.ds(start + two * 2 * block, block), :]
            x1 = buf[pl.ds(start + (two * 2 + 1) * block, block), :]
            y = mm(sort, jnp.concatenate([x0, x1], axis=1)).astype(jnp.bfloat16)
            for side in range(2):
                t = pl.ds(at + (2 * two + side) * tokens, tokens)
                for j in range(step):
                    kind, g = j // groups, j % groups
                    lane = (g % pair) * width
                    out[kind, g // pair, t, lane : lane + width] = y[
                        j * tokens : (j + 1) * tokens, side * width : (side + 1) * width
                    ]

    def blocks(x):
        return [x[:, i * 128 : (i + 1) * 128] for i in range(x.shape[1] // 128)]

    q_copy.wait()
    new_copy.wait()
    q_wide[...] = q_buf[...].astype(jnp.float32)
    new_wide[...] = new_buf[...].astype(jnp.float32)
    if pair > 1:
        q_rows[...] = jnp.zeros_like(q_rows)
    for g in range(groups):
        for r in range(repeat):
            at = (g % pair) * stack + r * rows
            lane = (g % pair) * width
            q_rows[g // pair, at : at + rows, lane : lane + width] = q_wide[
                pl.ds(g * repeat + r, rows, stride=heads), :
            ]

    def fresh(first, n):
        parts = [
            new_wide[pl.ds(first + n * pair + i, rows, stride=step), :] for i in range(pair)
        ]
        return jnp.concatenate(parts, axis=1).astype(jnp.bfloat16)

    row = lax.broadcasted_iota(jnp.int32, (rows, rows), 0)
    key = lax.broadcasted_iota(jnp.int32, (rows, rows), 1)
    fresh_ok = (row // NEW == key // NEW) & (key <= row)
    fresh_ok = jnp.concatenate([fresh_ok] * (pair * repeat), axis=0)
    for n in range(pairs):
        s = jnp.where(fresh_ok, mm_t(q_rows[n].astype(jnp.bfloat16), fresh(0, n)) * factor, NEG)
        fresh_scores[n] = s
        top[n] = jnp.broadcast_to(jnp.max(s, axis=1, keepdims=True), top.shape[1:])

    def quad_places(index):
        starts = [i * rows + index * 8 for i in range(pair * repeat)]
        return [slice(at, at + 8) for at in starts]

    quad_row = lax.broadcasted_iota(jnp.int32, (8, quad_keys), 0)
    quad_key = lax.broadcasted_iota(jnp.int32, (8, quad_keys), 1)
    for index in range(quads):
        tail_copy(index).wait()
        take_apart(tail_buf, index * quad_rows, quad_rows, tail_apart, index * quad_keys)
        reach = jnp.zeros((8, quad_keys), jnp.int32)
        for c in range(quad):
            reach = jnp.where(
                quad_key // tail == c, tail_len[0, index * quad + c] + c * tail, reach
            )
        ok = (quad_row // NEW == quad_key // tail) & (quad_key < reach)
        ok = jnp.concatenate([ok] * (pair * repeat), axis=0)
        keys = slice(index * quad_keys, (index + 1) * quad_keys)
        for n in range(pairs):
            q = jnp.concatenate([q_rows[n, a, :] for a in quad_places(index)], axis=0)
            s = mm_t(q.astype(jnp.bfloat16), tail_apart[0, n, keys, :]) * factor
            s = jnp.where(ok, s, NEG)
            tail_scores[n, index] = s
            high = functools.reduce(jnp.maximum, blocks(s))
            for i, a in enumerate(quad_places(index)):
                top[n, a, :] = jnp.maximum(top[n, a, :], high[i * 8 : (i + 1) * 8])

    place = lax.broadcasted_iota(jnp.int32, (8, chunk), 1)

    @pl.loop(0, chunks)
    def _(index):
        for i in range(chunk_pages):
            page_copy(index * chunk_pages + i).wait()
        first = pl.multiple_of(index * chunk, chunk)
        take_apart(pages, pl.multiple_of(index * chunk_rows, chunk_rows), chunk_rows, apart, first)
        ok = place[0:1] < length - index * chunk
        for n in range(pairs):
            s = mm_t(q_rows[n].astype(jnp.bfloat16), apart[0, n, pl.ds(first, chunk), :]) * factor
            s = jnp.where(ok, s, NEG)
            scores[n, :, pl.ds(first, chunk)] = s
            top[n] = functools.reduce(jnp.maximum, blocks(s), top[n])

    for n in range(pairs):
        high = jnp.broadcast_to(jnp.max(top[n], axis=1, keepdims=True), top.shape[1:])
        top[n] = high
        p = jnp.exp2(fresh_scores[n] - high[:, :rows])
        lane = lax.broadcasted_iota(jnp.int32, total.shape[1:], 1)
        total[n] = jnp.where(lane == 0, jnp.sum(p, axis=1, keepdims=True), 0.0)
        acc[n] = mm(p.astype(jnp.bfloat16), fresh(groups, n))

    def weigh(s, high):
        parts = [jnp.exp2(part - high) for part in blocks(s)]
        return jnp.concatenate(parts, axis=1).astype(jnp.bfloat16), functools.reduce(jnp.add, parts)

    for index in range(quads):
        keys = slice(index * quad_keys, (index + 1) * quad_keys)
        for n in range(pairs):
            high = jnp.concatenate([top[n, a, :] for a in quad_places(index)], axis=0)
            p, added = weigh(tail_scores[n, index], high)
            value = mm(p, tail_apart[1, n, keys, :])
            for i, a in enumerate(quad_places(index)):
                total[n, a, :] = total[n, a, :] + added[i * 8 : (i + 1) * 8]
                acc[n, a, :] = acc[n, a, :] + value[i * 8 : (i + 1) * 8]

    @pl.loop(0, chunks)
    def _(index):
        first = pl.multiple_of(index * chunk, chunk)
        for n in range(pairs):
            p, added = weigh(scores[n, :, pl.ds(first, chunk)], top[n])
            total[n] = total[n] + added
            acc[n] = acc[n] + mm(p, apart[1, n, pl.ds(first, chunk), :])

    for g in range(groups):
        at, lane = (g % pair) * stack, (g % pair) * width
        out = acc[g // pair, at : at + stack, lane : lane + width]
        out = out / jnp.sum(total[g // pair, at : at + stack, :], axis=1, keepdims=True)
        out = out.astype(jnp.bfloat16)
        for r in range(repeat):
            head = g * repeat + r
            attn[:, head * width : (head + 1) * width] = out[r * rows : (r + 1) * rows]
    w_copy.wait()
    resid_copy.wait()
    value = mm(attn[...], w_buf[...])
    own_ref[...] = value + resid_buf[...].astype(jnp.float32)
    send_ref[...] = value.astype(jnp.bfloat16)


def attention(queries, new_kv, resid, pool, table, prompt_len, tails, tail_len, out_w):
    rows, heads, width = queries.shape
    n_pages, page, _, groups, _ = pool.shape
    conts, tail = tails.shape[:2]
    step = 2 * groups
    features = out_w.shape[1]
    quads = conts * NEW // 8
    pair = 2 if groups % 2 == 0 else 1
    pairs = groups // pair
    repeat = heads // groups
    stack = pair * repeat * rows
    return pl.pallas_call(
        functools.partial(
            attention_kernel, (rows, heads, groups, width, n_pages, page, conts, tail, pair)
        ),
        out_shape=(
            jax.ShapeDtypeStruct((rows, features), jnp.float32),
            jax.ShapeDtypeStruct((rows, features), jnp.bfloat16),
        ),
        in_specs=[SMEM, SMEM, SMEM, ANY, ANY, ANY, ANY, ANY, ANY],
        out_specs=(VMEM, VMEM),
        scratch_shapes=[
            pltpu.VMEM((n_pages * page * step, width), jnp.bfloat16),
            pltpu.VMEM((conts * tail * step, width), jnp.bfloat16),
            pltpu.VMEM(out_w.shape, jnp.bfloat16),
            pltpu.VMEM((rows * heads, width), jnp.bfloat16),
            pltpu.VMEM((rows * step, width), jnp.bfloat16),
            pltpu.VMEM(resid.shape, jnp.bfloat16),
            pltpu.VMEM((2, pairs, n_pages * page, pair * width), jnp.bfloat16),
            pltpu.VMEM((2, pairs, conts * tail, pair * width), jnp.bfloat16),
            pltpu.VMEM((rows * heads, width), jnp.float32),
            pltpu.VMEM((pairs, stack, pair * width), jnp.float32),
            pltpu.VMEM((rows * step, width), jnp.float32),
            pltpu.VMEM((pairs, stack, rows), jnp.float32),
            pltpu.VMEM((pairs, quads, pair * repeat * 8, 8 // NEW * tail), jnp.float32),
            pltpu.VMEM((pairs, stack, n_pages * page), jnp.float32),
            pltpu.VMEM((pairs, stack, 128), jnp.float32),
            pltpu.VMEM((pairs, stack, 128), jnp.float32),
            pltpu.VMEM((pairs, stack, pair * width), jnp.float32),
            pltpu.VMEM((rows, heads * width), jnp.bfloat16),
            pltpu.SemaphoreType.DMA((n_pages,)),
            pltpu.SemaphoreType.DMA((quads,)),
            pltpu.SemaphoreType.DMA((4,)),
        ],
        compiler_params=pltpu.CompilerParams(vmem_limit_bytes=ATTENTION_VMEM),
        name="attention",
    )(
        table,
        prompt_len,
        tail_len,
        queries.reshape(rows * heads, width),
        new_kv.reshape(rows * step, width),
        resid,
        pool.reshape(n_pages * page * step, width),
        tails.reshape(conts * tail * step, width),
        out_w,
    )


def norm_kernel(place, own, other, gain, normed, middle, whole):
    copies, rows, features = normed.shape
    mid = own[...] + other[...].astype(jnp.float32)
    scale = lax.rsqrt(jnp.mean(mid * mid, axis=1, keepdims=True) + EPS)
    whole[...] = mid
    start = pl.multiple_of(place[0] * features, features)
    part = whole[:, pl.ds(start, features)]
    out = (part * scale * gain[:, pl.ds(start, features)]).astype(jnp.bfloat16)
    for index in range(copies):
        normed[index] = out
    middle[...] = part


def normalize(block, own, other, gain, features, copies):
    rows = own.shape[0]
    return pl.pallas_call(
        norm_kernel,
        out_shape=(
            jax.ShapeDtypeStruct((copies, rows, features), jnp.bfloat16),
            jax.ShapeDtypeStruct((rows, features), jnp.float32),
        ),
        in_specs=[SMEM, VMEM, VMEM, VMEM],
        out_specs=(VMEM, VMEM),
        scratch_shapes=[pltpu.VMEM(own.shape, jnp.float32)],
        compiler_params=pltpu.CompilerParams(vmem_limit_bytes=8 * MIB),
        name="normalize",
    )(block, own, other, gain.astype(jnp.float32).reshape(1, -1))


def units_kernel(n, place, *refs):
    pieces, gate_w, up_w, outs, held, sums = refs[:n], *refs[n : n + 2], refs[n + 2 : -2], *refs[-2:]
    at = 0
    for piece in pieces:
        held[at : at + piece.shape[0], :] = piece[...]
        at += piece.shape[0]
    units = gate_w.shape[1]
    sums[:, :units] = mm(held[...], gate_w[...])
    sums[:, units:] = mm(held[...], up_w[...])
    if len(outs) == 1:
        outs[0][...] = sums[...].astype(jnp.bfloat16)
        return
    keep, send = outs
    half = at // 2
    keep[...] = sums[pl.ds(pl.multiple_of(place[0] * half, half), half), :]
    send[...] = sums[pl.ds(pl.multiple_of((1 - place[0]) * half, half), half), :].astype(
        jnp.bfloat16
    )


def partial_units(split, block, pieces, gate_w, up_w):
    tokens = sum(piece.shape[0] for piece in pieces)
    features, units = gate_w.shape
    if split:
        out_shape = (
            jax.ShapeDtypeStruct((tokens // 2, 2 * units), jnp.float32),
            jax.ShapeDtypeStruct((tokens // 2, 2 * units), jnp.bfloat16),
        )
    else:
        out_shape = (jax.ShapeDtypeStruct((tokens, 2 * units), jnp.bfloat16),)
    return pl.pallas_call(
        functools.partial(units_kernel, len(pieces)),
        out_shape=out_shape,
        in_specs=[SMEM] + [VMEM] * (len(pieces) + 2),
        out_specs=(VMEM,) * len(out_shape),
        scratch_shapes=[
            pltpu.VMEM((tokens, features), jnp.bfloat16),
            pltpu.VMEM((tokens, 2 * units), jnp.float32),
        ],
        compiler_params=pltpu.CompilerParams(vmem_limit_bytes=16 * MIB),
        cost_estimate=pl.CostEstimate(
            flops=4 * tokens * features * units,
            bytes_accessed=2 * tokens * features + 4 * features * units,
            transcendentals=0,
        ),
        name="gate_up",
    )(block, *pieces, gate_w, up_w)


def hidden_kernel(*refs):
    sums, out = refs[:-1], refs[-1]
    both = functools.reduce(jnp.add, [ref[...].astype(jnp.float32) for ref in sums])
    units = out.shape[1]
    gate, up = both[:, :units], both[:, units:]
    out[...] = (gate / (1.0 + jnp.exp(-gate)) * up).astype(jnp.bfloat16)


def hidden_units(*sums):
    tokens, units = sums[0].shape[0], sums[0].shape[1] // 2
    return pl.pallas_call(
        hidden_kernel,
        out_shape=jax.ShapeDtypeStruct((tokens, units), jnp.bfloat16),
        in_specs=[VMEM] * len(sums),
        out_specs=VMEM,
        compiler_params=pltpu.CompilerParams(vmem_limit_bytes=8 * MIB),
        name="hidden",
    )(*sums)


def down_kernel(direct, n, place, *refs):
    parts, source, middle, down_w, keep, send, hidden, term = refs[:n], *refs[n:]
    tokens, features = term.shape
    rows = middle.shape[0]
    chip, core = place[0], place[1]
    at = 0
    for part in parts:
        hidden[at : at + part.shape[0], :] = part[...]
        at += part.shape[0]
    slot, local = source[:, 0:1], source[:, 1:2]
    pick = (lax.broadcasted_iota(jnp.int32, (tokens, tokens), 1) == slot).astype(jnp.bfloat16)
    moved = mm(pick, hidden[...]).astype(jnp.bfloat16)
    mine = lax.broadcasted_iota(jnp.int32, (tokens, rows), 1) == local
    mine = mine.astype(jnp.bfloat16)
    high = middle[...].astype(jnp.bfloat16)
    low = (middle[...] - high.astype(jnp.float32)).astype(jnp.bfloat16)
    term[...] = mm(moved, down_w[...]) + (mm(mine, high) + mm(mine, low))
    for index in range(tokens // rows // 2):
        at = slice(index * rows, (index + 1) * rows)
        dest = index ^ chip if direct else index
        start = pl.multiple_of((2 * dest + core) * rows, rows)
        keep[at, :] = term[pl.ds(start, rows), :]
        start = pl.multiple_of((2 * dest + (1 - core)) * rows, rows)
        send[at, :] = term[pl.ds(start, rows), :].astype(jnp.bfloat16)


def down(direct, place, parts, source, middle, down_w):
    tokens = source.shape[0]
    units, features = down_w.shape
    return pl.pallas_call(
        functools.partial(down_kernel, direct, len(parts)),
        out_shape=(
            jax.ShapeDtypeStruct((tokens // 2, features), jnp.float32),
            jax.ShapeDtypeStruct((tokens // 2, features), jnp.bfloat16),
        ),
        in_specs=[SMEM] + [VMEM] * (len(parts) + 3),
        out_specs=(VMEM, VMEM),
        scratch_shapes=[
            pltpu.VMEM((tokens, units), jnp.bfloat16),
            pltpu.VMEM((tokens, features), jnp.float32),
        ],
        compiler_params=pltpu.CompilerParams(vmem_limit_bytes=36 * MIB),
        name="down",
    )(place, *parts, source, middle, down_w)


def add_kernel(keep, other, *outs):
    rows = outs[0].shape[0]
    for index, out in enumerate(outs):
        at = slice(index * rows, (index + 1) * rows)
        out[...] = (keep[at, :] + other[at, :].astype(jnp.float32)).astype(out.dtype)


def add_parts(keep, other, rows):
    count = keep.shape[0] // rows
    features = keep.shape[1]
    return pl.pallas_call(
        add_kernel,
        out_shape=tuple(
            jax.ShapeDtypeStruct((rows, features), jnp.bfloat16 if i else jnp.float32)
            for i in range(count)
        ),
        in_specs=[VMEM, VMEM],
        out_specs=(VMEM,) * count,
        compiler_params=pltpu.CompilerParams(vmem_limit_bytes=8 * MIB),
        name="add_parts",
    )(keep, other)


def shards(
    n_chip,
    n_blk,
    resid,
    queries,
    new_kv,
    prefix_pool,
    page_table,
    prompt_len,
    tail_pool,
    tail_len,
    migration,
    out_w,
    mlp_gain,
    gate_w,
    up_w,
    down_w,
    final_gain,
    score_w,
):
    rows = resid.shape[0]
    features = gate_w.shape[0]
    chip = lax.axis_index("chip").astype(jnp.int32)
    core = lax.axis_index("core").astype(jnp.int32)
    block = lax.axis_index("blk").astype(jnp.int32).reshape(1)
    direct = n_chip == 8 and n_blk == 2

    def to_chip(value, index):
        return lax.ppermute(value, "chip", [(i, i ^ index) for i in range(n_chip)])

    def swap(value, axis):
        return lax.ppermute(value, axis, [(0, 1), (1, 0)])

    own, send = attention(
        queries, new_kv, resid, prefix_pool, page_table, prompt_len, tail_pool, tail_len, out_w
    )
    if direct:
        other = swap(send, "blk")
    else:
        own, other = resid.astype(jnp.float32), lax.psum(send, "blk")
    normed, middle = normalize(block, own, other, mlp_gain, features, 1 if direct else n_chip)

    token = migration[:, None] * NEW + jnp.arange(NEW, dtype=jnp.int32)[None, :]
    token = token.reshape(-1, 1)
    came, inner = token // rows, token % rows
    far_core = (came % 2) ^ core
    if direct:
        piece = normed.reshape(rows, features)
        z1, z3, z2, y0 = (to_chip(piece, index) for index in (2, 6, 4, 1))
        late = [z1, z3, to_chip(z1, 1), to_chip(z3, 1)]
        early = [piece, z2, y0, to_chip(z2, 1)]
        parts = []
        for near in (late, early):
            pieces = near + [swap(piece, "core") for piece in near]
            keep, away = partial_units(True, block, pieces, gate_w, up_w)
            hidden = hidden_units(keep, swap(away, "blk"))
            parts += [hidden, swap(hidden, "blk")]
        far = (came // 2) ^ chip
        slot = ((1 - far // 2 % 2) * 2 + (far_core ^ block[0])) * 4 + far % 2 * 2 + far // 4
        slot = slot * rows + inner
    else:
        near = lax.all_to_all(normed, "chip", 0, 0).reshape(n_chip * rows, features)
        units = partial_units(False, block, [near, swap(near, "core")], gate_w, up_w)[0]
        parts = [hidden_units(lax.psum(units, "blk"))]
        slot = far_core * (n_chip * rows) + (came // 2) * rows + inner
    local = token - (chip * 2 + core) * rows
    source = jnp.concatenate([slot, local], axis=1)

    place = jnp.stack([chip, core])
    keep, away = down(direct, place, parts, source, middle, down_w)
    other_sums = swap(away, "core")
    if direct:
        parts = add_parts(keep, other_sums, rows)
        moved = parts[0]
        for index in (6, 4, 7, 5, 2, 3, 1):
            moved = moved + to_chip(parts[index], index).astype(jnp.float32)
    else:
        sums = (keep + other_sums.astype(jnp.float32)).astype(jnp.bfloat16)
        parts = lax.all_to_all(sums.reshape(n_chip, rows, features), "chip", 0, 0)
        moved = jnp.sum(parts.astype(jnp.float32), axis=0)
    weighted = final_gain.astype(jnp.float32) * score_w.astype(jnp.float32)
    stats = jnp.stack([jnp.sum(moved * moved, -1), jnp.sum(moved * weighted, -1)])
    stats = stats + swap(stats, "blk") if direct else lax.psum(stats, "blk")
    score = stats[1] * lax.rsqrt(stats[0] / D + EPS)
    return (moved.astype(jnp.bfloat16), score)


def solution(mesh):
    n_chip, n_blk = mesh.shape["dp"] // 2, mesh.shape["blk"]
    split = Mesh(mesh.devices.reshape(n_chip, 2, n_blk), ("chip", "core", "blk"))
    dp = ("chip", "core")
    return jax.shard_map(
        functools.partial(shards, n_chip, n_blk),
        mesh=split,
        in_specs=(
            P(dp, None),
            P(dp, "blk", None),
            P(dp, None, "blk", None),
            P(dp, None, None, "blk", None),
            P(dp, None),
            P(dp),
            P(dp, None, None, "blk", None),
            P(dp, None),
            P(),
            P("blk", None),
            P(),
            P("blk", dp),
            P("blk", dp),
            P(dp, "blk"),
            P("blk"),
            P("blk"),
        ),
        out_specs=(P(dp, "blk"), P(dp)),
        check_vma=False,
    )
```

```python
import functools
import math

import jax
import jax.numpy as jnp
from jax import lax
from jax.experimental import pallas as pl
from jax.experimental.pallas import tpu as pltpu
from jax.sharding import Mesh
from jax.sharding import PartitionSpec as P

D = 2048
NEW = 2
NEG = -1e30
EPS = 1e-06
MIB = 1 << 20
ATTENTION_VMEM = 60 * MIB

VMEM = pl.BlockSpec(memory_space=pltpu.VMEM)
SMEM = pl.BlockSpec(memory_space=pltpu.SMEM)
ANY = pl.BlockSpec(memory_space=pl.ANY)


def mm(a, b):
    return jnp.dot(a, b, preferred_element_type=jnp.float32)


def mm_t(a, b):
    return lax.dot_general(a, b, (((1,), (1,)), ((), ())), preferred_element_type=jnp.float32)


def attention_kernel(
    dims,
    table,
    prompt_len,
    tail_len,
    queries,
    new_kv,
    pool,
    tails,
    out_w,
    own_ref,
    send_ref,
    pages,
    tail_buf,
    w_buf,
    q_buf,
    new_buf,
    apart,
    tail_apart,
    q_wide,
    q_rows,
    new_wide,
    fresh_scores,
    tail_scores,
    scores,
    top,
    total,
    acc,
    attn,
    page_sems,
    tail_sems,
    sems,
):
    rows, heads, groups, width, n_pages, page, conts, tail, pair = dims
    repeat = heads // groups
    step = 2 * groups
    pairs = groups // pair
    stack = repeat * rows
    page_rows = page * step
    chunk_pages = math.gcd(8, n_pages)
    chunk = chunk_pages * page
    chunk_rows = chunk * step
    quad = 8 // NEW
    quads = conts // quad
    quad_keys = quad * tail
    quad_rows = quad_keys * step
    factor = math.log2(math.e) / math.sqrt(width)
    length = prompt_len[0]
    chunks = (length + chunk - 1) // chunk

    def page_copy(logical):
        physical = table[0, logical]
        return pltpu.make_async_copy(
            pool.at[pl.ds(pl.multiple_of(physical * page_rows, page_rows), page_rows), :],
            pages.at[pl.ds(pl.multiple_of(logical * page_rows, page_rows), page_rows), :],
            page_sems.at[logical],
        )

    def tail_copy(index):
        return pltpu.make_async_copy(
            tails.at[pl.ds(index * quad_rows, quad_rows), :],
            tail_buf.at[pl.ds(index * quad_rows, quad_rows), :],
            tail_sems.at[index],
        )

    q_copy = pltpu.make_async_copy(queries, q_buf, sems.at[0])
    new_copy = pltpu.make_async_copy(new_kv, new_buf, sems.at[1])
    w_copy = pltpu.make_async_copy(out_w, w_buf, sems.at[2])
    q_copy.start()
    new_copy.start()
    for index in range(quads):
        tail_copy(index).start()

    @pl.loop(0, chunks * chunk_pages)
    def _(logical):
        page_copy(logical).start()

    w_copy.start()

    block = 256
    tokens = block // step
    to = lax.broadcasted_iota(jnp.int32, (block, block), 0)
    came = lax.broadcasted_iota(jnp.int32, (block, block), 1)
    sort = (came == (to % tokens) * step + to // tokens).astype(jnp.bfloat16)

    def take_apart(buf, start, count, out, at):
        for two in range(count // (2 * block)):
            x0 = buf[pl.ds(start + two * 2 * block, block), :]
            x1 = buf[pl.ds(start + (two * 2 + 1) * block, block), :]
            y = mm(sort, jnp.concatenate([x0, x1], axis=1)).astype(jnp.bfloat16)
            for side in range(2):
                t = pl.ds(at + (2 * two + side) * tokens, tokens)
                for j in range(step):
                    kind, g = j // groups, j % groups
                    lane = (g % pair) * width
                    out[kind, g // pair, t, lane : lane + width] = y[
                        j * tokens : (j + 1) * tokens, side * width : (side + 1) * width
                    ]

    def blocks(x):
        return [x[:, i * 128 : (i + 1) * 128] for i in range(x.shape[1] // 128)]

    q_copy.wait()
    new_copy.wait()
    q_wide[...] = q_buf[...].astype(jnp.float32)
    new_wide[...] = new_buf[...].astype(jnp.float32)
    if pair > 1:
        q_rows[...] = jnp.zeros_like(q_rows)
    for g in range(groups):
        for r in range(repeat):
            at = (g % pair) * stack + r * rows
            lane = (g % pair) * width
            q_rows[g // pair, at : at + rows, lane : lane + width] = q_wide[
                pl.ds(g * repeat + r, rows, stride=heads), :
            ]

    def fresh(first, n):
        parts = [
            new_wide[pl.ds(first + n * pair + i, rows, stride=step), :] for i in range(pair)
        ]
        return jnp.concatenate(parts, axis=1).astype(jnp.bfloat16)

    row = lax.broadcasted_iota(jnp.int32, (rows, rows), 0)
    key = lax.broadcasted_iota(jnp.int32, (rows, rows), 1)
    fresh_ok = (row // NEW == key // NEW) & (key <= row)
    fresh_ok = jnp.concatenate([fresh_ok] * (pair * repeat), axis=0)
    for n in range(pairs):
        s = jnp.where(fresh_ok, mm_t(q_rows[n].astype(jnp.bfloat16), fresh(0, n)) * factor, NEG)
        fresh_scores[n] = s
        top[n] = jnp.broadcast_to(jnp.max(s, axis=1, keepdims=True), top.shape[1:])

    def quad_places(index):
        starts = [i * rows + index * 8 for i in range(pair * repeat)]
        return [slice(at, at + 8) for at in starts]

    quad_row = lax.broadcasted_iota(jnp.int32, (8, quad_keys), 0)
    quad_key = lax.broadcasted_iota(jnp.int32, (8, quad_keys), 1)
    for index in range(quads):
        tail_copy(index).wait()
        take_apart(tail_buf, index * quad_rows, quad_rows, tail_apart, index * quad_keys)
        reach = jnp.zeros((8, quad_keys), jnp.int32)
        for c in range(quad):
            reach = jnp.where(
                quad_key // tail == c, tail_len[0, index * quad + c] + c * tail, reach
            )
        ok = (quad_row // NEW == quad_key // tail) & (quad_key < reach)
        ok = jnp.concatenate([ok] * (pair * repeat), axis=0)
        keys = slice(index * quad_keys, (index + 1) * quad_keys)
        for n in range(pairs):
            q = jnp.concatenate([q_rows[n, a, :] for a in quad_places(index)], axis=0)
            s = mm_t(q.astype(jnp.bfloat16), tail_apart[0, n, keys, :]) * factor
            s = jnp.where(ok, s, NEG)
            tail_scores[n, index] = s
            high = functools.reduce(jnp.maximum, blocks(s))
            for i, a in enumerate(quad_places(index)):
                top[n, a, :] = jnp.maximum(top[n, a, :], high[i * 8 : (i + 1) * 8])

    place = lax.broadcasted_iota(jnp.int32, (8, chunk), 1)

    @pl.loop(0, chunks)
    def _(index):
        for i in range(chunk_pages):
            page_copy(index * chunk_pages + i).wait()
        first = pl.multiple_of(index * chunk, chunk)
        take_apart(pages, pl.multiple_of(index * chunk_rows, chunk_rows), chunk_rows, apart, first)
        ok = place[0:1] < length - index * chunk
        for n in range(pairs):
            s = mm_t(q_rows[n].astype(jnp.bfloat16), apart[0, n, pl.ds(first, chunk), :]) * factor
            s = jnp.where(ok, s, NEG)
            scores[n, :, pl.ds(first, chunk)] = s
            top[n] = functools.reduce(jnp.maximum, blocks(s), top[n])

    for n in range(pairs):
        high = jnp.broadcast_to(jnp.max(top[n], axis=1, keepdims=True), top.shape[1:])
        top[n] = high
        p = jnp.exp2(fresh_scores[n] - high[:, :rows])
        lane = lax.broadcasted_iota(jnp.int32, total.shape[1:], 1)
        total[n] = jnp.where(lane == 0, jnp.sum(p, axis=1, keepdims=True), 0.0)
        acc[n] = mm(p.astype(jnp.bfloat16), fresh(groups, n))

    def weigh(s, high):
        parts = [jnp.exp2(part - high) for part in blocks(s)]
        return jnp.concatenate(parts, axis=1).astype(jnp.bfloat16), functools.reduce(jnp.add, parts)

    for index in range(quads):
        keys = slice(index * quad_keys, (index + 1) * quad_keys)
        for n in range(pairs):
            high = jnp.concatenate([top[n, a, :] for a in quad_places(index)], axis=0)
            p, added = weigh(tail_scores[n, index], high)
            value = mm(p, tail_apart[1, n, keys, :])
            for i, a in enumerate(quad_places(index)):
                total[n, a, :] = total[n, a, :] + added[i * 8 : (i + 1) * 8]
                acc[n, a, :] = acc[n, a, :] + value[i * 8 : (i + 1) * 8]

    @pl.loop(0, chunks)
    def _(index):
        first = pl.multiple_of(index * chunk, chunk)
        for n in range(pairs):
            p, added = weigh(scores[n, :, pl.ds(first, chunk)], top[n])
            total[n] = total[n] + added
            acc[n] = acc[n] + mm(p, apart[1, n, pl.ds(first, chunk), :])

    for g in range(groups):
        at, lane = (g % pair) * stack, (g % pair) * width
        out = acc[g // pair, at : at + stack, lane : lane + width]
        out = out / jnp.sum(total[g // pair, at : at + stack, :], axis=1, keepdims=True)
        out = out.astype(jnp.bfloat16)
        for r in range(repeat):
            head = g * repeat + r
            attn[:, head * width : (head + 1) * width] = out[r * rows : (r + 1) * rows]
    w_copy.wait()
    value = mm(attn[...], w_buf[...])
    own_ref[...] = value
    send_ref[...] = value.astype(jnp.bfloat16)


def attention(queries, new_kv, pool, table, prompt_len, tails, tail_len, out_w):
    rows, heads, width = queries.shape
    n_pages, page, _, groups, _ = pool.shape
    conts, tail = tails.shape[:2]
    step = 2 * groups
    features = out_w.shape[1]
    quads = conts * NEW // 8
    pair = 2 if groups % 2 == 0 else 1
    pairs = groups // pair
    repeat = heads // groups
    stack = pair * repeat * rows
    return pl.pallas_call(
        functools.partial(
            attention_kernel, (rows, heads, groups, width, n_pages, page, conts, tail, pair)
        ),
        out_shape=(
            jax.ShapeDtypeStruct((rows, features), jnp.float32),
            jax.ShapeDtypeStruct((rows, features), jnp.bfloat16),
        ),
        in_specs=[SMEM, SMEM, SMEM, ANY, ANY, ANY, ANY, ANY],
        out_specs=(VMEM, VMEM),
        scratch_shapes=[
            pltpu.VMEM((n_pages * page * step, width), jnp.bfloat16),
            pltpu.VMEM((conts * tail * step, width), jnp.bfloat16),
            pltpu.VMEM(out_w.shape, jnp.bfloat16),
            pltpu.VMEM((rows * heads, width), jnp.bfloat16),
            pltpu.VMEM((rows * step, width), jnp.bfloat16),
            pltpu.VMEM((2, pairs, n_pages * page, pair * width), jnp.bfloat16),
            pltpu.VMEM((2, pairs, conts * tail, pair * width), jnp.bfloat16),
            pltpu.VMEM((rows * heads, width), jnp.float32),
            pltpu.VMEM((pairs, stack, pair * width), jnp.float32),
            pltpu.VMEM((rows * step, width), jnp.float32),
            pltpu.VMEM((pairs, stack, rows), jnp.float32),
            pltpu.VMEM((pairs, quads, pair * repeat * 8, 8 // NEW * tail), jnp.float32),
            pltpu.VMEM((pairs, stack, n_pages * page), jnp.float32),
            pltpu.VMEM((pairs, stack, 128), jnp.float32),
            pltpu.VMEM((pairs, stack, 128), jnp.float32),
            pltpu.VMEM((pairs, stack, pair * width), jnp.float32),
            pltpu.VMEM((rows, heads * width), jnp.bfloat16),
            pltpu.SemaphoreType.DMA((n_pages,)),
            pltpu.SemaphoreType.DMA((quads,)),
            pltpu.SemaphoreType.DMA((3,)),
        ],
        compiler_params=pltpu.CompilerParams(vmem_limit_bytes=ATTENTION_VMEM),
        name="attention",
    )(
        table,
        prompt_len,
        tail_len,
        queries.reshape(rows * heads, width),
        new_kv.reshape(rows * step, width),
        pool.reshape(n_pages * page * step, width),
        tails.reshape(conts * tail * step, width),
        out_w,
    )


def norm_kernel(place, own, other, gain, normed, middle, whole):
    copies, rows, features = normed.shape
    mid = own[...] + other[...].astype(jnp.float32)
    scale = lax.rsqrt(jnp.mean(mid * mid, axis=1, keepdims=True) + EPS)
    whole[...] = mid
    start = pl.multiple_of(place[0] * features, features)
    part = whole[:, pl.ds(start, features)]
    out = (part * scale * gain[:, pl.ds(start, features)]).astype(jnp.bfloat16)
    for index in range(copies):
        normed[index] = out
    middle[...] = part


def normalize(block, own, other, gain, features, copies):
    rows = own.shape[0]
    return pl.pallas_call(
        norm_kernel,
        out_shape=(
            jax.ShapeDtypeStruct((copies, rows, features), jnp.bfloat16),
            jax.ShapeDtypeStruct((rows, features), jnp.float32),
        ),
        in_specs=[SMEM, VMEM, VMEM, VMEM],
        out_specs=(VMEM, VMEM),
        scratch_shapes=[pltpu.VMEM(own.shape, jnp.float32)],
        compiler_params=pltpu.CompilerParams(vmem_limit_bytes=8 * MIB),
        name="normalize",
    )(block, own, other, gain.astype(jnp.float32).reshape(1, -1))


def units_kernel(n, place, *refs):
    pieces, gate_w, up_w, outs, held, sums = refs[:n], *refs[n : n + 2], refs[n + 2 : -2], *refs[-2:]
    at = 0
    for piece in pieces:
        held[at : at + piece.shape[0], :] = piece[...]
        at += piece.shape[0]
    units = gate_w.shape[1]
    sums[:, :units] = mm(held[...], gate_w[...])
    sums[:, units:] = mm(held[...], up_w[...])
    if len(outs) == 1:
        outs[0][...] = sums[...].astype(jnp.bfloat16)
        return
    keep, send = outs
    half = at // 2
    keep[...] = sums[pl.ds(pl.multiple_of(place[0] * half, half), half), :]
    send[...] = sums[pl.ds(pl.multiple_of((1 - place[0]) * half, half), half), :].astype(
        jnp.bfloat16
    )


def partial_units(split, block, pieces, gate_w, up_w):
    tokens = sum(piece.shape[0] for piece in pieces)
    features, units = gate_w.shape
    if split:
        out_shape = (
            jax.ShapeDtypeStruct((tokens // 2, 2 * units), jnp.float32),
            jax.ShapeDtypeStruct((tokens // 2, 2 * units), jnp.bfloat16),
        )
    else:
        out_shape = (jax.ShapeDtypeStruct((tokens, 2 * units), jnp.bfloat16),)
    return pl.pallas_call(
        functools.partial(units_kernel, len(pieces)),
        out_shape=out_shape,
        in_specs=[SMEM] + [VMEM] * (len(pieces) + 2),
        out_specs=(VMEM,) * len(out_shape),
        scratch_shapes=[
            pltpu.VMEM((tokens, features), jnp.bfloat16),
            pltpu.VMEM((tokens, 2 * units), jnp.float32),
        ],
        compiler_params=pltpu.CompilerParams(vmem_limit_bytes=16 * MIB),
        cost_estimate=pl.CostEstimate(
            flops=4 * tokens * features * units,
            bytes_accessed=2 * tokens * features + 4 * features * units,
            transcendentals=0,
        ),
        name="gate_up",
    )(block, *pieces, gate_w, up_w)


def hidden_kernel(*refs):
    sums, out = refs[:-1], refs[-1]
    both = functools.reduce(jnp.add, [ref[...].astype(jnp.float32) for ref in sums])
    units = out.shape[1]
    gate, up = both[:, :units], both[:, units:]
    out[...] = (gate / (1.0 + jnp.exp(-gate)) * up).astype(jnp.bfloat16)


def hidden_units(*sums):
    tokens, units = sums[0].shape[0], sums[0].shape[1] // 2
    return pl.pallas_call(
        hidden_kernel,
        out_shape=jax.ShapeDtypeStruct((tokens, units), jnp.bfloat16),
        in_specs=[VMEM] * len(sums),
        out_specs=VMEM,
        compiler_params=pltpu.CompilerParams(vmem_limit_bytes=8 * MIB),
        name="hidden",
    )(*sums)


def down_kernel(orders, flip, n, place, *refs):
    parts, source, middle, down_w = refs[:n], *refs[n : n + 3]
    outs, hidden, term = refs[n + 3 : -2], *refs[-2:]
    tokens, features = term.shape
    rows = middle.shape[0]
    chip, core = place[0], place[1]
    at = 0
    for part in parts:
        hidden[at : at + part.shape[0], :] = part[...]
        at += part.shape[0]
    slot, local = source[:, 0:1], source[:, 1:2]
    pick = (lax.broadcasted_iota(jnp.int32, (tokens, tokens), 1) == slot).astype(jnp.bfloat16)
    moved = mm(pick, hidden[...]).astype(jnp.bfloat16)
    mine = lax.broadcasted_iota(jnp.int32, (tokens, rows), 1) == local
    mine = mine.astype(jnp.bfloat16)
    high = middle[...].astype(jnp.bfloat16)
    low = (middle[...] - high.astype(jnp.float32)).astype(jnp.bfloat16)
    term[...] = mm(moved, down_w[...]) + (mm(mine, high) + mm(mine, low))
    for order, keep, send in zip(orders, outs[::2], outs[1::2]):
        for index, dest in enumerate(order):
            at = slice(index * rows, (index + 1) * rows)
            dest = dest ^ chip if flip else dest
            start = pl.multiple_of((2 * dest + core) * rows, rows)
            keep[at, :] = term[pl.ds(start, rows), :]
            start = pl.multiple_of((2 * dest + (1 - core)) * rows, rows)
            send[at, :] = term[pl.ds(start, rows), :].astype(jnp.bfloat16)


def down(orders, flip, place, parts, source, middle, down_w):
    tokens = source.shape[0]
    units, features = down_w.shape
    rows = middle.shape[0]
    out_shape = ()
    for order in orders:
        shape = (len(order) * rows, features)
        out_shape += (
            jax.ShapeDtypeStruct(shape, jnp.float32),
            jax.ShapeDtypeStruct(shape, jnp.bfloat16),
        )
    outs = pl.pallas_call(
        functools.partial(down_kernel, orders, flip, len(parts)),
        out_shape=out_shape,
        in_specs=[SMEM] + [VMEM] * (len(parts) + 3),
        out_specs=(VMEM,) * len(out_shape),
        scratch_shapes=[
            pltpu.VMEM((tokens, units), jnp.bfloat16),
            pltpu.VMEM((tokens, features), jnp.float32),
        ],
        compiler_params=pltpu.CompilerParams(vmem_limit_bytes=36 * MIB),
        name="down",
    )(place, *parts, source, middle, down_w)
    return list(zip(outs[::2], outs[1::2]))


def pack_kernel(n, *refs):
    pieces, out = refs[:n], refs[-1]
    at = 0
    for piece in pieces:
        out[at : at + piece.shape[0], :] = piece[...]
        at += piece.shape[0]


def pack(pieces, after=()):
    rows = sum(piece.shape[0] for piece in pieces)
    return pl.pallas_call(
        functools.partial(pack_kernel, len(pieces)),
        out_shape=jax.ShapeDtypeStruct((rows, pieces[0].shape[1]), pieces[0].dtype),
        in_specs=[VMEM] * len(pieces) + [ANY] * len(after),
        out_specs=VMEM,
        compiler_params=pltpu.CompilerParams(vmem_limit_bytes=4 * MIB),
        name="pack",
    )(*pieces, *after)


def add_kernel(keep, other, *outs):
    at = 0
    for out in outs:
        to = at + out.shape[0]
        out[...] = (keep[at:to, :] + other[at:to, :].astype(jnp.float32)).astype(out.dtype)
        at = to


def add_parts(keep, other, kinds):
    rows, features = keep.shape
    return pl.pallas_call(
        add_kernel,
        out_shape=tuple(
            jax.ShapeDtypeStruct((rows // len(kinds), features), kind) for kind in kinds
        ),
        in_specs=[VMEM, VMEM],
        out_specs=(VMEM,) * len(kinds),
        compiler_params=pltpu.CompilerParams(vmem_limit_bytes=4 * MIB),
        name="add_parts",
    )(keep, other)


def finish_kernel(n, *refs):
    parts, gain, score, out, stats = refs[:n], *refs[n:]
    moved = functools.reduce(jnp.add, [part[...].astype(jnp.float32) for part in parts])
    out[...] = moved.astype(jnp.bfloat16)
    weighted = gain[...].astype(jnp.float32) * score[...].astype(jnp.float32)
    lane = lax.broadcasted_iota(jnp.int32, stats.shape, 1)
    squares = jnp.sum(moved * moved, axis=1, keepdims=True)
    terms = jnp.sum(moved * weighted, axis=1, keepdims=True)
    stats[...] = jnp.where(lane == 0, squares, terms)


def finish(parts, gain, score):
    rows, features = parts[0].shape
    return pl.pallas_call(
        functools.partial(finish_kernel, len(parts)),
        out_shape=(
            jax.ShapeDtypeStruct((rows, features), jnp.bfloat16),
            jax.ShapeDtypeStruct((rows, 128), jnp.float32),
        ),
        in_specs=[VMEM] * (len(parts) + 2),
        out_specs=(VMEM, VMEM),
        compiler_params=pltpu.CompilerParams(vmem_limit_bytes=4 * MIB),
        name="finish",
    )(*parts, gain.reshape(1, -1), score.reshape(1, -1))


def shards(
    n_chip,
    n_blk,
    resid,
    queries,
    new_kv,
    prefix_pool,
    page_table,
    prompt_len,
    tail_pool,
    tail_len,
    migration,
    out_w,
    mlp_gain,
    gate_w,
    up_w,
    down_w,
    final_gain,
    score_w,
):
    rows = resid.shape[0]
    features = gate_w.shape[0]
    chip = lax.axis_index("chip").astype(jnp.int32)
    core = lax.axis_index("core").astype(jnp.int32)
    block = lax.axis_index("blk").astype(jnp.int32).reshape(1)
    direct = n_chip == 8 and n_blk == 2

    def to_chip(value, index):
        return lax.ppermute(value, "chip", [(i, i ^ index) for i in range(n_chip)])

    def swap(value, axis):
        return lax.ppermute(value, axis, [(0, 1), (1, 0)])

    own, send = attention(
        queries, new_kv, prefix_pool, page_table, prompt_len, tail_pool, tail_len, out_w
    )
    if direct:
        own, other = own + resid.astype(jnp.float32), swap(send, "blk")
    else:
        own, other = resid.astype(jnp.float32), lax.psum(send, "blk")
    normed, middle = normalize(block, own, other, mlp_gain, features, 1 if direct else n_chip)

    token = migration[:, None] * NEW + jnp.arange(NEW, dtype=jnp.int32)[None, :]
    token = token.reshape(-1, 1)
    came, inner = token // rows, token % rows
    far_core = (came % 2) ^ core
    if direct:
        piece = normed.reshape(rows, features)
        z1, z3, z2, y0 = (to_chip(piece, index) for index in (2, 6, 4, 1))
        late = [z1, z3, to_chip(z1, 1), to_chip(z3, 1)]
        early = [piece, z2, y0, to_chip(z2, 1)]
        parts, after = [], ()
        for pieces in (early, late):
            near = pack(pieces, after)
            keep, away = partial_units(True, block, [near, swap(near, "core")], gate_w, up_w)
            hidden = hidden_units(keep, swap(away, "blk"))
            parts += [hidden, swap(hidden, "blk")]
            after = (keep,)
        far = (came // 2) ^ chip
        slot = (far // 2 % 2 * 2 + (far_core ^ block[0])) * 4 + far % 2 * 2 + far // 4
        slot = slot * rows + inner
    else:
        near = lax.all_to_all(normed, "chip", 0, 0).reshape(n_chip * rows, features)
        units = partial_units(False, block, [near, swap(near, "core")], gate_w, up_w)[0]
        parts = [hidden_units(lax.psum(units, "blk"))]
        slot = far_core * (n_chip * rows) + (came // 2) * rows + inner
    local = token - (chip * 2 + core) * rows
    source = jnp.concatenate([slot, local], axis=1)

    place = jnp.stack([chip, core])
    if direct:
        wide, far = down(((4, 6, 5, 7), (0, 2, 1, 3)), True, place, parts, source, middle, down_w)
        kinds = (jnp.float32, jnp.bfloat16)
        wide = add_parts(wide[0], swap(wide[1], "core"), kinds)
        far = add_parts(far[0], swap(far[1], "core"), kinds)
        to4, to6 = add_parts(wide[0], to_chip(wide[1], 1), (jnp.bfloat16, jnp.bfloat16))
        mine, to2 = add_parts(far[0], to_chip(far[1], 1), (jnp.float32, jnp.bfloat16))
        sums = [mine, to_chip(to4, 4), to_chip(to6, 6), to_chip(to2, 2)]
    else:
        order = tuple(range(n_chip))
        ((keep, away),) = down((order,), False, place, parts, source, middle, down_w)
        total = (keep + swap(away, "core").astype(jnp.float32)).astype(jnp.bfloat16)
        total = lax.all_to_all(total.reshape(n_chip, rows, features), "chip", 0, 0)
        sums = [jnp.sum(total.astype(jnp.float32), axis=0)]
    hidden_out, stats = finish(sums, final_gain, score_w)
    stats = stats + swap(stats, "blk") if direct else lax.psum(stats, "blk")
    score = stats[:, 1] * lax.rsqrt(stats[:, 0] / D + EPS)
    return (hidden_out, score)


def solution(mesh):
    n_chip, n_blk = mesh.shape["dp"] // 2, mesh.shape["blk"]
    split = Mesh(mesh.devices.reshape(n_chip, 2, n_blk), ("chip", "core", "blk"))
    dp = ("chip", "core")
    return jax.shard_map(
        functools.partial(shards, n_chip, n_blk),
        mesh=split,
        in_specs=(
            P(dp, None),
            P(dp, "blk", None),
            P(dp, None, "blk", None),
            P(dp, None, None, "blk", None),
            P(dp, None),
            P(dp),
            P(dp, None, None, "blk", None),
            P(dp, None),
            P(),
            P("blk", None),
            P(),
            P("blk", dp),
            P("blk", dp),
            P(dp, "blk"),
            P("blk"),
            P("blk"),
        ),
        out_specs=(P(dp, "blk"), P(dp)),
        check_vma=False,
    )
```

```python
import functools
import math

import jax
import jax.numpy as jnp
from jax import lax
from jax.experimental import pallas as pl
from jax.experimental.pallas import tpu as pltpu
from jax.sharding import Mesh
from jax.sharding import PartitionSpec as P

D = 2048
NEW = 2
NEG = -1e30
EPS = 1e-06
MIB = 1 << 20
ATTENTION_VMEM = 60 * MIB
UNITS_VMEM = 6 * MIB
DOWN_VMEM = 12 * MIB

VMEM = pl.BlockSpec(memory_space=pltpu.VMEM)
SMEM = pl.BlockSpec(memory_space=pltpu.SMEM)
ANY = pl.BlockSpec(memory_space=pl.ANY)


def mm(a, b):
    return jnp.dot(a, b, preferred_element_type=jnp.float32)


def mm_t(a, b):
    return lax.dot_general(a, b, (((1,), (1,)), ((), ())), preferred_element_type=jnp.float32)


def attention_kernel(
    dims,
    table,
    prompt_len,
    tail_len,
    queries,
    new_kv,
    pool,
    tails,
    out_w,
    own_ref,
    send_ref,
    pages,
    tail_buf,
    w_buf,
    q_buf,
    new_buf,
    apart,
    tail_apart,
    q_wide,
    q_rows,
    new_wide,
    fresh_scores,
    tail_scores,
    scores,
    top,
    total,
    acc,
    attn,
    page_sems,
    tail_sems,
    sems,
):
    rows, heads, groups, width, n_pages, page, conts, tail, pair = dims
    repeat = heads // groups
    step = 2 * groups
    pairs = groups // pair
    stack = repeat * rows
    page_rows = page * step
    chunk_pages = math.gcd(8, n_pages)
    chunk = chunk_pages * page
    chunk_rows = chunk * step
    quad = 8 // NEW
    quads = conts // quad
    quad_keys = quad * tail
    quad_rows = quad_keys * step
    factor = math.log2(math.e) / math.sqrt(width)
    length = prompt_len[0]
    chunks = (length + chunk - 1) // chunk

    def page_copy(logical):
        physical = table[0, logical]
        return pltpu.make_async_copy(
            pool.at[pl.ds(pl.multiple_of(physical * page_rows, page_rows), page_rows), :],
            pages.at[pl.ds(pl.multiple_of(logical * page_rows, page_rows), page_rows), :],
            page_sems.at[logical],
        )

    def tail_copy(index):
        return pltpu.make_async_copy(
            tails.at[pl.ds(index * quad_rows, quad_rows), :],
            tail_buf.at[pl.ds(index * quad_rows, quad_rows), :],
            tail_sems.at[index],
        )

    q_copy = pltpu.make_async_copy(queries, q_buf, sems.at[0])
    new_copy = pltpu.make_async_copy(new_kv, new_buf, sems.at[1])
    w_copy = pltpu.make_async_copy(out_w, w_buf, sems.at[2])
    q_copy.start()
    new_copy.start()
    for index in range(quads):
        tail_copy(index).start()

    @pl.loop(0, chunks * chunk_pages)
    def _(logical):
        page_copy(logical).start()

    w_copy.start()

    block = 256
    tokens = block // step
    to = lax.broadcasted_iota(jnp.int32, (block, block), 0)
    came = lax.broadcasted_iota(jnp.int32, (block, block), 1)
    sort = (came == (to % tokens) * step + to // tokens).astype(jnp.bfloat16)

    def take_apart(buf, start, count, out, at):
        for two in range(count // (2 * block)):
            x0 = buf[pl.ds(start + two * 2 * block, block), :]
            x1 = buf[pl.ds(start + (two * 2 + 1) * block, block), :]
            y = mm(sort, jnp.concatenate([x0, x1], axis=1)).astype(jnp.bfloat16)
            for side in range(2):
                t = pl.ds(at + (2 * two + side) * tokens, tokens)
                for j in range(step):
                    kind, g = j // groups, j % groups
                    lane = (g % pair) * width
                    out[kind, g // pair, t, lane : lane + width] = y[
                        j * tokens : (j + 1) * tokens, side * width : (side + 1) * width
                    ]

    def blocks(x):
        return [x[:, i * 128 : (i + 1) * 128] for i in range(x.shape[1] // 128)]

    q_copy.wait()
    new_copy.wait()
    q_wide[...] = q_buf[...].astype(jnp.float32)
    new_wide[...] = new_buf[...].astype(jnp.float32)
    if pair > 1:
        q_rows[...] = jnp.zeros_like(q_rows)
    for g in range(groups):
        for r in range(repeat):
            at = (g % pair) * stack + r * rows
            lane = (g % pair) * width
            q_rows[g // pair, at : at + rows, lane : lane + width] = q_wide[
                pl.ds(g * repeat + r, rows, stride=heads), :
            ]

    def fresh(first, n):
        parts = [
            new_wide[pl.ds(first + n * pair + i, rows, stride=step), :] for i in range(pair)
        ]
        return jnp.concatenate(parts, axis=1).astype(jnp.bfloat16)

    row = lax.broadcasted_iota(jnp.int32, (rows, rows), 0)
    key = lax.broadcasted_iota(jnp.int32, (rows, rows), 1)
    fresh_ok = (row // NEW == key // NEW) & (key <= row)
    fresh_ok = jnp.concatenate([fresh_ok] * (pair * repeat), axis=0)
    for n in range(pairs):
        s = jnp.where(fresh_ok, mm_t(q_rows[n].astype(jnp.bfloat16), fresh(0, n)) * factor, NEG)
        fresh_scores[n] = s
        top[n] = jnp.broadcast_to(jnp.max(s, axis=1, keepdims=True), top.shape[1:])

    def quad_places(index):
        starts = [i * rows + index * 8 for i in range(pair * repeat)]
        return [slice(at, at + 8) for at in starts]

    quad_row = lax.broadcasted_iota(jnp.int32, (8, quad_keys), 0)
    quad_key = lax.broadcasted_iota(jnp.int32, (8, quad_keys), 1)
    for index in range(quads):
        tail_copy(index).wait()
        take_apart(tail_buf, index * quad_rows, quad_rows, tail_apart, index * quad_keys)
        reach = jnp.zeros((8, quad_keys), jnp.int32)
        for c in range(quad):
            reach = jnp.where(
                quad_key // tail == c, tail_len[0, index * quad + c] + c * tail, reach
            )
        ok = (quad_row // NEW == quad_key // tail) & (quad_key < reach)
        ok = jnp.concatenate([ok] * (pair * repeat), axis=0)
        keys = slice(index * quad_keys, (index + 1) * quad_keys)
        for n in range(pairs):
            q = jnp.concatenate([q_rows[n, a, :] for a in quad_places(index)], axis=0)
            s = mm_t(q.astype(jnp.bfloat16), tail_apart[0, n, keys, :]) * factor
            s = jnp.where(ok, s, NEG)
            tail_scores[n, index] = s
            high = functools.reduce(jnp.maximum, blocks(s))
            for i, a in enumerate(quad_places(index)):
                top[n, a, :] = jnp.maximum(top[n, a, :], high[i * 8 : (i + 1) * 8])

    place = lax.broadcasted_iota(jnp.int32, (8, chunk), 1)

    @pl.loop(0, chunks)
    def _(index):
        for i in range(chunk_pages):
            page_copy(index * chunk_pages + i).wait()
        first = pl.multiple_of(index * chunk, chunk)
        take_apart(pages, pl.multiple_of(index * chunk_rows, chunk_rows), chunk_rows, apart, first)
        ok = place[0:1] < length - index * chunk
        for n in range(pairs):
            s = mm_t(q_rows[n].astype(jnp.bfloat16), apart[0, n, pl.ds(first, chunk), :]) * factor
            s = jnp.where(ok, s, NEG)
            scores[n, :, pl.ds(first, chunk)] = s
            top[n] = functools.reduce(jnp.maximum, blocks(s), top[n])

    for n in range(pairs):
        high = jnp.broadcast_to(jnp.max(top[n], axis=1, keepdims=True), top.shape[1:])
        top[n] = high
        p = jnp.exp2(fresh_scores[n] - high[:, :rows])
        lane = lax.broadcasted_iota(jnp.int32, total.shape[1:], 1)
        total[n] = jnp.where(lane == 0, jnp.sum(p, axis=1, keepdims=True), 0.0)
        acc[n] = mm(p.astype(jnp.bfloat16), fresh(groups, n))

    def weigh(s, high):
        parts = [jnp.exp2(part - high) for part in blocks(s)]
        return jnp.concatenate(parts, axis=1).astype(jnp.bfloat16), functools.reduce(jnp.add, parts)

    for index in range(quads):
        keys = slice(index * quad_keys, (index + 1) * quad_keys)
        for n in range(pairs):
            high = jnp.concatenate([top[n, a, :] for a in quad_places(index)], axis=0)
            p, added = weigh(tail_scores[n, index], high)
            value = mm(p, tail_apart[1, n, keys, :])
            for i, a in enumerate(quad_places(index)):
                total[n, a, :] = total[n, a, :] + added[i * 8 : (i + 1) * 8]
                acc[n, a, :] = acc[n, a, :] + value[i * 8 : (i + 1) * 8]

    @pl.loop(0, chunks)
    def _(index):
        first = pl.multiple_of(index * chunk, chunk)
        for n in range(pairs):
            p, added = weigh(scores[n, :, pl.ds(first, chunk)], top[n])
            total[n] = total[n] + added
            acc[n] = acc[n] + mm(p, apart[1, n, pl.ds(first, chunk), :])

    for g in range(groups):
        at, lane = (g % pair) * stack, (g % pair) * width
        out = acc[g // pair, at : at + stack, lane : lane + width]
        out = out / jnp.sum(total[g // pair, at : at + stack, :], axis=1, keepdims=True)
        out = out.astype(jnp.bfloat16)
        for r in range(repeat):
            head = g * repeat + r
            attn[:, head * width : (head + 1) * width] = out[r * rows : (r + 1) * rows]
    w_copy.wait()
    value = mm(attn[...], w_buf[...])
    own_ref[...] = value
    send_ref[...] = value.astype(jnp.bfloat16)


def attention(queries, new_kv, pool, table, prompt_len, tails, tail_len, out_w):
    rows, heads, width = queries.shape
    n_pages, page, _, groups, _ = pool.shape
    conts, tail = tails.shape[:2]
    step = 2 * groups
    features = out_w.shape[1]
    quads = conts * NEW // 8
    pair = 2 if groups % 2 == 0 else 1
    pairs = groups // pair
    repeat = heads // groups
    stack = pair * repeat * rows
    return pl.pallas_call(
        functools.partial(
            attention_kernel, (rows, heads, groups, width, n_pages, page, conts, tail, pair)
        ),
        out_shape=(
            jax.ShapeDtypeStruct((rows, features), jnp.float32),
            jax.ShapeDtypeStruct((rows, features), jnp.bfloat16),
        ),
        in_specs=[SMEM, SMEM, SMEM, ANY, ANY, ANY, ANY, ANY],
        out_specs=(VMEM, VMEM),
        scratch_shapes=[
            pltpu.VMEM((n_pages * page * step, width), jnp.bfloat16),
            pltpu.VMEM((conts * tail * step, width), jnp.bfloat16),
            pltpu.VMEM(out_w.shape, jnp.bfloat16),
            pltpu.VMEM((rows * heads, width), jnp.bfloat16),
            pltpu.VMEM((rows * step, width), jnp.bfloat16),
            pltpu.VMEM((2, pairs, n_pages * page, pair * width), jnp.bfloat16),
            pltpu.VMEM((2, pairs, conts * tail, pair * width), jnp.bfloat16),
            pltpu.VMEM((rows * heads, width), jnp.float32),
            pltpu.VMEM((pairs, stack, pair * width), jnp.float32),
            pltpu.VMEM((rows * step, width), jnp.float32),
            pltpu.VMEM((pairs, stack, rows), jnp.float32),
            pltpu.VMEM((pairs, quads, pair * repeat * 8, 8 // NEW * tail), jnp.float32),
            pltpu.VMEM((pairs, stack, n_pages * page), jnp.float32),
            pltpu.VMEM((pairs, stack, 128), jnp.float32),
            pltpu.VMEM((pairs, stack, 128), jnp.float32),
            pltpu.VMEM((pairs, stack, pair * width), jnp.float32),
            pltpu.VMEM((rows, heads * width), jnp.bfloat16),
            pltpu.SemaphoreType.DMA((n_pages,)),
            pltpu.SemaphoreType.DMA((quads,)),
            pltpu.SemaphoreType.DMA((3,)),
        ],
        compiler_params=pltpu.CompilerParams(vmem_limit_bytes=ATTENTION_VMEM),
        name="attention",
    )(
        table,
        prompt_len,
        tail_len,
        queries.reshape(rows * heads, width),
        new_kv.reshape(rows * step, width),
        pool.reshape(n_pages * page * step, width),
        tails.reshape(conts * tail * step, width),
        out_w,
    )


def norm_kernel(place, own, other, gain, normed, middle, whole):
    copies, rows, features = normed.shape
    mid = own[...] + other[...].astype(jnp.float32)
    scale = lax.rsqrt(jnp.mean(mid * mid, axis=1, keepdims=True) + EPS)
    whole[...] = mid
    start = pl.multiple_of(place[0] * features, features)
    part = whole[:, pl.ds(start, features)]
    out = (part * scale * gain[:, pl.ds(start, features)]).astype(jnp.bfloat16)
    for index in range(copies):
        normed[index] = out
    middle[...] = part


def normalize(block, own, other, gain, features, copies):
    rows = own.shape[0]
    return pl.pallas_call(
        norm_kernel,
        out_shape=(
            jax.ShapeDtypeStruct((copies, rows, features), jnp.bfloat16),
            jax.ShapeDtypeStruct((rows, features), jnp.float32),
        ),
        in_specs=[SMEM, VMEM, VMEM, VMEM],
        out_specs=(VMEM, VMEM),
        scratch_shapes=[pltpu.VMEM(own.shape, jnp.float32)],
        compiler_params=pltpu.CompilerParams(vmem_limit_bytes=4 * MIB),
        name="normalize",
    )(block, own, other, gain.astype(jnp.float32).reshape(1, -1))


def units_kernel(n, place, *refs):
    pieces, gate_w, up_w, outs, held, sums = refs[:n], *refs[n : n + 2], refs[n + 2 : -2], *refs[-2:]
    at = 0
    for piece in pieces:
        held[at : at + piece.shape[0], :] = piece[...]
        at += piece.shape[0]
    units = gate_w.shape[1]
    sums[:, :units] = mm(held[...], gate_w[...])
    sums[:, units:] = mm(held[...], up_w[...])
    if len(outs) == 1:
        outs[0][...] = sums[...].astype(jnp.bfloat16)
        return
    keep, away = outs[0], outs[1:]
    half, part = at // 2, away[0].shape[0]
    start = pl.multiple_of((1 - place[0]) * half, half)
    for index, out in enumerate(away):
        out[...] = sums[pl.ds(start + index * part, part), :].astype(jnp.bfloat16)
    keep[...] = sums[pl.ds(pl.multiple_of(place[0] * half, half), half), :]


def partial_units(split, block, pieces, gate_w, up_w):
    tokens = sum(piece.shape[0] for piece in pieces)
    features, units = gate_w.shape
    if split:
        out_shape = (
            jax.ShapeDtypeStruct((tokens // 2, 2 * units), jnp.float32),
            *[jax.ShapeDtypeStruct((tokens // 2 // split, 2 * units), jnp.bfloat16)] * split,
        )
    else:
        out_shape = (jax.ShapeDtypeStruct((tokens, 2 * units), jnp.bfloat16),)
    return pl.pallas_call(
        functools.partial(units_kernel, len(pieces)),
        out_shape=out_shape,
        in_specs=[SMEM] + [VMEM] * (len(pieces) + 2),
        out_specs=(VMEM,) * len(out_shape),
        scratch_shapes=[
            pltpu.VMEM((tokens, features), jnp.bfloat16),
            pltpu.VMEM((tokens, 2 * units), jnp.float32),
        ],
        compiler_params=pltpu.CompilerParams(vmem_limit_bytes=UNITS_VMEM),
        cost_estimate=pl.CostEstimate(
            flops=4 * tokens * features * units,
            bytes_accessed=2 * tokens * features + 4 * features * units,
            transcendentals=0,
        ),
        name="gate_up",
    )(block, *pieces, gate_w, up_w)


def hidden_kernel(sums, *refs):
    others, out = refs[:-1], refs[-1]
    units = out.shape[1]
    at = 0
    for other in others or (None,):
        to = at + (sums if other is None else other).shape[0]
        both = sums[at:to, :].astype(jnp.float32)
        if other is not None:
            both = both + other[...].astype(jnp.float32)
        gate, up = both[:, :units], both[:, units:]
        out[at:to, :] = (gate / (1.0 + jnp.exp(-gate)) * up).astype(jnp.bfloat16)
        at = to


def hidden_units(sums, *others):
    tokens, units = sums.shape[0], sums.shape[1] // 2
    return pl.pallas_call(
        hidden_kernel,
        out_shape=jax.ShapeDtypeStruct((tokens, units), jnp.bfloat16),
        in_specs=[VMEM] * (1 + len(others)),
        out_specs=VMEM,
        compiler_params=pltpu.CompilerParams(vmem_limit_bytes=4 * MIB),
        name="hidden",
    )(sums, *others)


def down_kernel(orders, flip, n, place, *refs):
    parts, source, middle, down_w = refs[:n], *refs[n : n + 3]
    outs, hidden, term = refs[n + 3 : -2], *refs[-2:]
    tokens, features = term.shape
    rows = middle.shape[0]
    chip, core = place[0], place[1]
    at = 0
    for part in parts:
        hidden[at : at + part.shape[0], :] = part[...]
        at += part.shape[0]
    slot, local = source[:, 0:1], source[:, 1:2]
    pick = (lax.broadcasted_iota(jnp.int32, (tokens, tokens), 1) == slot).astype(jnp.bfloat16)
    moved = mm(pick, hidden[...]).astype(jnp.bfloat16)
    mine = lax.broadcasted_iota(jnp.int32, (tokens, rows), 1) == local
    mine = mine.astype(jnp.bfloat16)
    high = middle[...].astype(jnp.bfloat16)
    low = (middle[...] - high.astype(jnp.float32)).astype(jnp.bfloat16)
    term[...] = mm(moved, down_w[...]) + (mm(mine, high) + mm(mine, low))
    for order, keep, send in zip(orders, outs[::2], outs[1::2]):
        for index, dest in enumerate(order):
            at = slice(index * rows, (index + 1) * rows)
            dest = dest ^ chip if flip else dest
            start = pl.multiple_of((2 * dest + core) * rows, rows)
            keep[at, :] = term[pl.ds(start, rows), :]
            start = pl.multiple_of((2 * dest + (1 - core)) * rows, rows)
            send[at, :] = term[pl.ds(start, rows), :].astype(jnp.bfloat16)


def down(orders, flip, place, parts, source, middle, down_w):
    tokens = source.shape[0]
    units, features = down_w.shape
    rows = middle.shape[0]
    out_shape = ()
    for order in orders:
        shape = (len(order) * rows, features)
        out_shape += (
            jax.ShapeDtypeStruct(shape, jnp.float32),
            jax.ShapeDtypeStruct(shape, jnp.bfloat16),
        )
    outs = pl.pallas_call(
        functools.partial(down_kernel, orders, flip, len(parts)),
        out_shape=out_shape,
        in_specs=[SMEM] + [VMEM] * (len(parts) + 3),
        out_specs=(VMEM,) * len(out_shape),
        scratch_shapes=[
            pltpu.VMEM((tokens, units), jnp.bfloat16),
            pltpu.VMEM((tokens, features), jnp.float32),
        ],
        compiler_params=pltpu.CompilerParams(vmem_limit_bytes=DOWN_VMEM),
        name="down",
    )(place, *parts, source, middle, down_w)
    return list(zip(outs[::2], outs[1::2]))


def pack_kernel(n, *refs):
    pieces, out = refs[:n], refs[-1]
    at = 0
    for piece in pieces:
        out[at : at + piece.shape[0], :] = piece[...]
        at += piece.shape[0]


def pack(pieces, after=()):
    rows = sum(piece.shape[0] for piece in pieces)
    return pl.pallas_call(
        functools.partial(pack_kernel, len(pieces)),
        out_shape=jax.ShapeDtypeStruct((rows, pieces[0].shape[1]), pieces[0].dtype),
        in_specs=[VMEM] * len(pieces) + [ANY] * len(after),
        out_specs=VMEM,
        compiler_params=pltpu.CompilerParams(vmem_limit_bytes=4 * MIB),
        name="pack",
    )(*pieces, *after)


def add_kernel(keep, other, *outs):
    at = 0
    for out in outs:
        to = at + out.shape[0]
        out[...] = (keep[at:to, :] + other[at:to, :].astype(jnp.float32)).astype(out.dtype)
        at = to


def add_parts(keep, other, kinds):
    rows, features = keep.shape
    return pl.pallas_call(
        add_kernel,
        out_shape=tuple(
            jax.ShapeDtypeStruct((rows // len(kinds), features), kind) for kind in kinds
        ),
        in_specs=[VMEM, VMEM],
        out_specs=(VMEM,) * len(kinds),
        compiler_params=pltpu.CompilerParams(vmem_limit_bytes=4 * MIB),
        name="add_parts",
    )(keep, other)


def finish_kernel(n, *refs):
    parts, gain, score, out, stats = refs[:n], *refs[n:]
    moved = functools.reduce(jnp.add, [part[...].astype(jnp.float32) for part in parts])
    out[...] = moved.astype(jnp.bfloat16)
    weighted = gain[...].astype(jnp.float32) * score[...].astype(jnp.float32)
    lane = lax.broadcasted_iota(jnp.int32, stats.shape, 1)
    squares = jnp.sum(moved * moved, axis=1, keepdims=True)
    terms = jnp.sum(moved * weighted, axis=1, keepdims=True)
    stats[...] = jnp.where(lane == 0, squares, terms)


def finish(parts, gain, score):
    rows, features = parts[0].shape
    return pl.pallas_call(
        functools.partial(finish_kernel, len(parts)),
        out_shape=(
            jax.ShapeDtypeStruct((rows, features), jnp.bfloat16),
            jax.ShapeDtypeStruct((rows, 128), jnp.float32),
        ),
        in_specs=[VMEM] * (len(parts) + 2),
        out_specs=(VMEM, VMEM),
        compiler_params=pltpu.CompilerParams(vmem_limit_bytes=4 * MIB),
        name="finish",
    )(*parts, gain.reshape(1, -1), score.reshape(1, -1))


def shards(
    n_chip,
    n_blk,
    resid,
    queries,
    new_kv,
    prefix_pool,
    page_table,
    prompt_len,
    tail_pool,
    tail_len,
    migration,
    out_w,
    mlp_gain,
    gate_w,
    up_w,
    down_w,
    final_gain,
    score_w,
):
    rows = resid.shape[0]
    features = gate_w.shape[0]
    chip = lax.axis_index("chip").astype(jnp.int32)
    core = lax.axis_index("core").astype(jnp.int32)
    block = lax.axis_index("blk").astype(jnp.int32).reshape(1)
    direct = n_chip == 8 and n_blk == 2

    def to_chip(value, index):
        return lax.ppermute(value, "chip", [(i, i ^ index) for i in range(n_chip)])

    def swap(value, axis):
        return lax.ppermute(value, axis, [(0, 1), (1, 0)])

    own, send = attention(
        queries, new_kv, prefix_pool, page_table, prompt_len, tail_pool, tail_len, out_w
    )
    if direct:
        own, other = own + resid.astype(jnp.float32), swap(send, "blk")
    else:
        own, other = resid.astype(jnp.float32), lax.psum(send, "blk")
    normed, middle = normalize(block, own, other, mlp_gain, features, 1 if direct else n_chip)

    token = migration[:, None] * NEW + jnp.arange(NEW, dtype=jnp.int32)[None, :]
    token = token.reshape(-1, 1)
    came, inner = token // rows, token % rows
    far_core = (came % 2) ^ core
    if direct:
        piece = normed.reshape(rows, features)
        z2, z3, z1 = (to_chip(piece, index) for index in (4, 6, 2))
        here = [pack([piece, z2]), pack([z1, z3])]
        there = [to_chip(part, 1) for part in here]
        parts, after = [], ()
        for near, split in ((here, 2), (there, 1)):
            if after:
                near = [pack(near, after)]
            pieces = near + [swap(part, "core") for part in near]
            keep, *away = partial_units(split, block, pieces, gate_w, up_w)
            others = [swap(part, "blk") for part in away]
            hidden = hidden_units(keep, *others)
            parts += [hidden, swap(hidden, "blk")]
            after = others
        far = (came // 2) ^ chip
        slot = (far % 2 * 2 + (far_core ^ block[0])) * 4 + far // 2 % 2 * 2 + far // 4
        slot = slot * rows + inner
    else:
        near = lax.all_to_all(normed, "chip", 0, 0).reshape(n_chip * rows, features)
        units = partial_units(0, block, [near, swap(near, "core")], gate_w, up_w)[0]
        parts = [hidden_units(lax.psum(units, "blk"))]
        slot = far_core * (n_chip * rows) + (came // 2) * rows + inner
    local = token - (chip * 2 + core) * rows
    source = jnp.concatenate([slot, local], axis=1)

    place = jnp.stack([chip, core])
    if direct:
        wide, far = down(((4, 6, 5, 7), (0, 2, 1, 3)), True, place, parts, source, middle, down_w)
        kinds = (jnp.float32, jnp.bfloat16)
        wide = add_parts(wide[0], swap(wide[1], "core"), kinds)
        far = add_parts(far[0], swap(far[1], "core"), kinds)
        to4, to6 = add_parts(wide[0], to_chip(wide[1], 1), (jnp.bfloat16, jnp.bfloat16))
        mine, to2 = add_parts(far[0], to_chip(far[1], 1), (jnp.float32, jnp.bfloat16))
        sums = [mine, to_chip(to4, 4), to_chip(to6, 6), to_chip(to2, 2)]
    else:
        order = tuple(range(n_chip))
        ((keep, away),) = down((order,), False, place, parts, source, middle, down_w)
        total = (keep + swap(away, "core").astype(jnp.float32)).astype(jnp.bfloat16)
        total = lax.all_to_all(total.reshape(n_chip, rows, features), "chip", 0, 0)
        sums = [jnp.sum(total.astype(jnp.float32), axis=0)]
    hidden_out, stats = finish(sums, final_gain, score_w)
    stats = stats + swap(stats, "blk") if direct else lax.psum(stats, "blk")
    score = stats[:, 1] * lax.rsqrt(stats[:, 0] / D + EPS)
    return (hidden_out, score)


def solution(mesh):
    n_chip, n_blk = mesh.shape["dp"] // 2, mesh.shape["blk"]
    split = Mesh(mesh.devices.reshape(n_chip, 2, n_blk), ("chip", "core", "blk"))
    dp = ("chip", "core")
    return jax.shard_map(
        functools.partial(shards, n_chip, n_blk),
        mesh=split,
        in_specs=(
            P(dp, None),
            P(dp, "blk", None),
            P(dp, None, "blk", None),
            P(dp, None, None, "blk", None),
            P(dp, None),
            P(dp),
            P(dp, None, None, "blk", None),
            P(dp, None),
            P(),
            P("blk", None),
            P(),
            P("blk", dp),
            P("blk", dp),
            P(dp, "blk"),
            P("blk"),
            P("blk"),
        ),
        out_specs=(P(dp, "blk"), P(dp)),
        check_vma=False,
    )
```

```python
import functools
import math

import jax
import jax.numpy as jnp
from jax import lax
from jax.experimental import pallas as pl
from jax.experimental.pallas import tpu as pltpu
from jax.sharding import Mesh
from jax.sharding import PartitionSpec as P

D = 2048
NEW = 2
NEG = -1e30
EPS = 1e-06
MIB = 1 << 20
ATTENTION_VMEM = 60 * MIB
UNITS_VMEM = 6 * MIB
DOWN_VMEM = 12 * MIB

VMEM = pl.BlockSpec(memory_space=pltpu.VMEM)
SMEM = pl.BlockSpec(memory_space=pltpu.SMEM)
ANY = pl.BlockSpec(memory_space=pl.ANY)


def mm(a, b):
    return jnp.dot(a, b, preferred_element_type=jnp.float32)


def mm_t(a, b):
    return lax.dot_general(a, b, (((1,), (1,)), ((), ())), preferred_element_type=jnp.float32)


def attention_kernel(
    dims,
    table,
    prompt_len,
    tail_len,
    queries,
    new_kv,
    pool,
    tails,
    out_w,
    own_ref,
    send_ref,
    pages,
    tail_buf,
    w_buf,
    q_buf,
    new_buf,
    apart,
    tail_apart,
    q_wide,
    q_rows,
    new_wide,
    fresh_scores,
    tail_scores,
    scores,
    top,
    total,
    acc,
    attn,
    page_sems,
    tail_sems,
    sems,
):
    rows, heads, groups, width, n_pages, page, conts, tail, pair = dims
    repeat = heads // groups
    step = 2 * groups
    pairs = groups // pair
    stack = repeat * rows
    page_rows = page * step
    chunk_pages = math.gcd(8, n_pages)
    chunk = chunk_pages * page
    chunk_rows = chunk * step
    quad = 8 // NEW
    quads = conts // quad
    quad_keys = quad * tail
    quad_rows = quad_keys * step
    factor = math.log2(math.e) / math.sqrt(width)
    length = prompt_len[0]
    chunks = (length + chunk - 1) // chunk

    def page_copy(logical):
        physical = table[0, logical]
        return pltpu.make_async_copy(
            pool.at[pl.ds(pl.multiple_of(physical * page_rows, page_rows), page_rows), :],
            pages.at[pl.ds(pl.multiple_of(logical * page_rows, page_rows), page_rows), :],
            page_sems.at[logical],
        )

    def tail_copy(index):
        return pltpu.make_async_copy(
            tails.at[pl.ds(index * quad_rows, quad_rows), :],
            tail_buf.at[pl.ds(index * quad_rows, quad_rows), :],
            tail_sems.at[index],
        )

    q_copy = pltpu.make_async_copy(queries, q_buf, sems.at[0])
    new_copy = pltpu.make_async_copy(new_kv, new_buf, sems.at[1])
    w_copy = pltpu.make_async_copy(out_w, w_buf, sems.at[2])
    q_copy.start()
    new_copy.start()
    for index in range(quads):
        tail_copy(index).start()

    @pl.loop(0, chunks * chunk_pages)
    def _(logical):
        page_copy(logical).start()

    w_copy.start()

    block = 256
    tokens = block // step
    to = lax.broadcasted_iota(jnp.int32, (block, block), 0)
    came = lax.broadcasted_iota(jnp.int32, (block, block), 1)
    sort = (came == (to % tokens) * step + to // tokens).astype(jnp.bfloat16)

    def take_apart(buf, start, count, out, at):
        for two in range(count // (2 * block)):
            x0 = buf[pl.ds(start + two * 2 * block, block), :]
            x1 = buf[pl.ds(start + (two * 2 + 1) * block, block), :]
            y = mm(sort, jnp.concatenate([x0, x1], axis=1)).astype(jnp.bfloat16)
            for side in range(2):
                t = pl.ds(at + (2 * two + side) * tokens, tokens)
                for j in range(step):
                    kind, g = j // groups, j % groups
                    lane = (g % pair) * width
                    out[kind, g // pair, t, lane : lane + width] = y[
                        j * tokens : (j + 1) * tokens, side * width : (side + 1) * width
                    ]

    def blocks(x):
        return [x[:, i * 128 : (i + 1) * 128] for i in range(x.shape[1] // 128)]

    q_copy.wait()
    new_copy.wait()
    q_wide[...] = q_buf[...].astype(jnp.float32)
    new_wide[...] = new_buf[...].astype(jnp.float32)
    if pair > 1:
        q_rows[...] = jnp.zeros_like(q_rows)
    for g in range(groups):
        for r in range(repeat):
            at = (g % pair) * stack + r * rows
            lane = (g % pair) * width
            q_rows[g // pair, at : at + rows, lane : lane + width] = q_wide[
                pl.ds(g * repeat + r, rows, stride=heads), :
            ]

    def fresh(first, n):
        parts = [
            new_wide[pl.ds(first + n * pair + i, rows, stride=step), :] for i in range(pair)
        ]
        return jnp.concatenate(parts, axis=1).astype(jnp.bfloat16)

    row = lax.broadcasted_iota(jnp.int32, (rows, rows), 0)
    key = lax.broadcasted_iota(jnp.int32, (rows, rows), 1)
    fresh_ok = (row // NEW == key // NEW) & (key <= row)
    fresh_ok = jnp.concatenate([fresh_ok] * (pair * repeat), axis=0)
    for n in range(pairs):
        s = jnp.where(fresh_ok, mm_t(q_rows[n].astype(jnp.bfloat16), fresh(0, n)) * factor, NEG)
        fresh_scores[n] = s
        top[n] = jnp.broadcast_to(jnp.max(s, axis=1, keepdims=True), top.shape[1:])

    def quad_places(index):
        starts = [i * rows + index * 8 for i in range(pair * repeat)]
        return [slice(at, at + 8) for at in starts]

    quad_row = lax.broadcasted_iota(jnp.int32, (8, quad_keys), 0)
    quad_key = lax.broadcasted_iota(jnp.int32, (8, quad_keys), 1)
    for index in range(quads):
        tail_copy(index).wait()
        take_apart(tail_buf, index * quad_rows, quad_rows, tail_apart, index * quad_keys)
        reach = jnp.zeros((8, quad_keys), jnp.int32)
        for c in range(quad):
            reach = jnp.where(
                quad_key // tail == c, tail_len[0, index * quad + c] + c * tail, reach
            )
        ok = (quad_row // NEW == quad_key // tail) & (quad_key < reach)
        ok = jnp.concatenate([ok] * (pair * repeat), axis=0)
        keys = slice(index * quad_keys, (index + 1) * quad_keys)
        for n in range(pairs):
            q = jnp.concatenate([q_rows[n, a, :] for a in quad_places(index)], axis=0)
            s = mm_t(q.astype(jnp.bfloat16), tail_apart[0, n, keys, :]) * factor
            s = jnp.where(ok, s, NEG)
            tail_scores[n, index] = s
            high = functools.reduce(jnp.maximum, blocks(s))
            for i, a in enumerate(quad_places(index)):
                top[n, a, :] = jnp.maximum(top[n, a, :], high[i * 8 : (i + 1) * 8])

    place = lax.broadcasted_iota(jnp.int32, (8, chunk), 1)

    @pl.loop(0, chunks)
    def _(index):
        for i in range(chunk_pages):
            page_copy(index * chunk_pages + i).wait()
        first = pl.multiple_of(index * chunk, chunk)
        take_apart(pages, pl.multiple_of(index * chunk_rows, chunk_rows), chunk_rows, apart, first)
        ok = place[0:1] < length - index * chunk
        for n in range(pairs):
            s = mm_t(q_rows[n].astype(jnp.bfloat16), apart[0, n, pl.ds(first, chunk), :]) * factor
            s = jnp.where(ok, s, NEG)
            scores[n, :, pl.ds(first, chunk)] = s
            top[n] = functools.reduce(jnp.maximum, blocks(s), top[n])

    for n in range(pairs):
        high = jnp.broadcast_to(jnp.max(top[n], axis=1, keepdims=True), top.shape[1:])
        top[n] = high
        p = jnp.exp2(fresh_scores[n] - high[:, :rows])
        lane = lax.broadcasted_iota(jnp.int32, total.shape[1:], 1)
        total[n] = jnp.where(lane == 0, jnp.sum(p, axis=1, keepdims=True), 0.0)
        acc[n] = mm(p.astype(jnp.bfloat16), fresh(groups, n))

    def weigh(s, high):
        parts = [jnp.exp2(part - high) for part in blocks(s)]
        return jnp.concatenate(parts, axis=1).astype(jnp.bfloat16), functools.reduce(jnp.add, parts)

    for index in range(quads):
        keys = slice(index * quad_keys, (index + 1) * quad_keys)
        for n in range(pairs):
            high = jnp.concatenate([top[n, a, :] for a in quad_places(index)], axis=0)
            p, added = weigh(tail_scores[n, index], high)
            value = mm(p, tail_apart[1, n, keys, :])
            for i, a in enumerate(quad_places(index)):
                total[n, a, :] = total[n, a, :] + added[i * 8 : (i + 1) * 8]
                acc[n, a, :] = acc[n, a, :] + value[i * 8 : (i + 1) * 8]

    @pl.loop(0, chunks)
    def _(index):
        first = pl.multiple_of(index * chunk, chunk)
        for n in range(pairs):
            p, added = weigh(scores[n, :, pl.ds(first, chunk)], top[n])
            total[n] = total[n] + added
            acc[n] = acc[n] + mm(p, apart[1, n, pl.ds(first, chunk), :])

    for g in range(groups):
        at, lane = (g % pair) * stack, (g % pair) * width
        out = acc[g // pair, at : at + stack, lane : lane + width]
        out = out / jnp.sum(total[g // pair, at : at + stack, :], axis=1, keepdims=True)
        out = out.astype(jnp.bfloat16)
        for r in range(repeat):
            head = g * repeat + r
            attn[:, head * width : (head + 1) * width] = out[r * rows : (r + 1) * rows]
    w_copy.wait()
    value = mm(attn[...], w_buf[...])
    own_ref[...] = value
    send_ref[...] = value.astype(jnp.bfloat16)


def attention(queries, new_kv, pool, table, prompt_len, tails, tail_len, out_w):
    rows, heads, width = queries.shape
    n_pages, page, _, groups, _ = pool.shape
    conts, tail = tails.shape[:2]
    step = 2 * groups
    features = out_w.shape[1]
    quads = conts * NEW // 8
    pair = 2 if groups % 2 == 0 else 1
    pairs = groups // pair
    repeat = heads // groups
    stack = pair * repeat * rows
    return pl.pallas_call(
        functools.partial(
            attention_kernel, (rows, heads, groups, width, n_pages, page, conts, tail, pair)
        ),
        out_shape=(
            jax.ShapeDtypeStruct((rows, features), jnp.float32),
            jax.ShapeDtypeStruct((rows, features), jnp.bfloat16),
        ),
        in_specs=[SMEM, SMEM, SMEM, ANY, ANY, ANY, ANY, ANY],
        out_specs=(VMEM, VMEM),
        scratch_shapes=[
            pltpu.VMEM((n_pages * page * step, width), jnp.bfloat16),
            pltpu.VMEM((conts * tail * step, width), jnp.bfloat16),
            pltpu.VMEM(out_w.shape, jnp.bfloat16),
            pltpu.VMEM((rows * heads, width), jnp.bfloat16),
            pltpu.VMEM((rows * step, width), jnp.bfloat16),
            pltpu.VMEM((2, pairs, n_pages * page, pair * width), jnp.bfloat16),
            pltpu.VMEM((2, pairs, conts * tail, pair * width), jnp.bfloat16),
            pltpu.VMEM((rows * heads, width), jnp.float32),
            pltpu.VMEM((pairs, stack, pair * width), jnp.float32),
            pltpu.VMEM((rows * step, width), jnp.float32),
            pltpu.VMEM((pairs, stack, rows), jnp.float32),
            pltpu.VMEM((pairs, quads, pair * repeat * 8, 8 // NEW * tail), jnp.float32),
            pltpu.VMEM((pairs, stack, n_pages * page), jnp.float32),
            pltpu.VMEM((pairs, stack, 128), jnp.float32),
            pltpu.VMEM((pairs, stack, 128), jnp.float32),
            pltpu.VMEM((pairs, stack, pair * width), jnp.float32),
            pltpu.VMEM((rows, heads * width), jnp.bfloat16),
            pltpu.SemaphoreType.DMA((n_pages,)),
            pltpu.SemaphoreType.DMA((quads,)),
            pltpu.SemaphoreType.DMA((3,)),
        ],
        compiler_params=pltpu.CompilerParams(vmem_limit_bytes=ATTENTION_VMEM),
        name="attention",
    )(
        table,
        prompt_len,
        tail_len,
        queries.reshape(rows * heads, width),
        new_kv.reshape(rows * step, width),
        pool.reshape(n_pages * page * step, width),
        tails.reshape(conts * tail * step, width),
        out_w,
    )


def norm_kernel(n, place, own, other, gain, *refs):
    normed, middle, whole = refs[n:]
    copies, rows, features = normed.shape
    mid = own[...] + other[...].astype(jnp.float32)
    scale = lax.rsqrt(jnp.mean(mid * mid, axis=1, keepdims=True) + EPS)
    whole[...] = mid
    start = pl.multiple_of(place[2] * features, features)
    part = whole[:, pl.ds(start, features)]
    out = (part * scale * gain[:, pl.ds(start, features)]).astype(jnp.bfloat16)
    for index in range(copies):
        normed[index] = out
    middle[...] = part


def normalize(place, own, other, gain, features, copies, ahead):
    rows = own.shape[0]
    return pl.pallas_call(
        functools.partial(norm_kernel, len(ahead)),
        out_shape=(
            jax.ShapeDtypeStruct((copies, rows, features), jnp.bfloat16),
            jax.ShapeDtypeStruct((rows, features), jnp.float32),
        ),
        in_specs=[SMEM, VMEM, VMEM, VMEM] + [ANY] * len(ahead),
        out_specs=(VMEM, VMEM),
        scratch_shapes=[pltpu.VMEM(own.shape, jnp.float32)],
        compiler_params=pltpu.CompilerParams(vmem_limit_bytes=4 * MIB),
        name="normalize",
    )(place, own, other, gain.astype(jnp.float32).reshape(1, -1), *ahead)


def units_kernel(n, place, *refs):
    pieces, gate_w, up_w, outs, held, sums = refs[:n], *refs[n : n + 2], refs[n + 2 : -2], *refs[-2:]
    at = 0
    for piece in pieces:
        held[at : at + piece.shape[0], :] = piece[...]
        at += piece.shape[0]
    units = gate_w.shape[1]
    sums[:, :units] = mm(held[...], gate_w[...])
    sums[:, units:] = mm(held[...], up_w[...])
    if len(outs) == 1:
        outs[0][...] = sums[...].astype(jnp.bfloat16)
        return
    keep, away = outs[0], outs[1:]
    half, part = at // 2, away[0].shape[0]
    start = pl.multiple_of((1 - place[2]) * half, half)
    for index, out in enumerate(away):
        out[...] = sums[pl.ds(start + index * part, part), :].astype(jnp.bfloat16)
    keep[...] = sums[pl.ds(pl.multiple_of(place[2] * half, half), half), :]


def partial_units(split, place, pieces, gate_w, up_w):
    tokens = sum(piece.shape[0] for piece in pieces)
    features, units = gate_w.shape
    if split:
        out_shape = (
            jax.ShapeDtypeStruct((tokens // 2, 2 * units), jnp.float32),
            *[jax.ShapeDtypeStruct((tokens // 2 // split, 2 * units), jnp.bfloat16)] * split,
        )
    else:
        out_shape = (jax.ShapeDtypeStruct((tokens, 2 * units), jnp.bfloat16),)
    return pl.pallas_call(
        functools.partial(units_kernel, len(pieces)),
        out_shape=out_shape,
        in_specs=[SMEM] + [VMEM] * (len(pieces) + 2),
        out_specs=(VMEM,) * len(out_shape),
        scratch_shapes=[
            pltpu.VMEM((tokens, features), jnp.bfloat16),
            pltpu.VMEM((tokens, 2 * units), jnp.float32),
        ],
        compiler_params=pltpu.CompilerParams(vmem_limit_bytes=UNITS_VMEM),
        cost_estimate=pl.CostEstimate(
            flops=4 * tokens * features * units,
            bytes_accessed=2 * tokens * features + 4 * features * units,
            transcendentals=0,
        ),
        name="gate_up",
    )(place, *pieces, gate_w, up_w)


def hidden_kernel(sums, *refs):
    others, out = refs[:-1], refs[-1]
    units = out.shape[1]
    at = 0
    for other in others or (None,):
        to = at + (sums if other is None else other).shape[0]
        both = sums[at:to, :].astype(jnp.float32)
        if other is not None:
            both = both + other[...].astype(jnp.float32)
        gate, up = both[:, :units], both[:, units:]
        out[at:to, :] = (gate / (1.0 + jnp.exp(-gate)) * up).astype(jnp.bfloat16)
        at = to


def hidden_units(sums, *others):
    tokens, units = sums.shape[0], sums.shape[1] // 2
    return pl.pallas_call(
        hidden_kernel,
        out_shape=jax.ShapeDtypeStruct((tokens, units), jnp.bfloat16),
        in_specs=[VMEM] * (1 + len(others)),
        out_specs=VMEM,
        compiler_params=pltpu.CompilerParams(vmem_limit_bytes=4 * MIB),
        name="hidden",
    )(sums, *others)


def down_kernel(orders, flip, n, place, *refs):
    parts, source, middle, down_w = refs[:n], *refs[n : n + 3]
    outs, hidden, term = refs[n + 3 : -2], *refs[-2:]
    tokens, features = term.shape
    rows = middle.shape[0]
    chip, core = place[0], place[1]
    at = 0
    for part in parts:
        hidden[at : at + part.shape[0], :] = part[...]
        at += part.shape[0]
    slot, local = source[:, 0:1], source[:, 1:2]
    pick = (lax.broadcasted_iota(jnp.int32, (tokens, tokens), 1) == slot).astype(jnp.bfloat16)
    moved = mm(pick, hidden[...]).astype(jnp.bfloat16)
    mine = lax.broadcasted_iota(jnp.int32, (tokens, rows), 1) == local
    mine = mine.astype(jnp.bfloat16)
    high = middle[...].astype(jnp.bfloat16)
    low = (middle[...] - high.astype(jnp.float32)).astype(jnp.bfloat16)
    term[...] = mm(moved, down_w[...]) + (mm(mine, high) + mm(mine, low))
    for order, keep, send in zip(orders, outs[::2], outs[1::2]):
        for index, dest in enumerate(order):
            at = slice(index * rows, (index + 1) * rows)
            dest = dest ^ chip if flip else dest
            start = pl.multiple_of((2 * dest + core) * rows, rows)
            keep[at, :] = term[pl.ds(start, rows), :]
            start = pl.multiple_of((2 * dest + (1 - core)) * rows, rows)
            send[at, :] = term[pl.ds(start, rows), :].astype(jnp.bfloat16)


def down(orders, flip, place, parts, source, middle, down_w):
    tokens = source.shape[0]
    units, features = down_w.shape
    rows = middle.shape[0]
    out_shape = ()
    for order in orders:
        shape = (len(order) * rows, features)
        out_shape += (
            jax.ShapeDtypeStruct(shape, jnp.float32),
            jax.ShapeDtypeStruct(shape, jnp.bfloat16),
        )
    outs = pl.pallas_call(
        functools.partial(down_kernel, orders, flip, len(parts)),
        out_shape=out_shape,
        in_specs=[SMEM] + [VMEM] * (len(parts) + 3),
        out_specs=(VMEM,) * len(out_shape),
        scratch_shapes=[
            pltpu.VMEM((tokens, units), jnp.bfloat16),
            pltpu.VMEM((tokens, features), jnp.float32),
        ],
        compiler_params=pltpu.CompilerParams(vmem_limit_bytes=DOWN_VMEM),
        name="down",
    )(place, *parts, source, middle, down_w)
    return list(zip(outs[::2], outs[1::2]))


def pack_kernel(n, *refs):
    pieces, out = refs[:n], refs[-1]
    at = 0
    for piece in pieces:
        out[at : at + piece.shape[0], :] = piece[...]
        at += piece.shape[0]


def pack(pieces, after=()):
    rows = sum(piece.shape[0] for piece in pieces)
    return pl.pallas_call(
        functools.partial(pack_kernel, len(pieces)),
        out_shape=jax.ShapeDtypeStruct((rows, pieces[0].shape[1]), pieces[0].dtype),
        in_specs=[VMEM] * len(pieces) + [ANY] * len(after),
        out_specs=VMEM,
        compiler_params=pltpu.CompilerParams(vmem_limit_bytes=4 * MIB),
        name="pack",
    )(*pieces, *after)


def add_kernel(n, keep, other, *refs):
    outs = refs[n:]
    at = 0
    for out in outs:
        to = at + out.shape[0]
        out[...] = (keep[at:to, :] + other[at:to, :].astype(jnp.float32)).astype(out.dtype)
        at = to


def add_parts(keep, other, kinds, after=()):
    rows, features = keep.shape
    return pl.pallas_call(
        functools.partial(add_kernel, len(after)),
        out_shape=tuple(
            jax.ShapeDtypeStruct((rows // len(kinds), features), kind) for kind in kinds
        ),
        in_specs=[VMEM, VMEM] + [ANY] * len(after),
        out_specs=(VMEM,) * len(kinds),
        compiler_params=pltpu.CompilerParams(vmem_limit_bytes=4 * MIB),
        name="add_parts",
    )(keep, other, *after)


def finish_kernel(n, *refs):
    parts, gain, score, out, stats = refs[:n], *refs[n:]
    moved = functools.reduce(jnp.add, [part[...].astype(jnp.float32) for part in parts])
    out[...] = moved.astype(jnp.bfloat16)
    weighted = gain[...].astype(jnp.float32) * score[...].astype(jnp.float32)
    lane = lax.broadcasted_iota(jnp.int32, (out.shape[0], 128), 1)
    squares = jnp.sum(moved * moved, axis=1, keepdims=True)
    terms = jnp.sum(moved * weighted, axis=1, keepdims=True)
    stats[...] = jnp.transpose(jnp.where(lane == 0, squares, terms))[:8]


def finish(parts, gain, score):
    rows, features = parts[0].shape
    return pl.pallas_call(
        functools.partial(finish_kernel, len(parts)),
        out_shape=(
            jax.ShapeDtypeStruct((rows, features), jnp.bfloat16),
            jax.ShapeDtypeStruct((8, rows), jnp.float32),
        ),
        in_specs=[VMEM] * (len(parts) + 2),
        out_specs=(VMEM, VMEM),
        compiler_params=pltpu.CompilerParams(vmem_limit_bytes=4 * MIB),
        name="finish",
    )(*parts, gain, score)


def shards(
    n_chip,
    n_blk,
    resid,
    queries,
    new_kv,
    prefix_pool,
    page_table,
    prompt_len,
    tail_pool,
    tail_len,
    migration,
    out_w,
    mlp_gain,
    gate_w,
    up_w,
    down_w,
    final_gain,
    score_w,
):
    rows = resid.shape[0]
    features = gate_w.shape[0]
    chip = lax.axis_index("chip").astype(jnp.int32)
    core = lax.axis_index("core").astype(jnp.int32)
    block = lax.axis_index("blk").astype(jnp.int32)
    direct = n_chip == 8 and n_blk == 2

    def to_chip(value, index):
        return lax.ppermute(value, "chip", [(i, i ^ index) for i in range(n_chip)])

    def swap(value, axis):
        return lax.ppermute(value, axis, [(0, 1), (1, 0)])

    own, send = attention(
        queries, new_kv, prefix_pool, page_table, prompt_len, tail_pool, tail_len, out_w
    )
    if direct:
        own, other = own + resid.astype(jnp.float32), swap(send, "blk")
    else:
        own, other = resid.astype(jnp.float32), lax.psum(send, "blk")
    place = jnp.stack([chip, core, block])
    token = migration[:, None] * NEW + jnp.arange(NEW, dtype=jnp.int32)[None, :]
    token = token.reshape(-1, 1)
    came, inner = token // rows, token % rows
    far, far_core = (came // 2) ^ chip, (came % 2) ^ core
    if direct:
        slot = (far % 2 * 2 + (far_core ^ block)) * 4 + far // 2 % 2 * 2 + far // 4
    else:
        slot = far_core * n_chip + came // 2
    local = token - (chip * 2 + core) * rows
    source = jnp.concatenate([slot * rows + inner, local], axis=1)
    gain_row, score_row = final_gain.reshape(1, -1), score_w.reshape(1, -1)

    normed, middle = normalize(
        place,
        own,
        other,
        mlp_gain,
        features,
        1 if direct else n_chip,
        (source, gain_row, score_row),
    )
    if direct:
        piece = normed.reshape(rows, features)
        z2, z3, z1 = (to_chip(piece, index) for index in (4, 6, 2))
        here = [pack([piece, z2]), pack([z1, z3])]
        there = [to_chip(part, 1) for part in here]
        parts, after = [], ()
        for near, split in ((here, 2), (there, 1)):
            if after:
                near = [pack(near, after)]
            pieces = near + [swap(part, "core") for part in near]
            keep, *away = partial_units(split, place, pieces, gate_w, up_w)
            others = [swap(part, "blk") for part in away]
            hidden = hidden_units(keep, *others)
            parts += [hidden, swap(hidden, "blk")]
            after = others
    else:
        near = lax.all_to_all(normed, "chip", 0, 0).reshape(n_chip * rows, features)
        units = partial_units(0, place, [near, swap(near, "core")], gate_w, up_w)[0]
        parts = [hidden_units(lax.psum(units, "blk"))]
    if direct:
        wide, far = down(((4, 6, 5, 7), (0, 2, 1, 3)), True, place, parts, source, middle, down_w)
        kinds = (jnp.float32, jnp.bfloat16)
        wide = add_parts(wide[0], swap(wide[1], "core"), kinds)
        far = add_parts(far[0], swap(far[1], "core"), kinds, (wide[0],))
        to4, to6 = add_parts(wide[0], to_chip(wide[1], 1), (jnp.bfloat16, jnp.bfloat16))
        mine, to2 = add_parts(far[0], to_chip(far[1], 1), (jnp.float32, jnp.bfloat16), (to4,))
        sums = [mine, to_chip(to4, 4), to_chip(to6, 6), to_chip(to2, 2)]
    else:
        order = tuple(range(n_chip))
        ((keep, away),) = down((order,), False, place, parts, source, middle, down_w)
        total = (keep + swap(away, "core").astype(jnp.float32)).astype(jnp.bfloat16)
        total = lax.all_to_all(total.reshape(n_chip, rows, features), "chip", 0, 0)
        sums = [jnp.sum(total.astype(jnp.float32), axis=0)]
    hidden_out, stats = finish(sums, gain_row, score_row)
    stats = stats + swap(stats, "blk") if direct else lax.psum(stats, "blk")
    score = stats[1] * lax.rsqrt(stats[0] / D + EPS)
    return (hidden_out, score)


def solution(mesh):
    n_chip, n_blk = mesh.shape["dp"] // 2, mesh.shape["blk"]
    split = Mesh(mesh.devices.reshape(n_chip, 2, n_blk), ("chip", "core", "blk"))
    dp = ("chip", "core")
    return jax.shard_map(
        functools.partial(shards, n_chip, n_blk),
        mesh=split,
        in_specs=(
            P(dp, None),
            P(dp, "blk", None),
            P(dp, None, "blk", None),
            P(dp, None, None, "blk", None),
            P(dp, None),
            P(dp),
            P(dp, None, None, "blk", None),
            P(dp, None),
            P(),
            P("blk", None),
            P(),
            P("blk", dp),
            P("blk", dp),
            P(dp, "blk"),
            P("blk"),
            P("blk"),
        ),
        out_specs=(P(dp, "blk"), P(dp)),
        check_vma=False,
    )
```

```python
import functools
import math

import jax
import jax.numpy as jnp
from jax import lax
from jax.experimental import pallas as pl
from jax.experimental.pallas import tpu as pltpu
from jax.sharding import Mesh
from jax.sharding import PartitionSpec as P

D = 2048
NEW = 2
NEG = -1e30
EPS = 1e-06
MIB = 1 << 20
ATTENTION_VMEM = 60 * MIB
UNITS_VMEM = 6 * MIB
DOWN_VMEM = 12 * MIB

VMEM = pl.BlockSpec(memory_space=pltpu.VMEM)
SMEM = pl.BlockSpec(memory_space=pltpu.SMEM)
ANY = pl.BlockSpec(memory_space=pl.ANY)


def mm(a, b):
    return jnp.dot(a, b, preferred_element_type=jnp.float32)


def mm_t(a, b):
    return lax.dot_general(a, b, (((1,), (1,)), ((), ())), preferred_element_type=jnp.float32)


def attention_kernel(
    dims,
    table,
    prompt_len,
    tail_len,
    queries,
    new_kv,
    pool,
    tails,
    out_w,
    own_ref,
    send_ref,
    pages,
    tail_buf,
    w_buf,
    q_buf,
    new_buf,
    apart,
    tail_apart,
    q_wide,
    q_rows,
    new_wide,
    fresh_scores,
    tail_scores,
    scores,
    top,
    total,
    acc,
    attn,
    page_sems,
    tail_sems,
    sems,
):
    rows, heads, groups, width, n_pages, page, conts, tail, pair = dims
    repeat = heads // groups
    step = 2 * groups
    pairs = groups // pair
    stack = repeat * rows
    page_rows = page * step
    chunk_pages = math.gcd(8, n_pages)
    chunk = chunk_pages * page
    chunk_rows = chunk * step
    quad = 8 // NEW
    quads = conts // quad
    quad_keys = quad * tail
    quad_rows = quad_keys * step
    factor = math.log2(math.e) / math.sqrt(width)
    length = prompt_len[0]
    chunks = (length + chunk - 1) // chunk

    def page_copy(logical):
        physical = table[0, logical]
        return pltpu.make_async_copy(
            pool.at[pl.ds(pl.multiple_of(physical * page_rows, page_rows), page_rows), :],
            pages.at[pl.ds(pl.multiple_of(logical * page_rows, page_rows), page_rows), :],
            page_sems.at[logical],
        )

    def tail_copy(index):
        return pltpu.make_async_copy(
            tails.at[pl.ds(index * quad_rows, quad_rows), :],
            tail_buf.at[pl.ds(index * quad_rows, quad_rows), :],
            tail_sems.at[index],
        )

    q_copy = pltpu.make_async_copy(queries, q_buf, sems.at[0])
    new_copy = pltpu.make_async_copy(new_kv, new_buf, sems.at[1])
    w_copy = pltpu.make_async_copy(out_w, w_buf, sems.at[2])
    q_copy.start()
    new_copy.start()
    for index in range(quads):
        tail_copy(index).start()

    @pl.loop(0, chunks * chunk_pages)
    def _(logical):
        page_copy(logical).start()

    w_copy.start()

    block = 256
    tokens = block // step
    to = lax.broadcasted_iota(jnp.int32, (block, block), 0)
    came = lax.broadcasted_iota(jnp.int32, (block, block), 1)
    sort = (came == (to % tokens) * step + to // tokens).astype(jnp.bfloat16)

    def take_apart(buf, start, count, out, at):
        for two in range(count // (2 * block)):
            x0 = buf[pl.ds(start + two * 2 * block, block), :]
            x1 = buf[pl.ds(start + (two * 2 + 1) * block, block), :]
            y = mm(sort, jnp.concatenate([x0, x1], axis=1)).astype(jnp.bfloat16)
            for side in range(2):
                t = pl.ds(at + (2 * two + side) * tokens, tokens)
                for j in range(step):
                    kind, g = j // groups, j % groups
                    lane = (g % pair) * width
                    out[kind, g // pair, t, lane : lane + width] = y[
                        j * tokens : (j + 1) * tokens, side * width : (side + 1) * width
                    ]

    def blocks(x):
        return [x[:, i * 128 : (i + 1) * 128] for i in range(x.shape[1] // 128)]

    q_copy.wait()
    new_copy.wait()
    q_wide[...] = q_buf[...].astype(jnp.float32)
    new_wide[...] = new_buf[...].astype(jnp.float32)
    if pair > 1:
        q_rows[...] = jnp.zeros_like(q_rows)
    for g in range(groups):
        for r in range(repeat):
            at = (g % pair) * stack + r * rows
            lane = (g % pair) * width
            q_rows[g // pair, at : at + rows, lane : lane + width] = q_wide[
                pl.ds(g * repeat + r, rows, stride=heads), :
            ]

    def fresh(first, n):
        parts = [
            new_wide[pl.ds(first + n * pair + i, rows, stride=step), :] for i in range(pair)
        ]
        return jnp.concatenate(parts, axis=1).astype(jnp.bfloat16)

    row = lax.broadcasted_iota(jnp.int32, (rows, rows), 0)
    key = lax.broadcasted_iota(jnp.int32, (rows, rows), 1)
    fresh_ok = (row // NEW == key // NEW) & (key <= row)
    fresh_ok = jnp.concatenate([fresh_ok] * (pair * repeat), axis=0)
    for n in range(pairs):
        s = jnp.where(fresh_ok, mm_t(q_rows[n].astype(jnp.bfloat16), fresh(0, n)) * factor, NEG)
        fresh_scores[n] = s
        top[n] = jnp.broadcast_to(jnp.max(s, axis=1, keepdims=True), top.shape[1:])

    def quad_places(index):
        starts = [i * rows + index * 8 for i in range(pair * repeat)]
        return [slice(at, at + 8) for at in starts]

    quad_row = lax.broadcasted_iota(jnp.int32, (8, quad_keys), 0)
    quad_key = lax.broadcasted_iota(jnp.int32, (8, quad_keys), 1)
    for index in range(quads):
        tail_copy(index).wait()
        take_apart(tail_buf, index * quad_rows, quad_rows, tail_apart, index * quad_keys)
        reach = jnp.zeros((8, quad_keys), jnp.int32)
        for c in range(quad):
            reach = jnp.where(
                quad_key // tail == c, tail_len[0, index * quad + c] + c * tail, reach
            )
        ok = (quad_row // NEW == quad_key // tail) & (quad_key < reach)
        ok = jnp.concatenate([ok] * (pair * repeat), axis=0)
        keys = slice(index * quad_keys, (index + 1) * quad_keys)
        for n in range(pairs):
            q = jnp.concatenate([q_rows[n, a, :] for a in quad_places(index)], axis=0)
            s = mm_t(q.astype(jnp.bfloat16), tail_apart[0, n, keys, :]) * factor
            s = jnp.where(ok, s, NEG)
            tail_scores[n, index] = s
            high = functools.reduce(jnp.maximum, blocks(s))
            for i, a in enumerate(quad_places(index)):
                top[n, a, :] = jnp.maximum(top[n, a, :], high[i * 8 : (i + 1) * 8])

    place = lax.broadcasted_iota(jnp.int32, (8, chunk), 1)

    @pl.loop(0, chunks)
    def _(index):
        for i in range(chunk_pages):
            page_copy(index * chunk_pages + i).wait()
        first = pl.multiple_of(index * chunk, chunk)
        take_apart(pages, pl.multiple_of(index * chunk_rows, chunk_rows), chunk_rows, apart, first)
        ok = place[0:1] < length - index * chunk
        for n in range(pairs):
            s = mm_t(q_rows[n].astype(jnp.bfloat16), apart[0, n, pl.ds(first, chunk), :]) * factor
            s = jnp.where(ok, s, NEG)
            scores[n, :, pl.ds(first, chunk)] = s
            top[n] = functools.reduce(jnp.maximum, blocks(s), top[n])

    for n in range(pairs):
        high = jnp.broadcast_to(jnp.max(top[n], axis=1, keepdims=True), top.shape[1:])
        top[n] = high
        p = jnp.exp2(fresh_scores[n] - high[:, :rows])
        lane = lax.broadcasted_iota(jnp.int32, total.shape[1:], 1)
        total[n] = jnp.where(lane == 0, jnp.sum(p, axis=1, keepdims=True), 0.0)
        acc[n] = mm(p.astype(jnp.bfloat16), fresh(groups, n))

    def weigh(s, high):
        parts = [jnp.exp2(part - high) for part in blocks(s)]
        return jnp.concatenate(parts, axis=1).astype(jnp.bfloat16), functools.reduce(jnp.add, parts)

    for index in range(quads):
        keys = slice(index * quad_keys, (index + 1) * quad_keys)
        for n in range(pairs):
            high = jnp.concatenate([top[n, a, :] for a in quad_places(index)], axis=0)
            p, added = weigh(tail_scores[n, index], high)
            value = mm(p, tail_apart[1, n, keys, :])
            for i, a in enumerate(quad_places(index)):
                total[n, a, :] = total[n, a, :] + added[i * 8 : (i + 1) * 8]
                acc[n, a, :] = acc[n, a, :] + value[i * 8 : (i + 1) * 8]

    @pl.loop(0, chunks)
    def _(index):
        first = pl.multiple_of(index * chunk, chunk)
        for n in range(pairs):
            p, added = weigh(scores[n, :, pl.ds(first, chunk)], top[n])
            total[n] = total[n] + added
            acc[n] = acc[n] + mm(p, apart[1, n, pl.ds(first, chunk), :])

    for g in range(groups):
        at, lane = (g % pair) * stack, (g % pair) * width
        out = acc[g // pair, at : at + stack, lane : lane + width]
        out = out / jnp.sum(total[g // pair, at : at + stack, :], axis=1, keepdims=True)
        out = out.astype(jnp.bfloat16)
        for r in range(repeat):
            head = g * repeat + r
            attn[:, head * width : (head + 1) * width] = out[r * rows : (r + 1) * rows]
    w_copy.wait()
    value = mm(attn[...], w_buf[...])
    own_ref[...] = value
    send_ref[...] = value.astype(jnp.bfloat16)


def attention(queries, new_kv, pool, table, prompt_len, tails, tail_len, out_w):
    rows, heads, width = queries.shape
    n_pages, page, _, groups, _ = pool.shape
    conts, tail = tails.shape[:2]
    step = 2 * groups
    features = out_w.shape[1]
    quads = conts * NEW // 8
    pair = 2 if groups % 2 == 0 else 1
    pairs = groups // pair
    repeat = heads // groups
    stack = pair * repeat * rows
    return pl.pallas_call(
        functools.partial(
            attention_kernel, (rows, heads, groups, width, n_pages, page, conts, tail, pair)
        ),
        out_shape=(
            jax.ShapeDtypeStruct((rows, features), jnp.float32),
            jax.ShapeDtypeStruct((rows, features), jnp.bfloat16),
        ),
        in_specs=[SMEM, SMEM, SMEM, ANY, ANY, ANY, ANY, ANY],
        out_specs=(VMEM, VMEM),
        scratch_shapes=[
            pltpu.VMEM((n_pages * page * step, width), jnp.bfloat16),
            pltpu.VMEM((conts * tail * step, width), jnp.bfloat16),
            pltpu.VMEM(out_w.shape, jnp.bfloat16),
            pltpu.VMEM((rows * heads, width), jnp.bfloat16),
            pltpu.VMEM((rows * step, width), jnp.bfloat16),
            pltpu.VMEM((2, pairs, n_pages * page, pair * width), jnp.bfloat16),
            pltpu.VMEM((2, pairs, conts * tail, pair * width), jnp.bfloat16),
            pltpu.VMEM((rows * heads, width), jnp.float32),
            pltpu.VMEM((pairs, stack, pair * width), jnp.float32),
            pltpu.VMEM((rows * step, width), jnp.float32),
            pltpu.VMEM((pairs, stack, rows), jnp.float32),
            pltpu.VMEM((pairs, quads, pair * repeat * 8, 8 // NEW * tail), jnp.float32),
            pltpu.VMEM((pairs, stack, n_pages * page), jnp.float32),
            pltpu.VMEM((pairs, stack, 128), jnp.float32),
            pltpu.VMEM((pairs, stack, 128), jnp.float32),
            pltpu.VMEM((pairs, stack, pair * width), jnp.float32),
            pltpu.VMEM((rows, heads * width), jnp.bfloat16),
            pltpu.SemaphoreType.DMA((n_pages,)),
            pltpu.SemaphoreType.DMA((quads,)),
            pltpu.SemaphoreType.DMA((3,)),
        ],
        compiler_params=pltpu.CompilerParams(vmem_limit_bytes=ATTENTION_VMEM),
        name="attention",
    )(
        table,
        prompt_len,
        tail_len,
        queries.reshape(rows * heads, width),
        new_kv.reshape(rows * step, width),
        pool.reshape(n_pages * page * step, width),
        tails.reshape(conts * tail * step, width),
        out_w,
    )


def norm_kernel(n, block, own, other, gain, *refs):
    normed, middle, whole = refs[n:]
    copies, rows, features = normed.shape
    mid = own[...] + other[...].astype(jnp.float32)
    scale = lax.rsqrt(jnp.mean(mid * mid, axis=1, keepdims=True) + EPS)
    whole[...] = mid
    start = pl.multiple_of(block[0] * features, features)
    part = whole[:, pl.ds(start, features)]
    out = (part * scale * gain[:, pl.ds(start, features)]).astype(jnp.bfloat16)
    for index in range(copies):
        normed[index] = out
    middle[...] = part


def normalize(block, own, other, gain, features, copies, ahead):
    rows = own.shape[0]
    return pl.pallas_call(
        functools.partial(norm_kernel, len(ahead)),
        out_shape=(
            jax.ShapeDtypeStruct((copies, rows, features), jnp.bfloat16),
            jax.ShapeDtypeStruct((rows, features), jnp.float32),
        ),
        in_specs=[SMEM, VMEM, VMEM, VMEM] + [ANY] * len(ahead),
        out_specs=(VMEM, VMEM),
        scratch_shapes=[pltpu.VMEM(own.shape, jnp.float32)],
        compiler_params=pltpu.CompilerParams(vmem_limit_bytes=4 * MIB),
        name="normalize",
    )(block, own, other, gain.astype(jnp.float32).reshape(1, -1), *ahead)


def units_kernel(n, block, *refs):
    pieces, gate_w, up_w, outs, held, sums = refs[:n], *refs[n : n + 2], refs[n + 2 : -2], *refs[-2:]
    at = 0
    for piece in pieces:
        held[at : at + piece.shape[0], :] = piece[...]
        at += piece.shape[0]
    units = gate_w.shape[1]
    sums[:, :units] = mm(held[...], gate_w[...])
    sums[:, units:] = mm(held[...], up_w[...])
    if len(outs) == 1:
        outs[0][...] = sums[...].astype(jnp.bfloat16)
        return
    keep, away = outs[0], outs[1:]
    half, part = at // 2, away[0].shape[0]
    start = pl.multiple_of((1 - block[0]) * half, half)
    for index, out in enumerate(away):
        out[...] = sums[pl.ds(start + index * part, part), :].astype(jnp.bfloat16)
    keep[...] = sums[pl.ds(pl.multiple_of(block[0] * half, half), half), :]


def partial_units(split, block, pieces, gate_w, up_w):
    tokens = sum(piece.shape[0] for piece in pieces)
    features, units = gate_w.shape
    if split:
        out_shape = (
            jax.ShapeDtypeStruct((tokens // 2, 2 * units), jnp.float32),
            *[jax.ShapeDtypeStruct((tokens // 2 // split, 2 * units), jnp.bfloat16)] * split,
        )
    else:
        out_shape = (jax.ShapeDtypeStruct((tokens, 2 * units), jnp.bfloat16),)
    return pl.pallas_call(
        functools.partial(units_kernel, len(pieces)),
        out_shape=out_shape,
        in_specs=[SMEM] + [VMEM] * (len(pieces) + 2),
        out_specs=(VMEM,) * len(out_shape),
        scratch_shapes=[
            pltpu.VMEM((tokens, features), jnp.bfloat16),
            pltpu.VMEM((tokens, 2 * units), jnp.float32),
        ],
        compiler_params=pltpu.CompilerParams(vmem_limit_bytes=UNITS_VMEM),
        cost_estimate=pl.CostEstimate(
            flops=4 * tokens * features * units,
            bytes_accessed=2 * tokens * features + 4 * features * units,
            transcendentals=0,
        ),
        name="gate_up",
    )(block, *pieces, gate_w, up_w)


def hidden_kernel(sums, *refs):
    others, out = refs[:-1], refs[-1]
    units = out.shape[1]
    at = 0
    for other in others or (None,):
        to = at + (sums if other is None else other).shape[0]
        both = sums[at:to, :].astype(jnp.float32)
        if other is not None:
            both = both + other[...].astype(jnp.float32)
        gate, up = both[:, :units], both[:, units:]
        out[at:to, :] = (gate / (1.0 + jnp.exp(-gate)) * up).astype(jnp.bfloat16)
        at = to


def hidden_units(sums, *others):
    tokens, units = sums.shape[0], sums.shape[1] // 2
    return pl.pallas_call(
        hidden_kernel,
        out_shape=jax.ShapeDtypeStruct((tokens, units), jnp.bfloat16),
        in_specs=[VMEM] * (1 + len(others)),
        out_specs=VMEM,
        compiler_params=pltpu.CompilerParams(vmem_limit_bytes=4 * MIB),
        name="hidden",
    )(sums, *others)


def down_kernel(orders, flip, n, chip_ref, core_ref, *refs):
    parts, source, middle, down_w = refs[:n], *refs[n : n + 3]
    outs, hidden, term = refs[n + 3 : -2], *refs[-2:]
    tokens, features = term.shape
    rows = middle.shape[0]
    chip, core = chip_ref[0], core_ref[0]
    at = 0
    for part in parts:
        hidden[at : at + part.shape[0], :] = part[...]
        at += part.shape[0]
    slot, local = source[:, 0:1], source[:, 1:2]
    pick = (lax.broadcasted_iota(jnp.int32, (tokens, tokens), 1) == slot).astype(jnp.bfloat16)
    moved = mm(pick, hidden[...]).astype(jnp.bfloat16)
    mine = lax.broadcasted_iota(jnp.int32, (tokens, rows), 1) == local
    mine = mine.astype(jnp.bfloat16)
    high = middle[...].astype(jnp.bfloat16)
    low = (middle[...] - high.astype(jnp.float32)).astype(jnp.bfloat16)
    term[...] = mm(moved, down_w[...]) + (mm(mine, high) + mm(mine, low))
    for order, keep, send in zip(orders, outs[::2], outs[1::2]):
        for index, dest in enumerate(order):
            at = slice(index * rows, (index + 1) * rows)
            dest = dest ^ chip if flip else dest
            start = pl.multiple_of((2 * dest + core) * rows, rows)
            keep[at, :] = term[pl.ds(start, rows), :]
            start = pl.multiple_of((2 * dest + (1 - core)) * rows, rows)
            send[at, :] = term[pl.ds(start, rows), :].astype(jnp.bfloat16)


def down(orders, flip, chip, core, parts, source, middle, down_w):
    tokens = source.shape[0]
    units, features = down_w.shape
    rows = middle.shape[0]
    out_shape = ()
    for order in orders:
        shape = (len(order) * rows, features)
        out_shape += (
            jax.ShapeDtypeStruct(shape, jnp.float32),
            jax.ShapeDtypeStruct(shape, jnp.bfloat16),
        )
    outs = pl.pallas_call(
        functools.partial(down_kernel, orders, flip, len(parts)),
        out_shape=out_shape,
        in_specs=[SMEM, SMEM] + [VMEM] * (len(parts) + 3),
        out_specs=(VMEM,) * len(out_shape),
        scratch_shapes=[
            pltpu.VMEM((tokens, units), jnp.bfloat16),
            pltpu.VMEM((tokens, features), jnp.float32),
        ],
        compiler_params=pltpu.CompilerParams(vmem_limit_bytes=DOWN_VMEM),
        name="down",
    )(chip, core, *parts, source, middle, down_w)
    return list(zip(outs[::2], outs[1::2]))


def pack_kernel(n, *refs):
    pieces, out = refs[:n], refs[-1]
    at = 0
    for piece in pieces:
        out[at : at + piece.shape[0], :] = piece[...]
        at += piece.shape[0]


def pack(pieces, after=()):
    rows = sum(piece.shape[0] for piece in pieces)
    return pl.pallas_call(
        functools.partial(pack_kernel, len(pieces)),
        out_shape=jax.ShapeDtypeStruct((rows, pieces[0].shape[1]), pieces[0].dtype),
        in_specs=[VMEM] * len(pieces) + [ANY] * len(after),
        out_specs=VMEM,
        compiler_params=pltpu.CompilerParams(vmem_limit_bytes=4 * MIB),
        name="pack",
    )(*pieces, *after)


def add_kernel(keep, other, *outs):
    at = 0
    for out in outs:
        to = at + out.shape[0]
        out[...] = (keep[at:to, :] + other[at:to, :].astype(jnp.float32)).astype(out.dtype)
        at = to


def add_parts(keep, other, kinds):
    rows, features = keep.shape
    return pl.pallas_call(
        add_kernel,
        out_shape=tuple(
            jax.ShapeDtypeStruct((rows // len(kinds), features), kind) for kind in kinds
        ),
        in_specs=[VMEM, VMEM],
        out_specs=(VMEM,) * len(kinds),
        compiler_params=pltpu.CompilerParams(vmem_limit_bytes=4 * MIB),
        name="add_parts",
    )(keep, other)


def finish_kernel(n, *refs):
    parts, gain, score, out, stats = refs[:n], *refs[n:]
    moved = functools.reduce(jnp.add, [part[...].astype(jnp.float32) for part in parts])
    out[...] = moved.astype(jnp.bfloat16)
    weighted = gain[...].astype(jnp.float32) * score[...].astype(jnp.float32)
    lane = lax.broadcasted_iota(jnp.int32, (out.shape[0], 128), 1)
    squares = jnp.sum(moved * moved, axis=1, keepdims=True)
    terms = jnp.sum(moved * weighted, axis=1, keepdims=True)
    stats[...] = jnp.transpose(jnp.where(lane == 0, squares, terms))[:8]


def finish(parts, gain, score):
    rows, features = parts[0].shape
    return pl.pallas_call(
        functools.partial(finish_kernel, len(parts)),
        out_shape=(
            jax.ShapeDtypeStruct((rows, features), jnp.bfloat16),
            jax.ShapeDtypeStruct((8, rows), jnp.float32),
        ),
        in_specs=[VMEM] * (len(parts) + 2),
        out_specs=(VMEM, VMEM),
        compiler_params=pltpu.CompilerParams(vmem_limit_bytes=4 * MIB),
        name="finish",
    )(*parts, gain, score)


def shards(
    n_chip,
    n_blk,
    resid,
    queries,
    new_kv,
    prefix_pool,
    page_table,
    prompt_len,
    tail_pool,
    tail_len,
    migration,
    out_w,
    mlp_gain,
    gate_w,
    up_w,
    down_w,
    final_gain,
    score_w,
):
    rows = resid.shape[0]
    features = gate_w.shape[0]
    chip = lax.axis_index("chip").astype(jnp.int32)
    core = lax.axis_index("core").astype(jnp.int32)
    block = lax.axis_index("blk").astype(jnp.int32)
    direct = n_chip == 8 and n_blk == 2

    def to_chip(value, index):
        return lax.ppermute(value, "chip", [(i, i ^ index) for i in range(n_chip)])

    def swap(value, axis):
        return lax.ppermute(value, axis, [(0, 1), (1, 0)])

    own, send = attention(
        queries, new_kv, prefix_pool, page_table, prompt_len, tail_pool, tail_len, out_w
    )
    if direct:
        own, other = own + resid.astype(jnp.float32), swap(send, "blk")
    else:
        own, other = resid.astype(jnp.float32), lax.psum(send, "blk")
    token = migration[:, None] * NEW + jnp.arange(NEW, dtype=jnp.int32)[None, :]
    token = token.reshape(-1, 1)
    came, inner = token // rows, token % rows
    far, far_core = (came // 2) ^ chip, (came % 2) ^ core
    if direct:
        slot = (far % 2 * 2 + (far_core ^ block)) * 4 + far // 2 % 2 * 2 + far // 4
    else:
        slot = far_core * n_chip + came // 2
    local = token - (chip * 2 + core) * rows
    source = jnp.concatenate([slot * rows + inner, local], axis=1)
    chip, core, block = (index.reshape(1) for index in (chip, core, block))
    gain_row, score_row = final_gain.reshape(1, -1), score_w.reshape(1, -1)

    normed, middle = normalize(
        block,
        own,
        other,
        mlp_gain,
        features,
        1 if direct else n_chip,
        (chip, core, source, gain_row, score_row),
    )
    if direct:
        piece = normed.reshape(rows, features)
        z2, z3, z1 = (to_chip(piece, index) for index in (4, 6, 2))
        here = [pack([piece, z2]), pack([z1, z3])]
        there = [to_chip(part, 1) for part in here]
        parts, after = [], ()
        for near, split in ((here, 2), (there, 1)):
            if after:
                near = [pack(near, after)]
            pieces = near + [swap(part, "core") for part in near]
            keep, *away = partial_units(split, block, pieces, gate_w, up_w)
            others = [swap(part, "blk") for part in away]
            hidden = hidden_units(keep, *others)
            parts += [hidden, swap(hidden, "blk")]
            after = others
    else:
        near = lax.all_to_all(normed, "chip", 0, 0).reshape(n_chip * rows, features)
        units = partial_units(0, block, [near, swap(near, "core")], gate_w, up_w)[0]
        parts = [hidden_units(lax.psum(units, "blk"))]
    if direct:
        near, wide = down(
            ((0, 4, 1, 5), (6, 2, 7, 3)), True, chip, core, parts, source, middle, down_w
        )
        kinds = (jnp.float32, jnp.bfloat16)
        near = add_parts(near[0], swap(near[1], "core"), kinds)
        wide = add_parts(wide[0], swap(wide[1], "core"), kinds)
        mine, to4 = add_parts(near[0], to_chip(near[1], 1), kinds)
        to6, to2 = add_parts(wide[0], to_chip(wide[1], 1), (jnp.bfloat16, jnp.bfloat16))
        sums = [mine, to_chip(to4, 4), to_chip(to6, 6), to_chip(to2, 2)]
    else:
        order = tuple(range(n_chip))
        ((keep, away),) = down((order,), False, chip, core, parts, source, middle, down_w)
        total = (keep + swap(away, "core").astype(jnp.float32)).astype(jnp.bfloat16)
        total = lax.all_to_all(total.reshape(n_chip, rows, features), "chip", 0, 0)
        sums = [jnp.sum(total.astype(jnp.float32), axis=0)]
    hidden_out, stats = finish(sums, gain_row, score_row)
    stats = stats + swap(stats, "blk") if direct else lax.psum(stats, "blk")
    score = stats[1] * lax.rsqrt(stats[0] / D + EPS)
    return (hidden_out, score)


def solution(mesh):
    n_chip, n_blk = mesh.shape["dp"] // 2, mesh.shape["blk"]
    split = Mesh(mesh.devices.reshape(n_chip, 2, n_blk), ("chip", "core", "blk"))
    dp = ("chip", "core")
    return jax.shard_map(
        functools.partial(shards, n_chip, n_blk),
        mesh=split,
        in_specs=(
            P(dp, None),
            P(dp, "blk", None),
            P(dp, None, "blk", None),
            P(dp, None, None, "blk", None),
            P(dp, None),
            P(dp),
            P(dp, None, None, "blk", None),
            P(dp, None),
            P(),
            P("blk", None),
            P(),
            P("blk", dp),
            P("blk", dp),
            P(dp, "blk"),
            P("blk"),
            P("blk"),
        ),
        out_specs=(P(dp, "blk"), P(dp)),
        check_vma=False,
    )
```

```python
import functools
import math

import jax
import jax.numpy as jnp
from jax import lax
from jax.experimental import pallas as pl
from jax.experimental.pallas import tpu as pltpu
from jax.sharding import Mesh
from jax.sharding import PartitionSpec as P

D = 2048
NEW = 2
NEG = -1e30
EPS = 1e-06
MIB = 1 << 20
ATTENTION_VMEM = 60 * MIB
UNITS_VMEM = 6 * MIB
DOWN_VMEM = 12 * MIB

VMEM = pl.BlockSpec(memory_space=pltpu.VMEM)
SMEM = pl.BlockSpec(memory_space=pltpu.SMEM)
ANY = pl.BlockSpec(memory_space=pl.ANY)


def mm(a, b):
    return jnp.dot(a, b, preferred_element_type=jnp.float32)


def mm_t(a, b):
    return lax.dot_general(a, b, (((1,), (1,)), ((), ())), preferred_element_type=jnp.float32)


def attention_kernel(
    dims,
    table,
    prompt_len,
    tail_len,
    queries,
    new_kv,
    pool,
    tails,
    out_w,
    own_ref,
    send_ref,
    pages,
    tail_buf,
    w_buf,
    q_buf,
    new_buf,
    keys_apart,
    apart,
    tail_keys,
    tail_apart,
    q_wide,
    q_rows,
    new_wide,
    fresh_scores,
    tail_scores,
    scores,
    top,
    total,
    acc,
    attn,
    page_sems,
    tail_sems,
    sems,
):
    rows, heads, groups, width, n_pages, page, conts, tail, pair = dims
    repeat = heads // groups
    step = 2 * groups
    pairs = groups // pair
    stack = repeat * rows
    page_rows = page * step
    chunk_pages = math.gcd(16, n_pages)
    chunk = chunk_pages * page
    chunk_rows = chunk * step
    quad = 8 // NEW
    quads = conts // quad
    quad_keys = quad * tail
    quad_rows = quad_keys * step
    factor = math.log2(math.e) / math.sqrt(width)
    length = prompt_len[0]
    chunks = (length + chunk - 1) // chunk

    def page_copy(logical):
        physical = table[0, logical]
        return pltpu.make_async_copy(
            pool.at[pl.ds(pl.multiple_of(physical * page_rows, page_rows), page_rows), :],
            pages.at[pl.ds(pl.multiple_of(logical * page_rows, page_rows), page_rows), :],
            page_sems.at[logical],
        )

    def tail_copy(index):
        return pltpu.make_async_copy(
            tails.at[pl.ds(index * quad_rows, quad_rows), :],
            tail_buf.at[pl.ds(index * quad_rows, quad_rows), :],
            tail_sems.at[index],
        )

    q_copy = pltpu.make_async_copy(queries, q_buf, sems.at[0])
    new_copy = pltpu.make_async_copy(new_kv, new_buf, sems.at[1])
    w_copy = pltpu.make_async_copy(out_w, w_buf, sems.at[2])
    q_copy.start()
    new_copy.start()
    for index in range(quads):
        tail_copy(index).start()

    @pl.loop(0, chunks * chunk_pages)
    def _(logical):
        page_copy(logical).start()

    w_copy.start()

    block = 256
    tokens = block // step
    to = lax.broadcasted_iota(jnp.int32, (block, block), 0)
    came = lax.broadcasted_iota(jnp.int32, (block, block), 1)
    sort = (came == (to % tokens) * step + to // tokens).astype(jnp.bfloat16)

    def take_apart(buf, start, count, outs, places):
        for two in range(count // (2 * block)):
            x0 = buf[pl.ds(start + two * 2 * block, block), :]
            x1 = buf[pl.ds(start + (two * 2 + 1) * block, block), :]
            y = mm(sort, jnp.concatenate([x0, x1], axis=1)).astype(jnp.bfloat16)
            for side in range(2):
                for j in range(step):
                    kind, g = j // groups, j % groups
                    t = pl.ds(places[kind] + (2 * two + side) * tokens, tokens)
                    lane = (g % pair) * width
                    outs[kind][g // pair, t, lane : lane + width] = y[
                        j * tokens : (j + 1) * tokens, side * width : (side + 1) * width
                    ]

    def blocks(x):
        return [x[:, i * 128 : (i + 1) * 128] for i in range(x.shape[1] // 128)]

    q_copy.wait()
    new_copy.wait()
    q_wide[...] = q_buf[...].astype(jnp.float32)
    new_wide[...] = new_buf[...].astype(jnp.float32)
    if pair > 1:
        q_rows[...] = jnp.zeros_like(q_rows)
    for g in range(groups):
        for r in range(repeat):
            at = (g % pair) * stack + r * rows
            lane = (g % pair) * width
            q_rows[g // pair, at : at + rows, lane : lane + width] = q_wide[
                pl.ds(g * repeat + r, rows, stride=heads), :
            ]

    def fresh(first, n):
        parts = [
            new_wide[pl.ds(first + n * pair + i, rows, stride=step), :] for i in range(pair)
        ]
        return jnp.concatenate(parts, axis=1).astype(jnp.bfloat16)

    row = lax.broadcasted_iota(jnp.int32, (rows, rows), 0)
    key = lax.broadcasted_iota(jnp.int32, (rows, rows), 1)
    fresh_ok = (row // NEW == key // NEW) & (key <= row)
    fresh_ok = jnp.concatenate([fresh_ok] * (pair * repeat), axis=0)
    for n in range(pairs):
        s = jnp.where(fresh_ok, mm_t(q_rows[n].astype(jnp.bfloat16), fresh(0, n)) * factor, NEG)
        fresh_scores[n] = s
        top[n] = jnp.broadcast_to(jnp.max(s, axis=1, keepdims=True), top.shape[1:])

    def quad_places(index):
        starts = [i * rows + index * 8 for i in range(pair * repeat)]
        return [slice(at, at + 8) for at in starts]

    quad_row = lax.broadcasted_iota(jnp.int32, (8, quad_keys), 0)
    quad_key = lax.broadcasted_iota(jnp.int32, (8, quad_keys), 1)
    for index in range(quads):
        tail_copy(index).wait()
    for index in range(quads):
        outs, at = (tail_keys, tail_apart), index * quad_keys
        take_apart(tail_buf, index * quad_rows, quad_rows, outs, (at, at))
        reach = jnp.zeros((8, quad_keys), jnp.int32)
        for c in range(quad):
            reach = jnp.where(
                quad_key // tail == c, tail_len[0, index * quad + c] + c * tail, reach
            )
        ok = (quad_row // NEW == quad_key // tail) & (quad_key < reach)
        ok = jnp.concatenate([ok] * (pair * repeat), axis=0)
        keys = slice(index * quad_keys, (index + 1) * quad_keys)
        for n in range(pairs):
            q = jnp.concatenate([q_rows[n, a, :] for a in quad_places(index)], axis=0)
            s = mm_t(q.astype(jnp.bfloat16), tail_keys[n, keys, :]) * factor
            s = jnp.where(ok, s, NEG)
            tail_scores[n, index] = s
            high = functools.reduce(jnp.maximum, blocks(s))
            for i, a in enumerate(quad_places(index)):
                top[n, a, :] = jnp.maximum(top[n, a, :], high[i * 8 : (i + 1) * 8])

    part = min(256, chunk)
    place = lax.broadcasted_iota(jnp.int32, (8, part), 1)

    @pl.loop(0, chunks)
    def _(index):
        for i in range(chunk_pages):
            page_copy(index * chunk_pages + i).wait()
        first = pl.multiple_of(index * chunk, chunk)
        row = pl.multiple_of(index * chunk_rows, chunk_rows)
        for at in range(0, chunk, part):
            outs, places = (keys_apart, apart), (at, first + at)
            take_apart(pages, row + at * step, part * step, outs, places)
            ok = place[0:1] < length - (index * chunk + at)
            for n in range(pairs):
                q = q_rows[n].astype(jnp.bfloat16)
                s = mm_t(q, keys_apart[n, at : at + part, :]) * factor
                s = jnp.where(ok, s, NEG)
                scores[n, :, pl.ds(first + at, part)] = s
                top[n] = functools.reduce(jnp.maximum, blocks(s), top[n])

    for n in range(pairs):
        high = jnp.broadcast_to(jnp.max(top[n], axis=1, keepdims=True), top.shape[1:])
        top[n] = high
        p = jnp.exp2(fresh_scores[n] - high[:, :rows])
        lane = lax.broadcasted_iota(jnp.int32, total.shape[1:], 1)
        total[n] = jnp.where(lane == 0, jnp.sum(p, axis=1, keepdims=True), 0.0)
        acc[n] = mm(p.astype(jnp.bfloat16), fresh(groups, n))

    def weigh(s, high):
        parts = [jnp.exp2(part - high) for part in blocks(s)]
        return jnp.concatenate(parts, axis=1).astype(jnp.bfloat16), functools.reduce(jnp.add, parts)

    for index in range(quads):
        keys = slice(index * quad_keys, (index + 1) * quad_keys)
        for n in range(pairs):
            high = jnp.concatenate([top[n, a, :] for a in quad_places(index)], axis=0)
            p, added = weigh(tail_scores[n, index], high)
            value = mm(p, tail_apart[n, keys, :])
            for i, a in enumerate(quad_places(index)):
                total[n, a, :] = total[n, a, :] + added[i * 8 : (i + 1) * 8]
                acc[n, a, :] = acc[n, a, :] + value[i * 8 : (i + 1) * 8]

    @pl.loop(0, chunks)
    def _(index):
        first = pl.multiple_of(index * chunk, chunk)
        for n in range(pairs):
            p, added = weigh(scores[n, :, pl.ds(first, chunk)], top[n])
            total[n] = total[n] + added
            acc[n] = acc[n] + mm(p, apart[n, pl.ds(first, chunk), :])

    for g in range(groups):
        at, lane = (g % pair) * stack, (g % pair) * width
        out = acc[g // pair, at : at + stack, lane : lane + width]
        out = out / jnp.sum(total[g // pair, at : at + stack, :], axis=1, keepdims=True)
        out = out.astype(jnp.bfloat16)
        for r in range(repeat):
            head = g * repeat + r
            attn[:, head * width : (head + 1) * width] = out[r * rows : (r + 1) * rows]
    w_copy.wait()
    value = mm(attn[...], w_buf[...])
    own_ref[...] = value
    send_ref[...] = value.astype(jnp.bfloat16)


def attention(queries, new_kv, pool, table, prompt_len, tails, tail_len, out_w):
    rows, heads, width = queries.shape
    n_pages, page, _, groups, _ = pool.shape
    conts, tail = tails.shape[:2]
    step = 2 * groups
    features = out_w.shape[1]
    quads = conts * NEW // 8
    pair = 2 if groups % 2 == 0 else 1
    pairs = groups // pair
    repeat = heads // groups
    stack = pair * repeat * rows
    return pl.pallas_call(
        functools.partial(
            attention_kernel, (rows, heads, groups, width, n_pages, page, conts, tail, pair)
        ),
        out_shape=(
            jax.ShapeDtypeStruct((rows, features), jnp.float32),
            jax.ShapeDtypeStruct((rows, features), jnp.bfloat16),
        ),
        in_specs=[SMEM, SMEM, SMEM, ANY, ANY, ANY, ANY, ANY],
        out_specs=(VMEM, VMEM),
        scratch_shapes=[
            pltpu.VMEM((n_pages * page * step, width), jnp.bfloat16),
            pltpu.VMEM((conts * tail * step, width), jnp.bfloat16),
            pltpu.VMEM(out_w.shape, jnp.bfloat16),
            pltpu.VMEM((rows * heads, width), jnp.bfloat16),
            pltpu.VMEM((rows * step, width), jnp.bfloat16),
            pltpu.VMEM((pairs, n_pages * page, pair * width), jnp.bfloat16),
            pltpu.VMEM((pairs, n_pages * page, pair * width), jnp.bfloat16),
            pltpu.VMEM((pairs, conts * tail, pair * width), jnp.bfloat16),
            pltpu.VMEM((pairs, conts * tail, pair * width), jnp.bfloat16),
            pltpu.VMEM((rows * heads, width), jnp.float32),
            pltpu.VMEM((pairs, stack, pair * width), jnp.float32),
            pltpu.VMEM((rows * step, width), jnp.float32),
            pltpu.VMEM((pairs, stack, rows), jnp.float32),
            pltpu.VMEM((pairs, quads, pair * repeat * 8, 8 // NEW * tail), jnp.float32),
            pltpu.VMEM((pairs, stack, n_pages * page), jnp.float32),
            pltpu.VMEM((pairs, stack, 128), jnp.float32),
            pltpu.VMEM((pairs, stack, 128), jnp.float32),
            pltpu.VMEM((pairs, stack, pair * width), jnp.float32),
            pltpu.VMEM((rows, heads * width), jnp.bfloat16),
            pltpu.SemaphoreType.DMA((n_pages,)),
            pltpu.SemaphoreType.DMA((quads,)),
            pltpu.SemaphoreType.DMA((3,)),
        ],
        compiler_params=pltpu.CompilerParams(vmem_limit_bytes=ATTENTION_VMEM),
        name="attention",
    )(
        table,
        prompt_len,
        tail_len,
        queries.reshape(rows * heads, width),
        new_kv.reshape(rows * step, width),
        pool.reshape(n_pages * page * step, width),
        tails.reshape(conts * tail * step, width),
        out_w,
    )


def norm_kernel(n, block, own, other, gain, *refs):
    normed, middle, whole = refs[n:]
    copies, rows, features = normed.shape
    mid = own[...] + other[...].astype(jnp.float32)
    scale = lax.rsqrt(jnp.mean(mid * mid, axis=1, keepdims=True) + EPS)
    whole[...] = mid
    start = pl.multiple_of(block[0] * features, features)
    part = whole[:, pl.ds(start, features)]
    out = (part * scale * gain[:, pl.ds(start, features)]).astype(jnp.bfloat16)
    for index in range(copies):
        normed[index] = out
    middle[...] = part


def normalize(block, own, other, gain, features, copies, ahead):
    rows = own.shape[0]
    return pl.pallas_call(
        functools.partial(norm_kernel, len(ahead)),
        out_shape=(
            jax.ShapeDtypeStruct((copies, rows, features), jnp.bfloat16),
            jax.ShapeDtypeStruct((rows, features), jnp.float32),
        ),
        in_specs=[SMEM, VMEM, VMEM, VMEM] + [ANY] * len(ahead),
        out_specs=(VMEM, VMEM),
        scratch_shapes=[pltpu.VMEM(own.shape, jnp.float32)],
        compiler_params=pltpu.CompilerParams(vmem_limit_bytes=4 * MIB),
        name="normalize",
    )(block, own, other, gain.astype(jnp.float32).reshape(1, -1), *ahead)


def units_kernel(n, block, *refs):
    pieces, gate_w, up_w, outs, held, sums = refs[:n], *refs[n : n + 2], refs[n + 2 : -2], *refs[-2:]
    at = 0
    for piece in pieces:
        held[at : at + piece.shape[0], :] = piece[...]
        at += piece.shape[0]
    units = gate_w.shape[1]
    sums[:, :units] = mm(held[...], gate_w[...])
    sums[:, units:] = mm(held[...], up_w[...])
    if len(outs) == 1:
        outs[0][...] = sums[...].astype(jnp.bfloat16)
        return
    keep, away = outs[0], outs[1:]
    half, part = at // 2, away[0].shape[0]
    start = pl.multiple_of((1 - block[0]) * half, half)
    for index, out in enumerate(away):
        out[...] = sums[pl.ds(start + index * part, part), :].astype(jnp.bfloat16)
    keep[...] = sums[pl.ds(pl.multiple_of(block[0] * half, half), half), :]


def partial_units(split, block, pieces, gate_w, up_w):
    tokens = sum(piece.shape[0] for piece in pieces)
    features, units = gate_w.shape
    if split:
        out_shape = (
            jax.ShapeDtypeStruct((tokens // 2, 2 * units), jnp.float32),
            *[jax.ShapeDtypeStruct((tokens // 2 // split, 2 * units), jnp.bfloat16)] * split,
        )
    else:
        out_shape = (jax.ShapeDtypeStruct((tokens, 2 * units), jnp.bfloat16),)
    return pl.pallas_call(
        functools.partial(units_kernel, len(pieces)),
        out_shape=out_shape,
        in_specs=[SMEM] + [VMEM] * (len(pieces) + 2),
        out_specs=(VMEM,) * len(out_shape),
        scratch_shapes=[
            pltpu.VMEM((tokens, features), jnp.bfloat16),
            pltpu.VMEM((tokens, 2 * units), jnp.float32),
        ],
        compiler_params=pltpu.CompilerParams(vmem_limit_bytes=UNITS_VMEM),
        cost_estimate=pl.CostEstimate(
            flops=4 * tokens * features * units,
            bytes_accessed=2 * tokens * features + 4 * features * units,
            transcendentals=0,
        ),
        name="gate_up",
    )(block, *pieces, gate_w, up_w)


def hidden_kernel(sums, *refs):
    others, out = refs[:-1], refs[-1]
    units = out.shape[1]
    at = 0
    for other in others or (None,):
        to = at + (sums if other is None else other).shape[0]
        both = sums[at:to, :].astype(jnp.float32)
        if other is not None:
            both = both + other[...].astype(jnp.float32)
        gate, up = both[:, :units], both[:, units:]
        out[at:to, :] = (gate / (1.0 + jnp.exp(-gate)) * up).astype(jnp.bfloat16)
        at = to


def hidden_units(sums, *others):
    tokens, units = sums.shape[0], sums.shape[1] // 2
    return pl.pallas_call(
        hidden_kernel,
        out_shape=jax.ShapeDtypeStruct((tokens, units), jnp.bfloat16),
        in_specs=[VMEM] * (1 + len(others)),
        out_specs=VMEM,
        compiler_params=pltpu.CompilerParams(vmem_limit_bytes=4 * MIB),
        name="hidden",
    )(sums, *others)


def down_kernel(orders, flip, n, chip_ref, core_ref, *refs):
    parts, source, middle, down_w = refs[:n], *refs[n : n + 3]
    outs, hidden, term = refs[n + 3 : -2], *refs[-2:]
    tokens, features = term.shape
    rows = middle.shape[0]
    chip, core = chip_ref[0], core_ref[0]
    at = 0
    for part in parts:
        hidden[at : at + part.shape[0], :] = part[...]
        at += part.shape[0]
    slot, local = source[:, 0:1], source[:, 1:2]
    pick = (lax.broadcasted_iota(jnp.int32, (tokens, tokens), 1) == slot).astype(jnp.bfloat16)
    moved = mm(pick, hidden[...]).astype(jnp.bfloat16)
    mine = lax.broadcasted_iota(jnp.int32, (tokens, rows), 1) == local
    mine = mine.astype(jnp.bfloat16)
    high = middle[...].astype(jnp.bfloat16)
    low = (middle[...] - high.astype(jnp.float32)).astype(jnp.bfloat16)
    term[...] = mm(moved, down_w[...]) + (mm(mine, high) + mm(mine, low))
    for order, keep, send in zip(orders, outs[::2], outs[1::2]):
        for index, dest in enumerate(order):
            at = slice(index * rows, (index + 1) * rows)
            dest = dest ^ chip if flip else dest
            start = pl.multiple_of((2 * dest + core) * rows, rows)
            keep[at, :] = term[pl.ds(start, rows), :]
            start = pl.multiple_of((2 * dest + (1 - core)) * rows, rows)
            send[at, :] = term[pl.ds(start, rows), :].astype(jnp.bfloat16)


def down(orders, flip, chip, core, parts, source, middle, down_w):
    tokens = source.shape[0]
    units, features = down_w.shape
    rows = middle.shape[0]
    out_shape = ()
    for order in orders:
        shape = (len(order) * rows, features)
        out_shape += (
            jax.ShapeDtypeStruct(shape, jnp.float32),
            jax.ShapeDtypeStruct(shape, jnp.bfloat16),
        )
    outs = pl.pallas_call(
        functools.partial(down_kernel, orders, flip, len(parts)),
        out_shape=out_shape,
        in_specs=[SMEM, SMEM] + [VMEM] * (len(parts) + 3),
        out_specs=(VMEM,) * len(out_shape),
        scratch_shapes=[
            pltpu.VMEM((tokens, units), jnp.bfloat16),
            pltpu.VMEM((tokens, features), jnp.float32),
        ],
        compiler_params=pltpu.CompilerParams(vmem_limit_bytes=DOWN_VMEM),
        name="down",
    )(chip, core, *parts, source, middle, down_w)
    return list(zip(outs[::2], outs[1::2]))


def pack_kernel(n, *refs):
    pieces, out = refs[:n], refs[-1]
    at = 0
    for piece in pieces:
        out[at : at + piece.shape[0], :] = piece[...]
        at += piece.shape[0]


def pack(pieces, after=()):
    rows = sum(piece.shape[0] for piece in pieces)
    return pl.pallas_call(
        functools.partial(pack_kernel, len(pieces)),
        out_shape=jax.ShapeDtypeStruct((rows, pieces[0].shape[1]), pieces[0].dtype),
        in_specs=[VMEM] * len(pieces) + [ANY] * len(after),
        out_specs=VMEM,
        compiler_params=pltpu.CompilerParams(vmem_limit_bytes=4 * MIB),
        name="pack",
    )(*pieces, *after)


def add_kernel(keep, other, *outs):
    at = 0
    for out in outs:
        to = at + out.shape[0]
        out[...] = (keep[at:to, :] + other[at:to, :].astype(jnp.float32)).astype(out.dtype)
        at = to


def add_parts(keep, other, kinds):
    rows, features = keep.shape
    return pl.pallas_call(
        add_kernel,
        out_shape=tuple(
            jax.ShapeDtypeStruct((rows // len(kinds), features), kind) for kind in kinds
        ),
        in_specs=[VMEM, VMEM],
        out_specs=(VMEM,) * len(kinds),
        compiler_params=pltpu.CompilerParams(vmem_limit_bytes=4 * MIB),
        name="add_parts",
    )(keep, other)


def finish_kernel(n, *refs):
    parts, gain, score, moved, stats = refs[:n], *refs[n:]
    total = functools.reduce(jnp.add, [part[...].astype(jnp.float32) for part in parts])
    moved[...] = total
    weighted = gain[...].astype(jnp.float32) * score[...].astype(jnp.float32)
    lane = lax.broadcasted_iota(jnp.int32, (total.shape[0], 128), 1)
    squares = jnp.sum(total * total, axis=1, keepdims=True)
    terms = jnp.sum(total * weighted, axis=1, keepdims=True)
    stats[...] = jnp.transpose(jnp.where(lane == 0, squares, terms))[:8]


def finish(parts, gain, score):
    rows, features = parts[0].shape
    return pl.pallas_call(
        functools.partial(finish_kernel, len(parts)),
        out_shape=(
            jax.ShapeDtypeStruct((rows, features), jnp.float32),
            jax.ShapeDtypeStruct((8, rows), jnp.float32),
        ),
        in_specs=[VMEM] * (len(parts) + 2),
        out_specs=(VMEM, VMEM),
        compiler_params=pltpu.CompilerParams(vmem_limit_bytes=4 * MIB),
        name="finish",
    )(*parts, gain, score)


def shards(
    n_chip,
    n_blk,
    resid,
    queries,
    new_kv,
    prefix_pool,
    page_table,
    prompt_len,
    tail_pool,
    tail_len,
    migration,
    out_w,
    mlp_gain,
    gate_w,
    up_w,
    down_w,
    final_gain,
    score_w,
):
    rows = resid.shape[0]
    features = gate_w.shape[0]
    chip = lax.axis_index("chip").astype(jnp.int32)
    core = lax.axis_index("core").astype(jnp.int32)
    block = lax.axis_index("blk").astype(jnp.int32)
    direct = n_chip == 8 and n_blk == 2

    def to_chip(value, index):
        return lax.ppermute(value, "chip", [(i, i ^ index) for i in range(n_chip)])

    def swap(value, axis):
        return lax.ppermute(value, axis, [(0, 1), (1, 0)])

    own, send = attention(
        queries, new_kv, prefix_pool, page_table, prompt_len, tail_pool, tail_len, out_w
    )
    if direct:
        own, other = own + resid.astype(jnp.float32), swap(send, "blk")
    else:
        own, other = resid.astype(jnp.float32), lax.psum(send, "blk")
    token = migration[:, None] * NEW + jnp.arange(NEW, dtype=jnp.int32)[None, :]
    token = token.reshape(-1, 1)
    came, inner = token // rows, token % rows
    far, far_core = (came // 2) ^ chip, (came % 2) ^ core
    if direct:
        slot = (far % 2 * 2 + (far_core ^ block)) * 4 + far // 2 % 2 * 2 + far // 4
    else:
        slot = far_core * n_chip + came // 2
    local = token - (chip * 2 + core) * rows
    source = jnp.concatenate([slot * rows + inner, local], axis=1)
    chip, core, block = (index.reshape(1) for index in (chip, core, block))
    gain_row, score_row = final_gain.reshape(1, -1), score_w.reshape(1, -1)

    normed, middle = normalize(
        block,
        own,
        other,
        mlp_gain,
        features,
        1 if direct else n_chip,
        (chip, core, source, gain_row, score_row),
    )
    if direct:
        piece = normed.reshape(rows, features)
        z2, z3, z1 = (to_chip(piece, index) for index in (4, 6, 2))
        here = [pack([piece, z2]), pack([z1, z3])]
        there = [to_chip(part, 1) for part in here]
        parts, after = [], ()
        for near, split in ((here, 2), (there, 1)):
            if after:
                near = [pack(near, after)]
            pieces = near + [swap(part, "core") for part in near]
            keep, *away = partial_units(split, block, pieces, gate_w, up_w)
            others = [swap(part, "blk") for part in away]
            hidden = hidden_units(keep, *others)
            parts += [hidden, swap(hidden, "blk")]
            after = others
    else:
        near = lax.all_to_all(normed, "chip", 0, 0).reshape(n_chip * rows, features)
        units = partial_units(0, block, [near, swap(near, "core")], gate_w, up_w)[0]
        parts = [hidden_units(lax.psum(units, "blk"))]
    if direct:
        near, wide = down(
            ((0, 4, 1, 5), (6, 2, 7, 3)), True, chip, core, parts, source, middle, down_w
        )
        kinds = (jnp.float32, jnp.bfloat16)
        near = add_parts(near[0], swap(near[1], "core"), kinds)
        wide = add_parts(wide[0], swap(wide[1], "core"), kinds)
        mine, to4 = add_parts(near[0], to_chip(near[1], 1), kinds)
        to6, to2 = add_parts(wide[0], to_chip(wide[1], 1), (jnp.bfloat16, jnp.bfloat16))
        sums = [mine, to_chip(to4, 4), to_chip(to6, 6), to_chip(to2, 2)]
    else:
        order = tuple(range(n_chip))
        ((keep, away),) = down((order,), False, chip, core, parts, source, middle, down_w)
        total = (keep + swap(away, "core").astype(jnp.float32)).astype(jnp.bfloat16)
        total = lax.all_to_all(total.reshape(n_chip, rows, features), "chip", 0, 0)
        sums = [jnp.sum(total.astype(jnp.float32), axis=0)]
    moved, stats = finish(sums, gain_row, score_row)
    stats = stats + swap(stats, "blk") if direct else lax.psum(stats, "blk")
    score = stats[1] * lax.rsqrt(stats[0] / D + EPS)
    return (moved.astype(jnp.bfloat16), score)


def solution(mesh):
    n_chip, n_blk = mesh.shape["dp"] // 2, mesh.shape["blk"]
    split = Mesh(mesh.devices.reshape(n_chip, 2, n_blk), ("chip", "core", "blk"))
    dp = ("chip", "core")
    return jax.shard_map(
        functools.partial(shards, n_chip, n_blk),
        mesh=split,
        in_specs=(
            P(dp, None),
            P(dp, "blk", None),
            P(dp, None, "blk", None),
            P(dp, None, None, "blk", None),
            P(dp, None),
            P(dp),
            P(dp, None, None, "blk", None),
            P(dp, None),
            P(),
            P("blk", None),
            P(),
            P("blk", dp),
            P("blk", dp),
            P(dp, "blk"),
            P("blk"),
            P("blk"),
        ),
        out_specs=(P(dp, "blk"), P(dp)),
        check_vma=False,
    )
```

```python
import functools
import math

import jax
import jax.numpy as jnp
from jax import lax
from jax.experimental import pallas as pl
from jax.experimental.pallas import tpu as pltpu
from jax.sharding import Mesh
from jax.sharding import PartitionSpec as P

D = 2048
NEW = 2
NEG = -1e30
EPS = 1e-06
MIB = 1 << 20
ATTENTION_VMEM = 60 * MIB
UNITS_VMEM = 6 * MIB
DOWN_VMEM = 12 * MIB

VMEM = pl.BlockSpec(memory_space=pltpu.VMEM)
SMEM = pl.BlockSpec(memory_space=pltpu.SMEM)
ANY = pl.BlockSpec(memory_space=pl.ANY)


def mm(a, b):
    return jnp.dot(a, b, preferred_element_type=jnp.float32)


def mm_t(a, b):
    return lax.dot_general(a, b, (((1,), (1,)), ((), ())), preferred_element_type=jnp.float32)


def attention_kernel(
    dims,
    table,
    prompt_len,
    tail_len,
    queries,
    new_kv,
    pool,
    tails,
    out_w,
    own_ref,
    send_ref,
    pages,
    tail_buf,
    w_buf,
    q_buf,
    new_buf,
    keys_apart,
    apart,
    tail_keys,
    tail_apart,
    q_wide,
    q_rows,
    new_wide,
    fresh_scores,
    tail_scores,
    scores,
    top,
    total,
    acc,
    attn,
    page_sems,
    tail_sems,
    sems,
):
    rows, heads, groups, width, n_pages, page, conts, tail, pair = dims
    repeat = heads // groups
    step = 2 * groups
    pairs = groups // pair
    stack = repeat * rows
    page_rows = page * step
    chunk_pages = math.gcd(16, n_pages)
    chunk = chunk_pages * page
    chunk_rows = chunk * step
    quad = 8 // NEW
    quads = conts // quad
    quad_keys = quad * tail
    quad_rows = quad_keys * step
    factor = math.log2(math.e) / math.sqrt(width)
    length = prompt_len[0]
    chunks = (length + chunk - 1) // chunk

    def page_copy(logical):
        physical = table[0, logical]
        return pltpu.make_async_copy(
            pool.at[pl.ds(pl.multiple_of(physical * page_rows, page_rows), page_rows), :],
            pages.at[pl.ds(pl.multiple_of(logical * page_rows, page_rows), page_rows), :],
            page_sems.at[logical],
        )

    def tail_copy(index):
        return pltpu.make_async_copy(
            tails.at[pl.ds(index * quad_rows, quad_rows), :],
            tail_buf.at[pl.ds(index * quad_rows, quad_rows), :],
            tail_sems.at[index],
        )

    q_copy = pltpu.make_async_copy(queries, q_buf, sems.at[0])
    new_copy = pltpu.make_async_copy(new_kv, new_buf, sems.at[1])
    w_copy = pltpu.make_async_copy(out_w, w_buf, sems.at[2])
    q_copy.start()
    new_copy.start()
    for index in range(quads):
        tail_copy(index).start()

    @pl.loop(0, chunks * chunk_pages)
    def _(logical):
        page_copy(logical).start()

    w_copy.start()

    block = 256
    tokens = block // step
    to = lax.broadcasted_iota(jnp.int32, (block, block), 0)
    came = lax.broadcasted_iota(jnp.int32, (block, block), 1)
    sort = (came == (to % tokens) * step + to // tokens).astype(jnp.bfloat16)

    def take_apart(buf, start, count, outs, places):
        for two in range(count // (2 * block)):
            x0 = buf[pl.ds(start + two * 2 * block, block), :]
            x1 = buf[pl.ds(start + (two * 2 + 1) * block, block), :]
            y = mm(sort, jnp.concatenate([x0, x1], axis=1)).astype(jnp.bfloat16)
            for side in range(2):
                for j in range(step):
                    kind, g = j // groups, j % groups
                    t = pl.ds(places[kind] + (2 * two + side) * tokens, tokens)
                    lane = (g % pair) * width
                    outs[kind][g // pair, t, lane : lane + width] = y[
                        j * tokens : (j + 1) * tokens, side * width : (side + 1) * width
                    ]

    def blocks(x):
        return [x[:, i * 128 : (i + 1) * 128] for i in range(x.shape[1] // 128)]

    q_copy.wait()
    new_copy.wait()
    q_wide[...] = q_buf[...].astype(jnp.float32)
    new_wide[...] = new_buf[...].astype(jnp.float32)
    if pair > 1:
        q_rows[...] = jnp.zeros_like(q_rows)
    for g in range(groups):
        for r in range(repeat):
            at = (g % pair) * stack + r * rows
            lane = (g % pair) * width
            q_rows[g // pair, at : at + rows, lane : lane + width] = q_wide[
                pl.ds(g * repeat + r, rows, stride=heads), :
            ]

    def fresh(first, n):
        parts = [
            new_wide[pl.ds(first + n * pair + i, rows, stride=step), :] for i in range(pair)
        ]
        return jnp.concatenate(parts, axis=1).astype(jnp.bfloat16)

    row = lax.broadcasted_iota(jnp.int32, (rows, rows), 0)
    key = lax.broadcasted_iota(jnp.int32, (rows, rows), 1)
    fresh_ok = (row // NEW == key // NEW) & (key <= row)
    fresh_ok = jnp.concatenate([fresh_ok] * (pair * repeat), axis=0)
    for n in range(pairs):
        s = jnp.where(fresh_ok, mm_t(q_rows[n].astype(jnp.bfloat16), fresh(0, n)) * factor, NEG)
        fresh_scores[n] = s
        top[n] = jnp.broadcast_to(jnp.max(s, axis=1, keepdims=True), top.shape[1:])

    def quad_places(index):
        starts = [i * rows + index * 8 for i in range(pair * repeat)]
        return [slice(at, at + 8) for at in starts]

    quad_row = lax.broadcasted_iota(jnp.int32, (8, quad_keys), 0)
    quad_key = lax.broadcasted_iota(jnp.int32, (8, quad_keys), 1)
    for index in range(quads):
        tail_copy(index).wait()
    for index in range(quads):
        outs, at = (tail_keys, tail_apart), index * quad_keys
        take_apart(tail_buf, index * quad_rows, quad_rows, outs, (at, at))
        reach = jnp.zeros((8, quad_keys), jnp.int32)
        for c in range(quad):
            reach = jnp.where(
                quad_key // tail == c, tail_len[0, index * quad + c] + c * tail, reach
            )
        ok = (quad_row // NEW == quad_key // tail) & (quad_key < reach)
        ok = jnp.concatenate([ok] * (pair * repeat), axis=0)
        keys = slice(index * quad_keys, (index + 1) * quad_keys)
        for n in range(pairs):
            q = jnp.concatenate([q_rows[n, a, :] for a in quad_places(index)], axis=0)
            s = mm_t(q.astype(jnp.bfloat16), tail_keys[n, keys, :]) * factor
            s = jnp.where(ok, s, NEG)
            tail_scores[n, index] = s
            high = functools.reduce(jnp.maximum, blocks(s))
            for i, a in enumerate(quad_places(index)):
                top[n, a, :] = jnp.maximum(top[n, a, :], high[i * 8 : (i + 1) * 8])

    part = min(256, chunk)
    place = lax.broadcasted_iota(jnp.int32, (8, part), 1)

    @pl.loop(0, chunks)
    def _(index):
        for i in range(chunk_pages):
            page_copy(index * chunk_pages + i).wait()
        first = pl.multiple_of(index * chunk, chunk)
        row = pl.multiple_of(index * chunk_rows, chunk_rows)
        for at in range(0, chunk, part):
            outs, places = (keys_apart, apart), (at, first + at)
            take_apart(pages, row + at * step, part * step, outs, places)
            ok = place[0:1] < length - (index * chunk + at)
            for n in range(pairs):
                q = q_rows[n].astype(jnp.bfloat16)
                s = mm_t(q, keys_apart[n, at : at + part, :]) * factor
                s = jnp.where(ok, s, NEG)
                scores[n, :, pl.ds(first + at, part)] = s
                top[n] = functools.reduce(jnp.maximum, blocks(s), top[n])

    for n in range(pairs):
        high = jnp.broadcast_to(jnp.max(top[n], axis=1, keepdims=True), top.shape[1:])
        top[n] = high
        p = jnp.exp2(fresh_scores[n] - high[:, :rows])
        lane = lax.broadcasted_iota(jnp.int32, total.shape[1:], 1)
        total[n] = jnp.where(lane == 0, jnp.sum(p, axis=1, keepdims=True), 0.0)
        acc[n] = mm(p.astype(jnp.bfloat16), fresh(groups, n))

    def weigh(s, high):
        parts = [jnp.exp2(part - high) for part in blocks(s)]
        return jnp.concatenate(parts, axis=1).astype(jnp.bfloat16), functools.reduce(jnp.add, parts)

    for index in range(quads):
        keys = slice(index * quad_keys, (index + 1) * quad_keys)
        for n in range(pairs):
            high = jnp.concatenate([top[n, a, :] for a in quad_places(index)], axis=0)
            p, added = weigh(tail_scores[n, index], high)
            value = mm(p, tail_apart[n, keys, :])
            for i, a in enumerate(quad_places(index)):
                total[n, a, :] = total[n, a, :] + added[i * 8 : (i + 1) * 8]
                acc[n, a, :] = acc[n, a, :] + value[i * 8 : (i + 1) * 8]

    @pl.loop(0, chunks)
    def _(index):
        first = pl.multiple_of(index * chunk, chunk)
        for n in range(pairs):
            p, added = weigh(scores[n, :, pl.ds(first, chunk)], top[n])
            total[n] = total[n] + added
            acc[n] = acc[n] + mm(p, apart[n, pl.ds(first, chunk), :])

    for g in range(groups):
        at, lane = (g % pair) * stack, (g % pair) * width
        out = acc[g // pair, at : at + stack, lane : lane + width]
        out = out / jnp.sum(total[g // pair, at : at + stack, :], axis=1, keepdims=True)
        out = out.astype(jnp.bfloat16)
        for r in range(repeat):
            head = g * repeat + r
            attn[:, head * width : (head + 1) * width] = out[r * rows : (r + 1) * rows]
    w_copy.wait()
    value = mm(attn[...], w_buf[...])
    own_ref[...] = value
    send_ref[...] = value.astype(jnp.bfloat16)


def attention(queries, new_kv, pool, table, prompt_len, tails, tail_len, out_w):
    rows, heads, width = queries.shape
    n_pages, page, _, groups, _ = pool.shape
    conts, tail = tails.shape[:2]
    step = 2 * groups
    features = out_w.shape[1]
    quads = conts * NEW // 8
    pair = 2 if groups % 2 == 0 else 1
    pairs = groups // pair
    repeat = heads // groups
    stack = pair * repeat * rows
    return pl.pallas_call(
        functools.partial(
            attention_kernel, (rows, heads, groups, width, n_pages, page, conts, tail, pair)
        ),
        out_shape=(
            jax.ShapeDtypeStruct((rows, features), jnp.float32),
            jax.ShapeDtypeStruct((rows, features), jnp.bfloat16),
        ),
        in_specs=[SMEM, SMEM, SMEM, ANY, ANY, ANY, ANY, ANY],
        out_specs=(VMEM, VMEM),
        scratch_shapes=[
            pltpu.VMEM((n_pages * page * step, width), jnp.bfloat16),
            pltpu.VMEM((conts * tail * step, width), jnp.bfloat16),
            pltpu.VMEM(out_w.shape, jnp.bfloat16),
            pltpu.VMEM((rows * heads, width), jnp.bfloat16),
            pltpu.VMEM((rows * step, width), jnp.bfloat16),
            pltpu.VMEM((pairs, n_pages * page, pair * width), jnp.bfloat16),
            pltpu.VMEM((pairs, n_pages * page, pair * width), jnp.bfloat16),
            pltpu.VMEM((pairs, conts * tail, pair * width), jnp.bfloat16),
            pltpu.VMEM((pairs, conts * tail, pair * width), jnp.bfloat16),
            pltpu.VMEM((rows * heads, width), jnp.float32),
            pltpu.VMEM((pairs, stack, pair * width), jnp.float32),
            pltpu.VMEM((rows * step, width), jnp.float32),
            pltpu.VMEM((pairs, stack, rows), jnp.float32),
            pltpu.VMEM((pairs, quads, pair * repeat * 8, 8 // NEW * tail), jnp.float32),
            pltpu.VMEM((pairs, stack, n_pages * page), jnp.float32),
            pltpu.VMEM((pairs, stack, 128), jnp.float32),
            pltpu.VMEM((pairs, stack, 128), jnp.float32),
            pltpu.VMEM((pairs, stack, pair * width), jnp.float32),
            pltpu.VMEM((rows, heads * width), jnp.bfloat16),
            pltpu.SemaphoreType.DMA((n_pages,)),
            pltpu.SemaphoreType.DMA((quads,)),
            pltpu.SemaphoreType.DMA((3,)),
        ],
        compiler_params=pltpu.CompilerParams(vmem_limit_bytes=ATTENTION_VMEM),
        name="attention",
    )(
        table,
        prompt_len,
        tail_len,
        queries.reshape(rows * heads, width),
        new_kv.reshape(rows * step, width),
        pool.reshape(n_pages * page * step, width),
        tails.reshape(conts * tail * step, width),
        out_w,
    )


def norm_kernel(n, block, own, other, gain, *refs):
    normed, middle, whole = refs[n:]
    copies, rows, features = normed.shape
    mid = own[...] + other[...].astype(jnp.float32)
    scale = lax.rsqrt(jnp.mean(mid * mid, axis=1, keepdims=True) + EPS)
    whole[...] = mid
    start = pl.multiple_of(block[0] * features, features)
    part = whole[:, pl.ds(start, features)]
    out = (part * scale * gain[:, pl.ds(start, features)]).astype(jnp.bfloat16)
    for index in range(copies):
        normed[index] = out
    middle[...] = part


def normalize(block, own, other, gain, features, copies, ahead):
    rows = own.shape[0]
    return pl.pallas_call(
        functools.partial(norm_kernel, len(ahead)),
        out_shape=(
            jax.ShapeDtypeStruct((copies, rows, features), jnp.bfloat16),
            jax.ShapeDtypeStruct((rows, features), jnp.float32),
        ),
        in_specs=[SMEM, VMEM, VMEM, VMEM] + [ANY] * len(ahead),
        out_specs=(VMEM, VMEM),
        scratch_shapes=[pltpu.VMEM(own.shape, jnp.float32)],
        compiler_params=pltpu.CompilerParams(vmem_limit_bytes=4 * MIB),
        name="normalize",
    )(block, own, other, gain.astype(jnp.float32).reshape(1, -1), *ahead)


def units_kernel(n, block, *refs):
    pieces, gate_w, up_w, outs, held, sums = refs[:n], *refs[n : n + 2], refs[n + 2 : -2], *refs[-2:]
    at = 0
    for piece in pieces:
        held[at : at + piece.shape[0], :] = piece[...]
        at += piece.shape[0]
    units = gate_w.shape[1]
    sums[:, :units] = mm(held[...], gate_w[...])
    sums[:, units:] = mm(held[...], up_w[...])
    if len(outs) == 1:
        outs[0][...] = sums[...].astype(jnp.bfloat16)
        return
    keep, away = outs[0], outs[1:]
    half, part = at // 2, away[0].shape[0]
    start = pl.multiple_of((1 - block[0]) * half, half)
    for index, out in enumerate(away):
        out[...] = sums[pl.ds(start + index * part, part), :].astype(jnp.bfloat16)
    keep[...] = sums[pl.ds(pl.multiple_of(block[0] * half, half), half), :]


def partial_units(split, block, pieces, gate_w, up_w):
    tokens = sum(piece.shape[0] for piece in pieces)
    features, units = gate_w.shape
    if split:
        out_shape = (
            jax.ShapeDtypeStruct((tokens // 2, 2 * units), jnp.float32),
            *[jax.ShapeDtypeStruct((tokens // 2 // split, 2 * units), jnp.bfloat16)] * split,
        )
    else:
        out_shape = (jax.ShapeDtypeStruct((tokens, 2 * units), jnp.bfloat16),)
    return pl.pallas_call(
        functools.partial(units_kernel, len(pieces)),
        out_shape=out_shape,
        in_specs=[SMEM] + [VMEM] * (len(pieces) + 2),
        out_specs=(VMEM,) * len(out_shape),
        scratch_shapes=[
            pltpu.VMEM((tokens, features), jnp.bfloat16),
            pltpu.VMEM((tokens, 2 * units), jnp.float32),
        ],
        compiler_params=pltpu.CompilerParams(vmem_limit_bytes=UNITS_VMEM),
        cost_estimate=pl.CostEstimate(
            flops=4 * tokens * features * units,
            bytes_accessed=2 * tokens * features + 4 * features * units,
            transcendentals=0,
        ),
        name="gate_up",
    )(block, *pieces, gate_w, up_w)


def hidden_kernel(n, *refs):
    sums, others, out = refs[:n], refs[n:-1], refs[-1]
    units = out.shape[1]
    both = jnp.concatenate([part[...].astype(jnp.float32) for part in sums], axis=0)
    if others:
        both = both + jnp.concatenate([part[...].astype(jnp.float32) for part in others], axis=0)
    gate, up = both[:, :units], both[:, units:]
    out[...] = (gate / (1.0 + jnp.exp(-gate)) * up).astype(jnp.bfloat16)


def hidden_units(sums, others=()):
    tokens, units = sum(part.shape[0] for part in sums), sums[0].shape[1] // 2
    return pl.pallas_call(
        functools.partial(hidden_kernel, len(sums)),
        out_shape=jax.ShapeDtypeStruct((tokens, units), jnp.bfloat16),
        in_specs=[VMEM] * (len(sums) + len(others)),
        out_specs=VMEM,
        compiler_params=pltpu.CompilerParams(vmem_limit_bytes=4 * MIB),
        name="hidden",
    )(*sums, *others)


def down_kernel(orders, flip, n, chip_ref, core_ref, *refs):
    parts, source, middle, down_w = refs[:n], *refs[n : n + 3]
    outs, hidden, term = refs[n + 3 : -2], *refs[-2:]
    tokens, features = term.shape
    rows = middle.shape[0]
    chip, core = chip_ref[0], core_ref[0]
    at = 0
    for part in parts:
        hidden[at : at + part.shape[0], :] = part[...]
        at += part.shape[0]
    slot, local = source[:, 0:1], source[:, 1:2]
    pick = (lax.broadcasted_iota(jnp.int32, (tokens, tokens), 1) == slot).astype(jnp.bfloat16)
    moved = mm(pick, hidden[...]).astype(jnp.bfloat16)
    mine = lax.broadcasted_iota(jnp.int32, (tokens, rows), 1) == local
    mine = mine.astype(jnp.bfloat16)
    high = middle[...].astype(jnp.bfloat16)
    low = (middle[...] - high.astype(jnp.float32)).astype(jnp.bfloat16)
    term[...] = mm(moved, down_w[...]) + (mm(mine, high) + mm(mine, low))
    for order, keep, send in zip(orders, outs[::2], outs[1::2]):
        for index, dest in enumerate(order):
            at = slice(index * rows, (index + 1) * rows)
            dest = dest ^ chip if flip else dest
            start = pl.multiple_of((2 * dest + core) * rows, rows)
            keep[at, :] = term[pl.ds(start, rows), :]
            start = pl.multiple_of((2 * dest + (1 - core)) * rows, rows)
            send[at, :] = term[pl.ds(start, rows), :].astype(jnp.bfloat16)


def down(orders, flip, chip, core, parts, source, middle, down_w):
    tokens = source.shape[0]
    units, features = down_w.shape
    rows = middle.shape[0]
    out_shape = ()
    for order in orders:
        shape = (len(order) * rows, features)
        out_shape += (
            jax.ShapeDtypeStruct(shape, jnp.float32),
            jax.ShapeDtypeStruct(shape, jnp.bfloat16),
        )
    outs = pl.pallas_call(
        functools.partial(down_kernel, orders, flip, len(parts)),
        out_shape=out_shape,
        in_specs=[SMEM, SMEM] + [VMEM] * (len(parts) + 3),
        out_specs=(VMEM,) * len(out_shape),
        scratch_shapes=[
            pltpu.VMEM((tokens, units), jnp.bfloat16),
            pltpu.VMEM((tokens, features), jnp.float32),
        ],
        compiler_params=pltpu.CompilerParams(vmem_limit_bytes=DOWN_VMEM),
        name="down",
    )(chip, core, *parts, source, middle, down_w)
    return list(zip(outs[::2], outs[1::2]))


def pack_kernel(n, *refs):
    pieces, out = refs[:n], refs[-1]
    at = 0
    for piece in pieces:
        out[at : at + piece.shape[0], :] = piece[...]
        at += piece.shape[0]


def pack(pieces, after=()):
    rows = sum(piece.shape[0] for piece in pieces)
    return pl.pallas_call(
        functools.partial(pack_kernel, len(pieces)),
        out_shape=jax.ShapeDtypeStruct((rows, pieces[0].shape[1]), pieces[0].dtype),
        in_specs=[VMEM] * len(pieces) + [ANY] * len(after),
        out_specs=VMEM,
        compiler_params=pltpu.CompilerParams(vmem_limit_bytes=4 * MIB),
        name="pack",
    )(*pieces, *after)


def add_kernel(keep, other, *outs):
    at = 0
    for out in outs:
        to = at + out.shape[0]
        out[...] = (keep[at:to, :] + other[at:to, :].astype(jnp.float32)).astype(out.dtype)
        at = to


def add_parts(keep, other, kinds):
    rows, features = keep.shape
    return pl.pallas_call(
        add_kernel,
        out_shape=tuple(
            jax.ShapeDtypeStruct((rows // len(kinds), features), kind) for kind in kinds
        ),
        in_specs=[VMEM, VMEM],
        out_specs=(VMEM,) * len(kinds),
        compiler_params=pltpu.CompilerParams(vmem_limit_bytes=4 * MIB),
        name="add_parts",
    )(keep, other)


def finish_kernel(n, *refs):
    parts, gain, score, moved, stats = refs[:n], *refs[n:]
    total = functools.reduce(jnp.add, [part[...].astype(jnp.float32) for part in parts])
    moved[...] = total
    weighted = gain[...].astype(jnp.float32) * score[...].astype(jnp.float32)
    lane = lax.broadcasted_iota(jnp.int32, (total.shape[0], 128), 1)
    squares = jnp.sum(total * total, axis=1, keepdims=True)
    terms = jnp.sum(total * weighted, axis=1, keepdims=True)
    stats[...] = jnp.transpose(jnp.where(lane == 0, squares, terms))[:8]


def finish(parts, gain, score):
    rows, features = parts[0].shape
    return pl.pallas_call(
        functools.partial(finish_kernel, len(parts)),
        out_shape=(
            jax.ShapeDtypeStruct((rows, features), jnp.float32),
            jax.ShapeDtypeStruct((8, rows), jnp.float32),
        ),
        in_specs=[VMEM] * (len(parts) + 2),
        out_specs=(VMEM, VMEM),
        compiler_params=pltpu.CompilerParams(vmem_limit_bytes=4 * MIB),
        name="finish",
    )(*parts, gain, score)


def shards(
    n_chip,
    n_blk,
    resid,
    queries,
    new_kv,
    prefix_pool,
    page_table,
    prompt_len,
    tail_pool,
    tail_len,
    migration,
    out_w,
    mlp_gain,
    gate_w,
    up_w,
    down_w,
    final_gain,
    score_w,
):
    rows = resid.shape[0]
    features = gate_w.shape[0]
    chip = lax.axis_index("chip").astype(jnp.int32)
    core = lax.axis_index("core").astype(jnp.int32)
    block = lax.axis_index("blk").astype(jnp.int32)
    direct = n_chip == 8 and n_blk == 2

    def to_chip(value, index):
        return lax.ppermute(value, "chip", [(i, i ^ index) for i in range(n_chip)])

    def swap(value, axis):
        return lax.ppermute(value, axis, [(0, 1), (1, 0)])

    own, send = attention(
        queries, new_kv, prefix_pool, page_table, prompt_len, tail_pool, tail_len, out_w
    )
    if direct:
        own, other = own + resid.astype(jnp.float32), swap(send, "blk")
    else:
        own, other = resid.astype(jnp.float32), lax.psum(send, "blk")
    token = migration[:, None] * NEW + jnp.arange(NEW, dtype=jnp.int32)[None, :]
    token = token.reshape(-1, 1)
    came, inner = token // rows, token % rows
    far, far_core = (came // 2) ^ chip, (came % 2) ^ core
    if direct:
        held = far // 2 % 2
        one = (far_core ^ block) * 4 + held * 2
        two = 8 + (held ^ block) * 4 + far_core * 2
        slot = jnp.where(far % 2 == 0, one, two) + far // 4
    else:
        slot = far_core * n_chip + came // 2
    local = token - (chip * 2 + core) * rows
    source = jnp.concatenate([slot * rows + inner, local], axis=1)
    chip, core, block = (index.reshape(1) for index in (chip, core, block))
    gain_row, score_row = final_gain.reshape(1, -1), score_w.reshape(1, -1)

    normed, middle = normalize(
        block,
        own,
        other,
        mlp_gain,
        features,
        1 if direct else n_chip,
        (chip, core, source, gain_row, score_row),
    )
    if direct:
        piece = normed.reshape(rows, features)
        z2, z3, z1 = (to_chip(piece, index) for index in (4, 6, 2))
        here = [pack([piece, z2]), pack([z1, z3])]
        there = [to_chip(part, 1) for part in here]

        def summed(split, pieces):
            keep, *away = partial_units(split, block, pieces, gate_w, up_w)
            return keep, *[swap(part, "blk") for part in away]

        first = summed(2, here + [swap(part, "core") for part in here])
        near = pack(there, first[1:])
        second, third = summed(1, [near]), summed(1, [swap(near, "core")])
        hidden = hidden_units(first[:1], first[1:])
        parts = [hidden, swap(hidden, "blk")]
        hidden = hidden_units((second[0], third[0]), (second[1], third[1]))
        parts += [hidden, swap(hidden, "blk")]
    else:
        near = lax.all_to_all(normed, "chip", 0, 0).reshape(n_chip * rows, features)
        units = partial_units(0, block, [near, swap(near, "core")], gate_w, up_w)[0]
        parts = [hidden_units([lax.psum(units, "blk")])]
    if direct:
        near, wide = down(
            ((0, 4, 1, 5), (6, 2, 7, 3)), True, chip, core, parts, source, middle, down_w
        )
        kinds = (jnp.float32, jnp.bfloat16)
        near = add_parts(near[0], swap(near[1], "core"), kinds)
        wide = add_parts(wide[0], swap(wide[1], "core"), kinds)
        mine, to4 = add_parts(near[0], to_chip(near[1], 1), kinds)
        to6, to2 = add_parts(wide[0], to_chip(wide[1], 1), (jnp.bfloat16, jnp.bfloat16))
        sums = [mine, to_chip(to4, 4), to_chip(to6, 6), to_chip(to2, 2)]
    else:
        order = tuple(range(n_chip))
        ((keep, away),) = down((order,), False, chip, core, parts, source, middle, down_w)
        total = (keep + swap(away, "core").astype(jnp.float32)).astype(jnp.bfloat16)
        total = lax.all_to_all(total.reshape(n_chip, rows, features), "chip", 0, 0)
        sums = [jnp.sum(total.astype(jnp.float32), axis=0)]
    moved, stats = finish(sums, gain_row, score_row)
    stats = stats + swap(stats, "blk") if direct else lax.psum(stats, "blk")
    score = stats[1] * lax.rsqrt(stats[0] / D + EPS)
    return (moved.astype(jnp.bfloat16), score)


def solution(mesh):
    n_chip, n_blk = mesh.shape["dp"] // 2, mesh.shape["blk"]
    split = Mesh(mesh.devices.reshape(n_chip, 2, n_blk), ("chip", "core", "blk"))
    dp = ("chip", "core")
    return jax.shard_map(
        functools.partial(shards, n_chip, n_blk),
        mesh=split,
        in_specs=(
            P(dp, None),
            P(dp, "blk", None),
            P(dp, None, "blk", None),
            P(dp, None, None, "blk", None),
            P(dp, None),
            P(dp),
            P(dp, None, None, "blk", None),
            P(dp, None),
            P(),
            P("blk", None),
            P(),
            P("blk", dp),
            P("blk", dp),
            P(dp, "blk"),
            P("blk"),
            P("blk"),
        ),
        out_specs=(P(dp, "blk"), P(dp)),
        check_vma=False,
    )
```

```python
import functools
import math

import jax
import jax.numpy as jnp
from jax import lax
from jax.experimental import pallas as pl
from jax.experimental.pallas import tpu as pltpu
from jax.sharding import Mesh
from jax.sharding import PartitionSpec as P

D = 2048
NEW = 2
NEG = -1e30
EPS = 1e-06
MIB = 1 << 20
ATTENTION_VMEM = 60 * MIB
UNITS_VMEM = 6 * MIB
DOWN_VMEM = 12 * MIB

VMEM = pl.BlockSpec(memory_space=pltpu.VMEM)
SMEM = pl.BlockSpec(memory_space=pltpu.SMEM)
ANY = pl.BlockSpec(memory_space=pl.ANY)


def mm(a, b):
    return jnp.dot(a, b, preferred_element_type=jnp.float32)


def mm_t(a, b):
    return lax.dot_general(a, b, (((1,), (1,)), ((), ())), preferred_element_type=jnp.float32)


def attention_kernel(
    dims,
    table,
    prompt_len,
    tail_len,
    queries,
    new_kv,
    pool,
    tails,
    out_w,
    own_ref,
    send_ref,
    pages,
    tail_buf,
    w_buf,
    q_buf,
    new_buf,
    keys_apart,
    apart,
    tail_keys,
    tail_apart,
    q_wide,
    q_rows,
    new_wide,
    fresh_scores,
    tail_scores,
    scores,
    top,
    total,
    acc,
    attn,
    page_sems,
    tail_sems,
    sems,
):
    rows, heads, groups, width, n_pages, page, conts, tail, pair = dims
    repeat = heads // groups
    step = 2 * groups
    pairs = groups // pair
    stack = repeat * rows
    page_rows = page * step
    chunk_pages = math.gcd(16, n_pages)
    chunk = chunk_pages * page
    chunk_rows = chunk * step
    quad = 8 // NEW
    quads = conts // quad
    quad_keys = quad * tail
    quad_rows = quad_keys * step
    factor = math.log2(math.e) / math.sqrt(width)
    length = prompt_len[0]
    chunks = (length + chunk - 1) // chunk

    def page_copy(logical):
        physical = table[0, logical]
        return pltpu.make_async_copy(
            pool.at[pl.ds(pl.multiple_of(physical * page_rows, page_rows), page_rows), :],
            pages.at[pl.ds(pl.multiple_of(logical * page_rows, page_rows), page_rows), :],
            page_sems.at[logical],
        )

    def tail_copy(index):
        return pltpu.make_async_copy(
            tails.at[pl.ds(index * quad_rows, quad_rows), :],
            tail_buf.at[pl.ds(index * quad_rows, quad_rows), :],
            tail_sems.at[index],
        )

    q_copy = pltpu.make_async_copy(queries, q_buf, sems.at[0])
    new_copy = pltpu.make_async_copy(new_kv, new_buf, sems.at[1])
    w_copy = pltpu.make_async_copy(out_w, w_buf, sems.at[2])
    q_copy.start()
    new_copy.start()
    for index in range(quads):
        tail_copy(index).start()

    @pl.loop(0, chunks * chunk_pages)
    def _(logical):
        page_copy(logical).start()

    w_copy.start()

    block = 256
    tokens = block // step
    to = lax.broadcasted_iota(jnp.int32, (block, block), 0)
    came = lax.broadcasted_iota(jnp.int32, (block, block), 1)
    sort = (came == (to % tokens) * step + to // tokens).astype(jnp.bfloat16)

    def take_apart(buf, start, count, outs, places):
        for two in range(count // (2 * block)):
            x0 = buf[pl.ds(start + two * 2 * block, block), :]
            x1 = buf[pl.ds(start + (two * 2 + 1) * block, block), :]
            y = mm(sort, jnp.concatenate([x0, x1], axis=1)).astype(jnp.bfloat16)
            for side in range(2):
                for j in range(step):
                    kind, g = j // groups, j % groups
                    t = pl.ds(places[kind] + (2 * two + side) * tokens, tokens)
                    lane = (g % pair) * width
                    outs[kind][g // pair, t, lane : lane + width] = y[
                        j * tokens : (j + 1) * tokens, side * width : (side + 1) * width
                    ]

    def blocks(x):
        return [x[:, i * 128 : (i + 1) * 128] for i in range(x.shape[1] // 128)]

    q_copy.wait()
    new_copy.wait()
    q_wide[...] = q_buf[...].astype(jnp.float32)
    new_wide[...] = new_buf[...].astype(jnp.float32)
    if pair > 1:
        q_rows[...] = jnp.zeros_like(q_rows)
    for g in range(groups):
        for r in range(repeat):
            at = (g % pair) * stack + r * rows
            lane = (g % pair) * width
            q_rows[g // pair, at : at + rows, lane : lane + width] = q_wide[
                pl.ds(g * repeat + r, rows, stride=heads), :
            ]

    def fresh(first, n):
        parts = [
            new_wide[pl.ds(first + n * pair + i, rows, stride=step), :] for i in range(pair)
        ]
        return jnp.concatenate(parts, axis=1).astype(jnp.bfloat16)

    row = lax.broadcasted_iota(jnp.int32, (rows, rows), 0)
    key = lax.broadcasted_iota(jnp.int32, (rows, rows), 1)
    fresh_ok = (row // NEW == key // NEW) & (key <= row)
    fresh_ok = jnp.concatenate([fresh_ok] * (pair * repeat), axis=0)
    for n in range(pairs):
        s = jnp.where(fresh_ok, mm_t(q_rows[n].astype(jnp.bfloat16), fresh(0, n)) * factor, NEG)
        fresh_scores[n] = s
        top[n] = jnp.broadcast_to(jnp.max(s, axis=1, keepdims=True), top.shape[1:])

    def quad_places(index):
        starts = [i * rows + index * 8 for i in range(pair * repeat)]
        return [slice(at, at + 8) for at in starts]

    quad_row = lax.broadcasted_iota(jnp.int32, (8, quad_keys), 0)
    quad_key = lax.broadcasted_iota(jnp.int32, (8, quad_keys), 1)
    def score_tails(index):
        reach = jnp.zeros((8, quad_keys), jnp.int32)
        for c in range(quad):
            reach = jnp.where(
                quad_key // tail == c, tail_len[0, index * quad + c] + c * tail, reach
            )
        ok = (quad_row // NEW == quad_key // tail) & (quad_key < reach)
        ok = jnp.concatenate([ok] * (pair * repeat), axis=0)
        keys = slice(index * quad_keys, (index + 1) * quad_keys)
        for n in range(pairs):
            q = jnp.concatenate([q_rows[n, a, :] for a in quad_places(index)], axis=0)
            s = mm_t(q.astype(jnp.bfloat16), tail_keys[n, keys, :]) * factor
            s = jnp.where(ok, s, NEG)
            tail_scores[n, index] = s
            high = functools.reduce(jnp.maximum, blocks(s))
            for i, a in enumerate(quad_places(index)):
                top[n, a, :] = jnp.maximum(top[n, a, :], high[i * 8 : (i + 1) * 8])

    for index in range(quads):
        tail_copy(index).wait()
        outs, at = (tail_keys, tail_apart), index * quad_keys
        take_apart(tail_buf, index * quad_rows, quad_rows, outs, (at, at))
        if index:
            score_tails(index - 1)
    score_tails(quads - 1)

    part = min(256, chunk)
    place = lax.broadcasted_iota(jnp.int32, (8, part), 1)

    @pl.loop(0, chunks)
    def _(index):
        for i in range(chunk_pages):
            page_copy(index * chunk_pages + i).wait()
        first = pl.multiple_of(index * chunk, chunk)
        row = pl.multiple_of(index * chunk_rows, chunk_rows)
        for at in range(0, chunk, part):
            outs, places = (keys_apart, apart), (at, first + at)
            take_apart(pages, row + at * step, part * step, outs, places)
            ok = place[0:1] < length - (index * chunk + at)
            for n in range(pairs):
                q = q_rows[n].astype(jnp.bfloat16)
                s = mm_t(q, keys_apart[n, at : at + part, :]) * factor
                s = jnp.where(ok, s, NEG)
                scores[n, :, pl.ds(first + at, part)] = s
                top[n] = functools.reduce(jnp.maximum, blocks(s), top[n])

    for n in range(pairs):
        high = jnp.broadcast_to(jnp.max(top[n], axis=1, keepdims=True), top.shape[1:])
        top[n] = high
        p = jnp.exp2(fresh_scores[n] - high[:, :rows])
        lane = lax.broadcasted_iota(jnp.int32, total.shape[1:], 1)
        total[n] = jnp.where(lane == 0, jnp.sum(p, axis=1, keepdims=True), 0.0)
        acc[n] = mm(p.astype(jnp.bfloat16), fresh(groups, n))

    def weigh(s, high):
        parts = [jnp.exp2(part - high) for part in blocks(s)]
        return jnp.concatenate(parts, axis=1).astype(jnp.bfloat16), functools.reduce(jnp.add, parts)

    for index in range(quads):
        keys = slice(index * quad_keys, (index + 1) * quad_keys)
        for n in range(pairs):
            high = jnp.concatenate([top[n, a, :] for a in quad_places(index)], axis=0)
            p, added = weigh(tail_scores[n, index], high)
            value = mm(p, tail_apart[n, keys, :])
            for i, a in enumerate(quad_places(index)):
                total[n, a, :] = total[n, a, :] + added[i * 8 : (i + 1) * 8]
                acc[n, a, :] = acc[n, a, :] + value[i * 8 : (i + 1) * 8]

    @pl.loop(0, chunks)
    def _(index):
        first = pl.multiple_of(index * chunk, chunk)
        for n in range(pairs):
            p, added = weigh(scores[n, :, pl.ds(first, chunk)], top[n])
            total[n] = total[n] + added
            acc[n] = acc[n] + mm(p, apart[n, pl.ds(first, chunk), :])

    for g in range(groups):
        at, lane = (g % pair) * stack, (g % pair) * width
        out = acc[g // pair, at : at + stack, lane : lane + width]
        out = out / jnp.sum(total[g // pair, at : at + stack, :], axis=1, keepdims=True)
        out = out.astype(jnp.bfloat16)
        for r in range(repeat):
            head = g * repeat + r
            attn[:, head * width : (head + 1) * width] = out[r * rows : (r + 1) * rows]
    w_copy.wait()
    value = mm(attn[...], w_buf[...])
    own_ref[...] = value
    send_ref[...] = value.astype(jnp.bfloat16)


def attention(queries, new_kv, pool, table, prompt_len, tails, tail_len, out_w):
    rows, heads, width = queries.shape
    n_pages, page, _, groups, _ = pool.shape
    conts, tail = tails.shape[:2]
    step = 2 * groups
    features = out_w.shape[1]
    quads = conts * NEW // 8
    pair = 2 if groups % 2 == 0 else 1
    pairs = groups // pair
    repeat = heads // groups
    stack = pair * repeat * rows
    return pl.pallas_call(
        functools.partial(
            attention_kernel, (rows, heads, groups, width, n_pages, page, conts, tail, pair)
        ),
        out_shape=(
            jax.ShapeDtypeStruct((rows, features), jnp.float32),
            jax.ShapeDtypeStruct((rows, features), jnp.bfloat16),
        ),
        in_specs=[SMEM, SMEM, SMEM, ANY, ANY, ANY, ANY, ANY],
        out_specs=(VMEM, VMEM),
        scratch_shapes=[
            pltpu.VMEM((n_pages * page * step, width), jnp.bfloat16),
            pltpu.VMEM((conts * tail * step, width), jnp.bfloat16),
            pltpu.VMEM(out_w.shape, jnp.bfloat16),
            pltpu.VMEM((rows * heads, width), jnp.bfloat16),
            pltpu.VMEM((rows * step, width), jnp.bfloat16),
            pltpu.VMEM((pairs, n_pages * page, pair * width), jnp.bfloat16),
            pltpu.VMEM((pairs, n_pages * page, pair * width), jnp.bfloat16),
            pltpu.VMEM((pairs, conts * tail, pair * width), jnp.bfloat16),
            pltpu.VMEM((pairs, conts * tail, pair * width), jnp.bfloat16),
            pltpu.VMEM((rows * heads, width), jnp.float32),
            pltpu.VMEM((pairs, stack, pair * width), jnp.float32),
            pltpu.VMEM((rows * step, width), jnp.float32),
            pltpu.VMEM((pairs, stack, rows), jnp.float32),
            pltpu.VMEM((pairs, quads, pair * repeat * 8, 8 // NEW * tail), jnp.float32),
            pltpu.VMEM((pairs, stack, n_pages * page), jnp.float32),
            pltpu.VMEM((pairs, stack, 128), jnp.float32),
            pltpu.VMEM((pairs, stack, 128), jnp.float32),
            pltpu.VMEM((pairs, stack, pair * width), jnp.float32),
            pltpu.VMEM((rows, heads * width), jnp.bfloat16),
            pltpu.SemaphoreType.DMA((n_pages,)),
            pltpu.SemaphoreType.DMA((quads,)),
            pltpu.SemaphoreType.DMA((3,)),
        ],
        compiler_params=pltpu.CompilerParams(vmem_limit_bytes=ATTENTION_VMEM),
        name="attention",
    )(
        table,
        prompt_len,
        tail_len,
        queries.reshape(rows * heads, width),
        new_kv.reshape(rows * step, width),
        pool.reshape(n_pages * page * step, width),
        tails.reshape(conts * tail * step, width),
        out_w,
    )


def norm_kernel(n, block, own, other, gain, *refs):
    normed, middle, whole = refs[n:]
    copies, rows, features = normed.shape
    mid = own[...] + other[...].astype(jnp.float32)
    scale = lax.rsqrt(jnp.mean(mid * mid, axis=1, keepdims=True) + EPS)
    whole[...] = mid
    start = pl.multiple_of(block[0] * features, features)
    part = whole[:, pl.ds(start, features)]
    out = (part * scale * gain[:, pl.ds(start, features)]).astype(jnp.bfloat16)
    for index in range(copies):
        normed[index] = out
    middle[...] = part


def normalize(block, own, other, gain, features, copies, ahead):
    rows = own.shape[0]
    return pl.pallas_call(
        functools.partial(norm_kernel, len(ahead)),
        out_shape=(
            jax.ShapeDtypeStruct((copies, rows, features), jnp.bfloat16),
            jax.ShapeDtypeStruct((rows, features), jnp.float32),
        ),
        in_specs=[SMEM, VMEM, VMEM, VMEM] + [ANY] * len(ahead),
        out_specs=(VMEM, VMEM),
        scratch_shapes=[pltpu.VMEM(own.shape, jnp.float32)],
        compiler_params=pltpu.CompilerParams(vmem_limit_bytes=4 * MIB),
        name="normalize",
    )(block, own, other, gain.astype(jnp.float32).reshape(1, -1), *ahead)


def units_kernel(n, block, *refs):
    pieces, gate_w, up_w, outs, held, sums = refs[:n], *refs[n : n + 2], refs[n + 2 : -2], *refs[-2:]
    at = 0
    for piece in pieces:
        held[at : at + piece.shape[0], :] = piece[...]
        at += piece.shape[0]
    units = gate_w.shape[1]
    sums[:, :units] = mm(held[...], gate_w[...])
    sums[:, units:] = mm(held[...], up_w[...])
    if len(outs) == 1:
        outs[0][...] = sums[...].astype(jnp.bfloat16)
        return
    keep, away = outs[0], outs[1:]
    half, part = at // 2, away[0].shape[0]
    start = pl.multiple_of((1 - block[0]) * half, half)
    for index, out in enumerate(away):
        out[...] = sums[pl.ds(start + index * part, part), :].astype(jnp.bfloat16)
    keep[...] = sums[pl.ds(pl.multiple_of(block[0] * half, half), half), :]


def partial_units(split, block, pieces, gate_w, up_w):
    tokens = sum(piece.shape[0] for piece in pieces)
    features, units = gate_w.shape
    if split:
        out_shape = (
            jax.ShapeDtypeStruct((tokens // 2, 2 * units), jnp.float32),
            *[jax.ShapeDtypeStruct((tokens // 2 // split, 2 * units), jnp.bfloat16)] * split,
        )
    else:
        out_shape = (jax.ShapeDtypeStruct((tokens, 2 * units), jnp.bfloat16),)
    return pl.pallas_call(
        functools.partial(units_kernel, len(pieces)),
        out_shape=out_shape,
        in_specs=[SMEM] + [VMEM] * (len(pieces) + 2),
        out_specs=(VMEM,) * len(out_shape),
        scratch_shapes=[
            pltpu.VMEM((tokens, features), jnp.bfloat16),
            pltpu.VMEM((tokens, 2 * units), jnp.float32),
        ],
        compiler_params=pltpu.CompilerParams(vmem_limit_bytes=UNITS_VMEM),
        cost_estimate=pl.CostEstimate(
            flops=4 * tokens * features * units,
            bytes_accessed=2 * tokens * features + 4 * features * units,
            transcendentals=0,
        ),
        name="gate_up",
    )(block, *pieces, gate_w, up_w)


def hidden_kernel(n, *refs):
    sums, others, out = refs[:n], refs[n:-1], refs[-1]
    units = out.shape[1]
    both = jnp.concatenate([part[...].astype(jnp.float32) for part in sums], axis=0)
    if others:
        both = both + jnp.concatenate([part[...].astype(jnp.float32) for part in others], axis=0)
    gate, up = both[:, :units], both[:, units:]
    out[...] = (gate / (1.0 + jnp.exp(-gate)) * up).astype(jnp.bfloat16)


def hidden_units(sums, others=()):
    tokens, units = sum(part.shape[0] for part in sums), sums[0].shape[1] // 2
    return pl.pallas_call(
        functools.partial(hidden_kernel, len(sums)),
        out_shape=jax.ShapeDtypeStruct((tokens, units), jnp.bfloat16),
        in_specs=[VMEM] * (len(sums) + len(others)),
        out_specs=VMEM,
        compiler_params=pltpu.CompilerParams(vmem_limit_bytes=4 * MIB),
        name="hidden",
    )(*sums, *others)


def down_kernel(orders, flip, n, chip_ref, core_ref, *refs):
    parts, source, middle, down_w = refs[:n], *refs[n : n + 3]
    outs, hidden, term = refs[n + 3 : -2], *refs[-2:]
    tokens, features = term.shape
    rows = middle.shape[0]
    chip, core = chip_ref[0], core_ref[0]
    at = 0
    for part in parts:
        hidden[at : at + part.shape[0], :] = part[...]
        at += part.shape[0]
    slot, local = source[:, 0:1], source[:, 1:2]
    pick = (lax.broadcasted_iota(jnp.int32, (tokens, tokens), 1) == slot).astype(jnp.bfloat16)
    moved = mm(pick, hidden[...]).astype(jnp.bfloat16)
    mine = lax.broadcasted_iota(jnp.int32, (tokens, rows), 1) == local
    mine = mine.astype(jnp.bfloat16)
    high = middle[...].astype(jnp.bfloat16)
    low = (middle[...] - high.astype(jnp.float32)).astype(jnp.bfloat16)
    term[...] = mm(moved, down_w[...]) + (mm(mine, high) + mm(mine, low))
    for order, keep, send in zip(orders, outs[::2], outs[1::2]):
        for index, dest in enumerate(order):
            at = slice(index * rows, (index + 1) * rows)
            dest = dest ^ chip if flip else dest
            start = pl.multiple_of((2 * dest + core) * rows, rows)
            keep[at, :] = term[pl.ds(start, rows), :]
            start = pl.multiple_of((2 * dest + (1 - core)) * rows, rows)
            send[at, :] = term[pl.ds(start, rows), :].astype(jnp.bfloat16)


def down(orders, flip, chip, core, parts, source, middle, down_w):
    tokens = source.shape[0]
    units, features = down_w.shape
    rows = middle.shape[0]
    out_shape = ()
    for order in orders:
        shape = (len(order) * rows, features)
        out_shape += (
            jax.ShapeDtypeStruct(shape, jnp.float32),
            jax.ShapeDtypeStruct(shape, jnp.bfloat16),
        )
    outs = pl.pallas_call(
        functools.partial(down_kernel, orders, flip, len(parts)),
        out_shape=out_shape,
        in_specs=[SMEM, SMEM] + [VMEM] * (len(parts) + 3),
        out_specs=(VMEM,) * len(out_shape),
        scratch_shapes=[
            pltpu.VMEM((tokens, units), jnp.bfloat16),
            pltpu.VMEM((tokens, features), jnp.float32),
        ],
        compiler_params=pltpu.CompilerParams(vmem_limit_bytes=DOWN_VMEM),
        name="down",
    )(chip, core, *parts, source, middle, down_w)
    return list(zip(outs[::2], outs[1::2]))


def pack_kernel(n, *refs):
    pieces, out = refs[:n], refs[-1]
    at = 0
    for piece in pieces:
        out[at : at + piece.shape[0], :] = piece[...]
        at += piece.shape[0]


def pack(pieces, after=()):
    rows = sum(piece.shape[0] for piece in pieces)
    return pl.pallas_call(
        functools.partial(pack_kernel, len(pieces)),
        out_shape=jax.ShapeDtypeStruct((rows, pieces[0].shape[1]), pieces[0].dtype),
        in_specs=[VMEM] * len(pieces) + [ANY] * len(after),
        out_specs=VMEM,
        compiler_params=pltpu.CompilerParams(vmem_limit_bytes=4 * MIB),
        name="pack",
    )(*pieces, *after)


def add_kernel(keep, other, *outs):
    at = 0
    for out in outs:
        to = at + out.shape[0]
        out[...] = (keep[at:to, :] + other[at:to, :].astype(jnp.float32)).astype(out.dtype)
        at = to


def add_parts(keep, other, kinds):
    rows, features = keep.shape
    return pl.pallas_call(
        add_kernel,
        out_shape=tuple(
            jax.ShapeDtypeStruct((rows // len(kinds), features), kind) for kind in kinds
        ),
        in_specs=[VMEM, VMEM],
        out_specs=(VMEM,) * len(kinds),
        compiler_params=pltpu.CompilerParams(vmem_limit_bytes=4 * MIB),
        name="add_parts",
    )(keep, other)


def finish_kernel(n, *refs):
    parts, gain, score, moved, stats = refs[:n], *refs[n:]
    total = functools.reduce(jnp.add, [part[...].astype(jnp.float32) for part in parts])
    moved[...] = total
    weighted = gain[...].astype(jnp.float32) * score[...].astype(jnp.float32)
    lane = lax.broadcasted_iota(jnp.int32, (total.shape[0], 128), 1)
    squares = jnp.sum(total * total, axis=1, keepdims=True)
    terms = jnp.sum(total * weighted, axis=1, keepdims=True)
    stats[...] = jnp.transpose(jnp.where(lane == 0, squares, terms))[:8]


def finish(parts, gain, score):
    rows, features = parts[0].shape
    return pl.pallas_call(
        functools.partial(finish_kernel, len(parts)),
        out_shape=(
            jax.ShapeDtypeStruct((rows, features), jnp.float32),
            jax.ShapeDtypeStruct((8, rows), jnp.float32),
        ),
        in_specs=[VMEM] * (len(parts) + 2),
        out_specs=(VMEM, VMEM),
        compiler_params=pltpu.CompilerParams(vmem_limit_bytes=4 * MIB),
        name="finish",
    )(*parts, gain, score)


def shards(
    n_chip,
    n_blk,
    resid,
    queries,
    new_kv,
    prefix_pool,
    page_table,
    prompt_len,
    tail_pool,
    tail_len,
    migration,
    out_w,
    mlp_gain,
    gate_w,
    up_w,
    down_w,
    final_gain,
    score_w,
):
    rows = resid.shape[0]
    features = gate_w.shape[0]
    chip = lax.axis_index("chip").astype(jnp.int32)
    core = lax.axis_index("core").astype(jnp.int32)
    block = lax.axis_index("blk").astype(jnp.int32)
    direct = n_chip == 8 and n_blk == 2

    def to_chip(value, index):
        return lax.ppermute(value, "chip", [(i, i ^ index) for i in range(n_chip)])

    def swap(value, axis):
        return lax.ppermute(value, axis, [(0, 1), (1, 0)])

    own, send = attention(
        queries, new_kv, prefix_pool, page_table, prompt_len, tail_pool, tail_len, out_w
    )
    if direct:
        own, other = own + resid.astype(jnp.float32), swap(send, "blk")
    else:
        own, other = resid.astype(jnp.float32), lax.psum(send, "blk")
    token = migration[:, None] * NEW + jnp.arange(NEW, dtype=jnp.int32)[None, :]
    token = token.reshape(-1, 1)
    came, inner = token // rows, token % rows
    far, far_core = (came // 2) ^ chip, (came % 2) ^ core
    if direct:
        held = far // 2 % 2
        one = (far_core ^ block) * 4 + held * 2
        two = 8 + far_core * 4 + (held ^ block) * 2
        slot = jnp.where(far % 2 == 0, one, two) + far // 4
    else:
        slot = far_core * n_chip + came // 2
    local = token - (chip * 2 + core) * rows
    source = jnp.concatenate([slot * rows + inner, local], axis=1)
    chip, core, block = (index.reshape(1) for index in (chip, core, block))
    gain_row, score_row = final_gain.reshape(1, -1), score_w.reshape(1, -1)

    normed, middle = normalize(
        block,
        own,
        other,
        mlp_gain,
        features,
        1 if direct else n_chip,
        (chip, core, source, gain_row, score_row),
    )
    if direct:
        piece = normed.reshape(rows, features)
        z2, z3, z1 = (to_chip(piece, index) for index in (4, 6, 2))
        here = [pack([piece, z2]), pack([z1, z3])]
        there = [to_chip(part, 1) for part in here]

        def summed(split, pieces):
            keep, *away = partial_units(split, block, pieces, gate_w, up_w)
            return keep, *[swap(part, "blk") for part in away]

        first = summed(2, here + [swap(part, "core") for part in here])
        near = pack(there, first[1:])
        second, third = summed(1, [near]), summed(1, [swap(near, "core")])
        parts = []
        for sums in (first, second, third):
            hidden = hidden_units(sums[:1], sums[1:])
            parts += [hidden, swap(hidden, "blk")]
    else:
        near = lax.all_to_all(normed, "chip", 0, 0).reshape(n_chip * rows, features)
        units = partial_units(0, block, [near, swap(near, "core")], gate_w, up_w)[0]
        parts = [hidden_units([lax.psum(units, "blk")])]
    if direct:
        near, wide = down(
            ((0, 4, 1, 5), (6, 2, 7, 3)), True, chip, core, parts, source, middle, down_w
        )
        kinds = (jnp.float32, jnp.bfloat16)
        near = add_parts(near[0], swap(near[1], "core"), kinds)
        wide = add_parts(wide[0], swap(wide[1], "core"), kinds)
        mine, to4 = add_parts(near[0], to_chip(near[1], 1), kinds)
        to6, to2 = add_parts(wide[0], to_chip(wide[1], 1), (jnp.bfloat16, jnp.bfloat16))
        sums = [mine, to_chip(to4, 4), to_chip(to6, 6), to_chip(to2, 2)]
    else:
        order = tuple(range(n_chip))
        ((keep, away),) = down((order,), False, chip, core, parts, source, middle, down_w)
        total = (keep + swap(away, "core").astype(jnp.float32)).astype(jnp.bfloat16)
        total = lax.all_to_all(total.reshape(n_chip, rows, features), "chip", 0, 0)
        sums = [jnp.sum(total.astype(jnp.float32), axis=0)]
    moved, stats = finish(sums, gain_row, score_row)
    stats = stats + swap(stats, "blk") if direct else lax.psum(stats, "blk")
    score = stats[1] * lax.rsqrt(stats[0] / D + EPS)
    return (moved.astype(jnp.bfloat16), score)


def solution(mesh):
    n_chip, n_blk = mesh.shape["dp"] // 2, mesh.shape["blk"]
    split = Mesh(mesh.devices.reshape(n_chip, 2, n_blk), ("chip", "core", "blk"))
    dp = ("chip", "core")
    return jax.shard_map(
        functools.partial(shards, n_chip, n_blk),
        mesh=split,
        in_specs=(
            P(dp, None),
            P(dp, "blk", None),
            P(dp, None, "blk", None),
            P(dp, None, None, "blk", None),
            P(dp, None),
            P(dp),
            P(dp, None, None, "blk", None),
            P(dp, None),
            P(),
            P("blk", None),
            P(),
            P("blk", dp),
            P("blk", dp),
            P(dp, "blk"),
            P("blk"),
            P("blk"),
        ),
        out_specs=(P(dp, "blk"), P(dp)),
        check_vma=False,
    )
```

```python
import functools
import math

import jax
import jax.numpy as jnp
from jax import lax
from jax.experimental import pallas as pl
from jax.experimental.pallas import tpu as pltpu
from jax.sharding import Mesh
from jax.sharding import PartitionSpec as P

D = 2048
NEW = 2
NEG = -1e30
EPS = 1e-06
MIB = 1 << 20
ATTENTION_VMEM = 60 * MIB
UNITS_VMEM = 6 * MIB
DOWN_VMEM = 12 * MIB

VMEM = pl.BlockSpec(memory_space=pltpu.VMEM)
SMEM = pl.BlockSpec(memory_space=pltpu.SMEM)
ANY = pl.BlockSpec(memory_space=pl.ANY)


def mm(a, b):
    return jnp.dot(a, b, preferred_element_type=jnp.float32)


def mm_t(a, b):
    return lax.dot_general(a, b, (((1,), (1,)), ((), ())), preferred_element_type=jnp.float32)


def attention_kernel(
    dims,
    table,
    prompt_len,
    tail_len,
    queries,
    new_kv,
    pool,
    tails,
    out_w,
    own_ref,
    send_ref,
    pages,
    tail_buf,
    w_buf,
    q_buf,
    new_buf,
    keys_apart,
    apart,
    q_wide,
    q_rows,
    scores,
    top,
    total,
    acc,
    side_top,
    side_total,
    side_acc,
    attn,
    page_sems,
    tail_sems,
    sems,
):
    rows, heads, groups, width, n_pages, page, conts, tail, pair = dims
    repeat = heads // groups
    step = 2 * groups
    pairs = groups // pair
    stack = repeat * rows
    page_rows = page * step
    chunk_pages = math.gcd(16, n_pages)
    chunk = chunk_pages * page
    chunk_rows = chunk * step
    quad = 8 // NEW
    quads = conts // quad
    quad_rows = quad * tail * step
    own_rows = NEW * heads
    few = max(1, 16 // own_rows)
    factor = math.log2(math.e) / math.sqrt(width)
    length = prompt_len[0]
    chunks = (length + chunk - 1) // chunk

    def page_copy(logical):
        physical = table[0, logical]
        return pltpu.make_async_copy(
            pool.at[pl.ds(pl.multiple_of(physical * page_rows, page_rows), page_rows), :],
            pages.at[pl.ds(pl.multiple_of(logical * page_rows, page_rows), page_rows), :],
            page_sems.at[logical],
        )

    def tail_copy(index):
        return pltpu.make_async_copy(
            tails.at[pl.ds(index * quad_rows, quad_rows), :],
            tail_buf.at[pl.ds(index * quad_rows, quad_rows), :],
            tail_sems.at[index],
        )

    q_copy = pltpu.make_async_copy(queries, q_buf, sems.at[0])
    new_copy = pltpu.make_async_copy(
        new_kv, new_buf.at[pl.ds(0, rows * step), :], sems.at[1]
    )
    w_copy = pltpu.make_async_copy(out_w, w_buf, sems.at[2])
    if new_buf.shape[0] > rows * step:
        new_buf[...] = jnp.zeros_like(new_buf)
    q_copy.start()
    new_copy.start()
    for index in range(quads):
        tail_copy(index).start()

    @pl.loop(0, chunks * chunk_pages)
    def _(logical):
        page_copy(logical).start()

    w_copy.start()

    block = 256
    tokens = block // step
    to = lax.broadcasted_iota(jnp.int32, (block, block), 0)
    came = lax.broadcasted_iota(jnp.int32, (block, block), 1)
    sort = (came == (to % tokens) * step + to // tokens).astype(jnp.bfloat16)

    def take_apart(buf, start, count, outs, places):
        for two in range(count // (2 * block)):
            x0 = buf[pl.ds(start + two * 2 * block, block), :]
            x1 = buf[pl.ds(start + (two * 2 + 1) * block, block), :]
            y = mm(sort, jnp.concatenate([x0, x1], axis=1)).astype(jnp.bfloat16)
            for side in range(2):
                for j in range(step):
                    kind, g = j // groups, j % groups
                    t = pl.ds(places[kind] + (2 * two + side) * tokens, tokens)
                    lane = (g % pair) * width
                    outs[kind][g // pair, t, lane : lane + width] = y[
                        j * tokens : (j + 1) * tokens, side * width : (side + 1) * width
                    ]

    def blocks(x):
        return [x[:, i * 128 : (i + 1) * 128] for i in range(x.shape[1] // 128)]

    q_copy.wait()
    new_copy.wait()
    q_wide[...] = q_buf[...].astype(jnp.float32)
    if pair > 1:
        q_rows[...] = jnp.zeros_like(q_rows)
    for g in range(groups):
        for r in range(repeat):
            at = (g % pair) * stack + r * rows
            lane = (g % pair) * width
            q_rows[g // pair, at : at + rows, lane : lane + width] = q_wide[
                pl.ds(g * repeat + r, rows, stride=heads), :
            ]
    top[...] = jnp.full_like(top, NEG)
    total[...] = jnp.zeros_like(total)
    acc[...] = jnp.zeros_like(acc)

    def wide_row(x):
        return jnp.broadcast_to(x, (x.shape[0], 128))

    shape = (rows * heads, new_buf.shape[0])
    row = lax.broadcasted_iota(jnp.int32, shape, 0)
    col = lax.broadcasted_iota(jnp.int32, shape, 1)
    ok = (row // own_rows == col // (NEW * step)) & (col // step <= row // heads)
    ok = ok & (col % step == row % heads // repeat)
    s = jnp.where(ok, mm_t(q_buf[...], new_buf[...]) * factor, NEG)
    high = jnp.max(s, axis=1, keepdims=True)
    p = jnp.exp2(s - high)
    side_top[...] = wide_row(high)
    side_total[...] = wide_row(jnp.sum(p, axis=1, keepdims=True))
    side_acc[...] = mm(pltpu.roll(p, groups, 1).astype(jnp.bfloat16), new_buf[...])

    span = few * tail * step
    shape = (few * own_rows, span)
    row = lax.broadcasted_iota(jnp.int32, shape, 0)
    col = lax.broadcasted_iota(jnp.int32, shape, 1)
    ok = (row // own_rows == col // (tail * step)) & (col % step == row % heads // repeat)
    place = jnp.where(ok, col // step, conts * tail)
    for index in range(conts // few):
        if index * few % quad == 0:
            tail_copy(index * few // quad).wait()
        at = slice(index * few * own_rows, (index + 1) * few * own_rows)
        reach = tail_len[0, index * few]
        for c in range(1, few):
            limit = tail_len[0, index * few + c] + c * tail
            reach = jnp.where(col // (tail * step) == c, limit, reach)
        x = tail_buf[index * span : (index + 1) * span, :]
        s = jnp.where(place < reach, mm_t(q_buf[at, :], x) * factor, NEG)
        old = side_top[at, 0:1]
        high = jnp.maximum(old, jnp.max(s, axis=1, keepdims=True))
        keep = jnp.exp2(old - high)
        p = jnp.exp2(s - high)
        side_top[at, :] = wide_row(high)
        side_total[at, :] = side_total[at, :] * keep + jnp.sum(p, axis=1, keepdims=True)
        value = mm(pltpu.roll(p, groups, 1).astype(jnp.bfloat16), x)
        side_acc[at, :] = side_acc[at, :] * keep + value

    part = min(256, chunk)
    place = lax.broadcasted_iota(jnp.int32, (8, part), 1)

    @pl.loop(0, chunks)
    def _(index):
        for i in range(chunk_pages):
            page_copy(index * chunk_pages + i).wait()
        first = pl.multiple_of(index * chunk, chunk)
        row = pl.multiple_of(index * chunk_rows, chunk_rows)
        for at in range(0, chunk, part):
            outs, places = (keys_apart, apart), (at, first + at)
            take_apart(pages, row + at * step, part * step, outs, places)
            ok = place[0:1] < length - (index * chunk + at)
            for n in range(pairs):
                q = q_rows[n].astype(jnp.bfloat16)
                s = mm_t(q, keys_apart[n, at : at + part, :]) * factor
                s = jnp.where(ok, s, NEG)
                scores[n, :, pl.ds(first + at, part)] = s
                top[n] = functools.reduce(jnp.maximum, blocks(s), top[n])

    for n in range(pairs):
        top[n] = jnp.broadcast_to(jnp.max(top[n], axis=1, keepdims=True), top.shape[1:])

    def weigh(s, high):
        parts = [jnp.exp2(part - high) for part in blocks(s)]
        return jnp.concatenate(parts, axis=1).astype(jnp.bfloat16), functools.reduce(jnp.add, parts)

    @pl.loop(0, chunks)
    def _(index):
        first = pl.multiple_of(index * chunk, chunk)
        for n in range(pairs):
            p, added = weigh(scores[n, :, pl.ds(first, chunk)], top[n])
            total[n] = total[n] + added
            acc[n] = acc[n] + mm(p, apart[n, pl.ds(first, chunk), :])

    for g in range(groups):
        lane = (g % pair) * width
        for r in range(repeat):
            head = g * repeat + r
            at = (g % pair) * stack + r * rows
            at = slice(at, at + rows)
            own = pl.ds(head, rows, stride=heads)
            one, two = top[g // pair, at, :], side_top[own, :]
            high = jnp.maximum(one, two)
            one, two = jnp.exp2(one - high), jnp.exp2(two - high)
            weight = jnp.sum(total[g // pair, at, :], axis=1, keepdims=True)
            weight = weight * one + side_total[own, :] * two
            out = acc[g // pair, at, lane : lane + width] * one[:, :width] + (
                side_acc[own, :] * two[:, :width]
            )
            attn[:, head * width : (head + 1) * width] = (out / weight[:, :width]).astype(
                jnp.bfloat16
            )
    w_copy.wait()
    value = mm(attn[...], w_buf[...])
    own_ref[...] = value
    send_ref[...] = value.astype(jnp.bfloat16)


def attention(queries, new_kv, pool, table, prompt_len, tails, tail_len, out_w):
    rows, heads, width = queries.shape
    n_pages, page, _, groups, _ = pool.shape
    conts, tail = tails.shape[:2]
    step = 2 * groups
    features = out_w.shape[1]
    quads = conts * NEW // 8
    pair = 2 if groups % 2 == 0 else 1
    pairs = groups // pair
    repeat = heads // groups
    stack = pair * repeat * rows
    return pl.pallas_call(
        functools.partial(
            attention_kernel, (rows, heads, groups, width, n_pages, page, conts, tail, pair)
        ),
        out_shape=(
            jax.ShapeDtypeStruct((rows, features), jnp.float32),
            jax.ShapeDtypeStruct((rows, features), jnp.bfloat16),
        ),
        in_specs=[SMEM, SMEM, SMEM, ANY, ANY, ANY, ANY, ANY],
        out_specs=(VMEM, VMEM),
        scratch_shapes=[
            pltpu.VMEM((n_pages * page * step, width), jnp.bfloat16),
            pltpu.VMEM((conts * tail * step, width), jnp.bfloat16),
            pltpu.VMEM(out_w.shape, jnp.bfloat16),
            pltpu.VMEM((rows * heads, width), jnp.bfloat16),
            pltpu.VMEM((max(rows * step, 128), width), jnp.bfloat16),
            pltpu.VMEM((pairs, n_pages * page, pair * width), jnp.bfloat16),
            pltpu.VMEM((pairs, n_pages * page, pair * width), jnp.bfloat16),
            pltpu.VMEM((rows * heads, width), jnp.float32),
            pltpu.VMEM((pairs, stack, pair * width), jnp.float32),
            pltpu.VMEM((pairs, stack, n_pages * page), jnp.float32),
            pltpu.VMEM((pairs, stack, 128), jnp.float32),
            pltpu.VMEM((pairs, stack, 128), jnp.float32),
            pltpu.VMEM((pairs, stack, pair * width), jnp.float32),
            pltpu.VMEM((rows * heads, 128), jnp.float32),
            pltpu.VMEM((rows * heads, 128), jnp.float32),
            pltpu.VMEM((rows * heads, width), jnp.float32),
            pltpu.VMEM((rows, heads * width), jnp.bfloat16),
            pltpu.SemaphoreType.DMA((n_pages,)),
            pltpu.SemaphoreType.DMA((quads,)),
            pltpu.SemaphoreType.DMA((3,)),
        ],
        compiler_params=pltpu.CompilerParams(vmem_limit_bytes=ATTENTION_VMEM),
        name="attention",
    )(
        table,
        prompt_len,
        tail_len,
        queries.reshape(rows * heads, width),
        new_kv.reshape(rows * step, width),
        pool.reshape(n_pages * page * step, width),
        tails.reshape(conts * tail * step, width),
        out_w,
    )


def norm_kernel(n, block, own, other, gain, *refs):
    normed, middle, whole = refs[n:]
    copies, rows, features = normed.shape
    mid = own[...] + other[...].astype(jnp.float32)
    scale = lax.rsqrt(jnp.mean(mid * mid, axis=1, keepdims=True) + EPS)
    whole[...] = mid
    start = pl.multiple_of(block[0] * features, features)
    part = whole[:, pl.ds(start, features)]
    out = (part * scale * gain[:, pl.ds(start, features)]).astype(jnp.bfloat16)
    for index in range(copies):
        normed[index] = out
    middle[...] = part


def normalize(block, own, other, gain, features, copies, ahead):
    rows = own.shape[0]
    return pl.pallas_call(
        functools.partial(norm_kernel, len(ahead)),
        out_shape=(
            jax.ShapeDtypeStruct((copies, rows, features), jnp.bfloat16),
            jax.ShapeDtypeStruct((rows, features), jnp.float32),
        ),
        in_specs=[SMEM, VMEM, VMEM, VMEM] + [ANY] * len(ahead),
        out_specs=(VMEM, VMEM),
        scratch_shapes=[pltpu.VMEM(own.shape, jnp.float32)],
        compiler_params=pltpu.CompilerParams(vmem_limit_bytes=4 * MIB),
        name="normalize",
    )(block, own, other, gain.astype(jnp.float32).reshape(1, -1), *ahead)


def units_kernel(n, block, *refs):
    pieces, gate_w, up_w, outs, held, sums = refs[:n], *refs[n : n + 2], refs[n + 2 : -2], *refs[-2:]
    at = 0
    for piece in pieces:
        held[at : at + piece.shape[0], :] = piece[...]
        at += piece.shape[0]
    units = gate_w.shape[1]
    sums[:, :units] = mm(held[...], gate_w[...])
    sums[:, units:] = mm(held[...], up_w[...])
    if len(outs) == 1:
        outs[0][...] = sums[...].astype(jnp.bfloat16)
        return
    keep, away = outs[0], outs[1:]
    half, part = at // 2, away[0].shape[0]
    start = pl.multiple_of((1 - block[0]) * half, half)
    for index, out in enumerate(away):
        out[...] = sums[pl.ds(start + index * part, part), :].astype(jnp.bfloat16)
    keep[...] = sums[pl.ds(pl.multiple_of(block[0] * half, half), half), :]


def partial_units(split, block, pieces, gate_w, up_w):
    tokens = sum(piece.shape[0] for piece in pieces)
    features, units = gate_w.shape
    if split:
        out_shape = (
            jax.ShapeDtypeStruct((tokens // 2, 2 * units), jnp.float32),
            *[jax.ShapeDtypeStruct((tokens // 2 // split, 2 * units), jnp.bfloat16)] * split,
        )
    else:
        out_shape = (jax.ShapeDtypeStruct((tokens, 2 * units), jnp.bfloat16),)
    return pl.pallas_call(
        functools.partial(units_kernel, len(pieces)),
        out_shape=out_shape,
        in_specs=[SMEM] + [VMEM] * (len(pieces) + 2),
        out_specs=(VMEM,) * len(out_shape),
        scratch_shapes=[
            pltpu.VMEM((tokens, features), jnp.bfloat16),
            pltpu.VMEM((tokens, 2 * units), jnp.float32),
        ],
        compiler_params=pltpu.CompilerParams(vmem_limit_bytes=UNITS_VMEM),
        cost_estimate=pl.CostEstimate(
            flops=4 * tokens * features * units,
            bytes_accessed=2 * tokens * features + 4 * features * units,
            transcendentals=0,
        ),
        name="gate_up",
    )(block, *pieces, gate_w, up_w)


def hidden_kernel(n, *refs):
    sums, others, out = refs[:n], refs[n:-1], refs[-1]
    units = out.shape[1]
    both = jnp.concatenate([part[...].astype(jnp.float32) for part in sums], axis=0)
    if others:
        both = both + jnp.concatenate([part[...].astype(jnp.float32) for part in others], axis=0)
    gate, up = both[:, :units], both[:, units:]
    out[...] = (gate / (1.0 + jnp.exp(-gate)) * up).astype(jnp.bfloat16)


def hidden_units(sums, others=()):
    tokens, units = sum(part.shape[0] for part in sums), sums[0].shape[1] // 2
    return pl.pallas_call(
        functools.partial(hidden_kernel, len(sums)),
        out_shape=jax.ShapeDtypeStruct((tokens, units), jnp.bfloat16),
        in_specs=[VMEM] * (len(sums) + len(others)),
        out_specs=VMEM,
        compiler_params=pltpu.CompilerParams(vmem_limit_bytes=4 * MIB),
        name="hidden",
    )(*sums, *others)


def down_kernel(orders, flip, n, chip_ref, core_ref, *refs):
    parts, source, middle, down_w = refs[:n], *refs[n : n + 3]
    outs, hidden, term = refs[n + 3 : -2], *refs[-2:]
    tokens, features = term.shape
    rows = middle.shape[0]
    chip, core = chip_ref[0], core_ref[0]
    at = 0
    for part in parts:
        hidden[at : at + part.shape[0], :] = part[...]
        at += part.shape[0]
    slot, local = source[:, 0:1], source[:, 1:2]
    pick = (lax.broadcasted_iota(jnp.int32, (tokens, tokens), 1) == slot).astype(jnp.bfloat16)
    moved = mm(pick, hidden[...]).astype(jnp.bfloat16)
    mine = lax.broadcasted_iota(jnp.int32, (tokens, rows), 1) == local
    mine = mine.astype(jnp.bfloat16)
    high = middle[...].astype(jnp.bfloat16)
    low = (middle[...] - high.astype(jnp.float32)).astype(jnp.bfloat16)
    term[...] = mm(moved, down_w[...]) + (mm(mine, high) + mm(mine, low))
    for order, keep, send in zip(orders, outs[::2], outs[1::2]):
        for index, dest in enumerate(order):
            at = slice(index * rows, (index + 1) * rows)
            dest = dest ^ chip if flip else dest
            start = pl.multiple_of((2 * dest + core) * rows, rows)
            keep[at, :] = term[pl.ds(start, rows), :]
            start = pl.multiple_of((2 * dest + (1 - core)) * rows, rows)
            send[at, :] = term[pl.ds(start, rows), :].astype(jnp.bfloat16)


def down(orders, flip, chip, core, parts, source, middle, down_w):
    tokens = source.shape[0]
    units, features = down_w.shape
    rows = middle.shape[0]
    out_shape = ()
    for order in orders:
        shape = (len(order) * rows, features)
        out_shape += (
            jax.ShapeDtypeStruct(shape, jnp.float32),
            jax.ShapeDtypeStruct(shape, jnp.bfloat16),
        )
    outs = pl.pallas_call(
        functools.partial(down_kernel, orders, flip, len(parts)),
        out_shape=out_shape,
        in_specs=[SMEM, SMEM] + [VMEM] * (len(parts) + 3),
        out_specs=(VMEM,) * len(out_shape),
        scratch_shapes=[
            pltpu.VMEM((tokens, units), jnp.bfloat16),
            pltpu.VMEM((tokens, features), jnp.float32),
        ],
        compiler_params=pltpu.CompilerParams(vmem_limit_bytes=DOWN_VMEM),
        name="down",
    )(chip, core, *parts, source, middle, down_w)
    return list(zip(outs[::2], outs[1::2]))


def pack_kernel(n, *refs):
    pieces, out = refs[:n], refs[-1]
    at = 0
    for piece in pieces:
        out[at : at + piece.shape[0], :] = piece[...]
        at += piece.shape[0]


def pack(pieces, after=()):
    rows = sum(piece.shape[0] for piece in pieces)
    return pl.pallas_call(
        functools.partial(pack_kernel, len(pieces)),
        out_shape=jax.ShapeDtypeStruct((rows, pieces[0].shape[1]), pieces[0].dtype),
        in_specs=[VMEM] * len(pieces) + [ANY] * len(after),
        out_specs=VMEM,
        compiler_params=pltpu.CompilerParams(vmem_limit_bytes=4 * MIB),
        name="pack",
    )(*pieces, *after)


def add_kernel(keep, other, *outs):
    at = 0
    for out in outs:
        to = at + out.shape[0]
        out[...] = (keep[at:to, :] + other[at:to, :].astype(jnp.float32)).astype(out.dtype)
        at = to


def add_parts(keep, other, kinds):
    rows, features = keep.shape
    return pl.pallas_call(
        add_kernel,
        out_shape=tuple(
            jax.ShapeDtypeStruct((rows // len(kinds), features), kind) for kind in kinds
        ),
        in_specs=[VMEM, VMEM],
        out_specs=(VMEM,) * len(kinds),
        compiler_params=pltpu.CompilerParams(vmem_limit_bytes=4 * MIB),
        name="add_parts",
    )(keep, other)


def finish_kernel(n, *refs):
    parts, gain, score, moved, stats = refs[:n], *refs[n:]
    total = functools.reduce(jnp.add, [part[...].astype(jnp.float32) for part in parts])
    moved[...] = total
    weighted = gain[...].astype(jnp.float32) * score[...].astype(jnp.float32)
    lane = lax.broadcasted_iota(jnp.int32, (total.shape[0], 128), 1)
    squares = jnp.sum(total * total, axis=1, keepdims=True)
    terms = jnp.sum(total * weighted, axis=1, keepdims=True)
    stats[...] = jnp.transpose(jnp.where(lane == 0, squares, terms))[:8]


def finish(parts, gain, score):
    rows, features = parts[0].shape
    return pl.pallas_call(
        functools.partial(finish_kernel, len(parts)),
        out_shape=(
            jax.ShapeDtypeStruct((rows, features), jnp.float32),
            jax.ShapeDtypeStruct((8, rows), jnp.float32),
        ),
        in_specs=[VMEM] * (len(parts) + 2),
        out_specs=(VMEM, VMEM),
        compiler_params=pltpu.CompilerParams(vmem_limit_bytes=4 * MIB),
        name="finish",
    )(*parts, gain, score)


def shards(
    n_chip,
    n_blk,
    resid,
    queries,
    new_kv,
    prefix_pool,
    page_table,
    prompt_len,
    tail_pool,
    tail_len,
    migration,
    out_w,
    mlp_gain,
    gate_w,
    up_w,
    down_w,
    final_gain,
    score_w,
):
    rows = resid.shape[0]
    features = gate_w.shape[0]
    chip = lax.axis_index("chip").astype(jnp.int32)
    core = lax.axis_index("core").astype(jnp.int32)
    block = lax.axis_index("blk").astype(jnp.int32)
    direct = n_chip == 8 and n_blk == 2

    def to_chip(value, index):
        return lax.ppermute(value, "chip", [(i, i ^ index) for i in range(n_chip)])

    def swap(value, axis):
        return lax.ppermute(value, axis, [(0, 1), (1, 0)])

    own, send = attention(
        queries, new_kv, prefix_pool, page_table, prompt_len, tail_pool, tail_len, out_w
    )
    if direct:
        own, other = own + resid.astype(jnp.float32), swap(send, "blk")
    else:
        own, other = resid.astype(jnp.float32), lax.psum(send, "blk")
    token = migration[:, None] * NEW + jnp.arange(NEW, dtype=jnp.int32)[None, :]
    token = token.reshape(-1, 1)
    came, inner = token // rows, token % rows
    far, far_core = (came // 2) ^ chip, (came % 2) ^ core
    if direct:
        held = far // 2 % 2
        one = (far_core ^ block) * 4 + held * 2
        two = 8 + far_core * 4 + (held ^ block) * 2
        slot = jnp.where(far % 2 == 0, one, two) + far // 4
    else:
        slot = far_core * n_chip + came // 2
    local = token - (chip * 2 + core) * rows
    source = jnp.concatenate([slot * rows + inner, local], axis=1)
    chip, core, block = (index.reshape(1) for index in (chip, core, block))
    gain_row, score_row = final_gain.reshape(1, -1), score_w.reshape(1, -1)

    normed, middle = normalize(
        block,
        own,
        other,
        mlp_gain,
        features,
        1 if direct else n_chip,
        (chip, core, source, gain_row, score_row),
    )
    if direct:
        piece = normed.reshape(rows, features)
        z2, z3, z1 = (to_chip(piece, index) for index in (4, 6, 2))
        here = [pack([piece, z2]), pack([z1, z3])]
        there = [to_chip(part, 1) for part in here]

        def summed(split, pieces):
            keep, *away = partial_units(split, block, pieces, gate_w, up_w)
            return keep, *[swap(part, "blk") for part in away]

        first = summed(2, here + [swap(part, "core") for part in here])
        near = pack(there, first[1:])
        second, third = summed(1, [near]), summed(1, [swap(near, "core")])
        parts = []
        for sums in (first, second, third):
            hidden = hidden_units(sums[:1], sums[1:])
            parts += [hidden, swap(hidden, "blk")]
    else:
        near = lax.all_to_all(normed, "chip", 0, 0).reshape(n_chip * rows, features)
        units = partial_units(0, block, [near, swap(near, "core")], gate_w, up_w)[0]
        parts = [hidden_units([lax.psum(units, "blk")])]
    if direct:
        near, wide = down(
            ((0, 4, 1, 5), (6, 2, 7, 3)), True, chip, core, parts, source, middle, down_w
        )
        kinds = (jnp.float32, jnp.bfloat16)
        near = add_parts(near[0], swap(near[1], "core"), kinds)
        wide = add_parts(wide[0], swap(wide[1], "core"), kinds)
        mine, to4 = add_parts(near[0], to_chip(near[1], 1), kinds)
        to6, to2 = add_parts(wide[0], to_chip(wide[1], 1), (jnp.bfloat16, jnp.bfloat16))
        sums = [mine, to_chip(to4, 4), to_chip(to6, 6), to_chip(to2, 2)]
    else:
        order = tuple(range(n_chip))
        ((keep, away),) = down((order,), False, chip, core, parts, source, middle, down_w)
        total = (keep + swap(away, "core").astype(jnp.float32)).astype(jnp.bfloat16)
        total = lax.all_to_all(total.reshape(n_chip, rows, features), "chip", 0, 0)
        sums = [jnp.sum(total.astype(jnp.float32), axis=0)]
    moved, stats = finish(sums, gain_row, score_row)
    stats = stats + swap(stats, "blk") if direct else lax.psum(stats, "blk")
    score = stats[1] * lax.rsqrt(stats[0] / D + EPS)
    return (moved.astype(jnp.bfloat16), score)


def solution(mesh):
    n_chip, n_blk = mesh.shape["dp"] // 2, mesh.shape["blk"]
    split = Mesh(mesh.devices.reshape(n_chip, 2, n_blk), ("chip", "core", "blk"))
    dp = ("chip", "core")
    return jax.shard_map(
        functools.partial(shards, n_chip, n_blk),
        mesh=split,
        in_specs=(
            P(dp, None),
            P(dp, "blk", None),
            P(dp, None, "blk", None),
            P(dp, None, None, "blk", None),
            P(dp, None),
            P(dp),
            P(dp, None, None, "blk", None),
            P(dp, None),
            P(),
            P("blk", None),
            P(),
            P("blk", dp),
            P("blk", dp),
            P(dp, "blk"),
            P("blk"),
            P("blk"),
        ),
        out_specs=(P(dp, "blk"), P(dp)),
        check_vma=False,
    )
```

```python
import functools
import math

import jax
import jax.numpy as jnp
from jax import lax
from jax.experimental import pallas as pl
from jax.experimental.pallas import tpu as pltpu
from jax.sharding import Mesh
from jax.sharding import PartitionSpec as P

D = 2048
NEW = 2
NEG = -1e30
EPS = 1e-06
MIB = 1 << 20
ATTENTION_VMEM = 60 * MIB
UNITS_VMEM = 6 * MIB
DOWN_VMEM = 12 * MIB

VMEM = pl.BlockSpec(memory_space=pltpu.VMEM)
SMEM = pl.BlockSpec(memory_space=pltpu.SMEM)
ANY = pl.BlockSpec(memory_space=pl.ANY)


def mm(a, b):
    return jnp.dot(a, b, preferred_element_type=jnp.float32)


def mm_t(a, b):
    return lax.dot_general(a, b, (((1,), (1,)), ((), ())), preferred_element_type=jnp.float32)


def attention_kernel(
    dims,
    table,
    prompt_len,
    tail_len,
    queries,
    new_kv,
    pool,
    tails,
    out_w,
    own_ref,
    send_ref,
    pages,
    tail_buf,
    w_buf,
    q_buf,
    new_buf,
    keys_apart,
    apart,
    tail_keys,
    tail_apart,
    q_wide,
    q_rows,
    q_pairs,
    new_wide,
    fresh_scores,
    tail_scores,
    scores,
    top,
    total,
    acc,
    attn,
    page_sems,
    tail_sems,
    sems,
):
    rows, heads, groups, width, n_pages, page, conts, tail, pair = dims
    repeat = heads // groups
    step = 2 * groups
    pairs = groups // pair
    stack = repeat * rows
    page_rows = page * step
    chunk_pages = math.gcd(16, n_pages)
    chunk = chunk_pages * page
    chunk_rows = chunk * step
    quad = 8 // NEW
    quads = conts // quad
    quad_keys = quad * tail
    quad_rows = quad_keys * step
    factor = math.log2(math.e) / math.sqrt(width)
    length = prompt_len[0]
    chunks = (length + chunk - 1) // chunk

    def page_copy(logical):
        physical = table[0, logical]
        return pltpu.make_async_copy(
            pool.at[pl.ds(pl.multiple_of(physical * page_rows, page_rows), page_rows), :],
            pages.at[pl.ds(pl.multiple_of(logical * page_rows, page_rows), page_rows), :],
            page_sems.at[logical],
        )

    def tail_copy(index):
        return pltpu.make_async_copy(
            tails.at[pl.ds(index * quad_rows, quad_rows), :],
            tail_buf.at[pl.ds(index * quad_rows, quad_rows), :],
            tail_sems.at[index],
        )

    q_copy = pltpu.make_async_copy(queries, q_buf, sems.at[0])
    new_copy = pltpu.make_async_copy(new_kv, new_buf, sems.at[1])
    w_copy = pltpu.make_async_copy(out_w, w_buf, sems.at[2])
    q_copy.start()
    new_copy.start()
    for index in range(quads):
        tail_copy(index).start()

    @pl.loop(0, chunks * chunk_pages)
    def _(logical):
        page_copy(logical).start()

    w_copy.start()

    block = 256
    tokens = block // step
    to = lax.broadcasted_iota(jnp.int32, (block, block), 0)
    came = lax.broadcasted_iota(jnp.int32, (block, block), 1)
    sort = (came == (to % tokens) * step + to // tokens).astype(jnp.bfloat16)

    def take_apart(buf, start, count, outs, places):
        for two in range(count // (2 * block)):
            x0 = buf[pl.ds(start + two * 2 * block, block), :]
            x1 = buf[pl.ds(start + (two * 2 + 1) * block, block), :]
            y = mm(sort, jnp.concatenate([x0, x1], axis=1)).astype(jnp.bfloat16)
            for side in range(2):
                for j in range(step):
                    kind, g = j // groups, j % groups
                    t = pl.ds(places[kind] + (2 * two + side) * tokens, tokens)
                    lane = (g % pair) * width
                    outs[kind][g // pair, t, lane : lane + width] = y[
                        j * tokens : (j + 1) * tokens, side * width : (side + 1) * width
                    ]

    def blocks(x):
        return [x[:, i * 128 : (i + 1) * 128] for i in range(x.shape[1] // 128)]

    q_copy.wait()
    new_copy.wait()
    q_wide[...] = q_buf[...].astype(jnp.float32)
    new_wide[...] = new_buf[...].astype(jnp.float32)
    if pair > 1:
        q_rows[...] = jnp.zeros_like(q_rows)
    for g in range(groups):
        for r in range(repeat):
            at = (g % pair) * stack + r * rows
            lane = (g % pair) * width
            q_rows[g // pair, at : at + rows, lane : lane + width] = q_wide[
                pl.ds(g * repeat + r, rows, stride=heads), :
            ]

    q_pairs[...] = q_rows[...].astype(jnp.bfloat16)

    def fresh(first, n):
        parts = [
            new_wide[pl.ds(first + n * pair + i, rows, stride=step), :] for i in range(pair)
        ]
        return jnp.concatenate(parts, axis=1).astype(jnp.bfloat16)

    row = lax.broadcasted_iota(jnp.int32, (rows, rows), 0)
    key = lax.broadcasted_iota(jnp.int32, (rows, rows), 1)
    fresh_ok = (row // NEW == key // NEW) & (key <= row)
    fresh_ok = jnp.concatenate([fresh_ok] * (pair * repeat), axis=0)
    for n in range(pairs):
        s = jnp.where(fresh_ok, mm_t(q_pairs[n], fresh(0, n)) * factor, NEG)
        fresh_scores[n] = s
        top[n] = jnp.broadcast_to(jnp.max(s, axis=1, keepdims=True), top.shape[1:])

    def quad_places(index):
        starts = [i * rows + index * 8 for i in range(pair * repeat)]
        return [slice(at, at + 8) for at in starts]

    quad_row = lax.broadcasted_iota(jnp.int32, (8, quad_keys), 0)
    quad_key = lax.broadcasted_iota(jnp.int32, (8, quad_keys), 1)
    for index in range(quads):
        tail_copy(index).wait()
    for index in range(quads):
        outs, at = (tail_keys, tail_apart), index * quad_keys
        take_apart(tail_buf, index * quad_rows, quad_rows, outs, (at, at))
        reach = jnp.zeros((8, quad_keys), jnp.int32)
        for c in range(quad):
            reach = jnp.where(
                quad_key // tail == c, tail_len[0, index * quad + c] + c * tail, reach
            )
        ok = (quad_row // NEW == quad_key // tail) & (quad_key < reach)
        ok = jnp.concatenate([ok] * (pair * repeat), axis=0)
        keys = slice(index * quad_keys, (index + 1) * quad_keys)
        for n in range(pairs):
            q = jnp.concatenate([q_rows[n, a, :] for a in quad_places(index)], axis=0)
            s = mm_t(q.astype(jnp.bfloat16), tail_keys[n, keys, :]) * factor
            s = jnp.where(ok, s, NEG)
            tail_scores[n, index] = s
            high = functools.reduce(jnp.maximum, blocks(s))
            for i, a in enumerate(quad_places(index)):
                top[n, a, :] = jnp.maximum(top[n, a, :], high[i * 8 : (i + 1) * 8])

    part = min(256, chunk)
    place = lax.broadcasted_iota(jnp.int32, (8, part), 1)

    @pl.loop(0, chunks)
    def _(index):
        for i in range(chunk_pages):
            page_copy(index * chunk_pages + i).wait()
        first = pl.multiple_of(index * chunk, chunk)
        row = pl.multiple_of(index * chunk_rows, chunk_rows)
        for at in range(0, chunk, part):
            outs, places = (keys_apart, apart), (at, first + at)
            take_apart(pages, row + at * step, part * step, outs, places)
            ok = place[0:1] < length - (index * chunk + at)
            for n in range(pairs):
                s = mm_t(q_pairs[n], keys_apart[n, at : at + part, :]) * factor
                s = jnp.where(ok, s, NEG)
                scores[n, :, pl.ds(first + at, part)] = s
                top[n] = functools.reduce(jnp.maximum, blocks(s), top[n])

    for n in range(pairs):
        high = jnp.broadcast_to(jnp.max(top[n], axis=1, keepdims=True), top.shape[1:])
        top[n] = high
        p = jnp.exp2(fresh_scores[n] - high[:, :rows])
        lane = lax.broadcasted_iota(jnp.int32, total.shape[1:], 1)
        total[n] = jnp.where(lane == 0, jnp.sum(p, axis=1, keepdims=True), 0.0)
        acc[n] = mm(p.astype(jnp.bfloat16), fresh(groups, n))

    def weigh(s, high):
        parts = [jnp.exp2(part - high) for part in blocks(s)]
        return jnp.concatenate(parts, axis=1).astype(jnp.bfloat16), functools.reduce(jnp.add, parts)

    for index in range(quads):
        keys = slice(index * quad_keys, (index + 1) * quad_keys)
        for n in range(pairs):
            high = jnp.concatenate([top[n, a, :] for a in quad_places(index)], axis=0)
            p, added = weigh(tail_scores[n, index], high)
            value = mm(p, tail_apart[n, keys, :])
            for i, a in enumerate(quad_places(index)):
                total[n, a, :] = total[n, a, :] + added[i * 8 : (i + 1) * 8]
                acc[n, a, :] = acc[n, a, :] + value[i * 8 : (i + 1) * 8]

    @pl.loop(0, chunks)
    def _(index):
        first = pl.multiple_of(index * chunk, chunk)
        for n in range(pairs):
            p, added = weigh(scores[n, :, pl.ds(first, chunk)], top[n])
            total[n] = total[n] + added
            acc[n] = acc[n] + mm(p, apart[n, pl.ds(first, chunk), :])

    for g in range(groups):
        at, lane = (g % pair) * stack, (g % pair) * width
        out = acc[g // pair, at : at + stack, lane : lane + width]
        out = out / jnp.sum(total[g // pair, at : at + stack, :], axis=1, keepdims=True)
        out = out.astype(jnp.bfloat16)
        for r in range(repeat):
            head = g * repeat + r
            attn[:, head * width : (head + 1) * width] = out[r * rows : (r + 1) * rows]
    w_copy.wait()
    value = mm(attn[...], w_buf[...])
    own_ref[...] = value
    send_ref[...] = value.astype(jnp.bfloat16)


def attention(queries, new_kv, pool, table, prompt_len, tails, tail_len, out_w):
    rows, heads, width = queries.shape
    n_pages, page, _, groups, _ = pool.shape
    conts, tail = tails.shape[:2]
    step = 2 * groups
    features = out_w.shape[1]
    quads = conts * NEW // 8
    pair = 2 if groups % 2 == 0 else 1
    pairs = groups // pair
    repeat = heads // groups
    stack = pair * repeat * rows
    return pl.pallas_call(
        functools.partial(
            attention_kernel, (rows, heads, groups, width, n_pages, page, conts, tail, pair)
        ),
        out_shape=(
            jax.ShapeDtypeStruct((rows, features), jnp.float32),
            jax.ShapeDtypeStruct((rows, features), jnp.bfloat16),
        ),
        in_specs=[SMEM, SMEM, SMEM, ANY, ANY, ANY, ANY, ANY],
        out_specs=(VMEM, VMEM),
        scratch_shapes=[
            pltpu.VMEM((n_pages * page * step, width), jnp.bfloat16),
            pltpu.VMEM((conts * tail * step, width), jnp.bfloat16),
            pltpu.VMEM(out_w.shape, jnp.bfloat16),
            pltpu.VMEM((rows * heads, width), jnp.bfloat16),
            pltpu.VMEM((rows * step, width), jnp.bfloat16),
            pltpu.VMEM((pairs, n_pages * page, pair * width), jnp.bfloat16),
            pltpu.VMEM((pairs, n_pages * page, pair * width), jnp.bfloat16),
            pltpu.VMEM((pairs, conts * tail, pair * width), jnp.bfloat16),
            pltpu.VMEM((pairs, conts * tail, pair * width), jnp.bfloat16),
            pltpu.VMEM((rows * heads, width), jnp.float32),
            pltpu.VMEM((pairs, stack, pair * width), jnp.float32),
            pltpu.VMEM((pairs, stack, pair * width), jnp.bfloat16),
            pltpu.VMEM((rows * step, width), jnp.float32),
            pltpu.VMEM((pairs, stack, rows), jnp.float32),
            pltpu.VMEM((pairs, quads, pair * repeat * 8, 8 // NEW * tail), jnp.float32),
            pltpu.VMEM((pairs, stack, n_pages * page), jnp.float32),
            pltpu.VMEM((pairs, stack, 128), jnp.float32),
            pltpu.VMEM((pairs, stack, 128), jnp.float32),
            pltpu.VMEM((pairs, stack, pair * width), jnp.float32),
            pltpu.VMEM((rows, heads * width), jnp.bfloat16),
            pltpu.SemaphoreType.DMA((n_pages,)),
            pltpu.SemaphoreType.DMA((quads,)),
            pltpu.SemaphoreType.DMA((3,)),
        ],
        compiler_params=pltpu.CompilerParams(vmem_limit_bytes=ATTENTION_VMEM),
        name="attention",
    )(
        table,
        prompt_len,
        tail_len,
        queries.reshape(rows * heads, width),
        new_kv.reshape(rows * step, width),
        pool.reshape(n_pages * page * step, width),
        tails.reshape(conts * tail * step, width),
        out_w,
    )


def norm_kernel(n, block, own, other, gain, *refs):
    normed, middle, whole = refs[n:]
    copies, rows, features = normed.shape
    mid = own[...] + other[...].astype(jnp.float32)
    scale = lax.rsqrt(jnp.mean(mid * mid, axis=1, keepdims=True) + EPS)
    whole[...] = mid
    start = pl.multiple_of(block[0] * features, features)
    part = whole[:, pl.ds(start, features)]
    out = (part * scale * gain[:, pl.ds(start, features)]).astype(jnp.bfloat16)
    for index in range(copies):
        normed[index] = out
    middle[...] = part


def normalize(block, own, other, gain, features, copies, ahead):
    rows = own.shape[0]
    return pl.pallas_call(
        functools.partial(norm_kernel, len(ahead)),
        out_shape=(
            jax.ShapeDtypeStruct((copies, rows, features), jnp.bfloat16),
            jax.ShapeDtypeStruct((rows, features), jnp.float32),
        ),
        in_specs=[SMEM, VMEM, VMEM, VMEM] + [ANY] * len(ahead),
        out_specs=(VMEM, VMEM),
        scratch_shapes=[pltpu.VMEM(own.shape, jnp.float32)],
        compiler_params=pltpu.CompilerParams(vmem_limit_bytes=4 * MIB),
        name="normalize",
    )(block, own, other, gain.astype(jnp.float32).reshape(1, -1), *ahead)


def units_kernel(n, block, *refs):
    pieces, gate_w, up_w, outs, held, sums = refs[:n], *refs[n : n + 2], refs[n + 2 : -2], *refs[-2:]
    at = 0
    for piece in pieces:
        held[at : at + piece.shape[0], :] = piece[...]
        at += piece.shape[0]
    units = gate_w.shape[1]
    sums[:, :units] = mm(held[...], gate_w[...])
    sums[:, units:] = mm(held[...], up_w[...])
    if len(outs) == 1:
        outs[0][...] = sums[...].astype(jnp.bfloat16)
        return
    keep, away = outs[0], outs[1:]
    half, part = at // 2, away[0].shape[0]
    start = pl.multiple_of((1 - block[0]) * half, half)
    for index, out in enumerate(away):
        out[...] = sums[pl.ds(start + index * part, part), :].astype(jnp.bfloat16)
    keep[...] = sums[pl.ds(pl.multiple_of(block[0] * half, half), half), :]


def partial_units(split, block, pieces, gate_w, up_w):
    tokens = sum(piece.shape[0] for piece in pieces)
    features, units = gate_w.shape
    if split:
        out_shape = (
            jax.ShapeDtypeStruct((tokens // 2, 2 * units), jnp.float32),
            *[jax.ShapeDtypeStruct((tokens // 2 // split, 2 * units), jnp.bfloat16)] * split,
        )
    else:
        out_shape = (jax.ShapeDtypeStruct((tokens, 2 * units), jnp.bfloat16),)
    return pl.pallas_call(
        functools.partial(units_kernel, len(pieces)),
        out_shape=out_shape,
        in_specs=[SMEM] + [VMEM] * (len(pieces) + 2),
        out_specs=(VMEM,) * len(out_shape),
        scratch_shapes=[
            pltpu.VMEM((tokens, features), jnp.bfloat16),
            pltpu.VMEM((tokens, 2 * units), jnp.float32),
        ],
        compiler_params=pltpu.CompilerParams(vmem_limit_bytes=UNITS_VMEM),
        cost_estimate=pl.CostEstimate(
            flops=4 * tokens * features * units,
            bytes_accessed=2 * tokens * features + 4 * features * units,
            transcendentals=0,
        ),
        name="gate_up",
    )(block, *pieces, gate_w, up_w)


def hidden_kernel(n, *refs):
    sums, others, out = refs[:n], refs[n:-1], refs[-1]
    units = out.shape[1]
    both = jnp.concatenate([part[...].astype(jnp.float32) for part in sums], axis=0)
    if others:
        both = both + jnp.concatenate([part[...].astype(jnp.float32) for part in others], axis=0)
    gate, up = both[:, :units], both[:, units:]
    out[...] = (gate / (1.0 + jnp.exp(-gate)) * up).astype(jnp.bfloat16)


def hidden_units(sums, others=()):
    tokens, units = sum(part.shape[0] for part in sums), sums[0].shape[1] // 2
    return pl.pallas_call(
        functools.partial(hidden_kernel, len(sums)),
        out_shape=jax.ShapeDtypeStruct((tokens, units), jnp.bfloat16),
        in_specs=[VMEM] * (len(sums) + len(others)),
        out_specs=VMEM,
        compiler_params=pltpu.CompilerParams(vmem_limit_bytes=4 * MIB),
        name="hidden",
    )(*sums, *others)


def down_kernel(order, flip, n, chip_ref, core_ref, *refs):
    parts, source, middle, down_w = refs[:n], *refs[n : n + 3]
    keep, send, hidden = refs[n + 3], refs[n + 4], refs[-1]
    tokens = hidden.shape[0]
    rows = middle.shape[0]
    chip, core = chip_ref[0], core_ref[0]
    at = 0
    for part in parts:
        hidden[at : at + part.shape[0], :] = part[...]
        at += part.shape[0]
    wanted = []
    for side in (core, 1 - core):
        for dest in order:
            dest = dest ^ chip if flip else dest
            wanted.append(source[pl.ds(pl.multiple_of((2 * dest + side) * rows, rows), rows), :])
    wanted = jnp.concatenate(wanted, axis=0)
    slot, local = wanted[:, 0:1], wanted[:, 1:2]
    count = wanted.shape[0]
    pick = (lax.broadcasted_iota(jnp.int32, (count, tokens), 1) == slot).astype(jnp.bfloat16)
    moved = mm(pick, hidden[...]).astype(jnp.bfloat16)
    mine = lax.broadcasted_iota(jnp.int32, (count, rows), 1) == local
    mine = mine.astype(jnp.bfloat16)
    high = middle[...].astype(jnp.bfloat16)
    low = (middle[...] - high.astype(jnp.float32)).astype(jnp.bfloat16)
    term = mm(moved, down_w[...]) + (mm(mine, high) + mm(mine, low))
    keep[...] = term[: count // 2]
    send[...] = term[count // 2 :].astype(jnp.bfloat16)


def down(order, flip, chip, core, parts, source, middle, down_w):
    units, features = down_w.shape
    tokens, rows = source.shape[0], middle.shape[0]
    shape = (len(order) * rows, features)
    return pl.pallas_call(
        functools.partial(down_kernel, order, flip, len(parts)),
        out_shape=(
            jax.ShapeDtypeStruct(shape, jnp.float32),
            jax.ShapeDtypeStruct(shape, jnp.bfloat16),
        ),
        in_specs=[SMEM, SMEM] + [VMEM] * (len(parts) + 3),
        out_specs=(VMEM, VMEM),
        scratch_shapes=[pltpu.VMEM((tokens, units), jnp.bfloat16)],
        compiler_params=pltpu.CompilerParams(vmem_limit_bytes=DOWN_VMEM),
        name="down",
    )(chip, core, *parts, source, middle, down_w)


def pack_kernel(n, *refs):
    pieces, out = refs[:n], refs[-1]
    at = 0
    for piece in pieces:
        out[at : at + piece.shape[0], :] = piece[...]
        at += piece.shape[0]


def pack(pieces, after=()):
    rows = sum(piece.shape[0] for piece in pieces)
    return pl.pallas_call(
        functools.partial(pack_kernel, len(pieces)),
        out_shape=jax.ShapeDtypeStruct((rows, pieces[0].shape[1]), pieces[0].dtype),
        in_specs=[VMEM] * len(pieces) + [ANY] * len(after),
        out_specs=VMEM,
        compiler_params=pltpu.CompilerParams(vmem_limit_bytes=4 * MIB),
        name="pack",
    )(*pieces, *after)


def add_kernel(keep, other, *outs):
    at = 0
    for out in outs:
        to = at + out.shape[0]
        out[...] = (keep[at:to, :] + other[at:to, :].astype(jnp.float32)).astype(out.dtype)
        at = to


def add_parts(keep, other, kinds):
    rows, features = keep.shape
    return pl.pallas_call(
        add_kernel,
        out_shape=tuple(
            jax.ShapeDtypeStruct((rows // len(kinds), features), kind) for kind in kinds
        ),
        in_specs=[VMEM, VMEM],
        out_specs=(VMEM,) * len(kinds),
        compiler_params=pltpu.CompilerParams(vmem_limit_bytes=4 * MIB),
        name="add_parts",
    )(keep, other)


def finish_kernel(n, *refs):
    parts, gain, score, moved, stats = refs[:n], *refs[n:]
    total = functools.reduce(jnp.add, [part[...].astype(jnp.float32) for part in parts])
    moved[...] = total
    weighted = gain[...].astype(jnp.float32) * score[...].astype(jnp.float32)
    lane = lax.broadcasted_iota(jnp.int32, (total.shape[0], 128), 1)
    squares = jnp.sum(total * total, axis=1, keepdims=True)
    terms = jnp.sum(total * weighted, axis=1, keepdims=True)
    stats[...] = jnp.transpose(jnp.where(lane == 0, squares, terms))[:8]


def finish(parts, gain, score):
    rows, features = parts[0].shape
    return pl.pallas_call(
        functools.partial(finish_kernel, len(parts)),
        out_shape=(
            jax.ShapeDtypeStruct((rows, features), jnp.float32),
            jax.ShapeDtypeStruct((8, rows), jnp.float32),
        ),
        in_specs=[VMEM] * (len(parts) + 2),
        out_specs=(VMEM, VMEM),
        compiler_params=pltpu.CompilerParams(vmem_limit_bytes=4 * MIB),
        name="finish",
    )(*parts, gain, score)


def shards(
    n_chip,
    n_blk,
    resid,
    queries,
    new_kv,
    prefix_pool,
    page_table,
    prompt_len,
    tail_pool,
    tail_len,
    migration,
    out_w,
    mlp_gain,
    gate_w,
    up_w,
    down_w,
    final_gain,
    score_w,
):
    rows = resid.shape[0]
    features = gate_w.shape[0]
    chip = lax.axis_index("chip").astype(jnp.int32)
    core = lax.axis_index("core").astype(jnp.int32)
    block = lax.axis_index("blk").astype(jnp.int32)
    direct = n_chip == 8 and n_blk == 2

    def to_chip(value, index):
        return lax.ppermute(value, "chip", [(i, i ^ index) for i in range(n_chip)])

    def swap(value, axis):
        return lax.ppermute(value, axis, [(0, 1), (1, 0)])

    own, send = attention(
        queries, new_kv, prefix_pool, page_table, prompt_len, tail_pool, tail_len, out_w
    )
    if direct:
        own, other = own + resid.astype(jnp.float32), swap(send, "blk")
    else:
        own, other = resid.astype(jnp.float32), lax.psum(send, "blk")
    token = migration[:, None] * NEW + jnp.arange(NEW, dtype=jnp.int32)[None, :]
    token = token.reshape(-1, 1)
    came, inner = token // rows, token % rows
    far, far_core = (came // 2) ^ chip, (came % 2) ^ core
    if direct:
        held = far // 2 % 2
        one = (far_core ^ block) * 4 + held * 2
        two = 8 + (held ^ block) * 4 + far_core * 2
        slot = jnp.where(far % 2 == 0, one, two) + far // 4
    else:
        slot = far_core * n_chip + came // 2
    local = token - (chip * 2 + core) * rows
    source = jnp.concatenate([slot * rows + inner, local], axis=1)
    chip, core, block = (index.reshape(1) for index in (chip, core, block))
    gain_row, score_row = final_gain.reshape(1, -1), score_w.reshape(1, -1)

    normed, middle = normalize(
        block,
        own,
        other,
        mlp_gain,
        features,
        1 if direct else n_chip,
        (chip, core, source, gain_row, score_row),
    )
    if direct:
        piece = normed.reshape(rows, features)
        z2, z3, z1 = (to_chip(piece, index) for index in (4, 6, 2))
        here = [pack([piece, z2]), pack([z1, z3])]
        there = [to_chip(part, 1) for part in here]

        def summed(split, pieces):
            keep, *away = partial_units(split, block, pieces, gate_w, up_w)
            return keep, *[swap(part, "blk") for part in away]

        first = summed(2, here + [swap(part, "core") for part in here])
        near = pack(there, first[1:])
        second, third = summed(1, [near]), summed(1, [swap(near, "core")])
        hidden = hidden_units(first[:1], first[1:])
        parts = [hidden, swap(hidden, "blk")]
        hidden = hidden_units((second[0], third[0]), (second[1], third[1]))
        parts += [hidden, swap(hidden, "blk")]
    else:
        near = lax.all_to_all(normed, "chip", 0, 0).reshape(n_chip * rows, features)
        units = partial_units(0, block, [near, swap(near, "core")], gate_w, up_w)[0]
        parts = [hidden_units([lax.psum(units, "blk")])]
    if direct:
        near, wide = (
            down(order, True, chip, core, parts, source, middle, down_w)
            for order in ((0, 2, 1, 3), (6, 4, 7, 5))
        )
        kinds = (jnp.float32, jnp.bfloat16)
        near = add_parts(near[0], swap(near[1], "core"), kinds)
        wide = add_parts(wide[0], swap(wide[1], "core"), kinds)
        mine, to2 = add_parts(near[0], to_chip(near[1], 1), kinds)
        to6, to4 = add_parts(wide[0], to_chip(wide[1], 1), (jnp.bfloat16, jnp.bfloat16))
        sums = [mine, to_chip(to4, 4), to_chip(to6, 6), to_chip(to2, 2)]
    else:
        order = tuple(range(n_chip))
        keep, away = down(order, False, chip, core, parts, source, middle, down_w)
        total = (keep + swap(away, "core").astype(jnp.float32)).astype(jnp.bfloat16)
        total = lax.all_to_all(total.reshape(n_chip, rows, features), "chip", 0, 0)
        sums = [jnp.sum(total.astype(jnp.float32), axis=0)]
    moved, stats = finish(sums, gain_row, score_row)
    stats = stats + swap(stats, "blk") if direct else lax.psum(stats, "blk")
    score = stats[1] * lax.rsqrt(stats[0] / D + EPS)
    return (moved.astype(jnp.bfloat16), score)


def solution(mesh):
    n_chip, n_blk = mesh.shape["dp"] // 2, mesh.shape["blk"]
    split = Mesh(mesh.devices.reshape(n_chip, 2, n_blk), ("chip", "core", "blk"))
    dp = ("chip", "core")
    return jax.shard_map(
        functools.partial(shards, n_chip, n_blk),
        mesh=split,
        in_specs=(
            P(dp, None),
            P(dp, "blk", None),
            P(dp, None, "blk", None),
            P(dp, None, None, "blk", None),
            P(dp, None),
            P(dp),
            P(dp, None, None, "blk", None),
            P(dp, None),
            P(),
            P("blk", None),
            P(),
            P("blk", dp),
            P("blk", dp),
            P(dp, "blk"),
            P("blk"),
            P("blk"),
        ),
        out_specs=(P(dp, "blk"), P(dp)),
        check_vma=False,
    )
```

```python
import functools
import math

import jax
import jax.numpy as jnp
from jax import lax
from jax.experimental import pallas as pl
from jax.experimental.pallas import tpu as pltpu
from jax.sharding import Mesh
from jax.sharding import PartitionSpec as P

D = 2048
NEW = 2
NEG = -1e30
EPS = 1e-06
MIB = 1 << 20
ATTENTION_VMEM = 60 * MIB
UNITS_VMEM = 6 * MIB
DOWN_VMEM = 12 * MIB

VMEM = pl.BlockSpec(memory_space=pltpu.VMEM)
SMEM = pl.BlockSpec(memory_space=pltpu.SMEM)
ANY = pl.BlockSpec(memory_space=pl.ANY)


def mm(a, b):
    return jnp.dot(a, b, preferred_element_type=jnp.float32)


def mm_t(a, b):
    return lax.dot_general(a, b, (((1,), (1,)), ((), ())), preferred_element_type=jnp.float32)


def attention_kernel(
    dims,
    table,
    prompt_len,
    tail_len,
    queries,
    new_kv,
    pool,
    tails,
    out_w,
    own_ref,
    send_ref,
    pages,
    tail_buf,
    w_buf,
    q_buf,
    new_buf,
    keys_apart,
    apart,
    tail_keys,
    tail_apart,
    q_wide,
    q_rows,
    q_pairs,
    new_wide,
    fresh_scores,
    tail_scores,
    scores,
    top,
    total,
    acc,
    attn,
    page_sems,
    tail_sems,
    sems,
):
    rows, heads, groups, width, n_pages, page, conts, tail, pair = dims
    repeat = heads // groups
    step = 2 * groups
    pairs = groups // pair
    stack = repeat * rows
    page_rows = page * step
    chunk_pages = math.gcd(16, n_pages)
    chunk = chunk_pages * page
    chunk_rows = chunk * step
    quad = 8 // NEW
    quads = conts // quad
    quad_keys = quad * tail
    quad_rows = quad_keys * step
    factor = math.log2(math.e) / math.sqrt(width)
    length = prompt_len[0]
    chunks = (length + chunk - 1) // chunk

    def page_copy(logical):
        physical = table[0, logical]
        return pltpu.make_async_copy(
            pool.at[pl.ds(pl.multiple_of(physical * page_rows, page_rows), page_rows), :],
            pages.at[pl.ds(pl.multiple_of(logical * page_rows, page_rows), page_rows), :],
            page_sems.at[logical],
        )

    def tail_copy(index):
        return pltpu.make_async_copy(
            tails.at[pl.ds(index * quad_rows, quad_rows), :],
            tail_buf.at[pl.ds(index * quad_rows, quad_rows), :],
            tail_sems.at[index],
        )

    q_copy = pltpu.make_async_copy(queries, q_buf, sems.at[0])
    new_copy = pltpu.make_async_copy(new_kv, new_buf, sems.at[1])
    w_copy = pltpu.make_async_copy(out_w, w_buf, sems.at[2])
    q_copy.start()
    new_copy.start()
    for index in range(quads):
        tail_copy(index).start()

    @pl.loop(0, chunks * chunk_pages)
    def _(logical):
        page_copy(logical).start()

    w_copy.start()

    block = 256
    tokens = block // step
    to = lax.broadcasted_iota(jnp.int32, (block, block), 0)
    came = lax.broadcasted_iota(jnp.int32, (block, block), 1)
    sort = (came == (to % tokens) * step + to // tokens).astype(jnp.bfloat16)

    def take_apart(buf, start, count, outs, places):
        def one(two):
            x0 = buf[pl.ds(start + two * 2 * block, block), :]
            x1 = buf[pl.ds(start + (two * 2 + 1) * block, block), :]
            y = mm(sort, jnp.concatenate([x0, x1], axis=1)).astype(jnp.bfloat16)
            for side in range(2):
                for j in range(step):
                    kind, g = j // groups, j % groups
                    t = pl.ds(places[kind] + (2 * two + side) * tokens, tokens)
                    lane = (g % pair) * width
                    outs[kind][g // pair, t, lane : lane + width] = y[
                        j * tokens : (j + 1) * tokens, side * width : (side + 1) * width
                    ]

        return [functools.partial(one, two) for two in range(count // (2 * block))]

    def alternate(works, others):
        shares = len(others) or 1
        for index in range(shares):
            for work in works[index * len(works) // shares : (index + 1) * len(works) // shares]:
                work()
            if others:
                others[index]()

    def blocks(x):
        return [x[:, i * 128 : (i + 1) * 128] for i in range(x.shape[1] // 128)]

    q_copy.wait()
    new_copy.wait()
    q_wide[...] = q_buf[...].astype(jnp.float32)
    new_wide[...] = new_buf[...].astype(jnp.float32)
    if pair > 1:
        q_rows[...] = jnp.zeros_like(q_rows)
    for g in range(groups):
        for r in range(repeat):
            at = (g % pair) * stack + r * rows
            lane = (g % pair) * width
            q_rows[g // pair, at : at + rows, lane : lane + width] = q_wide[
                pl.ds(g * repeat + r, rows, stride=heads), :
            ]

    q_pairs[...] = q_rows[...].astype(jnp.bfloat16)

    def fresh(first, n):
        parts = [
            new_wide[pl.ds(first + n * pair + i, rows, stride=step), :] for i in range(pair)
        ]
        return jnp.concatenate(parts, axis=1).astype(jnp.bfloat16)

    row = lax.broadcasted_iota(jnp.int32, (rows, rows), 0)
    key = lax.broadcasted_iota(jnp.int32, (rows, rows), 1)
    fresh_ok = (row // NEW == key // NEW) & (key <= row)
    fresh_ok = jnp.concatenate([fresh_ok] * (pair * repeat), axis=0)
    for n in range(pairs):
        s = jnp.where(fresh_ok, mm_t(q_pairs[n], fresh(0, n)) * factor, NEG)
        fresh_scores[n] = s
        top[n] = jnp.broadcast_to(jnp.max(s, axis=1, keepdims=True), top.shape[1:])

    def quad_places(index):
        starts = [i * rows + index * 8 for i in range(pair * repeat)]
        return [slice(at, at + 8) for at in starts]

    quad_row = lax.broadcasted_iota(jnp.int32, (8, quad_keys), 0)
    quad_key = lax.broadcasted_iota(jnp.int32, (8, quad_keys), 1)
    for index in range(quads):
        tail_copy(index).wait()
    def score_tails(index, n):
        reach = jnp.zeros((8, quad_keys), jnp.int32)
        for c in range(quad):
            reach = jnp.where(
                quad_key // tail == c, tail_len[0, index * quad + c] + c * tail, reach
            )
        ok = (quad_row // NEW == quad_key // tail) & (quad_key < reach)
        ok = jnp.concatenate([ok] * (pair * repeat), axis=0)
        keys = slice(index * quad_keys, (index + 1) * quad_keys)
        q = jnp.concatenate([q_rows[n, a, :] for a in quad_places(index)], axis=0)
        s = mm_t(q.astype(jnp.bfloat16), tail_keys[n, keys, :]) * factor
        s = jnp.where(ok, s, NEG)
        tail_scores[n, index] = s
        high = functools.reduce(jnp.maximum, blocks(s))
        for i, a in enumerate(quad_places(index)):
            top[n, a, :] = jnp.maximum(top[n, a, :], high[i * 8 : (i + 1) * 8])

    others = []
    for index in range(quads):
        outs, at = (tail_keys, tail_apart), index * quad_keys
        alternate(take_apart(tail_buf, index * quad_rows, quad_rows, outs, (at, at)), others)
        others = [functools.partial(score_tails, index, n) for n in range(pairs)]
    alternate([], others)

    part = min(256, chunk)
    place = lax.broadcasted_iota(jnp.int32, (8, part), 1)

    @pl.loop(0, chunks)
    def _(index):
        for i in range(chunk_pages):
            page_copy(index * chunk_pages + i).wait()
        first = pl.multiple_of(index * chunk, chunk)
        row = pl.multiple_of(index * chunk_rows, chunk_rows)

        def score(at, n):
            ok = place[0:1] < length - (index * chunk + at)
            s = mm_t(q_pairs[n], keys_apart[n, at : at + part, :]) * factor
            s = jnp.where(ok, s, NEG)
            scores[n, :, pl.ds(first + at, part)] = s
            top[n] = functools.reduce(jnp.maximum, blocks(s), top[n])

        others = []
        for at in range(0, chunk, part):
            outs, places = (keys_apart, apart), (at, first + at)
            alternate(take_apart(pages, row + at * step, part * step, outs, places), others)
            others = [functools.partial(score, at, n) for n in range(pairs)]
        alternate([], others)

    for n in range(pairs):
        high = jnp.broadcast_to(jnp.max(top[n], axis=1, keepdims=True), top.shape[1:])
        top[n] = high
        p = jnp.exp2(fresh_scores[n] - high[:, :rows])
        lane = lax.broadcasted_iota(jnp.int32, total.shape[1:], 1)
        total[n] = jnp.where(lane == 0, jnp.sum(p, axis=1, keepdims=True), 0.0)
        acc[n] = mm(p.astype(jnp.bfloat16), fresh(groups, n))

    def weigh(s, high):
        parts = [jnp.exp2(part - high) for part in blocks(s)]
        return jnp.concatenate(parts, axis=1).astype(jnp.bfloat16), functools.reduce(jnp.add, parts)

    for index in range(quads):
        keys = slice(index * quad_keys, (index + 1) * quad_keys)
        for n in range(pairs):
            high = jnp.concatenate([top[n, a, :] for a in quad_places(index)], axis=0)
            p, added = weigh(tail_scores[n, index], high)
            value = mm(p, tail_apart[n, keys, :])
            for i, a in enumerate(quad_places(index)):
                total[n, a, :] = total[n, a, :] + added[i * 8 : (i + 1) * 8]
                acc[n, a, :] = acc[n, a, :] + value[i * 8 : (i + 1) * 8]

    @pl.loop(0, chunks)
    def _(index):
        first = pl.multiple_of(index * chunk, chunk)
        for n in range(pairs):
            p, added = weigh(scores[n, :, pl.ds(first, chunk)], top[n])
            total[n] = total[n] + added
            acc[n] = acc[n] + mm(p, apart[n, pl.ds(first, chunk), :])

    for g in range(groups):
        at, lane = (g % pair) * stack, (g % pair) * width
        out = acc[g // pair, at : at + stack, lane : lane + width]
        out = out / jnp.sum(total[g // pair, at : at + stack, :], axis=1, keepdims=True)
        out = out.astype(jnp.bfloat16)
        for r in range(repeat):
            head = g * repeat + r
            attn[:, head * width : (head + 1) * width] = out[r * rows : (r + 1) * rows]
    w_copy.wait()
    value = mm(attn[...], w_buf[...])
    own_ref[...] = value
    send_ref[...] = value.astype(jnp.bfloat16)


def attention(queries, new_kv, pool, table, prompt_len, tails, tail_len, out_w):
    rows, heads, width = queries.shape
    n_pages, page, _, groups, _ = pool.shape
    conts, tail = tails.shape[:2]
    step = 2 * groups
    features = out_w.shape[1]
    quads = conts * NEW // 8
    pair = 2 if groups % 2 == 0 else 1
    pairs = groups // pair
    repeat = heads // groups
    stack = pair * repeat * rows
    return pl.pallas_call(
        functools.partial(
            attention_kernel, (rows, heads, groups, width, n_pages, page, conts, tail, pair)
        ),
        out_shape=(
            jax.ShapeDtypeStruct((rows, features), jnp.float32),
            jax.ShapeDtypeStruct((rows, features), jnp.bfloat16),
        ),
        in_specs=[SMEM, SMEM, SMEM, ANY, ANY, ANY, ANY, ANY],
        out_specs=(VMEM, VMEM),
        scratch_shapes=[
            pltpu.VMEM((n_pages * page * step, width), jnp.bfloat16),
            pltpu.VMEM((conts * tail * step, width), jnp.bfloat16),
            pltpu.VMEM(out_w.shape, jnp.bfloat16),
            pltpu.VMEM((rows * heads, width), jnp.bfloat16),
            pltpu.VMEM((rows * step, width), jnp.bfloat16),
            pltpu.VMEM((pairs, n_pages * page, pair * width), jnp.bfloat16),
            pltpu.VMEM((pairs, n_pages * page, pair * width), jnp.bfloat16),
            pltpu.VMEM((pairs, conts * tail, pair * width), jnp.bfloat16),
            pltpu.VMEM((pairs, conts * tail, pair * width), jnp.bfloat16),
            pltpu.VMEM((rows * heads, width), jnp.float32),
            pltpu.VMEM((pairs, stack, pair * width), jnp.float32),
            pltpu.VMEM((pairs, stack, pair * width), jnp.bfloat16),
            pltpu.VMEM((rows * step, width), jnp.float32),
            pltpu.VMEM((pairs, stack, rows), jnp.float32),
            pltpu.VMEM((pairs, quads, pair * repeat * 8, 8 // NEW * tail), jnp.float32),
            pltpu.VMEM((pairs, stack, n_pages * page), jnp.float32),
            pltpu.VMEM((pairs, stack, 128), jnp.float32),
            pltpu.VMEM((pairs, stack, 128), jnp.float32),
            pltpu.VMEM((pairs, stack, pair * width), jnp.float32),
            pltpu.VMEM((rows, heads * width), jnp.bfloat16),
            pltpu.SemaphoreType.DMA((n_pages,)),
            pltpu.SemaphoreType.DMA((quads,)),
            pltpu.SemaphoreType.DMA((3,)),
        ],
        compiler_params=pltpu.CompilerParams(vmem_limit_bytes=ATTENTION_VMEM),
        name="attention",
    )(
        table,
        prompt_len,
        tail_len,
        queries.reshape(rows * heads, width),
        new_kv.reshape(rows * step, width),
        pool.reshape(n_pages * page * step, width),
        tails.reshape(conts * tail * step, width),
        out_w,
    )


def norm_kernel(n, block, own, other, gain, *refs):
    normed, middle, whole = refs[n:]
    copies, rows, features = normed.shape
    mid = own[...] + other[...].astype(jnp.float32)
    scale = lax.rsqrt(jnp.mean(mid * mid, axis=1, keepdims=True) + EPS)
    whole[...] = mid
    start = pl.multiple_of(block[0] * features, features)
    part = whole[:, pl.ds(start, features)]
    out = (part * scale * gain[:, pl.ds(start, features)]).astype(jnp.bfloat16)
    for index in range(copies):
        normed[index] = out
    middle[...] = part


def normalize(block, own, other, gain, features, copies, ahead):
    rows = own.shape[0]
    return pl.pallas_call(
        functools.partial(norm_kernel, len(ahead)),
        out_shape=(
            jax.ShapeDtypeStruct((copies, rows, features), jnp.bfloat16),
            jax.ShapeDtypeStruct((rows, features), jnp.float32),
        ),
        in_specs=[SMEM, VMEM, VMEM, VMEM] + [ANY] * len(ahead),
        out_specs=(VMEM, VMEM),
        scratch_shapes=[pltpu.VMEM(own.shape, jnp.float32)],
        compiler_params=pltpu.CompilerParams(vmem_limit_bytes=4 * MIB),
        name="normalize",
    )(block, own, other, gain.astype(jnp.float32).reshape(1, -1), *ahead)


def units_kernel(n, block, *refs):
    pieces, gate_w, up_w, outs, held, sums = refs[:n], *refs[n : n + 2], refs[n + 2 : -2], *refs[-2:]
    at = 0
    for piece in pieces:
        held[at : at + piece.shape[0], :] = piece[...]
        at += piece.shape[0]
    units = gate_w.shape[1]
    sums[:, :units] = mm(held[...], gate_w[...])
    sums[:, units:] = mm(held[...], up_w[...])
    if len(outs) == 1:
        outs[0][...] = sums[...].astype(jnp.bfloat16)
        return
    keep, away = outs[0], outs[1:]
    half, part = at // 2, away[0].shape[0]
    start = pl.multiple_of((1 - block[0]) * half, half)
    for index, out in enumerate(away):
        out[...] = sums[pl.ds(start + index * part, part), :].astype(jnp.bfloat16)
    keep[...] = sums[pl.ds(pl.multiple_of(block[0] * half, half), half), :]


def partial_units(split, block, pieces, gate_w, up_w):
    tokens = sum(piece.shape[0] for piece in pieces)
    features, units = gate_w.shape
    if split:
        out_shape = (
            jax.ShapeDtypeStruct((tokens // 2, 2 * units), jnp.float32),
            *[jax.ShapeDtypeStruct((tokens // 2 // split, 2 * units), jnp.bfloat16)] * split,
        )
    else:
        out_shape = (jax.ShapeDtypeStruct((tokens, 2 * units), jnp.bfloat16),)
    return pl.pallas_call(
        functools.partial(units_kernel, len(pieces)),
        out_shape=out_shape,
        in_specs=[SMEM] + [VMEM] * (len(pieces) + 2),
        out_specs=(VMEM,) * len(out_shape),
        scratch_shapes=[
            pltpu.VMEM((tokens, features), jnp.bfloat16),
            pltpu.VMEM((tokens, 2 * units), jnp.float32),
        ],
        compiler_params=pltpu.CompilerParams(vmem_limit_bytes=UNITS_VMEM),
        cost_estimate=pl.CostEstimate(
            flops=4 * tokens * features * units,
            bytes_accessed=2 * tokens * features + 4 * features * units,
            transcendentals=0,
        ),
        name="gate_up",
    )(block, *pieces, gate_w, up_w)


def hidden_kernel(n, *refs):
    sums, others, out = refs[:n], refs[n:-1], refs[-1]
    units = out.shape[1]
    both = jnp.concatenate([part[...].astype(jnp.float32) for part in sums], axis=0)
    if others:
        both = both + jnp.concatenate([part[...].astype(jnp.float32) for part in others], axis=0)
    gate, up = both[:, :units], both[:, units:]
    out[...] = (gate / (1.0 + jnp.exp(-gate)) * up).astype(jnp.bfloat16)


def hidden_units(sums, others=()):
    tokens, units = sum(part.shape[0] for part in sums), sums[0].shape[1] // 2
    return pl.pallas_call(
        functools.partial(hidden_kernel, len(sums)),
        out_shape=jax.ShapeDtypeStruct((tokens, units), jnp.bfloat16),
        in_specs=[VMEM] * (len(sums) + len(others)),
        out_specs=VMEM,
        compiler_params=pltpu.CompilerParams(vmem_limit_bytes=4 * MIB),
        name="hidden",
    )(*sums, *others)


def down_kernel(order, flip, n, chip_ref, core_ref, *refs):
    parts, source, middle, down_w = refs[:n], *refs[n : n + 3]
    keep, send, hidden = refs[n + 3], refs[n + 4], refs[-1]
    tokens = hidden.shape[0]
    rows = middle.shape[0]
    chip, core = chip_ref[0], core_ref[0]
    at = 0
    for part in parts:
        hidden[at : at + part.shape[0], :] = part[...]
        at += part.shape[0]
    wanted = []
    for side in (core, 1 - core):
        for dest in order:
            dest = dest ^ chip if flip else dest
            wanted.append(source[pl.ds(pl.multiple_of((2 * dest + side) * rows, rows), rows), :])
    wanted = jnp.concatenate(wanted, axis=0)
    slot, local = wanted[:, 0:1], wanted[:, 1:2]
    count = wanted.shape[0]
    pick = (lax.broadcasted_iota(jnp.int32, (count, tokens), 1) == slot).astype(jnp.bfloat16)
    moved = mm(pick, hidden[...]).astype(jnp.bfloat16)
    mine = lax.broadcasted_iota(jnp.int32, (count, rows), 1) == local
    mine = mine.astype(jnp.bfloat16)
    high = middle[...].astype(jnp.bfloat16)
    low = (middle[...] - high.astype(jnp.float32)).astype(jnp.bfloat16)
    term = mm(moved, down_w[...]) + (mm(mine, high) + mm(mine, low))
    keep[...] = term[: count // 2]
    send[...] = term[count // 2 :].astype(jnp.bfloat16)


def down(order, flip, chip, core, parts, source, middle, down_w):
    units, features = down_w.shape
    tokens, rows = source.shape[0], middle.shape[0]
    shape = (len(order) * rows, features)
    return pl.pallas_call(
        functools.partial(down_kernel, order, flip, len(parts)),
        out_shape=(
            jax.ShapeDtypeStruct(shape, jnp.float32),
            jax.ShapeDtypeStruct(shape, jnp.bfloat16),
        ),
        in_specs=[SMEM, SMEM] + [VMEM] * (len(parts) + 3),
        out_specs=(VMEM, VMEM),
        scratch_shapes=[pltpu.VMEM((tokens, units), jnp.bfloat16)],
        compiler_params=pltpu.CompilerParams(vmem_limit_bytes=DOWN_VMEM),
        name="down",
    )(chip, core, *parts, source, middle, down_w)


def pack_kernel(n, *refs):
    pieces, out = refs[:n], refs[-1]
    at = 0
    for piece in pieces:
        out[at : at + piece.shape[0], :] = piece[...]
        at += piece.shape[0]


def pack(pieces, after=()):
    rows = sum(piece.shape[0] for piece in pieces)
    return pl.pallas_call(
        functools.partial(pack_kernel, len(pieces)),
        out_shape=jax.ShapeDtypeStruct((rows, pieces[0].shape[1]), pieces[0].dtype),
        in_specs=[VMEM] * len(pieces) + [ANY] * len(after),
        out_specs=VMEM,
        compiler_params=pltpu.CompilerParams(vmem_limit_bytes=4 * MIB),
        name="pack",
    )(*pieces, *after)


def add_kernel(keep, other, *outs):
    at = 0
    for out in outs:
        to = at + out.shape[0]
        out[...] = (keep[at:to, :] + other[at:to, :].astype(jnp.float32)).astype(out.dtype)
        at = to


def add_parts(keep, other, kinds):
    rows, features = keep.shape
    return pl.pallas_call(
        add_kernel,
        out_shape=tuple(
            jax.ShapeDtypeStruct((rows // len(kinds), features), kind) for kind in kinds
        ),
        in_specs=[VMEM, VMEM],
        out_specs=(VMEM,) * len(kinds),
        compiler_params=pltpu.CompilerParams(vmem_limit_bytes=4 * MIB),
        name="add_parts",
    )(keep, other)


def finish_kernel(n, *refs):
    parts, gain, score, moved, stats = refs[:n], *refs[n:]
    total = functools.reduce(jnp.add, [part[...].astype(jnp.float32) for part in parts])
    moved[...] = total
    weighted = gain[...].astype(jnp.float32) * score[...].astype(jnp.float32)
    lane = lax.broadcasted_iota(jnp.int32, (total.shape[0], 128), 1)
    squares = jnp.sum(total * total, axis=1, keepdims=True)
    terms = jnp.sum(total * weighted, axis=1, keepdims=True)
    stats[...] = jnp.transpose(jnp.where(lane == 0, squares, terms))[:8]


def finish(parts, gain, score):
    rows, features = parts[0].shape
    return pl.pallas_call(
        functools.partial(finish_kernel, len(parts)),
        out_shape=(
            jax.ShapeDtypeStruct((rows, features), jnp.float32),
            jax.ShapeDtypeStruct((8, rows), jnp.float32),
        ),
        in_specs=[VMEM] * (len(parts) + 2),
        out_specs=(VMEM, VMEM),
        compiler_params=pltpu.CompilerParams(vmem_limit_bytes=4 * MIB),
        name="finish",
    )(*parts, gain, score)


def shards(
    n_chip,
    n_blk,
    resid,
    queries,
    new_kv,
    prefix_pool,
    page_table,
    prompt_len,
    tail_pool,
    tail_len,
    migration,
    out_w,
    mlp_gain,
    gate_w,
    up_w,
    down_w,
    final_gain,
    score_w,
):
    rows = resid.shape[0]
    features = gate_w.shape[0]
    chip = lax.axis_index("chip").astype(jnp.int32)
    core = lax.axis_index("core").astype(jnp.int32)
    block = lax.axis_index("blk").astype(jnp.int32)
    direct = n_chip == 8 and n_blk == 2

    def to_chip(value, index):
        return lax.ppermute(value, "chip", [(i, i ^ index) for i in range(n_chip)])

    def swap(value, axis):
        return lax.ppermute(value, axis, [(0, 1), (1, 0)])

    own, send = attention(
        queries, new_kv, prefix_pool, page_table, prompt_len, tail_pool, tail_len, out_w
    )
    if direct:
        own, other = own + resid.astype(jnp.float32), swap(send, "blk")
    else:
        own, other = resid.astype(jnp.float32), lax.psum(send, "blk")
    token = migration[:, None] * NEW + jnp.arange(NEW, dtype=jnp.int32)[None, :]
    token = token.reshape(-1, 1)
    came, inner = token // rows, token % rows
    far, far_core = (came // 2) ^ chip, (came % 2) ^ core
    if direct:
        held = far // 2 % 2
        one = (far_core ^ block) * 4 + held * 2
        two = 8 + (held ^ block) * 4 + far_core * 2
        slot = jnp.where(far % 2 == 0, one, two) + far // 4
    else:
        slot = far_core * n_chip + came // 2
    local = token - (chip * 2 + core) * rows
    source = jnp.concatenate([slot * rows + inner, local], axis=1)
    chip, core, block = (index.reshape(1) for index in (chip, core, block))
    gain_row, score_row = final_gain.reshape(1, -1), score_w.reshape(1, -1)

    normed, middle = normalize(
        block,
        own,
        other,
        mlp_gain,
        features,
        1 if direct else n_chip,
        (chip, core, source, gain_row, score_row),
    )
    if direct:
        piece = normed.reshape(rows, features)
        z2, z3, z1 = (to_chip(piece, index) for index in (4, 6, 2))
        here = [pack([piece, z2]), pack([z1, z3])]
        there = [to_chip(part, 1) for part in here]

        def summed(split, pieces):
            keep, *away = partial_units(split, block, pieces, gate_w, up_w)
            return keep, *[swap(part, "blk") for part in away]

        first = summed(2, here + [swap(part, "core") for part in here])
        near = pack(there, first[1:])
        second, third = summed(1, [near]), summed(1, [swap(near, "core")])
        hidden = hidden_units(first[:1], first[1:])
        parts = [hidden, swap(hidden, "blk")]
        hidden = hidden_units((second[0], third[0]), (second[1], third[1]))
        parts += [hidden, swap(hidden, "blk")]
    else:
        near = lax.all_to_all(normed, "chip", 0, 0).reshape(n_chip * rows, features)
        units = partial_units(0, block, [near, swap(near, "core")], gate_w, up_w)[0]
        parts = [hidden_units([lax.psum(units, "blk")])]
    if direct:
        near, wide = (
            down(order, True, chip, core, parts, source, middle, down_w)
            for order in ((0, 2, 1, 3), (6, 4, 7, 5))
        )
        kinds = (jnp.float32, jnp.bfloat16)
        near = add_parts(near[0], swap(near[1], "core"), kinds)
        wide = add_parts(wide[0], swap(wide[1], "core"), kinds)
        mine, to2 = add_parts(near[0], to_chip(near[1], 1), kinds)
        to6, to4 = add_parts(wide[0], to_chip(wide[1], 1), (jnp.bfloat16, jnp.bfloat16))
        sums = [mine, to_chip(to4, 4), to_chip(to6, 6), to_chip(to2, 2)]
    else:
        order = tuple(range(n_chip))
        keep, away = down(order, False, chip, core, parts, source, middle, down_w)
        total = (keep + swap(away, "core").astype(jnp.float32)).astype(jnp.bfloat16)
        total = lax.all_to_all(total.reshape(n_chip, rows, features), "chip", 0, 0)
        sums = [jnp.sum(total.astype(jnp.float32), axis=0)]
    moved, stats = finish(sums, gain_row, score_row)
    stats = stats + swap(stats, "blk") if direct else lax.psum(stats, "blk")
    score = stats[1] * lax.rsqrt(stats[0] / D + EPS)
    return (moved.astype(jnp.bfloat16), score)


def solution(mesh):
    n_chip, n_blk = mesh.shape["dp"] // 2, mesh.shape["blk"]
    split = Mesh(mesh.devices.reshape(n_chip, 2, n_blk), ("chip", "core", "blk"))
    dp = ("chip", "core")
    return jax.shard_map(
        functools.partial(shards, n_chip, n_blk),
        mesh=split,
        in_specs=(
            P(dp, None),
            P(dp, "blk", None),
            P(dp, None, "blk", None),
            P(dp, None, None, "blk", None),
            P(dp, None),
            P(dp),
            P(dp, None, None, "blk", None),
            P(dp, None),
            P(),
            P("blk", None),
            P(),
            P("blk", dp),
            P("blk", dp),
            P(dp, "blk"),
            P("blk"),
            P("blk"),
        ),
        out_specs=(P(dp, "blk"), P(dp)),
        check_vma=False,
    )
```

```python
import functools
import math

import jax
import jax.numpy as jnp
from jax import lax
from jax.experimental import pallas as pl
from jax.experimental.pallas import tpu as pltpu
from jax.sharding import Mesh
from jax.sharding import PartitionSpec as P

D = 2048
NEW = 2
NEG = -1e30
EPS = 1e-06
MIB = 1 << 20
ATTENTION_VMEM = 60 * MIB
UNITS_VMEM = 6 * MIB
DOWN_VMEM = 12 * MIB

VMEM = pl.BlockSpec(memory_space=pltpu.VMEM)
SMEM = pl.BlockSpec(memory_space=pltpu.SMEM)
ANY = pl.BlockSpec(memory_space=pl.ANY)


def mm(a, b):
    return jnp.dot(a, b, preferred_element_type=jnp.float32)


def mm_t(a, b):
    return lax.dot_general(a, b, (((1,), (1,)), ((), ())), preferred_element_type=jnp.float32)


def attention_kernel(
    dims,
    table,
    prompt_len,
    tail_len,
    queries,
    new_kv,
    pool,
    tails,
    out_w,
    own_ref,
    send_ref,
    pages,
    tail_buf,
    w_buf,
    q_buf,
    new_buf,
    keys_apart,
    apart,
    tail_keys,
    tail_apart,
    q_wide,
    q_rows,
    q_pairs,
    new_wide,
    fresh_scores,
    tail_scores,
    scores,
    top,
    total,
    acc,
    attn,
    page_sems,
    tail_sems,
    sems,
):
    rows, heads, groups, width, n_pages, page, conts, tail, pair = dims
    repeat = heads // groups
    step = 2 * groups
    pairs = groups // pair
    stack = repeat * rows
    page_rows = page * step
    chunk_pages = math.gcd(16, n_pages)
    chunk = chunk_pages * page
    chunk_rows = chunk * step
    quad = 8 // NEW
    quads = conts // quad
    quad_keys = quad * tail
    quad_rows = quad_keys * step
    factor = math.log2(math.e) / math.sqrt(width)
    length = prompt_len[0]
    chunks = (length + chunk - 1) // chunk

    def page_copy(logical):
        physical = table[0, logical]
        return pltpu.make_async_copy(
            pool.at[pl.ds(pl.multiple_of(physical * page_rows, page_rows), page_rows), :],
            pages.at[pl.ds(pl.multiple_of(logical * page_rows, page_rows), page_rows), :],
            page_sems.at[logical],
        )

    def tail_copy(index):
        return pltpu.make_async_copy(
            tails.at[pl.ds(index * quad_rows, quad_rows), :],
            tail_buf.at[pl.ds(index * quad_rows, quad_rows), :],
            tail_sems.at[index],
        )

    q_copy = pltpu.make_async_copy(queries, q_buf, sems.at[0])
    new_copy = pltpu.make_async_copy(new_kv, new_buf, sems.at[1])
    w_copy = pltpu.make_async_copy(out_w, w_buf, sems.at[2])
    q_copy.start()
    new_copy.start()
    for index in range(quads):
        tail_copy(index).start()

    @pl.loop(0, chunks * chunk_pages)
    def _(logical):
        page_copy(logical).start()

    w_copy.start()

    block = 256
    tokens = block // step
    to = lax.broadcasted_iota(jnp.int32, (block, block), 0)
    came = lax.broadcasted_iota(jnp.int32, (block, block), 1)
    sort = (came == (to % tokens) * step + to // tokens).astype(jnp.bfloat16)

    def take_apart(buf, start, count, outs, places):
        def one(two):
            x0 = buf[pl.ds(start + two * 2 * block, block), :]
            x1 = buf[pl.ds(start + (two * 2 + 1) * block, block), :]
            y = mm(sort, jnp.concatenate([x0, x1], axis=1)).astype(jnp.bfloat16)
            for side in range(2):
                for j in range(step):
                    kind, g = j // groups, j % groups
                    t = pl.ds(places[kind] + (2 * two + side) * tokens, tokens)
                    lane = (g % pair) * width
                    outs[kind][g // pair, t, lane : lane + width] = y[
                        j * tokens : (j + 1) * tokens, side * width : (side + 1) * width
                    ]

        return [functools.partial(one, two) for two in range(count // (2 * block))]

    def alternate(works, others):
        shares = len(others) or 1
        for index in range(shares):
            for work in works[index * len(works) // shares : (index + 1) * len(works) // shares]:
                work()
            if others:
                others[index]()

    def blocks(x):
        return [x[:, i * 128 : (i + 1) * 128] for i in range(x.shape[1] // 128)]

    q_copy.wait()
    new_copy.wait()
    q_wide[...] = q_buf[...].astype(jnp.float32)
    new_wide[...] = new_buf[...].astype(jnp.float32)
    if pair > 1:
        q_rows[...] = jnp.zeros_like(q_rows)
    for g in range(groups):
        for r in range(repeat):
            at = (g % pair) * stack + r * rows
            lane = (g % pair) * width
            q_rows[g // pair, at : at + rows, lane : lane + width] = q_wide[
                pl.ds(g * repeat + r, rows, stride=heads), :
            ]

    q_pairs[...] = q_rows[...].astype(jnp.bfloat16)

    def fresh(first, n):
        parts = [
            new_wide[pl.ds(first + n * pair + i, rows, stride=step), :] for i in range(pair)
        ]
        return jnp.concatenate(parts, axis=1).astype(jnp.bfloat16)

    row = lax.broadcasted_iota(jnp.int32, (rows, rows), 0)
    key = lax.broadcasted_iota(jnp.int32, (rows, rows), 1)
    fresh_ok = (row // NEW == key // NEW) & (key <= row)
    fresh_ok = jnp.concatenate([fresh_ok] * (pair * repeat), axis=0)
    for n in range(pairs):
        s = jnp.where(fresh_ok, mm_t(q_pairs[n], fresh(0, n)) * factor, NEG)
        fresh_scores[n] = s
        top[n] = jnp.broadcast_to(jnp.max(s, axis=1, keepdims=True), top.shape[1:])

    def quad_places(index):
        starts = [i * rows + index * 8 for i in range(pair * repeat)]
        return [slice(at, at + 8) for at in starts]

    quad_row = lax.broadcasted_iota(jnp.int32, (8, quad_keys), 0)
    quad_key = lax.broadcasted_iota(jnp.int32, (8, quad_keys), 1)
    for index in range(quads):
        tail_copy(index).wait()
    def score_tails(index, n):
        reach = jnp.zeros((8, quad_keys), jnp.int32)
        for c in range(quad):
            reach = jnp.where(
                quad_key // tail == c, tail_len[0, index * quad + c] + c * tail, reach
            )
        ok = (quad_row // NEW == quad_key // tail) & (quad_key < reach)
        ok = jnp.concatenate([ok] * (pair * repeat), axis=0)
        keys = slice(index * quad_keys, (index + 1) * quad_keys)
        q = jnp.concatenate([q_rows[n, a, :] for a in quad_places(index)], axis=0)
        s = mm_t(q.astype(jnp.bfloat16), tail_keys[n, keys, :]) * factor
        s = jnp.where(ok, s, NEG)
        tail_scores[n, index] = s
        high = functools.reduce(jnp.maximum, blocks(s))
        for i, a in enumerate(quad_places(index)):
            top[n, a, :] = jnp.maximum(top[n, a, :], high[i * 8 : (i + 1) * 8])

    others = []
    for index in range(quads):
        outs, at = (tail_keys, tail_apart), index * quad_keys
        alternate(take_apart(tail_buf, index * quad_rows, quad_rows, outs, (at, at)), others)
        others = [functools.partial(score_tails, index, n) for n in range(pairs)]
    alternate([], others)

    part = min(256, chunk)
    place = lax.broadcasted_iota(jnp.int32, (8, part), 1)

    @pl.loop(0, chunks)
    def _(index):
        for i in range(chunk_pages):
            page_copy(index * chunk_pages + i).wait()
        first = pl.multiple_of(index * chunk, chunk)
        row = pl.multiple_of(index * chunk_rows, chunk_rows)

        def score(at, n):
            ok = place[0:1] < length - (index * chunk + at)
            s = mm_t(q_pairs[n], keys_apart[n, at : at + part, :]) * factor
            s = jnp.where(ok, s, NEG)
            scores[n, :, pl.ds(first + at, part)] = s
            top[n] = functools.reduce(jnp.maximum, blocks(s), top[n])

        others = []
        for at in range(0, chunk, part):
            outs, places = (keys_apart, apart), (at, first + at)
            alternate(take_apart(pages, row + at * step, part * step, outs, places), others)
            others = [functools.partial(score, at, n) for n in range(pairs)]
        alternate([], others)

    for n in range(pairs):
        high = jnp.broadcast_to(jnp.max(top[n], axis=1, keepdims=True), top.shape[1:])
        top[n] = high
        p = jnp.exp2(fresh_scores[n] - high[:, :rows])
        lane = lax.broadcasted_iota(jnp.int32, total.shape[1:], 1)
        total[n] = jnp.where(lane == 0, jnp.sum(p, axis=1, keepdims=True), 0.0)
        acc[n] = mm(p.astype(jnp.bfloat16), fresh(groups, n))

    def weigh(s, high):
        parts = [jnp.exp2(part - high) for part in blocks(s)]
        return jnp.concatenate(parts, axis=1).astype(jnp.bfloat16), functools.reduce(jnp.add, parts)

    for index in range(quads):
        keys = slice(index * quad_keys, (index + 1) * quad_keys)
        for n in range(pairs):
            high = jnp.concatenate([top[n, a, :] for a in quad_places(index)], axis=0)
            p, added = weigh(tail_scores[n, index], high)
            value = mm(p, tail_apart[n, keys, :])
            for i, a in enumerate(quad_places(index)):
                total[n, a, :] = total[n, a, :] + added[i * 8 : (i + 1) * 8]
                acc[n, a, :] = acc[n, a, :] + value[i * 8 : (i + 1) * 8]

    @pl.loop(0, chunks)
    def _(index):
        first = pl.multiple_of(index * chunk, chunk)
        def add_values(n, p, at):
            acc[n] = acc[n] + mm(p, apart[n, pl.ds(first + at, size), :])

        size = min(512, chunk)
        last = None
        for at in range(0, chunk, size):
            for n in range(pairs):
                p, added = weigh(scores[n, :, pl.ds(first + at, size)], top[n])
                total[n] = total[n] + added
                if last:
                    last()
                last = functools.partial(add_values, n, p, at)
        last()

    for g in range(groups):
        at, lane = (g % pair) * stack, (g % pair) * width
        out = acc[g // pair, at : at + stack, lane : lane + width]
        out = out / jnp.sum(total[g // pair, at : at + stack, :], axis=1, keepdims=True)
        out = out.astype(jnp.bfloat16)
        for r in range(repeat):
            head = g * repeat + r
            attn[:, head * width : (head + 1) * width] = out[r * rows : (r + 1) * rows]
    w_copy.wait()
    value = mm(attn[...], w_buf[...])
    own_ref[...] = value
    send_ref[...] = value.astype(jnp.bfloat16)


def attention(queries, new_kv, pool, table, prompt_len, tails, tail_len, out_w):
    rows, heads, width = queries.shape
    n_pages, page, _, groups, _ = pool.shape
    conts, tail = tails.shape[:2]
    step = 2 * groups
    features = out_w.shape[1]
    quads = conts * NEW // 8
    pair = 2 if groups % 2 == 0 else 1
    pairs = groups // pair
    repeat = heads // groups
    stack = pair * repeat * rows
    return pl.pallas_call(
        functools.partial(
            attention_kernel, (rows, heads, groups, width, n_pages, page, conts, tail, pair)
        ),
        out_shape=(
            jax.ShapeDtypeStruct((rows, features), jnp.float32),
            jax.ShapeDtypeStruct((rows, features), jnp.bfloat16),
        ),
        in_specs=[SMEM, SMEM, SMEM, ANY, ANY, ANY, ANY, ANY],
        out_specs=(VMEM, VMEM),
        scratch_shapes=[
            pltpu.VMEM((n_pages * page * step, width), jnp.bfloat16),
            pltpu.VMEM((conts * tail * step, width), jnp.bfloat16),
            pltpu.VMEM(out_w.shape, jnp.bfloat16),
            pltpu.VMEM((rows * heads, width), jnp.bfloat16),
            pltpu.VMEM((rows * step, width), jnp.bfloat16),
            pltpu.VMEM((pairs, n_pages * page, pair * width), jnp.bfloat16),
            pltpu.VMEM((pairs, n_pages * page, pair * width), jnp.bfloat16),
            pltpu.VMEM((pairs, conts * tail, pair * width), jnp.bfloat16),
            pltpu.VMEM((pairs, conts * tail, pair * width), jnp.bfloat16),
            pltpu.VMEM((rows * heads, width), jnp.float32),
            pltpu.VMEM((pairs, stack, pair * width), jnp.float32),
            pltpu.VMEM((pairs, stack, pair * width), jnp.bfloat16),
            pltpu.VMEM((rows * step, width), jnp.float32),
            pltpu.VMEM((pairs, stack, rows), jnp.float32),
            pltpu.VMEM((pairs, quads, pair * repeat * 8, 8 // NEW * tail), jnp.float32),
            pltpu.VMEM((pairs, stack, n_pages * page), jnp.float32),
            pltpu.VMEM((pairs, stack, 128), jnp.float32),
            pltpu.VMEM((pairs, stack, 128), jnp.float32),
            pltpu.VMEM((pairs, stack, pair * width), jnp.float32),
            pltpu.VMEM((rows, heads * width), jnp.bfloat16),
            pltpu.SemaphoreType.DMA((n_pages,)),
            pltpu.SemaphoreType.DMA((quads,)),
            pltpu.SemaphoreType.DMA((3,)),
        ],
        compiler_params=pltpu.CompilerParams(vmem_limit_bytes=ATTENTION_VMEM),
        name="attention",
    )(
        table,
        prompt_len,
        tail_len,
        queries.reshape(rows * heads, width),
        new_kv.reshape(rows * step, width),
        pool.reshape(n_pages * page * step, width),
        tails.reshape(conts * tail * step, width),
        out_w,
    )


def norm_kernel(n, block, own, other, gain, *refs):
    normed, middle, whole = refs[n:]
    copies, rows, features = normed.shape
    mid = own[...] + other[...].astype(jnp.float32)
    scale = lax.rsqrt(jnp.mean(mid * mid, axis=1, keepdims=True) + EPS)
    whole[...] = mid
    start = pl.multiple_of(block[0] * features, features)
    part = whole[:, pl.ds(start, features)]
    out = (part * scale * gain[:, pl.ds(start, features)]).astype(jnp.bfloat16)
    for index in range(copies):
        normed[index] = out
    middle[...] = part


def normalize(block, own, other, gain, features, copies, ahead):
    rows = own.shape[0]
    return pl.pallas_call(
        functools.partial(norm_kernel, len(ahead)),
        out_shape=(
            jax.ShapeDtypeStruct((copies, rows, features), jnp.bfloat16),
            jax.ShapeDtypeStruct((rows, features), jnp.float32),
        ),
        in_specs=[SMEM, VMEM, VMEM, VMEM] + [ANY] * len(ahead),
        out_specs=(VMEM, VMEM),
        scratch_shapes=[pltpu.VMEM(own.shape, jnp.float32)],
        compiler_params=pltpu.CompilerParams(vmem_limit_bytes=4 * MIB),
        name="normalize",
    )(block, own, other, gain.astype(jnp.float32).reshape(1, -1), *ahead)


def units_kernel(n, block, *refs):
    pieces, gate_w, up_w, outs, held, sums = refs[:n], *refs[n : n + 2], refs[n + 2 : -2], *refs[-2:]
    at = 0
    for piece in pieces:
        held[at : at + piece.shape[0], :] = piece[...]
        at += piece.shape[0]
    units = gate_w.shape[1]
    sums[:, :units] = mm(held[...], gate_w[...])
    sums[:, units:] = mm(held[...], up_w[...])
    if len(outs) == 1:
        outs[0][...] = sums[...].astype(jnp.bfloat16)
        return
    keep, away = outs[0], outs[1:]
    half, part = at // 2, away[0].shape[0]
    start = pl.multiple_of((1 - block[0]) * half, half)
    for index, out in enumerate(away):
        out[...] = sums[pl.ds(start + index * part, part), :].astype(jnp.bfloat16)
    keep[...] = sums[pl.ds(pl.multiple_of(block[0] * half, half), half), :]


def partial_units(split, block, pieces, gate_w, up_w):
    tokens = sum(piece.shape[0] for piece in pieces)
    features, units = gate_w.shape
    if split:
        out_shape = (
            jax.ShapeDtypeStruct((tokens // 2, 2 * units), jnp.float32),
            *[jax.ShapeDtypeStruct((tokens // 2 // split, 2 * units), jnp.bfloat16)] * split,
        )
    else:
        out_shape = (jax.ShapeDtypeStruct((tokens, 2 * units), jnp.bfloat16),)
    return pl.pallas_call(
        functools.partial(units_kernel, len(pieces)),
        out_shape=out_shape,
        in_specs=[SMEM] + [VMEM] * (len(pieces) + 2),
        out_specs=(VMEM,) * len(out_shape),
        scratch_shapes=[
            pltpu.VMEM((tokens, features), jnp.bfloat16),
            pltpu.VMEM((tokens, 2 * units), jnp.float32),
        ],
        compiler_params=pltpu.CompilerParams(vmem_limit_bytes=UNITS_VMEM),
        cost_estimate=pl.CostEstimate(
            flops=4 * tokens * features * units,
            bytes_accessed=2 * tokens * features + 4 * features * units,
            transcendentals=0,
        ),
        name="gate_up",
    )(block, *pieces, gate_w, up_w)


def hidden_kernel(n, *refs):
    sums, others, out = refs[:n], refs[n:-1], refs[-1]
    units = out.shape[1]
    both = jnp.concatenate([part[...].astype(jnp.float32) for part in sums], axis=0)
    if others:
        both = both + jnp.concatenate([part[...].astype(jnp.float32) for part in others], axis=0)
    gate, up = both[:, :units], both[:, units:]
    out[...] = (gate / (1.0 + jnp.exp(-gate)) * up).astype(jnp.bfloat16)


def hidden_units(sums, others=()):
    tokens, units = sum(part.shape[0] for part in sums), sums[0].shape[1] // 2
    return pl.pallas_call(
        functools.partial(hidden_kernel, len(sums)),
        out_shape=jax.ShapeDtypeStruct((tokens, units), jnp.bfloat16),
        in_specs=[VMEM] * (len(sums) + len(others)),
        out_specs=VMEM,
        compiler_params=pltpu.CompilerParams(vmem_limit_bytes=4 * MIB),
        name="hidden",
    )(*sums, *others)


def down_kernel(order, flip, n, chip_ref, core_ref, *refs):
    parts, source, middle, down_w = refs[:n], *refs[n : n + 3]
    keep, send, hidden = refs[n + 3], refs[n + 4], refs[-1]
    tokens = hidden.shape[0]
    rows = middle.shape[0]
    chip, core = chip_ref[0], core_ref[0]
    at = 0
    for part in parts:
        hidden[at : at + part.shape[0], :] = part[...]
        at += part.shape[0]
    wanted = []
    for side in (core, 1 - core):
        for dest in order:
            dest = dest ^ chip if flip else dest
            wanted.append(source[pl.ds(pl.multiple_of((2 * dest + side) * rows, rows), rows), :])
    wanted = jnp.concatenate(wanted, axis=0)
    slot, local = wanted[:, 0:1], wanted[:, 1:2]
    count = wanted.shape[0]
    pick = (lax.broadcasted_iota(jnp.int32, (count, tokens), 1) == slot).astype(jnp.bfloat16)
    moved = mm(pick, hidden[...]).astype(jnp.bfloat16)
    mine = lax.broadcasted_iota(jnp.int32, (count, rows), 1) == local
    mine = mine.astype(jnp.bfloat16)
    high = middle[...].astype(jnp.bfloat16)
    low = (middle[...] - high.astype(jnp.float32)).astype(jnp.bfloat16)
    term = mm(moved, down_w[...]) + (mm(mine, high) + mm(mine, low))
    keep[...] = term[: count // 2]
    send[...] = term[count // 2 :].astype(jnp.bfloat16)


def down(order, flip, chip, core, parts, source, middle, down_w):
    units, features = down_w.shape
    tokens, rows = source.shape[0], middle.shape[0]
    shape = (len(order) * rows, features)
    return pl.pallas_call(
        functools.partial(down_kernel, order, flip, len(parts)),
        out_shape=(
            jax.ShapeDtypeStruct(shape, jnp.float32),
            jax.ShapeDtypeStruct(shape, jnp.bfloat16),
        ),
        in_specs=[SMEM, SMEM] + [VMEM] * (len(parts) + 3),
        out_specs=(VMEM, VMEM),
        scratch_shapes=[pltpu.VMEM((tokens, units), jnp.bfloat16)],
        compiler_params=pltpu.CompilerParams(vmem_limit_bytes=DOWN_VMEM),
        name="down",
    )(chip, core, *parts, source, middle, down_w)


def pack_kernel(n, *refs):
    pieces, out = refs[:n], refs[-1]
    at = 0
    for piece in pieces:
        out[at : at + piece.shape[0], :] = piece[...]
        at += piece.shape[0]


def pack(pieces, after=()):
    rows = sum(piece.shape[0] for piece in pieces)
    return pl.pallas_call(
        functools.partial(pack_kernel, len(pieces)),
        out_shape=jax.ShapeDtypeStruct((rows, pieces[0].shape[1]), pieces[0].dtype),
        in_specs=[VMEM] * len(pieces) + [ANY] * len(after),
        out_specs=VMEM,
        compiler_params=pltpu.CompilerParams(vmem_limit_bytes=4 * MIB),
        name="pack",
    )(*pieces, *after)


def add_kernel(keep, other, *outs):
    at = 0
    for out in outs:
        to = at + out.shape[0]
        out[...] = (keep[at:to, :] + other[at:to, :].astype(jnp.float32)).astype(out.dtype)
        at = to


def add_parts(keep, other, kinds):
    rows, features = keep.shape
    return pl.pallas_call(
        add_kernel,
        out_shape=tuple(
            jax.ShapeDtypeStruct((rows // len(kinds), features), kind) for kind in kinds
        ),
        in_specs=[VMEM, VMEM],
        out_specs=(VMEM,) * len(kinds),
        compiler_params=pltpu.CompilerParams(vmem_limit_bytes=4 * MIB),
        name="add_parts",
    )(keep, other)


def finish_kernel(n, *refs):
    parts, gain, score, moved, stats = refs[:n], *refs[n:]
    total = functools.reduce(jnp.add, [part[...].astype(jnp.float32) for part in parts])
    moved[...] = total
    weighted = gain[...].astype(jnp.float32) * score[...].astype(jnp.float32)
    lane = lax.broadcasted_iota(jnp.int32, (total.shape[0], 128), 1)
    squares = jnp.sum(total * total, axis=1, keepdims=True)
    terms = jnp.sum(total * weighted, axis=1, keepdims=True)
    stats[...] = jnp.transpose(jnp.where(lane == 0, squares, terms))[:8]


def finish(parts, gain, score):
    rows, features = parts[0].shape
    return pl.pallas_call(
        functools.partial(finish_kernel, len(parts)),
        out_shape=(
            jax.ShapeDtypeStruct((rows, features), jnp.float32),
            jax.ShapeDtypeStruct((8, rows), jnp.float32),
        ),
        in_specs=[VMEM] * (len(parts) + 2),
        out_specs=(VMEM, VMEM),
        compiler_params=pltpu.CompilerParams(vmem_limit_bytes=4 * MIB),
        name="finish",
    )(*parts, gain, score)


def shards(
    n_chip,
    n_blk,
    resid,
    queries,
    new_kv,
    prefix_pool,
    page_table,
    prompt_len,
    tail_pool,
    tail_len,
    migration,
    out_w,
    mlp_gain,
    gate_w,
    up_w,
    down_w,
    final_gain,
    score_w,
):
    rows = resid.shape[0]
    features = gate_w.shape[0]
    chip = lax.axis_index("chip").astype(jnp.int32)
    core = lax.axis_index("core").astype(jnp.int32)
    block = lax.axis_index("blk").astype(jnp.int32)
    direct = n_chip == 8 and n_blk == 2

    def to_chip(value, index):
        return lax.ppermute(value, "chip", [(i, i ^ index) for i in range(n_chip)])

    def swap(value, axis):
        return lax.ppermute(value, axis, [(0, 1), (1, 0)])

    own, send = attention(
        queries, new_kv, prefix_pool, page_table, prompt_len, tail_pool, tail_len, out_w
    )
    if direct:
        own, other = own + resid.astype(jnp.float32), swap(send, "blk")
    else:
        own, other = resid.astype(jnp.float32), lax.psum(send, "blk")
    token = migration[:, None] * NEW + jnp.arange(NEW, dtype=jnp.int32)[None, :]
    token = token.reshape(-1, 1)
    came, inner = token // rows, token % rows
    far, far_core = (came // 2) ^ chip, (came % 2) ^ core
    if direct:
        held = far // 2 % 2
        one = (far_core ^ block) * 4 + held * 2
        two = 8 + (held ^ block) * 4 + far_core * 2
        slot = jnp.where(far % 2 == 0, one, two) + far // 4
    else:
        slot = far_core * n_chip + came // 2
    local = token - (chip * 2 + core) * rows
    source = jnp.concatenate([slot * rows + inner, local], axis=1)
    chip, core, block = (index.reshape(1) for index in (chip, core, block))
    gain_row, score_row = final_gain.reshape(1, -1), score_w.reshape(1, -1)

    normed, middle = normalize(
        block,
        own,
        other,
        mlp_gain,
        features,
        1 if direct else n_chip,
        (chip, core, source, gain_row, score_row),
    )
    if direct:
        piece = normed.reshape(rows, features)
        z2, z3, z1 = (to_chip(piece, index) for index in (4, 6, 2))
        here = [pack([piece, z2]), pack([z1, z3])]
        there = [to_chip(part, 1) for part in here]

        def summed(split, pieces):
            keep, *away = partial_units(split, block, pieces, gate_w, up_w)
            return keep, *[swap(part, "blk") for part in away]

        first = summed(2, here + [swap(part, "core") for part in here])
        near = pack(there, first[1:])
        second, third = summed(1, [near]), summed(1, [swap(near, "core")])
        hidden = hidden_units(first[:1], first[1:])
        parts = [hidden, swap(hidden, "blk")]
        hidden = hidden_units((second[0], third[0]), (second[1], third[1]))
        parts += [hidden, swap(hidden, "blk")]
    else:
        near = lax.all_to_all(normed, "chip", 0, 0).reshape(n_chip * rows, features)
        units = partial_units(0, block, [near, swap(near, "core")], gate_w, up_w)[0]
        parts = [hidden_units([lax.psum(units, "blk")])]
    if direct:
        near, wide = (
            down(order, True, chip, core, parts, source, middle, down_w)
            for order in ((0, 2, 1, 3), (6, 4, 7, 5))
        )
        kinds = (jnp.float32, jnp.bfloat16)
        near = add_parts(near[0], swap(near[1], "core"), kinds)
        wide = add_parts(wide[0], swap(wide[1], "core"), kinds)
        mine, to2 = add_parts(near[0], to_chip(near[1], 1), kinds)
        to6, to4 = add_parts(wide[0], to_chip(wide[1], 1), (jnp.bfloat16, jnp.bfloat16))
        sums = [mine, to_chip(to4, 4), to_chip(to6, 6), to_chip(to2, 2)]
    else:
        order = tuple(range(n_chip))
        keep, away = down(order, False, chip, core, parts, source, middle, down_w)
        total = (keep + swap(away, "core").astype(jnp.float32)).astype(jnp.bfloat16)
        total = lax.all_to_all(total.reshape(n_chip, rows, features), "chip", 0, 0)
        sums = [jnp.sum(total.astype(jnp.float32), axis=0)]
    moved, stats = finish(sums, gain_row, score_row)
    stats = stats + swap(stats, "blk") if direct else lax.psum(stats, "blk")
    score = stats[1] * lax.rsqrt(stats[0] / D + EPS)
    return (moved.astype(jnp.bfloat16), score)


def solution(mesh):
    n_chip, n_blk = mesh.shape["dp"] // 2, mesh.shape["blk"]
    split = Mesh(mesh.devices.reshape(n_chip, 2, n_blk), ("chip", "core", "blk"))
    dp = ("chip", "core")
    return jax.shard_map(
        functools.partial(shards, n_chip, n_blk),
        mesh=split,
        in_specs=(
            P(dp, None),
            P(dp, "blk", None),
            P(dp, None, "blk", None),
            P(dp, None, None, "blk", None),
            P(dp, None),
            P(dp),
            P(dp, None, None, "blk", None),
            P(dp, None),
            P(),
            P("blk", None),
            P(),
            P("blk", dp),
            P("blk", dp),
            P(dp, "blk"),
            P("blk"),
            P("blk"),
        ),
        out_specs=(P(dp, "blk"), P(dp)),
        check_vma=False,
    )
```

```python
import functools
import math

import jax
import jax.numpy as jnp
from jax import lax
from jax.experimental import pallas as pl
from jax.experimental.pallas import tpu as pltpu
from jax.sharding import Mesh
from jax.sharding import PartitionSpec as P

D = 2048
NEW = 2
NEG = -1e30
EPS = 1e-06
MIB = 1 << 20
ATTENTION_VMEM = 60 * MIB
UNITS_VMEM = 6 * MIB
DOWN_VMEM = 12 * MIB

VMEM = pl.BlockSpec(memory_space=pltpu.VMEM)
SMEM = pl.BlockSpec(memory_space=pltpu.SMEM)
ANY = pl.BlockSpec(memory_space=pl.ANY)


def mm(a, b):
    return jnp.dot(a, b, preferred_element_type=jnp.float32)


def mm_t(a, b):
    return lax.dot_general(a, b, (((1,), (1,)), ((), ())), preferred_element_type=jnp.float32)


def attention_kernel(
    dims,
    table,
    prompt_len,
    tail_len,
    queries,
    new_kv,
    pool,
    tails,
    out_w,
    own_ref,
    send_ref,
    pages,
    tail_buf,
    w_buf,
    q_buf,
    new_buf,
    keys_apart,
    apart,
    tail_keys,
    tail_apart,
    q_wide,
    q_rows,
    q_pairs,
    new_wide,
    fresh_scores,
    tail_scores,
    scores,
    top,
    total,
    acc,
    attn,
    page_sems,
    tail_sems,
    sems,
):
    rows, heads, groups, width, n_pages, page, conts, tail, pair = dims
    repeat = heads // groups
    step = 2 * groups
    pairs = groups // pair
    stack = repeat * rows
    page_rows = page * step
    chunk_pages = math.gcd(16, n_pages)
    chunk = chunk_pages * page
    chunk_rows = chunk * step
    quad = 8 // NEW
    quads = conts // quad
    quad_keys = quad * tail
    quad_rows = quad_keys * step
    factor = math.log2(math.e) / math.sqrt(width)
    length = prompt_len[0]
    chunks = (length + chunk - 1) // chunk

    def page_copy(logical):
        physical = table[0, logical]
        return pltpu.make_async_copy(
            pool.at[pl.ds(pl.multiple_of(physical * page_rows, page_rows), page_rows), :],
            pages.at[pl.ds(pl.multiple_of(logical * page_rows, page_rows), page_rows), :],
            page_sems.at[logical],
        )

    def tail_copy(index):
        return pltpu.make_async_copy(
            tails.at[pl.ds(index * quad_rows, quad_rows), :],
            tail_buf.at[pl.ds(index * quad_rows, quad_rows), :],
            tail_sems.at[index],
        )

    q_copy = pltpu.make_async_copy(queries, q_buf, sems.at[0])
    new_copy = pltpu.make_async_copy(new_kv, new_buf, sems.at[1])
    w_copy = pltpu.make_async_copy(out_w, w_buf, sems.at[2])
    q_copy.start()
    new_copy.start()
    for index in range(quads):
        tail_copy(index).start()

    @pl.loop(0, chunks * chunk_pages)
    def _(logical):
        page_copy(logical).start()

    w_copy.start()

    block = 256
    tokens = block // step
    to = lax.broadcasted_iota(jnp.int32, (block, block), 0)
    came = lax.broadcasted_iota(jnp.int32, (block, block), 1)
    sort = (came == (to % tokens) * step + to // tokens).astype(jnp.bfloat16)

    def take_apart(buf, start, count, outs, places):
        def one(two):
            x0 = buf[pl.ds(start + two * 2 * block, block), :]
            x1 = buf[pl.ds(start + (two * 2 + 1) * block, block), :]
            y = mm(sort, jnp.concatenate([x0, x1], axis=1)).astype(jnp.bfloat16)
            for side in range(2):
                for j in range(step):
                    kind, g = j // groups, j % groups
                    t = pl.ds(places[kind] + (2 * two + side) * tokens, tokens)
                    lane = (g % pair) * width
                    outs[kind][g // pair, t, lane : lane + width] = y[
                        j * tokens : (j + 1) * tokens, side * width : (side + 1) * width
                    ]

        return [functools.partial(one, two) for two in range(count // (2 * block))]

    def alternate(works, others):
        shares = len(others) or 1
        for index in range(shares):
            for work in works[index * len(works) // shares : (index + 1) * len(works) // shares]:
                work()
            if others:
                others[index]()

    def blocks(x):
        return [x[:, i * 128 : (i + 1) * 128] for i in range(x.shape[1] // 128)]

    q_copy.wait()
    new_copy.wait()
    q_wide[...] = q_buf[...].astype(jnp.float32)
    new_wide[...] = new_buf[...].astype(jnp.float32)
    if pair > 1:
        q_rows[...] = jnp.zeros_like(q_rows)
    for g in range(groups):
        for r in range(repeat):
            at = (g % pair) * stack + r * rows
            lane = (g % pair) * width
            q_rows[g // pair, at : at + rows, lane : lane + width] = q_wide[
                pl.ds(g * repeat + r, rows, stride=heads), :
            ]

    q_pairs[...] = q_rows[...].astype(jnp.bfloat16)

    def fresh(first, n):
        parts = [
            new_wide[pl.ds(first + n * pair + i, rows, stride=step), :] for i in range(pair)
        ]
        return jnp.concatenate(parts, axis=1).astype(jnp.bfloat16)

    row = lax.broadcasted_iota(jnp.int32, (rows, rows), 0)
    key = lax.broadcasted_iota(jnp.int32, (rows, rows), 1)
    fresh_ok = (row // NEW == key // NEW) & (key <= row)
    fresh_ok = jnp.concatenate([fresh_ok] * (pair * repeat), axis=0)
    for n in range(pairs):
        s = jnp.where(fresh_ok, mm_t(q_pairs[n], fresh(0, n)) * factor, NEG)
        fresh_scores[n] = s
        top[n] = jnp.broadcast_to(jnp.max(s, axis=1, keepdims=True), top.shape[1:])

    def quad_places(index):
        starts = [i * rows + index * 8 for i in range(pair * repeat)]
        return [slice(at, at + 8) for at in starts]

    quad_row = lax.broadcasted_iota(jnp.int32, (8, quad_keys), 0)
    quad_key = lax.broadcasted_iota(jnp.int32, (8, quad_keys), 1)
    for index in range(quads):
        tail_copy(index).wait()
    def score_tails(index, n):
        reach = jnp.zeros((8, quad_keys), jnp.int32)
        for c in range(quad):
            reach = jnp.where(
                quad_key // tail == c, tail_len[0, index * quad + c] + c * tail, reach
            )
        ok = (quad_row // NEW == quad_key // tail) & (quad_key < reach)
        ok = jnp.concatenate([ok] * (pair * repeat), axis=0)
        keys = slice(index * quad_keys, (index + 1) * quad_keys)
        q = jnp.concatenate([q_rows[n, a, :] for a in quad_places(index)], axis=0)
        s = mm_t(q.astype(jnp.bfloat16), tail_keys[n, keys, :]) * factor
        s = jnp.where(ok, s, NEG)
        tail_scores[n, index] = s
        high = functools.reduce(jnp.maximum, blocks(s))
        for i, a in enumerate(quad_places(index)):
            top[n, a, :] = jnp.maximum(top[n, a, :], high[i * 8 : (i + 1) * 8])

    others = []
    for index in range(quads):
        outs, at = (tail_keys, tail_apart), index * quad_keys
        alternate(take_apart(tail_buf, index * quad_rows, quad_rows, outs, (at, at)), others)
        others = [functools.partial(score_tails, index, n) for n in range(pairs)]
    alternate([], others)

    part = min(256, chunk)
    place = lax.broadcasted_iota(jnp.int32, (8, part), 1)

    @pl.loop(0, chunks)
    def _(index):
        for i in range(chunk_pages):
            page_copy(index * chunk_pages + i).wait()
        first = pl.multiple_of(index * chunk, chunk)
        row = pl.multiple_of(index * chunk_rows, chunk_rows)

        def score(at, n):
            ok = place[0:1] < length - (index * chunk + at)
            s = mm_t(q_pairs[n], keys_apart[n, at : at + part, :]) * factor
            s = jnp.where(ok, s, NEG)
            scores[n, :, pl.ds(first + at, part)] = s
            top[n] = functools.reduce(jnp.maximum, blocks(s), top[n])

        others = []
        for at in range(0, chunk, part):
            outs, places = (keys_apart, apart), (at, first + at)
            alternate(take_apart(pages, row + at * step, part * step, outs, places), others)
            others = [functools.partial(score, at, n) for n in range(pairs)]
        alternate([], others)

    for n in range(pairs):
        high = jnp.broadcast_to(jnp.max(top[n], axis=1, keepdims=True), top.shape[1:])
        top[n] = high
        p = jnp.exp2(fresh_scores[n] - high[:, :rows])
        lane = lax.broadcasted_iota(jnp.int32, total.shape[1:], 1)
        total[n] = jnp.where(lane == 0, jnp.sum(p, axis=1, keepdims=True), 0.0)
        acc[n] = mm(p.astype(jnp.bfloat16), fresh(groups, n))

    def weigh(s, high):
        parts = [jnp.exp2(part - high) for part in blocks(s)]
        return jnp.concatenate(parts, axis=1).astype(jnp.bfloat16), functools.reduce(jnp.add, parts)

    weighed = []
    for index in range(quads):
        keys = slice(index * quad_keys, (index + 1) * quad_keys)
        for n in range(pairs):
            high = jnp.concatenate([top[n, a, :] for a in quad_places(index)], axis=0)
            p, added = weigh(tail_scores[n, index], high)
            weighed.append((index, n, keys, p, added))
    for index, n, keys, p, added in weighed:
        value = mm(p, tail_apart[n, keys, :])
        for i, a in enumerate(quad_places(index)):
            total[n, a, :] = total[n, a, :] + added[i * 8 : (i + 1) * 8]
            acc[n, a, :] = acc[n, a, :] + value[i * 8 : (i + 1) * 8]

    @pl.loop(0, chunks)
    def _(index):
        first = pl.multiple_of(index * chunk, chunk)
        def add_values(n, p, at):
            acc[n] = acc[n] + mm(p, apart[n, pl.ds(first + at, size), :])

        size = min(512, chunk)
        last = None
        for at in range(0, chunk, size):
            for n in range(pairs):
                p, added = weigh(scores[n, :, pl.ds(first + at, size)], top[n])
                total[n] = total[n] + added
                if last:
                    last()
                last = functools.partial(add_values, n, p, at)
        last()

    for g in range(groups):
        at, lane = (g % pair) * stack, (g % pair) * width
        out = acc[g // pair, at : at + stack, lane : lane + width]
        out = out / jnp.sum(total[g // pair, at : at + stack, :], axis=1, keepdims=True)
        out = out.astype(jnp.bfloat16)
        for r in range(repeat):
            head = g * repeat + r
            attn[:, head * width : (head + 1) * width] = out[r * rows : (r + 1) * rows]
    w_copy.wait()
    value = mm(attn[...], w_buf[...])
    own_ref[...] = value
    send_ref[...] = value.astype(jnp.bfloat16)


def attention(queries, new_kv, pool, table, prompt_len, tails, tail_len, out_w):
    rows, heads, width = queries.shape
    n_pages, page, _, groups, _ = pool.shape
    conts, tail = tails.shape[:2]
    step = 2 * groups
    features = out_w.shape[1]
    quads = conts * NEW // 8
    pair = 2 if groups % 2 == 0 else 1
    pairs = groups // pair
    repeat = heads // groups
    stack = pair * repeat * rows
    return pl.pallas_call(
        functools.partial(
            attention_kernel, (rows, heads, groups, width, n_pages, page, conts, tail, pair)
        ),
        out_shape=(
            jax.ShapeDtypeStruct((rows, features), jnp.float32),
            jax.ShapeDtypeStruct((rows, features), jnp.bfloat16),
        ),
        in_specs=[SMEM, SMEM, SMEM, ANY, ANY, ANY, ANY, ANY],
        out_specs=(VMEM, VMEM),
        scratch_shapes=[
            pltpu.VMEM((n_pages * page * step, width), jnp.bfloat16),
            pltpu.VMEM((conts * tail * step, width), jnp.bfloat16),
            pltpu.VMEM(out_w.shape, jnp.bfloat16),
            pltpu.VMEM((rows * heads, width), jnp.bfloat16),
            pltpu.VMEM((rows * step, width), jnp.bfloat16),
            pltpu.VMEM((pairs, n_pages * page, pair * width), jnp.bfloat16),
            pltpu.VMEM((pairs, n_pages * page, pair * width), jnp.bfloat16),
            pltpu.VMEM((pairs, conts * tail, pair * width), jnp.bfloat16),
            pltpu.VMEM((pairs, conts * tail, pair * width), jnp.bfloat16),
            pltpu.VMEM((rows * heads, width), jnp.float32),
            pltpu.VMEM((pairs, stack, pair * width), jnp.float32),
            pltpu.VMEM((pairs, stack, pair * width), jnp.bfloat16),
            pltpu.VMEM((rows * step, width), jnp.float32),
            pltpu.VMEM((pairs, stack, rows), jnp.float32),
            pltpu.VMEM((pairs, quads, pair * repeat * 8, 8 // NEW * tail), jnp.float32),
            pltpu.VMEM((pairs, stack, n_pages * page), jnp.float32),
            pltpu.VMEM((pairs, stack, 128), jnp.float32),
            pltpu.VMEM((pairs, stack, 128), jnp.float32),
            pltpu.VMEM((pairs, stack, pair * width), jnp.float32),
            pltpu.VMEM((rows, heads * width), jnp.bfloat16),
            pltpu.SemaphoreType.DMA((n_pages,)),
            pltpu.SemaphoreType.DMA((quads,)),
            pltpu.SemaphoreType.DMA((3,)),
        ],
        compiler_params=pltpu.CompilerParams(vmem_limit_bytes=ATTENTION_VMEM),
        name="attention",
    )(
        table,
        prompt_len,
        tail_len,
        queries.reshape(rows * heads, width),
        new_kv.reshape(rows * step, width),
        pool.reshape(n_pages * page * step, width),
        tails.reshape(conts * tail * step, width),
        out_w,
    )


def norm_kernel(n, block, own, other, gain, *refs):
    normed, middle, whole = refs[n:]
    copies, rows, features = normed.shape
    mid = own[...] + other[...].astype(jnp.float32)
    scale = lax.rsqrt(jnp.mean(mid * mid, axis=1, keepdims=True) + EPS)
    whole[...] = mid
    start = pl.multiple_of(block[0] * features, features)
    part = whole[:, pl.ds(start, features)]
    out = (part * scale * gain[:, pl.ds(start, features)]).astype(jnp.bfloat16)
    for index in range(copies):
        normed[index] = out
    middle[...] = part


def normalize(block, own, other, gain, features, copies, ahead):
    rows = own.shape[0]
    return pl.pallas_call(
        functools.partial(norm_kernel, len(ahead)),
        out_shape=(
            jax.ShapeDtypeStruct((copies, rows, features), jnp.bfloat16),
            jax.ShapeDtypeStruct((rows, features), jnp.float32),
        ),
        in_specs=[SMEM, VMEM, VMEM, VMEM] + [ANY] * len(ahead),
        out_specs=(VMEM, VMEM),
        scratch_shapes=[pltpu.VMEM(own.shape, jnp.float32)],
        compiler_params=pltpu.CompilerParams(vmem_limit_bytes=4 * MIB),
        name="normalize",
    )(block, own, other, gain.astype(jnp.float32).reshape(1, -1), *ahead)


def units_kernel(n, block, *refs):
    pieces, gate_w, up_w, outs, held, sums = refs[:n], *refs[n : n + 2], refs[n + 2 : -2], *refs[-2:]
    at = 0
    for piece in pieces:
        held[at : at + piece.shape[0], :] = piece[...]
        at += piece.shape[0]
    units = gate_w.shape[1]
    sums[:, :units] = mm(held[...], gate_w[...])
    sums[:, units:] = mm(held[...], up_w[...])
    if len(outs) == 1:
        outs[0][...] = sums[...].astype(jnp.bfloat16)
        return
    keep, away = outs[0], outs[1:]
    half, part = at // 2, away[0].shape[0]
    start = pl.multiple_of((1 - block[0]) * half, half)
    for index, out in enumerate(away):
        out[...] = sums[pl.ds(start + index * part, part), :].astype(jnp.bfloat16)
    keep[...] = sums[pl.ds(pl.multiple_of(block[0] * half, half), half), :]


def partial_units(split, block, pieces, gate_w, up_w):
    tokens = sum(piece.shape[0] for piece in pieces)
    features, units = gate_w.shape
    if split:
        out_shape = (
            jax.ShapeDtypeStruct((tokens // 2, 2 * units), jnp.float32),
            *[jax.ShapeDtypeStruct((tokens // 2 // split, 2 * units), jnp.bfloat16)] * split,
        )
    else:
        out_shape = (jax.ShapeDtypeStruct((tokens, 2 * units), jnp.bfloat16),)
    return pl.pallas_call(
        functools.partial(units_kernel, len(pieces)),
        out_shape=out_shape,
        in_specs=[SMEM] + [VMEM] * (len(pieces) + 2),
        out_specs=(VMEM,) * len(out_shape),
        scratch_shapes=[
            pltpu.VMEM((tokens, features), jnp.bfloat16),
            pltpu.VMEM((tokens, 2 * units), jnp.float32),
        ],
        compiler_params=pltpu.CompilerParams(vmem_limit_bytes=UNITS_VMEM),
        cost_estimate=pl.CostEstimate(
            flops=4 * tokens * features * units,
            bytes_accessed=2 * tokens * features + 4 * features * units,
            transcendentals=0,
        ),
        name="gate_up",
    )(block, *pieces, gate_w, up_w)


def hidden_kernel(n, *refs):
    sums, others, out = refs[:n], refs[n:-1], refs[-1]
    units = out.shape[1]
    both = jnp.concatenate([part[...].astype(jnp.float32) for part in sums], axis=0)
    if others:
        both = both + jnp.concatenate([part[...].astype(jnp.float32) for part in others], axis=0)
    gate, up = both[:, :units], both[:, units:]
    out[...] = (gate / (1.0 + jnp.exp(-gate)) * up).astype(jnp.bfloat16)


def hidden_units(sums, others=()):
    tokens, units = sum(part.shape[0] for part in sums), sums[0].shape[1] // 2
    return pl.pallas_call(
        functools.partial(hidden_kernel, len(sums)),
        out_shape=jax.ShapeDtypeStruct((tokens, units), jnp.bfloat16),
        in_specs=[VMEM] * (len(sums) + len(others)),
        out_specs=VMEM,
        compiler_params=pltpu.CompilerParams(vmem_limit_bytes=4 * MIB),
        name="hidden",
    )(*sums, *others)


def down_kernel(order, flip, n, chip_ref, core_ref, *refs):
    parts, source, middle, down_w = refs[:n], *refs[n : n + 3]
    keep, send, hidden = refs[n + 3], refs[n + 4], refs[-1]
    tokens = hidden.shape[0]
    rows = middle.shape[0]
    chip, core = chip_ref[0], core_ref[0]
    at = 0
    for part in parts:
        hidden[at : at + part.shape[0], :] = part[...]
        at += part.shape[0]
    wanted = []
    for side in (core, 1 - core):
        for dest in order:
            dest = dest ^ chip if flip else dest
            wanted.append(source[pl.ds(pl.multiple_of((2 * dest + side) * rows, rows), rows), :])
    wanted = jnp.concatenate(wanted, axis=0)
    slot, local = wanted[:, 0:1], wanted[:, 1:2]
    count = wanted.shape[0]
    pick = (lax.broadcasted_iota(jnp.int32, (count, tokens), 1) == slot).astype(jnp.bfloat16)
    moved = mm(pick, hidden[...]).astype(jnp.bfloat16)
    mine = lax.broadcasted_iota(jnp.int32, (count, rows), 1) == local
    mine = mine.astype(jnp.bfloat16)
    high = middle[...].astype(jnp.bfloat16)
    low = (middle[...] - high.astype(jnp.float32)).astype(jnp.bfloat16)
    term = mm(moved, down_w[...]) + (mm(mine, high) + mm(mine, low))
    keep[...] = term[: count // 2]
    send[...] = term[count // 2 :].astype(jnp.bfloat16)


def down(order, flip, chip, core, parts, source, middle, down_w):
    units, features = down_w.shape
    tokens, rows = source.shape[0], middle.shape[0]
    shape = (len(order) * rows, features)
    return pl.pallas_call(
        functools.partial(down_kernel, order, flip, len(parts)),
        out_shape=(
            jax.ShapeDtypeStruct(shape, jnp.float32),
            jax.ShapeDtypeStruct(shape, jnp.bfloat16),
        ),
        in_specs=[SMEM, SMEM] + [VMEM] * (len(parts) + 3),
        out_specs=(VMEM, VMEM),
        scratch_shapes=[pltpu.VMEM((tokens, units), jnp.bfloat16)],
        compiler_params=pltpu.CompilerParams(vmem_limit_bytes=DOWN_VMEM),
        name="down",
    )(chip, core, *parts, source, middle, down_w)


def pack_kernel(n, *refs):
    pieces, out = refs[:n], refs[-1]
    at = 0
    for piece in pieces:
        out[at : at + piece.shape[0], :] = piece[...]
        at += piece.shape[0]


def pack(pieces, after=()):
    rows = sum(piece.shape[0] for piece in pieces)
    return pl.pallas_call(
        functools.partial(pack_kernel, len(pieces)),
        out_shape=jax.ShapeDtypeStruct((rows, pieces[0].shape[1]), pieces[0].dtype),
        in_specs=[VMEM] * len(pieces) + [ANY] * len(after),
        out_specs=VMEM,
        compiler_params=pltpu.CompilerParams(vmem_limit_bytes=4 * MIB),
        name="pack",
    )(*pieces, *after)


def add_kernel(keep, other, *outs):
    at = 0
    for out in outs:
        to = at + out.shape[0]
        out[...] = (keep[at:to, :] + other[at:to, :].astype(jnp.float32)).astype(out.dtype)
        at = to


def add_parts(keep, other, kinds):
    rows, features = keep.shape
    return pl.pallas_call(
        add_kernel,
        out_shape=tuple(
            jax.ShapeDtypeStruct((rows // len(kinds), features), kind) for kind in kinds
        ),
        in_specs=[VMEM, VMEM],
        out_specs=(VMEM,) * len(kinds),
        compiler_params=pltpu.CompilerParams(vmem_limit_bytes=4 * MIB),
        name="add_parts",
    )(keep, other)


def finish_kernel(n, *refs):
    parts, gain, score, moved, stats = refs[:n], *refs[n:]
    total = functools.reduce(jnp.add, [part[...].astype(jnp.float32) for part in parts])
    moved[...] = total
    weighted = gain[...].astype(jnp.float32) * score[...].astype(jnp.float32)
    lane = lax.broadcasted_iota(jnp.int32, (total.shape[0], 128), 1)
    squares = jnp.sum(total * total, axis=1, keepdims=True)
    terms = jnp.sum(total * weighted, axis=1, keepdims=True)
    stats[...] = jnp.transpose(jnp.where(lane == 0, squares, terms))[:8]


def finish(parts, gain, score):
    rows, features = parts[0].shape
    return pl.pallas_call(
        functools.partial(finish_kernel, len(parts)),
        out_shape=(
            jax.ShapeDtypeStruct((rows, features), jnp.float32),
            jax.ShapeDtypeStruct((8, rows), jnp.float32),
        ),
        in_specs=[VMEM] * (len(parts) + 2),
        out_specs=(VMEM, VMEM),
        compiler_params=pltpu.CompilerParams(vmem_limit_bytes=4 * MIB),
        name="finish",
    )(*parts, gain, score)


def shards(
    n_chip,
    n_blk,
    resid,
    queries,
    new_kv,
    prefix_pool,
    page_table,
    prompt_len,
    tail_pool,
    tail_len,
    migration,
    out_w,
    mlp_gain,
    gate_w,
    up_w,
    down_w,
    final_gain,
    score_w,
):
    rows = resid.shape[0]
    features = gate_w.shape[0]
    chip = lax.axis_index("chip").astype(jnp.int32)
    core = lax.axis_index("core").astype(jnp.int32)
    block = lax.axis_index("blk").astype(jnp.int32)
    direct = n_chip == 8 and n_blk == 2

    def to_chip(value, index):
        return lax.ppermute(value, "chip", [(i, i ^ index) for i in range(n_chip)])

    def swap(value, axis):
        return lax.ppermute(value, axis, [(0, 1), (1, 0)])

    own, send = attention(
        queries, new_kv, prefix_pool, page_table, prompt_len, tail_pool, tail_len, out_w
    )
    if direct:
        own, other = own + resid.astype(jnp.float32), swap(send, "blk")
    else:
        own, other = resid.astype(jnp.float32), lax.psum(send, "blk")
    token = migration[:, None] * NEW + jnp.arange(NEW, dtype=jnp.int32)[None, :]
    token = token.reshape(-1, 1)
    came, inner = token // rows, token % rows
    far, far_core = (came // 2) ^ chip, (came % 2) ^ core
    if direct:
        held = far // 2 % 2
        one = (far_core ^ block) * 4 + held * 2
        two = 8 + (held ^ block) * 4 + far_core * 2
        slot = jnp.where(far % 2 == 0, one, two) + far // 4
    else:
        slot = far_core * n_chip + came // 2
    local = token - (chip * 2 + core) * rows
    source = jnp.concatenate([slot * rows + inner, local], axis=1)
    chip, core, block = (index.reshape(1) for index in (chip, core, block))
    gain_row, score_row = final_gain.reshape(1, -1), score_w.reshape(1, -1)

    normed, middle = normalize(
        block,
        own,
        other,
        mlp_gain,
        features,
        1 if direct else n_chip,
        (chip, core, source, gain_row, score_row),
    )
    if direct:
        piece = normed.reshape(rows, features)
        z2, z3, z1 = (to_chip(piece, index) for index in (4, 6, 2))
        here = [pack([piece, z2]), pack([z1, z3])]
        there = [to_chip(part, 1) for part in here]

        def summed(split, pieces):
            keep, *away = partial_units(split, block, pieces, gate_w, up_w)
            return keep, *[swap(part, "blk") for part in away]

        first = summed(2, here + [swap(part, "core") for part in here])
        near = pack(there, first[1:])
        second, third = summed(1, [near]), summed(1, [swap(near, "core")])
        hidden = hidden_units(first[:1], first[1:])
        parts = [hidden, swap(hidden, "blk")]
        hidden = hidden_units((second[0], third[0]), (second[1], third[1]))
        parts += [hidden, swap(hidden, "blk")]
    else:
        near = lax.all_to_all(normed, "chip", 0, 0).reshape(n_chip * rows, features)
        units = partial_units(0, block, [near, swap(near, "core")], gate_w, up_w)[0]
        parts = [hidden_units([lax.psum(units, "blk")])]
    if direct:
        near, wide = (
            down(order, True, chip, core, parts, source, middle, down_w)
            for order in ((0, 2, 1, 3), (6, 4, 7, 5))
        )
        kinds = (jnp.float32, jnp.bfloat16)
        near = add_parts(near[0], swap(near[1], "core"), kinds)
        wide = add_parts(wide[0], swap(wide[1], "core"), kinds)
        mine, to2 = add_parts(near[0], to_chip(near[1], 1), kinds)
        to6, to4 = add_parts(wide[0], to_chip(wide[1], 1), (jnp.bfloat16, jnp.bfloat16))
        sums = [mine, to_chip(to4, 4), to_chip(to6, 6), to_chip(to2, 2)]
    else:
        order = tuple(range(n_chip))
        keep, away = down(order, False, chip, core, parts, source, middle, down_w)
        total = (keep + swap(away, "core").astype(jnp.float32)).astype(jnp.bfloat16)
        total = lax.all_to_all(total.reshape(n_chip, rows, features), "chip", 0, 0)
        sums = [jnp.sum(total.astype(jnp.float32), axis=0)]
    moved, stats = finish(sums, gain_row, score_row)
    stats = stats + swap(stats, "blk") if direct else lax.psum(stats, "blk")
    score = stats[1] * lax.rsqrt(stats[0] / D + EPS)
    return (moved.astype(jnp.bfloat16), score)


def solution(mesh):
    n_chip, n_blk = mesh.shape["dp"] // 2, mesh.shape["blk"]
    split = Mesh(mesh.devices.reshape(n_chip, 2, n_blk), ("chip", "core", "blk"))
    dp = ("chip", "core")
    return jax.shard_map(
        functools.partial(shards, n_chip, n_blk),
        mesh=split,
        in_specs=(
            P(dp, None),
            P(dp, "blk", None),
            P(dp, None, "blk", None),
            P(dp, None, None, "blk", None),
            P(dp, None),
            P(dp),
            P(dp, None, None, "blk", None),
            P(dp, None),
            P(),
            P("blk", None),
            P(),
            P("blk", dp),
            P("blk", dp),
            P(dp, "blk"),
            P("blk"),
            P("blk"),
        ),
        out_specs=(P(dp, "blk"), P(dp)),
        check_vma=False,
    )
```
